32 devices in a mesh: seq: 8 (over z, y), fsdp: 4 (over x, core).
Axes of the slice: x: 2, y: 2, z: 4, core: 2. Of those that a mesh axis runs over, the one named last changes fastest.
Arguments:
- inputs: bfloat16 [4, 1024, 2560], P('fsdp', 'seq'), may hold values from -6 to 6
- block_flags: int32 [4, 16], P('fsdp', 'seq'), may hold values from 0 to 1, as said below
- decay_seed: int32 [2560], replicated, may hold values from 0 to 7
- vectors: float32 [10, 2560], replicated, may hold values from -3 to 3, as said below
- in_y: bfloat16 [2560, 2560], P(None, 'fsdp'), may hold values from -0.125 to 0.125
- in_x: bfloat16 [2560, 2560], P(None, 'fsdp'), may hold values from -0.125 to 0.125
- gate_weight: bfloat16 [2560, 512], P(None, 'fsdp'), may hold values from -0.375 to 0.375
- out_proj: bfloat16 [2560, 2560], P(None, 'fsdp'), may hold values from -0.5 to 0.5
- mlp_gate: bfloat16 [2560, 7680], P(None, 'fsdp'), may hold values from -0.125 to 0.125
- mlp_up: bfloat16 [2560, 7680], P(None, 'fsdp'), may hold values from -0.125 to 0.125
- mlp_down: bfloat16 [2560, 7680], P(None, 'fsdp'), may hold values from -0.125 to 0.125
- cotangent: bfloat16 [4, 1024, 2560], P('fsdp', 'seq'), may hold values from -6 to 6
Outputs:
- output: bfloat16 [4, 1024, 2560], P('fsdp', 'seq')
- input_grad: bfloat16 [4, 1024, 2560], P('fsdp', 'seq')
- vectors_grad: float32 [10, 2560], replicated
- in_y_grad: float32 [2560, 2560], P(('seq', 'fsdp'))
- in_x_grad: float32 [2560, 2560], P(('seq', 'fsdp'))
- gate_grad: float32 [2560, 512], P(('seq', 'fsdp'))
- out_proj_grad: float32 [2560, 2560], P(('seq', 'fsdp'))
- mlp_gate_grad: float32 [2560, 7680], P('seq', 'fsdp')
- mlp_up_grad: float32 [2560, 7680], P('seq', 'fsdp')
- mlp_down_grad: float32 [2560, 7680], P('seq', 'fsdp')
The draws below stay inside these ranges and needn't reach their ends.
Inputs may be any that keep to these rules, and one draw needn't show every extreme that they name: `block_flags`: in each group block 0 is flagged, one more flag may lie among the first 2 blocks and one more among the last 1 block; no other block is flagged. `vectors`: rows 0 and 1 lie in 0.6 to 1.4.
All inputs are finite; a program needn't handle non-finite values.
Results may differ from the reference program's by a relative error of at most 0.015.
Values may be sent and summed in bfloat16 or wider, within the bound.
No kernel may reach another device: no remote copies, remote signals or barrier semaphores. Data moves between devices by JAX's collectives and lax.ppermute only.
A program may use at most 640 MiB of HBM per device.

```python
import jax
import jax.numpy as jnp
from jax import lax

D = 2560
FF = 7680
HEADS = 10
BLK = 256
FBLK = 64
GROUPS = 4
SEQ_TOK = 1024
BLK_DEV = 2
GROUP_BLK = 16


def draw_block_flags(key, part):
    key = jax.random.fold_in(key, 17)
    key_first, key_last = jax.random.split(key)
    first = jax.random.randint(key_first, (GROUPS, 1), 0, BLK_DEV)
    last = jax.random.randint(key_last, (GROUPS, 1), GROUP_BLK - BLK_DEV + 1, GROUP_BLK + 1)
    position = jnp.arange(GROUP_BLK)[None, :]
    starts = (position == 0) | (position == first) | (position == last)
    return starts.astype(jnp.int32)


def draw_vectors(key, part):
    key = jax.random.fold_in(key, 29)
    key_noise, key_gain = jax.random.split(key)
    noise = jnp.clip(jax.random.normal(key_noise, (8, D), jnp.float32), -3.0, 3.0)
    gains = 1.0 + 0.4 * jax.random.uniform(key_gain, (2, D), jnp.float32, -1.0, 1.0)
    spreads = jnp.array([0.5, 0.5, 0.5, 0.5, 0.3, 1.0, 1.0, 0.5], jnp.float32)[:, None]
    return jnp.concatenate([gains, noise * spreads], axis=0)


def set_ends(values, stream_key, smallest, top_value):
    longest = values.shape.index(max(values.shape))
    spots = []
    for shift in (0, 1):
        where = [jax.random.randint(jax.random.fold_in(stream_key, axis), (), 0, length) for axis, length in enumerate(values.shape)]
        where[longest] = (where[longest] + shift) % values.shape[longest]
        spots.append(tuple(where))
    return values.at[spots[0]].set(smallest).at[spots[1]].set(top_value)


def block_levels(rng, extent, cuts, least, top_value):
    level, own = 1.0, jax.random.fold_in(rng, 6)
    for dim, shards_of in cuts:
        draws = jnp.exp(jax.random.uniform(jax.random.fold_in(own, dim), (shards_of,), jnp.float32, least / len(cuts), top_value / len(cuts)))
        level = level * jnp.repeat(draws, extent[dim] // shards_of).reshape([-1 if axis == dim else 1 for axis in range(len(extent))])
    return level


def normal_values(rng, shape, spread, most, pieces=(), held_as=jnp.bfloat16):
    drawn = jax.random.normal(rng, shape, jnp.float32) * spread
    if len(pieces) > 0:
        drawn = block_levels(rng, shape, pieces, -0.22, 0.18) * drawn
    return jnp.clip(drawn, min=-most, max=most).astype(held_as)


def setup_inputs(seed: int = 0) -> dict:
    arg_keys = jax.random.split(jax.random.key(seed), 13)
    return {
        "inputs": normal_values(arg_keys[0], (GROUPS, SEQ_TOK, D), 1.0, 6.0, ((0, 4), (1, 8))),
        "block_flags": draw_block_flags(jax.random.fold_in(arg_keys[12], 71), 0),
        "decay_seed": set_ends(jax.random.randint(arg_keys[2], (D,), 0, 8), jax.random.fold_in(arg_keys[2], 1), 0, 7).astype(jnp.int32),
        "vectors": draw_vectors(jax.random.fold_in(arg_keys[12], 71), 0),
        "in_y": normal_values(arg_keys[4], (D, D), D ** -0.5, 0.125, ((1, 4),)),
        "in_x": normal_values(arg_keys[5], (D, D), D ** -0.5, 0.125, ((1, 4),)),
        "gate_weight": normal_values(arg_keys[6], (D, 2 * BLK), BLK ** -0.5, 0.375, ((1, 4),)),
        "out_proj": normal_values(arg_keys[7], (D, D), (D // 16) ** -0.5, 0.5, ((1, 4),)),
        "mlp_gate": normal_values(arg_keys[8], (D, FF), D ** -0.5, 0.125, ((1, 4),)),
        "mlp_up": normal_values(arg_keys[9], (D, FF), D ** -0.5, 0.125, ((1, 4),)),
        "mlp_down": normal_values(arg_keys[10], (D, FF), (FF // 4) ** -0.5, 0.125, ((1, 4),)),
        "cotangent": normal_values(arg_keys[11], (GROUPS, SEQ_TOK, D), 1.0, 6.0, ((0, 4), (1, 8))),
    }


@jax.custom_vjp
def low(v):
    return lax.optimization_barrier(v.astype(jnp.bfloat16)).astype(jnp.float32)

@jax.custom_vjp
def low_back(v):
    return v

def low_keep(v):
    return (low(v), None)

def low_pass(kept, grad):
    return (grad,)

def back_keep(v):
    return (v, None)

def back_low(kept, grad):
    return (low(grad),)
low.defvjp(low_keep, low_pass)
low_back.defvjp(back_keep, back_low)
epsilon = 1e-06
highest = lax.Precision.HIGHEST

def chain_link(earlier, later):
    return (earlier[0] * later[0], later[0] * earlier[1] + later[1])

def matmul(left, right):
    return jnp.dot(left, right, precision=highest, preferred_element_type=jnp.float32)

def rms_scaled(values):
    return values * lax.rsqrt(lax.optimization_barrier(jnp.mean(values * values, axis=-1, keepdims=True)) + epsilon)

def gelu_tanh(values):
    return jax.nn.gelu(values, approximate=True)

def reference(inputs, block_flags, decay_seed, vectors, in_y, in_x, gate_weight, out_proj, mlp_gate, mlp_up, mlp_down, cotangent):
    total = inputs.shape[0] * inputs.shape[1]
    width = inputs.shape[2]
    token_flag = jnp.repeat(block_flags.reshape(-1), FBLK)
    offset = jnp.arange(total) % FBLK
    start_mask = ((token_flag == 1) & (offset == 0)).astype(jnp.float32)[:, None]
    keep_mask = 1.0 - start_mask
    valid_masks = [1.0 - ((token_flag == 1) & (offset < lag)).astype(jnp.float32)[:, None] for lag in range(4)]
    seed_float = decay_seed.astype(jnp.float32)

    def forward(x_in, vector_rows, weight_y, weight_x, weight_gate, weight_out, weight_mg, weight_mu, weight_md):
        normed_one = low(rms_scaled(x_in) * vector_rows[0])
        y_pre = low_back(matmul(normed_one, weight_y))
        x_low = low(low_back(matmul(normed_one, weight_x)))
        padded = jnp.concatenate([jnp.zeros((3, width), jnp.float32), x_low], axis=0)
        conv_out = vector_rows[6] + jnp.zeros((total, width), jnp.float32)
        for lag in range(4):
            conv_out = conv_out + vector_rows[2 + lag] * padded[3 - lag:3 - lag + total] * valid_masks[lag]
        conv_low = low(conv_out)
        heads_in = conv_low.reshape(total, HEADS, BLK)
        blocks = weight_gate.reshape(HEADS, BLK, 2 * BLK)
        gate_prod = low_back(jnp.einsum('thi,hij->thj', heads_in, blocks, precision=highest))
        input_gate = jax.nn.sigmoid(gate_prod[:, :, :BLK].reshape(total, width) + vector_rows[7])
        decay_gate = jax.nn.sigmoid(gate_prod[:, :, BLK:].reshape(total, width) + vector_rows[8])
        rate = jax.nn.softplus(-5.0 - seed_float + vector_rows[9])
        log_decay = -8.0 * decay_gate * rate
        decay = jnp.exp(log_decay) * keep_mask
        scale_in = jnp.sqrt(keep_mask * -jnp.expm1(2.0 * log_decay) + start_mask)
        drive = scale_in * input_gate * conv_low
        products, state = lax.associative_scan(chain_link, (decay, drive), axis=0)
        mixed = low(state * gelu_tanh(y_pre))
        middle = x_in + low_back(matmul(mixed, weight_out))
        normed_two = low(rms_scaled(middle) * vector_rows[1])
        gate_val = low_back(matmul(normed_two, weight_mg))
        up_val = low_back(matmul(normed_two, weight_mu))
        hidden = low(gelu_tanh(gate_val) * up_val)
        return middle + low_back(matmul(hidden, weight_md.T))
    floats = (inputs.reshape(total, width).astype(jnp.float32), vectors.astype(jnp.float32), in_y.astype(jnp.float32), in_x.astype(jnp.float32), gate_weight.astype(jnp.float32), out_proj.astype(jnp.float32), mlp_gate.astype(jnp.float32), mlp_up.astype(jnp.float32), mlp_down.astype(jnp.float32))
    result, pullback = jax.vjp(forward, *floats)
    grads = pullback(cotangent.reshape(total, width).astype(jnp.float32))
    output = result.astype(jnp.bfloat16).reshape(inputs.shape)
    input_grad = grads[0].astype(jnp.bfloat16).reshape(inputs.shape)
    return (output, input_grad, grads[1], grads[2], grads[3], grads[4], grads[5], grads[6], grads[7], grads[8])
```

```python
import functools

import jax
import jax.numpy as jnp
from jax import lax
from jax.experimental import pallas as pl
from jax.experimental.pallas import tpu as pltpu
from jax.sharding import PartitionSpec as P

HEADS = 10
BLK = 256
FBLK = 64
EPS = 1e-06
ALL = ("seq", "fsdp")
F32 = jnp.float32
BF16 = jnp.bfloat16
GELU_C = 0.7978845608028654
GELU_A = 0.044715


def norm_scale(values):
    inverse = lax.rsqrt(jnp.mean(values * values, axis=-1, keepdims=True) + EPS)
    return (values * inverse, inverse)


def norm_back(grad_normed, scaled, inverse, gain_row):
    grad_gain = jnp.sum(grad_normed * scaled, axis=0)
    inner_term = grad_normed * gain_row
    grad_input = inverse * (
        inner_term - scaled * jnp.mean(inner_term * scaled, axis=-1, keepdims=True)
    )
    return (grad_input, grad_gain)


def gelu_pair(values):
    square = values * values
    t = jnp.tanh(GELU_C * values * (1.0 + GELU_A * square))
    half = 0.5 * (1.0 + t)
    slope = half + 0.5 * values * (1.0 - t * t) * GELU_C * (1.0 + 3.0 * GELU_A * square)
    return (values * half, slope)


def dot(left, right):
    return jnp.dot(left, right, preferred_element_type=F32)


def dot_rows(left, right):
    return lax.dot_general(left, right, (((0,), (0,)), ((), ())), preferred_element_type=F32)


def dot_cols(left, right):
    return lax.dot_general(left, right, (((1,), (1,)), ((), ())), preferred_element_type=F32)


class Lay:
    def __init__(self):
        self.seq = lax.axis_size("seq")
        self.nz = self.seq // 2
        seq, fsdp = (lax.axis_index("seq"), lax.axis_index("fsdp"))
        self.z, self.y = (seq // 2, seq % 2)
        self.x, self.c = (fsdp // 2, fsdp % 2)

    def pairs(self, target):
        found = []
        for s in range(self.seq):
            for f in range(4):
                z, y, x, c = (s // 2, s % 2, f // 2, f % 2)
                to = target(z, y, x, c)
                if to is not None:
                    found.append((s * 4 + f, ((to[0] * 2 + to[1]) * 2 + to[2]) * 2 + to[3]))
        return found

    def send(self, value, target):
        return lax.ppermute(value, ALL, self.pairs(target))

    def over_c(self, value):
        return self.send(value, lambda z, y, x, c: (z, y, x, 1 - c))

    def over_x(self, value):
        return self.send(value, lambda z, y, x, c: (z, y, 1 - x, c))

    def over_y(self, value):
        return self.send(value, lambda z, y, x, c: (z, 1 - y, x, c))

    def over_seq_bit(self, value, bit):
        def to(z, y, x, c):
            other = (2 * z + y) ^ bit
            return (other // 2, other % 2, x, c)

        return self.send(value, to)

    def over_seq(self, value, by):
        def to(z, y, x, c):
            other = 2 * z + y + by
            return (other // 2, other % 2, x, c) if 0 <= other < self.seq else None

        return self.send(value, to)


def row_iota(rows, cols):
    return lax.broadcasted_iota(jnp.int32, (rows, cols), 0)


def token_masks(flags_ref, g, rows, cols):
    row = row_iota(rows, cols)
    block = row // FBLK
    offset = row % FBLK
    flagged = jnp.zeros((rows, cols), F32)
    for b in range(rows // FBLK):
        flagged = jnp.where(block == b, flags_ref[g, b], flagged)
    valid = [jnp.where(offset < lag, 1.0 - flagged, 1.0) for lag in range(4)]
    start = jnp.where(offset == 0, flagged, 0.0)
    return start, valid


def neg_expm1(v):
    series = 1.0 + v * (1.0 / 6.0)
    for n in (5.0, 4.0, 3.0, 2.0):
        series = 1.0 + v * (1.0 / n) * series
    return jnp.where(v > -0.25, -v * series, 1.0 - jnp.exp(v))


def shifted_inputs(xl_ref, halo_ref, g):
    ext = jnp.concatenate([halo_ref[g].astype(F32), xl_ref[g].astype(F32)], axis=0)
    pad = halo_ref.shape[1]
    return [ext[pad:] if k == 0 else pltpu.roll(ext, k, 0)[pad:] for k in range(4)]


def mixer_forward(flags_ref, xl_ref, halo_ref, gw_ref, vec_ref, rate_ref,
                  conv_ref, ig_ref, dg_ref, prod_ref, local_ref, sum_ref):
    groups, rows, cols = xl_ref.shape
    row = row_iota(rows, cols)
    for g in range(groups):
        start, valid = token_masks(flags_ref, g, rows, cols)
        lagged = shifted_inputs(xl_ref, halo_ref, g)
        conv = vec_ref[6:7, :] + jnp.zeros((rows, cols), F32)
        for k in range(4):
            conv = conv + vec_ref[2 + k : 3 + k, :] * lagged[k] * valid[k]
        conv_low = conv.astype(BF16)
        conv_ref[g] = conv_low
        prod = jnp.dot(conv_low, gw_ref[...], preferred_element_type=F32)
        ig = jax.nn.sigmoid(prod[:, :cols] + vec_ref[7:8, :])
        dg = jax.nn.sigmoid(prod[:, cols:] + vec_ref[8:9, :])
        ig_ref[g] = ig
        dg_ref[g] = dg
        keep = 1.0 - start
        log_decay = -8.0 * dg * rate_ref[0:1, :]
        p = jnp.exp(log_decay) * keep
        s = jnp.sqrt(keep * neg_expm1(2.0 * log_decay) + start) * ig * conv_low.astype(F32)
        step = 1
        while step < rows:
            inside = row >= step
            p_prev = jnp.where(inside, pltpu.roll(p, step, 0), 1.0)
            s_prev = jnp.where(inside, pltpu.roll(s, step, 0), 0.0)
            s = p * s_prev + s
            p = p * p_prev
            step *= 2
        prod_ref[g] = p
        local_ref[g] = s
        sum_ref[g : g + 1, :] = p[rows - 1 :, :]
        sum_ref[groups + g : groups + g + 1, :] = s[rows - 1 :, :]


def mixer_back_scan(flags_ref, gm_ref, y_ref, dg_ref, prod_ref, local_ref, sin_ref, rate_ref,
                    gy_ref, bprod_ref, blocal_ref, sum_ref):
    groups, rows, cols = gm_ref.shape
    row = row_iota(rows, cols)
    for g in range(groups):
        start, _ = token_masks(flags_ref, g, rows, cols)
        state = local_ref[g] + prod_ref[g] * sin_ref[g : g + 1, :]
        gelu, slope = gelu_pair(y_ref[g])
        gm = gm_ref[g]
        gy_ref[g] = (gm * state * slope).astype(BF16)
        decay = jnp.exp(-8.0 * dg_ref[g] * rate_ref[0:1, :]) * (1.0 - start)
        s = gm * gelu
        p = jnp.where(row == rows - 1, 1.0, pltpu.roll(decay, rows - 1, 0))
        step = 1
        while step < rows:
            inside = row < rows - step
            p_next = jnp.where(inside, pltpu.roll(p, rows - step, 0), 1.0)
            s_next = jnp.where(inside, pltpu.roll(s, rows - step, 0), 0.0)
            s = p * s_next + s
            p = p * p_next
            step *= 2
        bprod_ref[g] = p
        blocal_ref[g] = s
        sum_ref[g : g + 1, :] = decay[:1, :] * p[:1, :]
        sum_ref[groups + g : groups + g + 1, :] = decay[:1, :] * s[:1, :]


def mixer_backward(flags_ref, bprod_ref, blocal_ref, bin_ref, prod_ref, local_ref, sin_ref,
                   ig_ref, dg_ref, conv_ref, xl_ref, halo_ref, gw_ref, vec_ref, rate_ref,
                   gip_ref, gdp_ref, gx_ref, tail_ref, edge_ref, rows_ref):
    groups, rows, cols = xl_ref.shape
    row = row_iota(rows, cols)
    sums = [jnp.zeros((1, cols), F32) for _ in range(8)]
    tail = tail_ref.shape[1]
    pad = edge_ref.shape[1]
    for g in range(groups):
        start, valid = token_masks(flags_ref, g, rows, cols)
        keep = 1.0 - start
        rate = rate_ref[0:1, :]
        state_in = sin_ref[g : g + 1, :]
        state = local_ref[g] + prod_ref[g] * state_in
        prev = jnp.where(row == 0, state_in, pltpu.roll(state, 1, 0))
        sg = blocal_ref[g] + bprod_ref[g] * bin_ref[g : g + 1, :]
        ig, dg = (ig_ref[g], dg_ref[g])
        cf = conv_ref[g].astype(F32)
        log_decay = -8.0 * dg * rate
        decay = jnp.exp(log_decay) * keep
        scale = jnp.sqrt(keep * neg_expm1(2.0 * log_decay) + start)
        gscale = sg * ig * cf
        glog = sg * prev * decay - gscale * keep * jnp.exp(2.0 * log_decay) / scale
        gip = sg * scale * cf * ig * (1.0 - ig)
        gdp = -8.0 * rate * glog * dg * (1.0 - dg)
        gip_low, gdp_low = (gip.astype(BF16), gdp.astype(BF16))
        gip_ref[g] = gip_low
        gdp_ref[g] = gdp_low
        gconv = sg * scale * ig + lax.dot_general(
            jnp.concatenate([gip_low, gdp_low], axis=1), gw_ref[...],
            (((1,), (1,)), ((), ())), preferred_element_type=F32)
        lagged = shifted_inputs(xl_ref, halo_ref, g)
        spread = jnp.zeros((rows + pad, cols), F32)
        for k in range(4):
            masked = gconv * valid[k]
            sums[k] = sums[k] + jnp.sum(masked * lagged[k], axis=0, keepdims=True)
            full = jnp.concatenate(
                [jnp.zeros((pad, cols), F32), vec_ref[2 + k : 3 + k, :] * masked], axis=0)
            spread = spread + (full if k == 0 else pltpu.roll(full, rows + pad - k, 0))
        gx_ref[g] = spread[pad:].astype(BF16)
        tail_ref[g] = spread[pad + rows - tail :]
        edge_ref[g] = spread[:pad]
        sums[4] = sums[4] + jnp.sum(gconv, axis=0, keepdims=True)
        sums[5] = sums[5] + jnp.sum(gip, axis=0, keepdims=True)
        sums[6] = sums[6] + jnp.sum(gdp, axis=0, keepdims=True)
        sums[7] = sums[7] + jnp.sum(-8.0 * dg * glog, axis=0, keepdims=True) * rate_ref[1:2, :]
    rows_ref[...] = jnp.concatenate(sums, axis=0)


def by_head(body, flags, operands, outs):
    def spec(shape, rows_are_channels):
        if rows_are_channels:
            return pl.BlockSpec((BLK, shape[1]), lambda h: (h, 0))
        lead = shape[:-1]
        return pl.BlockSpec(lead + (BLK,), lambda h: (0,) * len(lead) + (h,))

    heads = outs[0].shape[-1] // BLK
    in_specs = [pl.BlockSpec(memory_space=pltpu.SMEM)]
    values = [flags]
    for value, is_gate in operands:
        in_specs.append(spec(value.shape, is_gate))
        values.append(value)
    size = sum(v.size * v.dtype.itemsize for v in values) + sum(
        o.size * o.dtype.itemsize for o in outs)
    return pl.pallas_call(
        body,
        grid=(heads,),
        in_specs=in_specs,
        out_specs=[spec(o.shape, False) for o in outs],
        out_shape=outs,
        compiler_params=pltpu.CompilerParams(vmem_limit_bytes=48 * 1024 * 1024),
        cost_estimate=pl.CostEstimate(
            flops=200 * outs[0].size, bytes_accessed=size, transcendentals=4 * outs[0].size),
    )(*values)


def entering(lay, summary, groups, backward):
    prod, state = (summary[:groups], summary[groups : 2 * groups])
    before_p, before_s = (jnp.ones_like(prod), jnp.zeros_like(state))
    mine = lax.axis_index("seq")
    bit = 1
    while bit < lay.seq:
        other = lay.over_seq_bit(jnp.concatenate([prod, state], axis=0), bit)
        other_p, other_s = (other[:groups], other[groups:])
        is_later = (mine & bit) != 0
        take = jnp.logical_not(is_later) if backward else is_later
        before_s = jnp.where(take, before_p * other_s + before_s, before_s)
        before_p = jnp.where(take, before_p * other_p, before_p)
        state = jnp.where(take, prod * other_s + state, other_p * state + other_s)
        prod = prod * other_p
        bit *= 2
    return before_s


def line_sum(lay, blocks):
    nz, z = (lay.nz, lay.z)

    def pick(t):
        return lax.dynamic_index_in_dim(blocks, jnp.clip(t, 0, nz - 1), 0, keepdims=False).astype(F32)

    right = left = None
    for dist in range(nz - 1, 0, -1):
        up, down = (pick(z + dist), pick(z - dist))
        if right is not None:
            up, down = (up + right.astype(F32), down + left.astype(F32))
        right = lay.send(
            up.astype(BF16), lambda z, y, x, c: (z + 1, y, x, c) if z + dist < nz else None)
        left = lay.send(
            down.astype(BF16), lambda z, y, x, c: (z - 1, y, x, c) if z - dist >= 0 else None)
    return pick(z) + right.astype(F32) + left.astype(F32)


def local(inputs, block_flags, decay_seed, vectors, in_y, in_x, gate_weight, out_proj,
          mlp_gate, mlp_up, mlp_down, cotangent):
    lay = Lay()
    nz, x, y, z, c = (lay.nz, lay.x, lay.y, lay.z, lay.c)
    tokens, width = inputs.shape[1:]
    half = width // 2
    quarter = width // 4
    first = c == 0

    def order_c(own, other, axis):
        return jnp.where(first, jnp.concatenate([own, other], axis),
                         jnp.concatenate([other, own], axis))

    def order_f(rel):
        b = rel.shape[-1] // 4
        p = [rel[..., i * b : (i + 1) * b] for i in range(4)]
        by_c = jnp.where(first, rel, jnp.concatenate([p[1], p[0], p[3], p[2]], -1))
        return jnp.where(x == 0, by_c, jnp.concatenate([by_c[..., 2 * b :], by_c[..., : 2 * b]], -1))

    halo_raw = lay.over_seq(inputs[0, tokens - 16 :], 1)
    residual = inputs[0].astype(F32)
    scaled_one, inverse_one = norm_scale(residual)
    normed_own = (scaled_one * vectors[0]).astype(BF16)
    normed_x = lay.over_x(normed_own)
    halo_own = (norm_scale(halo_raw.astype(F32))[0] * vectors[0]).astype(BF16)
    flag_row = jnp.pad(block_flags.astype(BF16), ((0, 0), (0, width - block_flags.shape[1])))
    halo_x = lay.over_x(jnp.concatenate([flag_row, halo_own[1:]], axis=0))
    n_flags = block_flags.shape[1]
    flags = jnp.concatenate(
        [block_flags.astype(F32), halo_x[:1, :n_flags].astype(F32)], axis=0)

    wy, wx = (in_y, in_x)
    wy_c, wx_c = (lay.over_c(in_y), lay.over_c(in_x))
    rows_mine = lax.dynamic_slice_in_dim(gate_weight, x * half, half, 0)
    rows_theirs = lax.dynamic_slice_in_dim(gate_weight, (1 - x) * half, half, 0)
    gate_x = lay.over_x(rows_theirs)
    gate_c, gate_xc = (lay.over_c(rows_mine), lay.over_c(gate_x))
    gates = order_f(jnp.concatenate([rows_mine, gate_c, gate_x, gate_xc], axis=1))
    out_mine = lax.dynamic_slice_in_dim(out_proj, x * half, half, 0)
    out_x = lay.over_x(lax.dynamic_slice_in_dim(out_proj, (1 - x) * half, half, 0))
    out_c, out_xc = (lay.over_c(out_mine), lay.over_c(out_x))
    out_rel = jnp.concatenate([out_mine, out_c, out_x, out_xc], axis=1)
    cot = cotangent[0]
    cot_c = lay.over_c(cot)
    cot_x = lay.over_x(cot)
    cot_xc = lay.over_c(cot_x)

    normed = jnp.concatenate([normed_own, normed_x, halo_own, halo_x], axis=0)
    two = 2 * tokens
    y_pre = order_c(dot(normed[:two], wy), dot(normed[:two], wy_c), 1).reshape(2, tokens, half)
    x_all = order_c(dot(normed, wx).astype(BF16), dot(normed, wx_c).astype(BF16), 1)
    x_low = x_all[:two].reshape(2, tokens, half)
    halo = x_all[two:].reshape(2, 16, half)
    vec_half = lax.dynamic_slice_in_dim(vectors, x * half, half, 1)
    base = -5.0 - decay_seed.astype(F32) + vectors[9]
    rates = lax.dynamic_slice_in_dim(
        jnp.stack([jax.nn.softplus(base), jax.nn.sigmoid(base)]), x * half, half, 1)
    shape3 = lambda dt: jax.ShapeDtypeStruct((2, tokens, half), dt)
    summary_shape = jax.ShapeDtypeStruct((4, half), F32)
    conv_low, ig, dg, prods, local_state, summary = by_head(
        mixer_forward, flags,
        [(x_low, False), (halo, False), (gates, True), (vec_half, False), (rates, False)],
        [shape3(BF16), shape3(F32), shape3(F32), shape3(F32), shape3(F32), summary_shape])
    state_in = entering(lay, summary, 2, False)
    state = local_state + prods * state_in[:, None, :]
    mixed = (state * jax.nn.gelu(y_pre, approximate=True)).astype(BF16)
    part_x = dot(mixed[1], out_rel).astype(BF16)
    part_x = lay.over_x(part_x)
    part_own = dot(mixed[0], out_rel)
    swapped = jnp.concatenate([part_x[:, half:], part_x[:, :half]], axis=1)
    mid = residual + order_f(part_own + swapped.astype(F32))

    scaled_two, inverse_two = norm_scale(mid)
    n2 = (scaled_two * vectors[1]).astype(BF16)
    n2_c = lay.over_c(n2)
    n2_x = lay.over_x(n2)
    n2_xc = lay.over_c(n2_x)

    def mlp(normed_in, cot_in):
        gate_val = dot(normed_in, mlp_gate)
        up_val = dot(normed_in, mlp_up)
        grad_hidden = dot(cot_in, mlp_down)
        gelu, slope = gelu_pair(gate_val)
        hidden = (gelu * up_val).astype(BF16)
        grad_gate = (grad_hidden * up_val * slope).astype(BF16)
        grad_up = (grad_hidden * gelu).astype(BF16)
        return hidden, grad_gate, grad_up

    near_n2, near_cot = (jnp.concatenate([n2, n2_c], 0), jnp.concatenate([cot, cot_c], 0))
    far_n2, far_cot = (jnp.concatenate([n2_x, n2_xc], 0), jnp.concatenate([cot_x, cot_xc], 0))
    near = mlp(near_n2, near_cot)
    far = mlp(far_n2, far_cot)

    def to_owners(of):
        far_part = of(far)
        far_sum = far_part[:tokens] + lay.over_c(far_part[tokens:].astype(BF16)).astype(F32)
        arriving = lay.over_x(far_sum.astype(BF16))
        near_part = of(near)
        near_sum = near_part[:tokens] + lay.over_c(near_part[tokens:].astype(BF16)).astype(F32)
        return near_sum + arriving.astype(F32)

    grad_n2 = to_owners(lambda t: dot_cols(t[1], mlp_gate) + dot_cols(t[2], mlp_up))
    output = (mid + to_owners(lambda t: dot_cols(t[0], mlp_down))).astype(BF16)[None]

    n2_y = lay.over_y(jnp.concatenate([n2, n2_x], 0))
    cot_y = lay.over_y(jnp.concatenate([cot, cot_x], 0))
    n2_y = jnp.concatenate([n2_y, lay.over_c(n2_y)], 0)
    cot_y = jnp.concatenate([cot_y, lay.over_c(cot_y)], 0)
    side = mlp(n2_y, cot_y)
    each = width // lay.seq

    def rows_of_y(value, which):
        return lax.dynamic_index_in_dim(
            value.reshape(value.shape[0], nz, 2, each), which, 2, keepdims=False
        ).reshape(value.shape[0], nz * each)

    n2_rows = rows_of_y(jnp.concatenate([near_n2, far_n2, n2_y], 0), y)
    cot_rows = rows_of_y(jnp.concatenate([near_cot, far_cot, cot_y], 0), y)
    hidden_all, gg_all, gu_all = [
        jnp.concatenate([near[i], far[i], side[i]], 0) for i in range(3)]
    mlp_grads = []
    for left, right in ((cot_rows, hidden_all), (n2_rows, gg_all), (n2_rows, gu_all)):
        part = dot_rows(left, right).astype(BF16).reshape(nz, each, right.shape[1])
        mlp_grads.append(line_sum(lay, part))
    mlp_down_grad, mlp_gate_grad, mlp_up_grad = mlp_grads

    grad_mid_norm, grad_gain_two = norm_back(grad_n2, scaled_two, inverse_two, vectors[1])
    grad_mid = cot.astype(F32) + grad_mid_norm
    branch = grad_mid.astype(BF16)
    branch_rel = order_f(branch)
    arriving = lay.over_x(branch_rel)
    branch_x_rel = jnp.concatenate([arriving[:, half:], arriving[:, :half]], axis=1)
    grad_mixed = dot_cols(jnp.concatenate([branch_rel, branch_x_rel], 0), out_rel)
    gy, bprod, blocal, back_summary = by_head(
        mixer_back_scan, flags,
        [(grad_mixed.reshape(2, tokens, half), False), (y_pre, False), (dg, False), (prods, False),
         (local_state, False), (state_in, False), (rates, False)],
        [shape3(BF16), shape3(F32), shape3(F32), summary_shape])
    back_in = entering(lay, back_summary, 2, True)
    gip, gdp, gx_main, gx_tail, edge, vec_rows = by_head(
        mixer_backward, flags,
        [(bprod, False), (blocal, False), (back_in, False), (prods, False), (local_state, False),
         (state_in, False), (ig, False), (dg, False), (conv_low, False), (x_low, False),
         (halo, False), (gates, True), (vec_half, False), (rates, False)],
        [shape3(BF16), shape3(BF16), shape3(BF16), jax.ShapeDtypeStruct((2, 16, half), F32),
         jax.ShapeDtypeStruct((2, 8, half), F32), jax.ShapeDtypeStruct((8, half), F32)])
    edge_next = lay.over_seq(edge, -1)
    gx_last = (gx_tail + jnp.pad(edge_next, ((0, 0), (8, 0), (0, 0)))).astype(BF16)
    gx = jnp.concatenate([gx_main[:, : tokens - 16], gx_last], axis=1).reshape(two, half)
    gy = gy.reshape(two, half)

    def own_cols(value, which):
        return lax.dynamic_slice_in_dim(value, which * quarter, quarter, 1)

    gy_o, gy_c, gx_o, gx_c = (
        own_cols(gy, c), own_cols(gy, 1 - c), own_cols(gx, c), own_cols(gx, 1 - c))

    def grad_n1_of(rows):
        return (dot_cols(gy_o[rows], wy) + dot_cols(gy_c[rows], wy_c)
                + dot_cols(gx_o[rows], wx) + dot_cols(gx_c[rows], wx_c))

    arriving = lay.over_x(grad_n1_of(slice(tokens, two)).astype(BF16))
    grad_n1 = grad_n1_of(slice(0, tokens)) + arriving.astype(F32)
    grad_in_norm, grad_gain_one = norm_back(grad_n1, scaled_one, inverse_one, vectors[0])
    input_grad = (grad_mid + grad_in_norm).astype(BF16)[None]

    rows_full = lax.dynamic_update_slice_in_dim(
        jnp.zeros((8, width), F32), vec_rows, x * half, 1)
    vec = jnp.concatenate([grad_gain_one[None], grad_gain_two[None], rows_full], axis=0)
    vec = vec + lay.over_c(vec)
    vec = vec + lay.over_x(vec)
    bit = 1
    while bit < lay.seq:
        vec = vec + lay.over_seq_bit(vec, bit)
        bit *= 2

    n1_two = jnp.concatenate([normed_own, normed_x], 0)
    n1_four = jnp.concatenate([n1_two, lay.over_c(n1_two)], 0)
    n1_rows = jnp.concatenate(
        [rows_of_y(n1_four, y), lay.over_y(rows_of_y(n1_four, 1 - y))], 0)
    keep = jnp.where(first, gy, gx)
    g_four = jnp.concatenate([keep, lay.over_c(jnp.where(first, gx, gy))], 0)
    g_all = jnp.concatenate([g_four, lay.over_y(g_four)], 0)
    in_part = dot_rows(n1_rows, g_all).astype(BF16).reshape(nz, each, half)

    mixed_two = mixed.reshape(two, half)
    mixed_four = jnp.concatenate([mixed_two, lay.over_c(mixed_two)], 0)
    branch_two = jnp.concatenate([branch, order_f(branch_x_rel)], 0)

    def half_cols(value, which, n):
        return lax.dynamic_slice_in_dim(value, which * n, n, 1)

    branch_four = jnp.concatenate(
        [half_cols(branch_two, c, half), lay.over_c(half_cols(branch_two, 1 - c, half))], 0)
    mixed_rows = jnp.concatenate(
        [half_cols(mixed_four, y, quarter), lay.over_y(half_cols(mixed_four, 1 - y, quarter))], 0)
    branch_all = jnp.concatenate([branch_four, lay.over_y(branch_four)], 0)
    fine = quarter // nz
    out_part = dot_rows(mixed_rows, branch_all).astype(BF16).reshape(nz, fine, half)

    conv_two = conv_low.reshape(two, half)
    conv_four = jnp.concatenate([conv_two, lay.over_c(conv_two)], 0)
    gip2, gdp2 = (gip.reshape(two, half), gdp.reshape(two, half))
    gp_four = jnp.concatenate(
        [jnp.where(first, gip2, gdp2), lay.over_c(jnp.where(first, gdp2, gip2))], 0)
    heads = half // BLK
    gate_part = jnp.einsum(
        "thi,thj->hij", conv_four.reshape(2 * two, heads, BLK),
        gp_four.reshape(2 * two, heads, BLK), preferred_element_type=F32).reshape(half, BLK)
    gate_keep = lax.dynamic_slice_in_dim(gate_part, y * quarter, quarter, 0)
    gate_send = lax.dynamic_slice_in_dim(gate_part, (1 - y) * quarter, quarter, 0).astype(BF16)
    gate_sum = (gate_keep + lay.over_y(gate_send).astype(F32)).astype(BF16)
    gate_sum = gate_sum.reshape(nz, fine * BLK // half, half)

    done = line_sum(lay, jnp.concatenate([in_part, out_part, gate_sum], axis=1)).astype(BF16)
    own80 = each // 4
    in_done = done[:each].reshape(2, 2, own80, half)
    out_done = done[each : each + fine].reshape(2, own80, half)
    gate_done = done[each + fine :].reshape(2, own80, BLK)

    def by_core(value, axis):
        mine = lax.dynamic_index_in_dim(value, c, axis, keepdims=False)
        theirs = lax.dynamic_index_in_dim(value, 1 - c, axis, keepdims=False)
        return mine, lay.over_c(theirs)

    in_keep, in_recv = by_core(in_done, 1)
    out_keep, out_recv = by_core(out_done, 0)
    gate_keep, gate_recv = by_core(gate_done, 0)
    both = jnp.stack([jnp.where(first, in_keep, in_recv), jnp.where(first, in_recv, in_keep)])
    mine = lax.dynamic_index_in_dim(both, x, 1, keepdims=False)
    theirs = lay.over_x(lax.dynamic_index_in_dim(both, 1 - x, 1, keepdims=False))
    in_full = jnp.where(x == 0, jnp.concatenate([mine, theirs], -1),
                        jnp.concatenate([theirs, mine], -1)).astype(F32)
    last = jnp.concatenate(
        [order_c(out_keep, out_recv, 1), order_c(gate_keep, gate_recv, 1)], axis=1)

    def final(z, y, x, c):
        at = ((x * 2 + y) * nz + z) * 2 + c
        s, f = (at // 4, at % 4)
        return (s // 2, s % 2, f // 2, f % 2)

    last = lay.send(last, final).astype(F32)
    return (output, input_grad, vec, in_full[0], in_full[1], last[:, width:], last[:, :width],
            mlp_gate_grad, mlp_up_grad, mlp_down_grad)


def solution(mesh):
    return jax.shard_map(
        local,
        mesh=mesh,
        in_specs=(
            P("fsdp", "seq", None),
            P("fsdp", "seq"),
            P(),
            P(),
            P(None, "fsdp"),
            P(None, "fsdp"),
            P(None, "fsdp"),
            P(None, "fsdp"),
            P(None, "fsdp"),
            P(None, "fsdp"),
            P(None, "fsdp"),
            P("fsdp", "seq", None),
        ),
        out_specs=(
            P("fsdp", "seq", None),
            P("fsdp", "seq", None),
            P(),
            P(("seq", "fsdp"), None),
            P(("seq", "fsdp"), None),
            P(("seq", "fsdp"), None),
            P(("seq", "fsdp"), None),
            P("seq", "fsdp"),
            P("seq", "fsdp"),
            P("seq", "fsdp"),
        ),
        check_vma=False,
    )
```

```python
import functools

import jax
import jax.numpy as jnp
from jax import lax
from jax.experimental import pallas as pl
from jax.experimental.pallas import tpu as pltpu
from jax.sharding import PartitionSpec as P

HEADS = 10
BLK = 256
FBLK = 64
EPS = 1e-06
ALL = ("seq", "fsdp")
F32 = jnp.float32
BF16 = jnp.bfloat16
GELU_C = 0.7978845608028654
GELU_A = 0.044715


def norm_scale(values):
    inverse = lax.rsqrt(jnp.mean(values * values, axis=-1, keepdims=True) + EPS)
    return (values * inverse, inverse)


def norm_back(grad_normed, scaled, inverse, gain_row):
    grad_gain = jnp.sum(grad_normed * scaled, axis=0)
    inner_term = grad_normed * gain_row
    grad_input = inverse * (
        inner_term - scaled * jnp.mean(inner_term * scaled, axis=-1, keepdims=True)
    )
    return (grad_input, grad_gain)


def gelu_pair(values):
    square = values * values
    t = jnp.tanh(GELU_C * values * (1.0 + GELU_A * square))
    half = 0.5 * (1.0 + t)
    slope = half + 0.5 * values * (1.0 - t * t) * GELU_C * (1.0 + 3.0 * GELU_A * square)
    return (values * half, slope)


def dot(left, right):
    return jnp.dot(left, right, preferred_element_type=F32)


def dot_rows(left, right):
    return lax.dot_general(left, right, (((0,), (0,)), ((), ())), preferred_element_type=F32)


def dot_cols(left, right):
    return lax.dot_general(left, right, (((1,), (1,)), ((), ())), preferred_element_type=F32)


class Lay:
    def __init__(self):
        self.seq = lax.axis_size("seq")
        self.nz = self.seq // 2
        seq, fsdp = (lax.axis_index("seq"), lax.axis_index("fsdp"))
        self.z, self.y = (seq // 2, seq % 2)
        self.x, self.c = (fsdp // 2, fsdp % 2)

    def pairs(self, target):
        found = []
        for s in range(self.seq):
            for f in range(4):
                z, y, x, c = (s // 2, s % 2, f // 2, f % 2)
                to = target(z, y, x, c)
                if to is not None:
                    found.append((s * 4 + f, ((to[0] * 2 + to[1]) * 2 + to[2]) * 2 + to[3]))
        return found

    def send(self, value, target):
        return lax.ppermute(value, ALL, self.pairs(target))

    def over_c(self, value):
        return self.send(value, lambda z, y, x, c: (z, y, x, 1 - c))

    def over_x(self, value):
        return self.send(value, lambda z, y, x, c: (z, y, 1 - x, c))

    def over_y(self, value):
        return self.send(value, lambda z, y, x, c: (z, 1 - y, x, c))

    def over_seq_bit(self, value, bit):
        def to(z, y, x, c):
            other = (2 * z + y) ^ bit
            return (other // 2, other % 2, x, c)

        return self.send(value, to)

    def over_z(self, value):
        return self.send(value, lambda z, y, x, c: (self.nz - 1 - z, y, x, c))

    def over_seq(self, value, by):
        def to(z, y, x, c):
            other = 2 * z + y + by
            return (other // 2, other % 2, x, c) if 0 <= other < self.seq else None

        return self.send(value, to)


def row_iota(rows, cols):
    return lax.broadcasted_iota(jnp.int32, (rows, cols), 0)


def token_masks(flags_ref, g, rows, cols):
    row = row_iota(rows, cols)
    block = row // FBLK
    offset = row % FBLK
    flagged = jnp.zeros((rows, cols), F32)
    for b in range(rows // FBLK):
        flagged = jnp.where(block == b, flags_ref[g, b], flagged)
    valid = [jnp.where(offset < lag, 1.0 - flagged, 1.0) for lag in range(4)]
    start = jnp.where(offset == 0, flagged, 0.0)
    return start, valid


def neg_expm1(v):
    series = 1.0 + v * (1.0 / 6.0)
    for n in (5.0, 4.0, 3.0, 2.0):
        series = 1.0 + v * (1.0 / n) * series
    return jnp.where(v > -0.25, -v * series, 1.0 - jnp.exp(v))


def shifted_inputs(xl_ref, halo_ref, g):
    ext = jnp.concatenate([halo_ref[g].astype(F32), xl_ref[g].astype(F32)], axis=0)
    pad = halo_ref.shape[1]
    return [ext[pad:] if k == 0 else pltpu.roll(ext, k, 0)[pad:] for k in range(4)]


def mixer_forward(flags_ref, xl_ref, halo_ref, gw_ref, vec_ref, rate_ref,
                  conv_ref, ig_ref, dg_ref, prod_ref, local_ref, sum_ref):
    groups, rows, cols = xl_ref.shape
    row = row_iota(rows, cols)
    for g in range(groups):
        start, valid = token_masks(flags_ref, g, rows, cols)
        lagged = shifted_inputs(xl_ref, halo_ref, g)
        conv = vec_ref[6:7, :] + jnp.zeros((rows, cols), F32)
        for k in range(4):
            conv = conv + vec_ref[2 + k : 3 + k, :] * lagged[k] * valid[k]
        conv_low = conv.astype(BF16)
        conv_ref[g] = conv_low
        prod = jnp.dot(conv_low, gw_ref[...], preferred_element_type=F32)
        ig = jax.nn.sigmoid(prod[:, :cols] + vec_ref[7:8, :])
        dg = jax.nn.sigmoid(prod[:, cols:] + vec_ref[8:9, :])
        ig_ref[g] = ig
        dg_ref[g] = dg
        keep = 1.0 - start
        log_decay = -8.0 * dg * rate_ref[0:1, :]
        p = jnp.exp(log_decay) * keep
        s = jnp.sqrt(keep * neg_expm1(2.0 * log_decay) + start) * ig * conv_low.astype(F32)
        step = 1
        while step < rows:
            inside = row >= step
            p_prev = jnp.where(inside, pltpu.roll(p, step, 0), 1.0)
            s_prev = jnp.where(inside, pltpu.roll(s, step, 0), 0.0)
            s = p * s_prev + s
            p = p * p_prev
            step *= 2
        prod_ref[g] = p
        local_ref[g] = s
        sum_ref[g : g + 1, :] = p[rows - 1 :, :]
        sum_ref[groups + g : groups + g + 1, :] = s[rows - 1 :, :]


def mixer_back_scan(flags_ref, gm_ref, y_ref, dg_ref, prod_ref, local_ref, sin_ref, rate_ref,
                    gy_ref, bprod_ref, blocal_ref, sum_ref):
    groups, rows, cols = gm_ref.shape
    row = row_iota(rows, cols)
    for g in range(groups):
        start, _ = token_masks(flags_ref, g, rows, cols)
        state = local_ref[g] + prod_ref[g] * sin_ref[g : g + 1, :]
        gelu, slope = gelu_pair(y_ref[g])
        gm = gm_ref[g]
        gy_ref[g] = (gm * state * slope).astype(BF16)
        decay = jnp.exp(-8.0 * dg_ref[g] * rate_ref[0:1, :]) * (1.0 - start)
        s = gm * gelu
        p = jnp.where(row == rows - 1, 1.0, pltpu.roll(decay, rows - 1, 0))
        step = 1
        while step < rows:
            inside = row < rows - step
            p_next = jnp.where(inside, pltpu.roll(p, rows - step, 0), 1.0)
            s_next = jnp.where(inside, pltpu.roll(s, rows - step, 0), 0.0)
            s = p * s_next + s
            p = p * p_next
            step *= 2
        bprod_ref[g] = p
        blocal_ref[g] = s
        sum_ref[g : g + 1, :] = decay[:1, :] * p[:1, :]
        sum_ref[groups + g : groups + g + 1, :] = decay[:1, :] * s[:1, :]


def mixer_backward(flags_ref, bprod_ref, blocal_ref, bin_ref, prod_ref, local_ref, sin_ref,
                   ig_ref, dg_ref, conv_ref, xl_ref, halo_ref, gw_ref, vec_ref, rate_ref,
                   gip_ref, gdp_ref, gx_ref, tail_ref, edge_ref, rows_ref):
    groups, rows, cols = xl_ref.shape
    row = row_iota(rows, cols)
    sums = [jnp.zeros((1, cols), F32) for _ in range(8)]
    tail = tail_ref.shape[1]
    pad = edge_ref.shape[1]
    for g in range(groups):
        start, valid = token_masks(flags_ref, g, rows, cols)
        keep = 1.0 - start
        rate = rate_ref[0:1, :]
        state_in = sin_ref[g : g + 1, :]
        state = local_ref[g] + prod_ref[g] * state_in
        prev = jnp.where(row == 0, state_in, pltpu.roll(state, 1, 0))
        sg = blocal_ref[g] + bprod_ref[g] * bin_ref[g : g + 1, :]
        ig, dg = (ig_ref[g], dg_ref[g])
        cf = conv_ref[g].astype(F32)
        log_decay = -8.0 * dg * rate
        decay = jnp.exp(log_decay) * keep
        scale = jnp.sqrt(keep * neg_expm1(2.0 * log_decay) + start)
        gscale = sg * ig * cf
        glog = sg * prev * decay - gscale * keep * jnp.exp(2.0 * log_decay) / scale
        gip = sg * scale * cf * ig * (1.0 - ig)
        gdp = -8.0 * rate * glog * dg * (1.0 - dg)
        gip_low, gdp_low = (gip.astype(BF16), gdp.astype(BF16))
        gip_ref[g] = gip_low
        gdp_ref[g] = gdp_low
        gconv = sg * scale * ig + lax.dot_general(
            jnp.concatenate([gip_low, gdp_low], axis=1), gw_ref[...],
            (((1,), (1,)), ((), ())), preferred_element_type=F32)
        lagged = shifted_inputs(xl_ref, halo_ref, g)
        spread = jnp.zeros((rows + pad, cols), F32)
        for k in range(4):
            masked = gconv * valid[k]
            sums[k] = sums[k] + jnp.sum(masked * lagged[k], axis=0, keepdims=True)
            full = jnp.concatenate(
                [jnp.zeros((pad, cols), F32), vec_ref[2 + k : 3 + k, :] * masked], axis=0)
            spread = spread + (full if k == 0 else pltpu.roll(full, rows + pad - k, 0))
        gx_ref[g] = spread[pad:].astype(BF16)
        tail_ref[g] = spread[pad + rows - tail :]
        edge_ref[g] = spread[:pad]
        sums[4] = sums[4] + jnp.sum(gconv, axis=0, keepdims=True)
        sums[5] = sums[5] + jnp.sum(gip, axis=0, keepdims=True)
        sums[6] = sums[6] + jnp.sum(gdp, axis=0, keepdims=True)
        sums[7] = sums[7] + jnp.sum(-8.0 * dg * glog, axis=0, keepdims=True) * rate_ref[1:2, :]
    rows_ref[...] = jnp.concatenate(sums, axis=0)


def by_head(body, flags, operands, outs):
    def spec(shape, rows_are_channels):
        if rows_are_channels:
            return pl.BlockSpec((BLK, shape[1]), lambda h: (h, 0))
        lead = shape[:-1]
        return pl.BlockSpec(lead + (BLK,), lambda h: (0,) * len(lead) + (h,))

    heads = outs[0].shape[-1] // BLK
    in_specs = [pl.BlockSpec(memory_space=pltpu.SMEM)]
    values = [flags]
    for value, is_gate in operands:
        in_specs.append(spec(value.shape, is_gate))
        values.append(value)
    size = sum(v.size * v.dtype.itemsize for v in values) + sum(
        o.size * o.dtype.itemsize for o in outs)
    return pl.pallas_call(
        body,
        grid=(heads,),
        in_specs=in_specs,
        out_specs=[spec(o.shape, False) for o in outs],
        out_shape=outs,
        compiler_params=pltpu.CompilerParams(vmem_limit_bytes=48 * 1024 * 1024),
        cost_estimate=pl.CostEstimate(
            flops=200 * outs[0].size, bytes_accessed=size, transcendentals=4 * outs[0].size),
    )(*values)


def entering(lay, summary, groups, backward):
    prod, state = (summary[:groups], summary[groups : 2 * groups])
    before_p, before_s = (jnp.ones_like(prod), jnp.zeros_like(state))
    mine = lax.axis_index("seq")
    bit = 1
    while bit < lay.seq:
        other = lay.over_seq_bit(jnp.concatenate([prod, state], axis=0), bit)
        other_p, other_s = (other[:groups], other[groups:])
        is_later = (mine & bit) != 0
        take = jnp.logical_not(is_later) if backward else is_later
        before_s = jnp.where(take, before_p * other_s + before_s, before_s)
        before_p = jnp.where(take, before_p * other_p, before_p)
        state = jnp.where(take, prod * other_s + state, other_p * state + other_s)
        prod = prod * other_p
        bit *= 2
    return before_s


def line_sum(lay, blocks):
    nz, z = (lay.nz, lay.z)

    def pick(t):
        return lax.dynamic_index_in_dim(blocks, jnp.clip(t, 0, nz - 1), 0, keepdims=False).astype(F32)

    right = left = None
    for dist in range(nz - 1, 0, -1):
        up, down = (pick(z + dist), pick(z - dist))
        if right is not None:
            up, down = (up + right.astype(F32), down + left.astype(F32))
        right = lay.send(
            up.astype(BF16), lambda z, y, x, c: (z + 1, y, x, c) if z + dist < nz else None)
        left = lay.send(
            down.astype(BF16), lambda z, y, x, c: (z - 1, y, x, c) if z - dist >= 0 else None)
    return pick(z) + right.astype(F32) + left.astype(F32)


def local(inputs, block_flags, decay_seed, vectors, in_y, in_x, gate_weight, out_proj,
          mlp_gate, mlp_up, mlp_down, cotangent):
    lay = Lay()
    nz, x, y, z, c = (lay.nz, lay.x, lay.y, lay.z, lay.c)
    tokens, width = inputs.shape[1:]
    half = width // 2
    quarter = width // 4
    first = c == 0

    def order_c(own, other, axis):
        return jnp.where(first, jnp.concatenate([own, other], axis),
                         jnp.concatenate([other, own], axis))

    def order_f(rel):
        b = rel.shape[-1] // 4
        p = [rel[..., i * b : (i + 1) * b] for i in range(4)]
        by_c = jnp.where(first, rel, jnp.concatenate([p[1], p[0], p[3], p[2]], -1))
        return jnp.where(x == 0, by_c, jnp.concatenate([by_c[..., 2 * b :], by_c[..., : 2 * b]], -1))

    halo_raw = lay.over_seq(inputs[0, tokens - 16 :], 1)
    residual = inputs[0].astype(F32)
    scaled_one, inverse_one = norm_scale(residual)
    normed_own = (scaled_one * vectors[0]).astype(BF16)
    normed_x = lay.over_x(normed_own)
    halo_own = (norm_scale(halo_raw.astype(F32))[0] * vectors[0]).astype(BF16)
    flag_row = jnp.pad(block_flags.astype(BF16), ((0, 0), (0, width - block_flags.shape[1])))
    halo_x = lay.over_x(jnp.concatenate([flag_row, halo_own[1:]], axis=0))
    n_flags = block_flags.shape[1]
    flags = jnp.concatenate(
        [block_flags.astype(F32), halo_x[:1, :n_flags].astype(F32)], axis=0)

    wy, wx = (in_y, in_x)
    wy_c, wx_c = (lay.over_c(in_y), lay.over_c(in_x))
    rows_mine = lax.dynamic_slice_in_dim(gate_weight, x * half, half, 0)
    rows_theirs = lax.dynamic_slice_in_dim(gate_weight, (1 - x) * half, half, 0)
    gate_x = lay.over_x(rows_theirs)
    gate_c, gate_xc = (lay.over_c(rows_mine), lay.over_c(gate_x))
    gates = order_f(jnp.concatenate([rows_mine, gate_c, gate_x, gate_xc], axis=1))
    out_mine = lax.dynamic_slice_in_dim(out_proj, x * half, half, 0)
    out_x = lay.over_x(lax.dynamic_slice_in_dim(out_proj, (1 - x) * half, half, 0))
    out_c, out_xc = (lay.over_c(out_mine), lay.over_c(out_x))
    out_rel = jnp.concatenate([out_mine, out_c, out_x, out_xc], axis=1)
    cot = cotangent[0]
    cot_c = lay.over_c(cot)
    cot_x = lay.over_x(cot)
    cot_xc = lay.over_c(cot_x)

    normed = jnp.concatenate([normed_own, normed_x, halo_own, halo_x], axis=0)
    two = 2 * tokens
    y_pre = order_c(dot(normed[:two], wy), dot(normed[:two], wy_c), 1).reshape(2, tokens, half)
    x_all = order_c(dot(normed, wx).astype(BF16), dot(normed, wx_c).astype(BF16), 1)
    x_low = x_all[:two].reshape(2, tokens, half)
    halo = x_all[two:].reshape(2, 16, half)
    vec_half = lax.dynamic_slice_in_dim(vectors, x * half, half, 1)
    base = -5.0 - decay_seed.astype(F32) + vectors[9]
    rates = lax.dynamic_slice_in_dim(
        jnp.stack([jax.nn.softplus(base), jax.nn.sigmoid(base)]), x * half, half, 1)
    shape3 = lambda dt: jax.ShapeDtypeStruct((2, tokens, half), dt)
    summary_shape = jax.ShapeDtypeStruct((4, half), F32)
    conv_low, ig, dg, prods, local_state, summary = by_head(
        mixer_forward, flags,
        [(x_low, False), (halo, False), (gates, True), (vec_half, False), (rates, False)],
        [shape3(BF16), shape3(F32), shape3(F32), shape3(F32), shape3(F32), summary_shape])
    state_in = entering(lay, summary, 2, False)
    state = local_state + prods * state_in[:, None, :]
    mixed = (state * jax.nn.gelu(y_pre, approximate=True)).astype(BF16)
    part_x = dot(mixed[1], out_rel).astype(BF16)
    part_x = lay.over_x(part_x)
    part_own = dot(mixed[0], out_rel)
    swapped = jnp.concatenate([part_x[:, half:], part_x[:, :half]], axis=1)
    mid = residual + order_f(part_own + swapped.astype(F32))

    scaled_two, inverse_two = norm_scale(mid)
    n2 = (scaled_two * vectors[1]).astype(BF16)
    n2_c = lay.over_c(n2)
    n2_x = lay.over_x(n2)
    n2_xc = lay.over_c(n2_x)

    def mlp(normed_in, cot_in):
        gate_val = dot(normed_in, mlp_gate)
        up_val = dot(normed_in, mlp_up)
        grad_hidden = dot(cot_in, mlp_down)
        gelu, slope = gelu_pair(gate_val)
        hidden = (gelu * up_val).astype(BF16)
        grad_gate = (grad_hidden * up_val * slope).astype(BF16)
        grad_up = (grad_hidden * gelu).astype(BF16)
        return hidden, grad_gate, grad_up

    main_n2 = jnp.concatenate([n2, n2_c, n2_x, n2_xc], 0)
    main_cot = jnp.concatenate([cot, cot_c, cot_x, cot_xc], 0)
    main = mlp(main_n2, main_cot)

    def to_owners(of):
        far_part = of(slice(two, 2 * two))
        far_sum = far_part[:tokens] + lay.over_c(far_part[tokens:].astype(BF16)).astype(F32)
        arriving = lay.over_x(far_sum.astype(BF16))
        near_part = of(slice(0, two))
        near_sum = near_part[:tokens] + lay.over_c(near_part[tokens:].astype(BF16)).astype(F32)
        return near_sum + arriving.astype(F32)

    grad_n2 = to_owners(
        lambda rows: dot_cols(main[1][rows], mlp_gate) + dot_cols(main[2][rows], mlp_up))
    output = (mid + to_owners(lambda rows: dot_cols(main[0][rows], mlp_down))).astype(BF16)[None]

    n2_z, n2_xz = (lay.over_z(n2), lay.over_z(n2_x))
    cot_z, cot_xz = (lay.over_z(cot), lay.over_z(cot_x))
    side_n2 = jnp.concatenate([n2_z, lay.over_c(n2_z), n2_xz, lay.over_c(n2_xz)], 0)
    side_cot = jnp.concatenate([cot_z, lay.over_c(cot_z), cot_xz, lay.over_c(cot_xz)], 0)
    side = mlp(side_n2, side_cot)
    each = width // lay.seq
    seq_at = 2 * z + y
    upper = seq_at // nz

    def window(value):
        return lax.dynamic_slice_in_dim(value, upper * half, half, 1)

    n2_rows = jnp.concatenate([window(main_n2), window(side_n2)], 0)
    cot_rows = jnp.concatenate([window(main_cot), window(side_cot)], 0)
    hidden_all, gg_all, gu_all = [jnp.concatenate([main[i], side[i]], 0) for i in range(3)]

    def halve(blocks, bits):
        own = seq_at % nz

        def pick(j):
            return lax.dynamic_index_in_dim(blocks, own ^ j, 0, keepdims=False).astype(F32)

        def joined(old, come, at):
            return old() + come[at].astype(F32)

        held = {j: functools.partial(pick, j) for j in range(nz)}
        for bit in bits:
            leaving = sorted(j for j in held if j & bit)
            sent = jnp.stack([held[j]().astype(BF16) for j in leaving])
            come = lay.over_seq_bit(sent, bit)
            held = {
                j ^ bit: functools.partial(joined, held[j ^ bit], come, i)
                for i, j in enumerate(leaving)
            }
        return held[0]()

    bits = []
    bit = 1
    while bit < nz:
        bits.append(bit)
        bit *= 2
    mlp_grads = []
    for left, right, order in (
        (cot_rows, hidden_all, bits), (n2_rows, gg_all, bits[::-1]), (n2_rows, gu_all, bits)):
        part = dot_rows(left, right).astype(BF16).reshape(nz, each, right.shape[1])
        mlp_grads.append(halve(part, order))
    mlp_down_grad, mlp_gate_grad, mlp_up_grad = mlp_grads

    grad_mid_norm, grad_gain_two = norm_back(grad_n2, scaled_two, inverse_two, vectors[1])
    grad_mid = cot.astype(F32) + grad_mid_norm
    branch = grad_mid.astype(BF16)
    branch_rel = order_f(branch)
    arriving = lay.over_x(branch_rel)
    branch_x_rel = jnp.concatenate([arriving[:, half:], arriving[:, :half]], axis=1)
    grad_mixed = dot_cols(jnp.concatenate([branch_rel, branch_x_rel], 0), out_rel)
    gy, bprod, blocal, back_summary = by_head(
        mixer_back_scan, flags,
        [(grad_mixed.reshape(2, tokens, half), False), (y_pre, False), (dg, False), (prods, False),
         (local_state, False), (state_in, False), (rates, False)],
        [shape3(BF16), shape3(F32), shape3(F32), summary_shape])
    back_in = entering(lay, back_summary, 2, True)
    gip, gdp, gx_main, gx_tail, edge, vec_rows = by_head(
        mixer_backward, flags,
        [(bprod, False), (blocal, False), (back_in, False), (prods, False), (local_state, False),
         (state_in, False), (ig, False), (dg, False), (conv_low, False), (x_low, False),
         (halo, False), (gates, True), (vec_half, False), (rates, False)],
        [shape3(BF16), shape3(BF16), shape3(BF16), jax.ShapeDtypeStruct((2, 16, half), F32),
         jax.ShapeDtypeStruct((2, 8, half), F32), jax.ShapeDtypeStruct((8, half), F32)])
    edge_next = lay.over_seq(edge, -1)
    gx_last = (gx_tail + jnp.pad(edge_next, ((0, 0), (8, 0), (0, 0)))).astype(BF16)
    gx = jnp.concatenate([gx_main[:, : tokens - 16], gx_last], axis=1).reshape(two, half)
    gy = gy.reshape(two, half)

    def own_cols(value, which):
        return lax.dynamic_slice_in_dim(value, which * quarter, quarter, 1)

    gy_o, gy_c, gx_o, gx_c = (
        own_cols(gy, c), own_cols(gy, 1 - c), own_cols(gx, c), own_cols(gx, 1 - c))

    def grad_n1_of(rows):
        return (dot_cols(gy_o[rows], wy) + dot_cols(gy_c[rows], wy_c)
                + dot_cols(gx_o[rows], wx) + dot_cols(gx_c[rows], wx_c))

    arriving = lay.over_x(grad_n1_of(slice(tokens, two)).astype(BF16))
    grad_n1 = grad_n1_of(slice(0, tokens)) + arriving.astype(F32)
    grad_in_norm, grad_gain_one = norm_back(grad_n1, scaled_one, inverse_one, vectors[0])
    input_grad = (grad_mid + grad_in_norm).astype(BF16)[None]

    rows_full = lax.dynamic_update_slice_in_dim(
        jnp.zeros((8, width), F32), vec_rows, x * half, 1)
    vec = jnp.concatenate([grad_gain_one[None], grad_gain_two[None], rows_full], axis=0)
    vec = vec + lay.over_c(vec)
    vec = vec + lay.over_x(vec)
    bit = 1
    while bit < lay.seq:
        vec = vec + lay.over_seq_bit(vec, bit)
        bit *= 2

    own80 = each // 4

    def spread_rows(value, where):
        by_yc = where(value.T)
        by_c = lax.dynamic_index_in_dim(by_yc, c, 1, keepdims=False)
        other_c = lax.dynamic_index_in_dim(by_yc, 1 - c, 1, keepdims=False)
        pair = jnp.concatenate([by_c, lay.over_c(other_c)], axis=2)
        by_y = lax.dynamic_index_in_dim(pair, y, 0, keepdims=False)
        other_y = lax.dynamic_index_in_dim(pair, 1 - y, 0, keepdims=False)
        return jnp.concatenate([by_y, lay.over_y(other_y)], axis=1)

    def all_tokens(value):
        other_y = lay.over_y(value)
        return jnp.concatenate([value, lay.over_c(value), other_y, lay.over_c(other_y)], 0)

    def where_n1(rows):
        split = rows.reshape(nz, 2, 2, 2, own80, two)
        return split.transpose(1, 3, 0, 2, 4, 5).reshape(2, 2, nz * 2 * own80, two)

    def where_mixed(rows):
        split = rows.reshape(2, nz, 2, own80, two)
        return split.transpose(0, 2, 1, 3, 4).reshape(2, 2, nz * own80, two)

    n1_rows = spread_rows(jnp.concatenate([normed_own, normed_x], 0), where_n1)
    mixed_rows = spread_rows(mixed.reshape(two, half), where_mixed)
    branch_all = all_tokens(jnp.concatenate([branch, order_f(branch_x_rel)], 0))
    out_part = dot(mixed_rows, branch_all).astype(BF16).reshape(nz, 2 * own80, half)
    in_y_part = dot(n1_rows, all_tokens(gy)).astype(BF16).reshape(nz, 2 * own80, half)
    done_one = line_sum(lay, jnp.concatenate([in_y_part, out_part], axis=1)).astype(BF16)

    heads = half // BLK
    gate_part = jnp.einsum(
        "thi,thj->hij", conv_low.reshape(two, heads, BLK),
        jnp.concatenate([gip.reshape(two, heads, BLK), gdp.reshape(two, heads, BLK)], 2),
        preferred_element_type=F32).reshape(2, nz, 2, own80, 2 * BLK)
    keep = lax.dynamic_index_in_dim(gate_part, c, 2, keepdims=False)
    away = lax.dynamic_index_in_dim(gate_part, 1 - c, 2, keepdims=False)
    gate_part = keep + lay.over_c(away.astype(BF16)).astype(F32)
    keep = lax.dynamic_index_in_dim(gate_part, y, 0, keepdims=False)
    away = lax.dynamic_index_in_dim(gate_part, 1 - y, 0, keepdims=False)
    gate_part = (keep + lay.over_y(away.astype(BF16)).astype(F32)).astype(BF16)
    in_x_part = dot(n1_rows, all_tokens(gx)).astype(BF16).reshape(nz, 2 * own80, half)
    done_two = line_sum(lay, jnp.concatenate(
        [in_x_part, gate_part.reshape(nz, own80 * 2 * BLK // half, half)], axis=1)).astype(BF16)

    def over_columns(value):
        split = value.reshape(2, own80, half)
        mine = lax.dynamic_index_in_dim(split, x, 0, keepdims=False)
        theirs = lay.over_x(lax.dynamic_index_in_dim(split, 1 - x, 0, keepdims=False))
        return jnp.where(x == 0, jnp.concatenate([mine, theirs], -1),
                         jnp.concatenate([theirs, mine], -1)).astype(F32)

    in_y_grad = over_columns(done_one[: 2 * own80])
    in_x_grad = over_columns(done_two[: 2 * own80])
    def final(z, y, x, c):
        at = ((x * 2 + y) * nz + z) * 2 + c
        s, f = (at // 4, at % 4)
        return (s // 2, s % 2, f // 2, f % 2)

    out_grad = lay.send(done_one[2 * own80 :].reshape(own80, width), final).astype(F32)
    gate_grad = lay.send(done_two[2 * own80 :].reshape(own80, 2 * BLK), final).astype(F32)
    return (output, input_grad, vec, in_y_grad, in_x_grad, gate_grad, out_grad,
            mlp_gate_grad, mlp_up_grad, mlp_down_grad)


def solution(mesh):
    return jax.shard_map(
        local,
        mesh=mesh,
        in_specs=(
            P("fsdp", "seq", None),
            P("fsdp", "seq"),
            P(),
            P(),
            P(None, "fsdp"),
            P(None, "fsdp"),
            P(None, "fsdp"),
            P(None, "fsdp"),
            P(None, "fsdp"),
            P(None, "fsdp"),
            P(None, "fsdp"),
            P("fsdp", "seq", None),
        ),
        out_specs=(
            P("fsdp", "seq", None),
            P("fsdp", "seq", None),
            P(),
            P(("seq", "fsdp"), None),
            P(("seq", "fsdp"), None),
            P(("seq", "fsdp"), None),
            P(("seq", "fsdp"), None),
            P("seq", "fsdp"),
            P("seq", "fsdp"),
            P("seq", "fsdp"),
        ),
        check_vma=False,
    )
```

```python
import functools

import jax
import jax.numpy as jnp
from jax import lax
from jax.experimental import pallas as pl
from jax.experimental.pallas import tpu as pltpu
from jax.sharding import PartitionSpec as P

HEADS = 10
BLK = 256
FBLK = 64
EPS = 1e-06
ALL = ("seq", "fsdp")
F32 = jnp.float32
BF16 = jnp.bfloat16
GELU_C = 0.7978845608028654
GELU_A = 0.044715
VMEM_MAX = 60 * 1024 * 1024
ANY = pl.BlockSpec(memory_space=pl.ANY)


def norm_scale(values):
    inverse = lax.rsqrt(jnp.mean(values * values, axis=-1, keepdims=True) + EPS)
    return (values * inverse, inverse)


def norm_back(grad_normed, scaled, inverse, gain_row):
    grad_gain = jnp.sum(grad_normed * scaled, axis=0)
    inner_term = grad_normed * gain_row
    grad_input = inverse * (
        inner_term - scaled * jnp.mean(inner_term * scaled, axis=-1, keepdims=True)
    )
    return (grad_input, grad_gain)


def gelu_pair(values):
    square = values * values
    t = jnp.tanh(values * (GELU_C + GELU_C * GELU_A * square))
    half = 0.5 + 0.5 * t
    slope = half * (1.0 + (1.0 - t) * values * (GELU_C + 3.0 * GELU_C * GELU_A * square))
    return (values * half, slope)


def dot(left, right):
    return jnp.dot(left, right, preferred_element_type=F32)


def dot_rows(left, right):
    return lax.dot_general(left, right, (((0,), (0,)), ((), ())), preferred_element_type=F32)


def dot_cols(left, right):
    return lax.dot_general(left, right, (((1,), (1,)), ((), ())), preferred_element_type=F32)


class Lay:
    def __init__(self):
        self.seq = lax.axis_size("seq")
        self.nz = self.seq // 2
        seq, fsdp = (lax.axis_index("seq"), lax.axis_index("fsdp"))
        self.z, self.y = (seq // 2, seq % 2)
        self.x, self.c = (fsdp // 2, fsdp % 2)

    def pairs(self, target):
        found = []
        for s in range(self.seq):
            for f in range(4):
                z, y, x, c = (s // 2, s % 2, f // 2, f % 2)
                to = target(z, y, x, c)
                if to is not None:
                    found.append((s * 4 + f, ((to[0] * 2 + to[1]) * 2 + to[2]) * 2 + to[3]))
        return found

    def send(self, value, target):
        return lax.ppermute(value, ALL, self.pairs(target))

    def over_c(self, value):
        return self.send(value, lambda z, y, x, c: (z, y, x, 1 - c))

    def over_x(self, value):
        return self.send(value, lambda z, y, x, c: (z, y, 1 - x, c))

    def over_y(self, value):
        return self.send(value, lambda z, y, x, c: (z, 1 - y, x, c))

    def over_seq_bit(self, value, bit):
        def to(z, y, x, c):
            other = (2 * z + y) ^ bit
            return (other // 2, other % 2, x, c)

        return self.send(value, to)

    def over_z(self, value):
        return self.send(value, lambda z, y, x, c: (self.nz - 1 - z, y, x, c))

    def over_seq(self, value, by):
        def to(z, y, x, c):
            other = 2 * z + y + by
            return (other // 2, other % 2, x, c) if 0 <= other < self.seq else None

        return self.send(value, to)


def row_iota(rows, cols):
    return lax.broadcasted_iota(jnp.int32, (rows, cols), 0)


def token_masks(flags_ref, g, rows, cols):
    row = row_iota(rows, cols)
    block = row // FBLK
    offset = row % FBLK
    flagged = jnp.zeros((rows, cols), F32)
    for b in range(rows // FBLK):
        flagged = jnp.where(block == b, flags_ref[g, b], flagged)
    valid = [jnp.where(offset < lag, 1.0 - flagged, 1.0) for lag in range(4)]
    start = jnp.where(offset == 0, flagged, 0.0)
    return start, valid


def neg_expm1(v):
    series = 1.0 + v * (1.0 / 6.0)
    for n in (5.0, 4.0, 3.0, 2.0):
        series = 1.0 + v * (1.0 / n) * series
    return jnp.where(v > -0.25, -v * series, 1.0 - jnp.exp(v))


def shifted_inputs(xl_ref, halo_ref, g):
    ext = jnp.concatenate([halo_ref[g].astype(F32), xl_ref[g].astype(F32)], axis=0)
    pad = halo_ref.shape[1]
    return [ext[pad:] if k == 0 else pltpu.roll(ext, k, 0)[pad:] for k in range(4)]


def mixer_forward(flags_ref, xl_ref, halo_ref, gw_ref, vec_ref, rate_ref,
                  conv_ref, ig_ref, dg_ref, prod_ref, local_ref, sum_ref):
    groups, rows, cols = xl_ref.shape
    row = row_iota(rows, cols)
    for g in range(groups):
        start, valid = token_masks(flags_ref, g, rows, cols)
        lagged = shifted_inputs(xl_ref, halo_ref, g)
        conv = vec_ref[6:7, :] + jnp.zeros((rows, cols), F32)
        for k in range(4):
            conv = conv + vec_ref[2 + k : 3 + k, :] * lagged[k] * valid[k]
        conv_low = conv.astype(BF16)
        conv_ref[g] = conv_low
        prod = jnp.dot(conv_low, gw_ref[...], preferred_element_type=F32)
        ig = jax.nn.sigmoid(prod[:, :cols] + vec_ref[7:8, :])
        dg = jax.nn.sigmoid(prod[:, cols:] + vec_ref[8:9, :])
        ig_ref[g] = ig
        dg_ref[g] = dg
        keep = 1.0 - start
        log_decay = -8.0 * dg * rate_ref[0:1, :]
        p = jnp.exp(log_decay) * keep
        s = jnp.sqrt(keep * neg_expm1(2.0 * log_decay) + start) * ig * conv_low.astype(F32)
        step = 1
        while step < rows:
            inside = row >= step
            p_prev = jnp.where(inside, pltpu.roll(p, step, 0), 1.0)
            s_prev = jnp.where(inside, pltpu.roll(s, step, 0), 0.0)
            s = p * s_prev + s
            p = p * p_prev
            step *= 2
        prod_ref[g] = p
        local_ref[g] = s
        sum_ref[g : g + 1, :] = p[rows - 1 :, :]
        sum_ref[groups + g : groups + g + 1, :] = s[rows - 1 :, :]


def mixer_back_scan(flags_ref, gm_ref, y_ref, dg_ref, prod_ref, local_ref, sin_ref, rate_ref,
                    gy_ref, bprod_ref, blocal_ref, sum_ref):
    groups, rows, cols = gm_ref.shape
    row = row_iota(rows, cols)
    for g in range(groups):
        start, _ = token_masks(flags_ref, g, rows, cols)
        state = local_ref[g] + prod_ref[g] * sin_ref[g : g + 1, :]
        gelu, slope = gelu_pair(y_ref[g])
        gm = gm_ref[g]
        gy_ref[g] = (gm * state * slope).astype(BF16)
        decay = jnp.exp(-8.0 * dg_ref[g] * rate_ref[0:1, :]) * (1.0 - start)
        s = gm * gelu
        p = jnp.where(row == rows - 1, 1.0, pltpu.roll(decay, rows - 1, 0))
        step = 1
        while step < rows:
            inside = row < rows - step
            p_next = jnp.where(inside, pltpu.roll(p, rows - step, 0), 1.0)
            s_next = jnp.where(inside, pltpu.roll(s, rows - step, 0), 0.0)
            s = p * s_next + s
            p = p * p_next
            step *= 2
        bprod_ref[g] = p
        blocal_ref[g] = s
        sum_ref[g : g + 1, :] = decay[:1, :] * p[:1, :]
        sum_ref[groups + g : groups + g + 1, :] = decay[:1, :] * s[:1, :]


def mixer_backward(flags_ref, bprod_ref, blocal_ref, bin_ref, prod_ref, local_ref, sin_ref,
                   ig_ref, dg_ref, conv_ref, xl_ref, halo_ref, gw_ref, vec_ref, rate_ref,
                   gip_ref, gdp_ref, gx_ref, tail_ref, edge_ref, rows_ref):
    groups, rows, cols = xl_ref.shape
    row = row_iota(rows, cols)
    sums = [jnp.zeros((1, cols), F32) for _ in range(8)]
    tail = tail_ref.shape[1]
    pad = edge_ref.shape[1]
    for g in range(groups):
        start, valid = token_masks(flags_ref, g, rows, cols)
        keep = 1.0 - start
        rate = rate_ref[0:1, :]
        state_in = sin_ref[g : g + 1, :]
        state = local_ref[g] + prod_ref[g] * state_in
        prev = jnp.where(row == 0, state_in, pltpu.roll(state, 1, 0))
        sg = blocal_ref[g] + bprod_ref[g] * bin_ref[g : g + 1, :]
        ig, dg = (ig_ref[g], dg_ref[g])
        cf = conv_ref[g].astype(F32)
        log_decay = -8.0 * dg * rate
        decay = jnp.exp(log_decay) * keep
        scale = jnp.sqrt(keep * neg_expm1(2.0 * log_decay) + start)
        gscale = sg * ig * cf
        glog = sg * prev * decay - gscale * keep * jnp.exp(2.0 * log_decay) / scale
        gip = sg * scale * cf * ig * (1.0 - ig)
        gdp = -8.0 * rate * glog * dg * (1.0 - dg)
        gip_low, gdp_low = (gip.astype(BF16), gdp.astype(BF16))
        gip_ref[g] = gip_low
        gdp_ref[g] = gdp_low
        gconv = sg * scale * ig + lax.dot_general(
            jnp.concatenate([gip_low, gdp_low], axis=1), gw_ref[...],
            (((1,), (1,)), ((), ())), preferred_element_type=F32)
        lagged = shifted_inputs(xl_ref, halo_ref, g)
        spread = jnp.zeros((rows + pad, cols), F32)
        for k in range(4):
            masked = gconv * valid[k]
            sums[k] = sums[k] + jnp.sum(masked * lagged[k], axis=0, keepdims=True)
            full = jnp.concatenate(
                [jnp.zeros((pad, cols), F32), vec_ref[2 + k : 3 + k, :] * masked], axis=0)
            spread = spread + (full if k == 0 else pltpu.roll(full, rows + pad - k, 0))
        gx_ref[g] = spread[pad:].astype(BF16)
        tail_ref[g] = spread[pad + rows - tail :]
        edge_ref[g] = spread[:pad]
        sums[4] = sums[4] + jnp.sum(gconv, axis=0, keepdims=True)
        sums[5] = sums[5] + jnp.sum(gip, axis=0, keepdims=True)
        sums[6] = sums[6] + jnp.sum(gdp, axis=0, keepdims=True)
        sums[7] = sums[7] + jnp.sum(-8.0 * dg * glog, axis=0, keepdims=True) * rate_ref[1:2, :]
    rows_ref[...] = jnp.concatenate(sums, axis=0)


def by_head(body, flags, operands, outs):
    def spec(shape, rows_are_channels):
        if rows_are_channels:
            return pl.BlockSpec((BLK, shape[1]), lambda h: (h, 0))
        lead = shape[:-1]
        return pl.BlockSpec(lead + (BLK,), lambda h: (0,) * len(lead) + (h,))

    heads = outs[0].shape[-1] // BLK
    in_specs = [pl.BlockSpec(memory_space=pltpu.SMEM)]
    values = [flags]
    for value, is_gate in operands:
        in_specs.append(spec(value.shape, is_gate))
        values.append(value)
    size = sum(v.size * v.dtype.itemsize for v in values) + sum(
        o.size * o.dtype.itemsize for o in outs)
    return pl.pallas_call(
        body,
        grid=(heads,),
        in_specs=in_specs,
        out_specs=[spec(o.shape, False) for o in outs],
        out_shape=outs,
        compiler_params=pltpu.CompilerParams(vmem_limit_bytes=48 * 1024 * 1024),
        cost_estimate=pl.CostEstimate(
            flops=200 * outs[0].size, bytes_accessed=size, transcendentals=4 * outs[0].size),
    )(*values)


def grad_hidden_of(parts, w_down):
    count = len(parts)
    rows, width = parts[0].shape
    total = count * rows
    ff = w_down.shape[1]

    def body(*refs):
        c_refs, (w_ref, out_ref, held, sem) = (refs[:count], refs[count:])

        @pl.when(pl.program_id(0) == 0)
        def _():
            copies = [
                pltpu.make_async_copy(c_refs[i], held.at[pl.ds(i * rows, rows)], sem.at[i])
                for i in range(count)
            ]
            for copy in copies:
                copy.start()
            for copy in copies:
                copy.wait()

        out_ref[...] = dot(held[...], w_ref[...])

    return pl.pallas_call(
        body,
        grid=(pl.cdiv(ff, BLK),),
        in_specs=[ANY] * count + [pl.BlockSpec((width, BLK), lambda j: (0, j))],
        out_specs=pl.BlockSpec((total, BLK), lambda j: (0, j)),
        out_shape=jax.ShapeDtypeStruct((total, ff), F32),
        scratch_shapes=[pltpu.VMEM((total, width), BF16), pltpu.SemaphoreType.DMA((count,))],
        compiler_params=pltpu.CompilerParams(vmem_limit_bytes=VMEM_MAX),
        cost_estimate=pl.CostEstimate(
            flops=2 * total * width * ff, bytes_accessed=2 * width * ff + 4 * total * ff,
            transcendentals=0),
    )(*parts, w_down)


def sections_of(total):
    found, at = ([], 0)
    while at < total:
        size = min(768, total - at)
        found.append((at, size))
        at += size
    return found


def mlp_forward(n2_parts, grad_hidden, w_gate, w_up):
    count = len(n2_parts)
    rows, width = n2_parts[0].shape
    total = count * rows
    ff = w_gate.shape[1]
    parts = sections_of(ff)
    widest = parts[0][1]
    far = total // 2

    def body(*refs):
        n_refs = refs[:count]
        gh_ref, wg_ref, wu_ref = refs[count : count + 3]
        hid_ref, gg_ref, gu_ref, far_ref, far_c_ref = refs[count + 3 : count + 8]
        n2_s, gh_s, wg_s, wu_s, acc, sem_n, sem_w = refs[count + 8 :]

        def load(k):
            at, size = parts[k]
            slot = k % 2
            return [
                pltpu.make_async_copy(
                    wg_ref.at[:, pl.ds(at, size)], wg_s.at[slot, :, pl.ds(0, size)], sem_w.at[slot, 0]),
                pltpu.make_async_copy(
                    wu_ref.at[:, pl.ds(at, size)], wu_s.at[slot, :, pl.ds(0, size)], sem_w.at[slot, 1]),
                pltpu.make_async_copy(
                    gh_ref.at[:, pl.ds(at, size)], gh_s.at[slot, :, pl.ds(0, size)], sem_w.at[slot, 2]),
            ]

        first = [
            pltpu.make_async_copy(n_refs[i], n2_s.at[pl.ds(i * rows, rows)], sem_n.at[i])
            for i in range(count)
        ]
        for copy in first + load(0):
            copy.start()
        for copy in first:
            copy.wait()
        for k, (at, size) in enumerate(parts):
            if k + 1 < len(parts):
                for copy in load(k + 1):
                    copy.start()
            for copy in load(k):
                copy.wait()
            slot = k % 2
            wg, wu = (wg_s[slot, :, :size], wu_s[slot, :, :size])
            gelu, slope = gelu_pair(dot(n2_s[...], wg))
            up = dot(n2_s[...], wu)
            gh = gh_s[slot, :, :size]
            hid_ref[:, at : at + size] = (gelu * up).astype(BF16)
            gg = (gh * up * slope).astype(BF16)
            gu = (gh * gelu).astype(BF16)
            gg_ref[:, at : at + size] = gg
            gu_ref[:, at : at + size] = gu

            def far_rows(v):
                return jnp.concatenate([v[rows : 2 * rows], v[3 * rows :]], axis=0)

            part = dot_cols(far_rows(gg), wg) + dot_cols(far_rows(gu), wu)
            if k == 0:
                acc[...] = part
            else:
                acc[...] += part
        far_ref[...] = acc[:rows]
        far_c_ref[...] = acc[rows:].astype(BF16)

    act = jax.ShapeDtypeStruct((total, ff), BF16)
    return pl.pallas_call(
        body,
        in_specs=[ANY] * (count + 3),
        out_shape=[act, act, act, jax.ShapeDtypeStruct((rows, width), F32),
                   jax.ShapeDtypeStruct((rows, width), BF16)],
        scratch_shapes=[
            pltpu.VMEM((total, width), BF16),
            pltpu.VMEM((2, total, widest), F32),
            pltpu.VMEM((2, width, widest), BF16),
            pltpu.VMEM((2, width, widest), BF16),
            pltpu.VMEM((far, width), F32),
            pltpu.SemaphoreType.DMA((count,)),
            pltpu.SemaphoreType.DMA((2, 3)),
        ],
        compiler_params=pltpu.CompilerParams(vmem_limit_bytes=VMEM_MAX),
        cost_estimate=pl.CostEstimate(
            flops=6 * total * width * ff, bytes_accessed=4 * width * ff + 16 * total * ff,
            transcendentals=total * ff),
    )(*n2_parts, grad_hidden, w_gate, w_up)


def mlp_rest(hidden, grad_gate, grad_up, w_gate, w_up, w_down, rows):
    total, ff = hidden.shape
    width = w_gate.shape[0]
    block = 512

    def body(hid_ref, gg_ref, gu_ref, wg_ref, wu_ref, wd_ref, gn_ref, gn_c_ref, out_ref, out_c_ref):
        def near(ref):
            return jnp.concatenate([ref[:rows], ref[2 * rows : 3 * rows]], axis=0)

        gn = dot_cols(near(gg_ref), wg_ref[...]) + dot_cols(near(gu_ref), wu_ref[...])
        gn_ref[...] = gn[:rows]
        gn_c_ref[...] = gn[rows:].astype(BF16)
        out = dot_cols(hid_ref[...], wd_ref[...])
        out_ref[...] = out[: total // 2]
        out_c_ref[...] = out[total // 2 :].astype(BF16)

    whole = pl.BlockSpec((total, ff), lambda j: (0, 0))
    weight = pl.BlockSpec((block, ff), lambda j: (j, 0))
    tall = lambda n: pl.BlockSpec((n, block), lambda j: (0, j))
    shape = lambda n, dt: jax.ShapeDtypeStruct((n, width), dt)
    return pl.pallas_call(
        body,
        grid=(width // block,),
        in_specs=[whole] * 3 + [weight] * 3,
        out_specs=[tall(rows), tall(rows), tall(total // 2), tall(total // 2)],
        out_shape=[shape(rows, F32), shape(rows, BF16), shape(total // 2, F32), shape(total // 2, BF16)],
        compiler_params=pltpu.CompilerParams(vmem_limit_bytes=VMEM_MAX),
        cost_estimate=pl.CostEstimate(
            flops=4 * total * width * ff, bytes_accessed=6 * width * ff + 6 * total * ff,
            transcendentals=0),
    )(hidden, grad_gate, grad_up, w_gate, w_up, w_down)


def rows_of_tokens(parts, place, rows_out, each):
    tokens, width = parts[0].shape
    half = width // 2
    count = len(parts)

    def body(place_ref, *refs):
        out_ref, turned = (refs[count], refs[count + 1])
        for k in range(count):
            turned[...] = refs[k][...].T
            for i in range(rows_out // each):
                at = pl.multiple_of((2 * i + place_ref[1]) * each, 16)
                out_ref[i * each : (i + 1) * each, k * tokens : (k + 1) * tokens] = turned[pl.ds(at, each), :]

    return pl.pallas_call(
        body,
        grid_spec=pltpu.PrefetchScalarGridSpec(
            num_scalar_prefetch=1,
            grid=(1,),
            in_specs=[pl.BlockSpec((tokens, half), lambda i, place: (0, place[0]))] * count,
            out_specs=pl.BlockSpec((rows_out, count * tokens), lambda i, place: (0, 0)),
            scratch_shapes=[pltpu.VMEM((half, tokens), BF16)],
        ),
        out_shape=jax.ShapeDtypeStruct((rows_out, count * tokens), BF16),
        compiler_params=pltpu.CompilerParams(vmem_limit_bytes=VMEM_MAX),
        cost_estimate=pl.CostEstimate(
            flops=0, bytes_accessed=6 * rows_out * count * tokens, transcendentals=0),
    )(place, *parts)


def mlp_weight_grads(n2_parts, grad_hiddens, acts, n2_rows, cot_rows, weights, at, size):
    groups = len(n2_parts)
    per = len(n2_parts[0])
    tokens, width = n2_parts[0][0].shape
    group = per * tokens
    both = group // 2
    rows = n2_rows[0].shape[0]
    ff = weights[0].shape[1]
    flat_n = [p for g in n2_parts for p in g]
    total = len(flat_n)

    def body(*refs):
        n_refs, h_refs = (refs[:total], refs[total : total + groups])
        wg_ref, wu_ref, hid_ref, gg_ref, gu_ref, nm, no, cm, co = refs[total + groups : total + groups + 9]
        out_ref = refs[total + groups + 9]
        n2_s, gh_s, acc, sem = refs[total + groups + 10 :]

        def load(g, slot):
            found = []
            for i in range(per):
                to = pl.ds(i * tokens, tokens)
                found.append(pltpu.make_async_copy(n_refs[g * per + i], n2_s.at[slot, to], sem.at[slot, i]))
            found.append(pltpu.make_async_copy(
                h_refs[g].at[:, pl.ds(at, size)], gh_s.at[slot], sem.at[slot, per]))
            return found

        for copy in load(0, 0):
            copy.start()

        def add(g, act, fresh):
            start = g * both if isinstance(g, int) else pl.multiple_of(g * both, both)
            for i, (mine, other) in enumerate(((cm, co), (nm, no), (nm, no))):
                part = dot(mine[:, pl.ds(start, both)], act[i][:both]) + dot(
                    other[:, pl.ds(start, both)], act[i][both:])
                if fresh:
                    acc[i] = part
                else:
                    acc[i] += part

        add(0, (hid_ref[...], gg_ref[...], gu_ref[...]), True)

        def step(g, carry):
            slot = lax.rem(g, 2)
            for k in range(1, groups):
                @pl.when(g + 1 == k)
                def _():
                    for copy in load(k, k % 2):
                        copy.start()

            for copy in load(0, slot):
                copy.wait()
            gelu, slope = gelu_pair(dot(n2_s[slot], wg_ref[...]))
            up = dot(n2_s[slot], wu_ref[...])
            gh = gh_s[slot]
            add(g + 1, ((gelu * up).astype(BF16), (gh * up * slope).astype(BF16), (gh * gelu).astype(BF16)), False)
            return carry

        lax.fori_loop(0, groups, step, 0)
        for i in range(3):
            out_ref[:, i * size : (i + 1) * size] = acc[i].astype(BF16)

    index = at // size
    column = lambda n: pl.BlockSpec((n, size), lambda j: (0, index))
    whole = pl.BlockSpec(n2_rows[0].shape, lambda j: (0, 0))
    return pl.pallas_call(
        body,
        grid=(1,),
        in_specs=[ANY] * (total + groups) + [column(width)] * 2 + [column(group)] * 3 + [whole] * 4,
        out_specs=pl.BlockSpec((rows, 3 * size), lambda j: (0, 0)),
        out_shape=jax.ShapeDtypeStruct((rows, 3 * size), BF16),
        scratch_shapes=[
            pltpu.VMEM((2, group, width), BF16),
            pltpu.VMEM((2, group, size), F32),
            pltpu.VMEM((3, rows, size), F32),
            pltpu.SemaphoreType.DMA((2, per + 1)),
        ],
        compiler_params=pltpu.CompilerParams(vmem_limit_bytes=VMEM_MAX),
        cost_estimate=pl.CostEstimate(
            flops=4 * groups * group * width * size + 6 * (groups + 1) * group * rows * size,
            bytes_accessed=4 * width * size + 4 * groups * group * width,
            transcendentals=groups * group * size),
    )(*flat_n, *grad_hiddens, *weights, *acts, *n2_rows, *cot_rows)


def after(value, *others):
    return lax.optimization_barrier((value, others))[0]


def entering(lay, summary, groups, backward):
    prod, state = (summary[:groups], summary[groups : 2 * groups])
    before_p, before_s = (jnp.ones_like(prod), jnp.zeros_like(state))
    mine = lax.axis_index("seq")
    bit = 1
    while bit < lay.seq:
        other = lay.over_seq_bit(jnp.concatenate([prod, state], axis=0), bit)
        other_p, other_s = (other[:groups], other[groups:])
        is_later = (mine & bit) != 0
        take = jnp.logical_not(is_later) if backward else is_later
        before_s = jnp.where(take, before_p * other_s + before_s, before_s)
        before_p = jnp.where(take, before_p * other_p, before_p)
        state = jnp.where(take, prod * other_s + state, other_p * state + other_s)
        prod = prod * other_p
        bit *= 2
    return before_s


def line_sum(lay, blocks):
    nz, z = (lay.nz, lay.z)

    def pick(t):
        return lax.dynamic_index_in_dim(blocks, jnp.clip(t, 0, nz - 1), 0, keepdims=False).astype(F32)

    right = left = None
    for dist in range(nz - 1, 0, -1):
        up, down = (pick(z + dist), pick(z - dist))
        if right is not None:
            up, down = (up + right.astype(F32), down + left.astype(F32))
        right = lay.send(
            up.astype(BF16), lambda z, y, x, c: (z + 1, y, x, c) if z + dist < nz else None)
        left = lay.send(
            down.astype(BF16), lambda z, y, x, c: (z - 1, y, x, c) if z - dist >= 0 else None)
    return pick(z) + right.astype(F32) + left.astype(F32)


def local(inputs, block_flags, decay_seed, vectors, in_y, in_x, gate_weight, out_proj,
          mlp_gate, mlp_up, mlp_down, cotangent):
    lay = Lay()
    nz, x, y, z, c = (lay.nz, lay.x, lay.y, lay.z, lay.c)
    tokens, width = inputs.shape[1:]
    half = width // 2
    quarter = width // 4
    first = c == 0

    def order_c(own, other, axis):
        return jnp.where(first, jnp.concatenate([own, other], axis),
                         jnp.concatenate([other, own], axis))

    def order_f(rel):
        b = rel.shape[-1] // 4
        p = [rel[..., i * b : (i + 1) * b] for i in range(4)]
        by_c = jnp.where(first, rel, jnp.concatenate([p[1], p[0], p[3], p[2]], -1))
        return jnp.where(x == 0, by_c, jnp.concatenate([by_c[..., 2 * b :], by_c[..., : 2 * b]], -1))

    halo_raw = lay.over_seq(inputs[0, tokens - 16 :], 1)
    residual = inputs[0].astype(F32)
    scaled_one, inverse_one = norm_scale(residual)
    normed_own = (scaled_one * vectors[0]).astype(BF16)
    normed_x = lay.over_x(normed_own)
    halo_own = (norm_scale(halo_raw.astype(F32))[0] * vectors[0]).astype(BF16)
    flag_row = jnp.pad(block_flags.astype(BF16), ((0, 0), (0, width - block_flags.shape[1])))
    halo_x = lay.over_x(jnp.concatenate([flag_row, halo_own[1:]], axis=0))
    n_flags = block_flags.shape[1]
    flags = jnp.concatenate(
        [block_flags.astype(F32), halo_x[:1, :n_flags].astype(F32)], axis=0)

    wy, wx = (in_y, in_x)
    wy_c, wx_c = (lay.over_c(in_y), lay.over_c(in_x))
    rows_mine = lax.dynamic_slice_in_dim(gate_weight, x * half, half, 0)
    rows_theirs = lax.dynamic_slice_in_dim(gate_weight, (1 - x) * half, half, 0)
    gate_x = lay.over_x(rows_theirs)
    gate_c, gate_xc = (lay.over_c(rows_mine), lay.over_c(gate_x))
    gates = order_f(jnp.concatenate([rows_mine, gate_c, gate_x, gate_xc], axis=1))
    out_later = after(out_proj, halo_own)
    out_mine = lax.dynamic_slice_in_dim(out_later, x * half, half, 0)
    out_x = lay.over_x(lax.dynamic_slice_in_dim(out_later, (1 - x) * half, half, 0))
    out_c, out_xc = (lay.over_c(out_mine), lay.over_c(out_x))
    out_rel = jnp.concatenate([out_mine, out_c, out_x, out_xc], axis=1)
    cot = cotangent[0]
    cot_y, cot_z = (lay.over_y(cot), lay.over_z(cot))
    cot_x = lay.over_x(after(cot, normed_own))
    cot_xz, cot_xy = (lay.over_x(cot_z), lay.over_y(cot_x))

    normed = jnp.concatenate([normed_own, normed_x, halo_own, halo_x], axis=0)
    two = 2 * tokens
    y_pre = order_c(dot(normed[:two], wy), dot(normed[:two], wy_c), 1).reshape(2, tokens, half)
    x_all = order_c(dot(normed, wx).astype(BF16), dot(normed, wx_c).astype(BF16), 1)
    x_low = x_all[:two].reshape(2, tokens, half)
    halo = x_all[two:].reshape(2, 16, half)
    vec_half = lax.dynamic_slice_in_dim(vectors, x * half, half, 1)
    base = -5.0 - decay_seed.astype(F32) + vectors[9]
    rates = lax.dynamic_slice_in_dim(
        jnp.stack([jax.nn.softplus(base), jax.nn.sigmoid(base)]), x * half, half, 1)
    shape3 = lambda dt: jax.ShapeDtypeStruct((2, tokens, half), dt)
    summary_shape = jax.ShapeDtypeStruct((4, half), F32)
    conv_low, ig, dg, prods, local_state, summary = by_head(
        mixer_forward, flags,
        [(x_low, False), (halo, False), (gates, True), (vec_half, False), (rates, False)],
        [shape3(BF16), shape3(F32), shape3(F32), shape3(F32), shape3(F32), summary_shape])
    state_in = entering(lay, summary, 2, False)
    cot_yz = lay.over_y(after(cot_z, state_in))
    cot_xyz = lay.over_y(after(cot_xz, state_in))
    cots = [[cot, cot_x], [cot_y, cot_xy], [cot_z, cot_xz], [cot_yz, cot_xyz]]
    cots_c = [[lay.over_c(part) for part in group] for group in cots]
    grad_hiddens = [
        grad_hidden_of(group + group_c, mlp_down) for group, group_c in zip(cots, cots_c)]
    state = local_state + prods * state_in[:, None, :]
    mixed = (state * jax.nn.gelu(y_pre, approximate=True)).astype(BF16)
    part_x = dot(mixed[1], out_rel).astype(BF16)
    part_x = lay.over_x(part_x)
    part_own = dot(mixed[0], out_rel)
    swapped = jnp.concatenate([part_x[:, half:], part_x[:, :half]], axis=1)
    mid = residual + order_f(part_own + swapped.astype(F32))

    scaled_two, inverse_two = norm_scale(mid)
    n2 = (scaled_two * vectors[1]).astype(BF16)
    n2_x = lay.over_x(n2)
    n2_y, n2_z = (lay.over_y(n2), lay.over_z(n2))
    n2_xy, n2_xz = (lay.over_y(n2_x), lay.over_z(n2_x))
    n2_yz, n2_xyz = (lay.over_y(n2_z), lay.over_y(n2_xz))
    n2s = [[n2, n2_x], [n2_y, n2_xy], [n2_z, n2_xz], [n2_yz, n2_xyz]]
    n2s_c = [[lay.over_c(part) for part in group] for group in n2s]
    hidden, grad_gate, grad_up, far, far_c = mlp_forward(
        n2s[0] + n2s_c[0], grad_hiddens[0], mlp_gate, mlp_up)
    arriving = lay.over_x((far + lay.over_c(far_c).astype(F32)).astype(BF16))
    near, near_c, out, out_c = mlp_rest(
        hidden, grad_gate, grad_up, mlp_gate, mlp_up, mlp_down, tokens)
    grad_n2 = near + lay.over_c(near_c).astype(F32) + arriving.astype(F32)
    out_sum = out + lay.over_c(out_c).astype(F32)

    grad_mid_norm, grad_gain_two = norm_back(grad_n2, scaled_two, inverse_two, vectors[1])
    grad_mid = cot.astype(F32) + grad_mid_norm
    branch = grad_mid.astype(BF16)
    branch_rel = order_f(branch)
    arriving = lay.over_x(branch_rel)
    branch_x_rel = jnp.concatenate([arriving[:, half:], arriving[:, :half]], axis=1)
    out_arriving = lay.over_x(after(out_sum[tokens:].astype(BF16), branch))
    output = (mid + out_sum[:tokens] + out_arriving.astype(F32)).astype(BF16)[None]
    grad_mixed = dot_cols(jnp.concatenate([branch_rel, branch_x_rel], 0), out_rel)
    gy, bprod, blocal, back_summary = by_head(
        mixer_back_scan, flags,
        [(grad_mixed.reshape(2, tokens, half), False), (y_pre, False), (dg, False), (prods, False),
         (local_state, False), (state_in, False), (rates, False)],
        [shape3(BF16), shape3(F32), shape3(F32), summary_shape])
    back_in = entering(lay, back_summary, 2, True)
    gip, gdp, gx_main, gx_tail, edge, vec_rows = by_head(
        mixer_backward, flags,
        [(bprod, False), (blocal, False), (back_in, False), (prods, False), (local_state, False),
         (state_in, False), (ig, False), (dg, False), (conv_low, False), (x_low, False),
         (halo, False), (gates, True), (vec_half, False), (rates, False)],
        [shape3(BF16), shape3(BF16), shape3(BF16), jax.ShapeDtypeStruct((2, 16, half), F32),
         jax.ShapeDtypeStruct((2, 8, half), F32), jax.ShapeDtypeStruct((8, half), F32)])
    edge_next = lay.over_seq(edge, -1)
    gx_last = (gx_tail + jnp.pad(edge_next, ((0, 0), (8, 0), (0, 0)))).astype(BF16)
    gx = jnp.concatenate([gx_main[:, : tokens - 16], gx_last], axis=1).reshape(two, half)
    gy = gy.reshape(two, half)

    def own_cols(value, which):
        return lax.dynamic_slice_in_dim(value, which * quarter, quarter, 1)

    gy_o, gy_c, gx_o, gx_c = (
        own_cols(gy, c), own_cols(gy, 1 - c), own_cols(gx, c), own_cols(gx, 1 - c))

    def grad_n1_of(rows):
        return (dot_cols(gy_o[rows], wy) + dot_cols(gy_c[rows], wy_c)
                + dot_cols(gx_o[rows], wx) + dot_cols(gx_c[rows], wx_c))

    grad_n1_far = grad_n1_of(slice(tokens, two)).astype(BF16)
    arriving = lay.over_x(grad_n1_far)
    grad_n1 = grad_n1_of(slice(0, tokens)) + arriving.astype(F32)
    grad_in_norm, grad_gain_one = norm_back(grad_n1, scaled_one, inverse_one, vectors[0])
    input_grad = (grad_mid + grad_in_norm).astype(BF16)[None]

    each = width // lay.seq
    seq_at = 2 * z + y
    place = jnp.stack([seq_at // nz, y]).astype(jnp.int32)
    n2_rows = rows_of_tokens([p for group in n2s for p in group], place, half // 2, each)
    cot_rows = rows_of_tokens([p for group in cots for p in group], place, half // 2, each)
    row_pairs = ((n2_rows, lay.over_c(n2_rows)), (cot_rows, lay.over_c(cot_rows)))
    acts = (hidden, grad_gate, grad_up)
    sides = [group + group_c for group, group_c in zip(n2s[1:], n2s_c[1:])]
    share = [
        [2 * (upper * (nz // 2) + low) + side for low in range(nz // 2)]
        for upper in range(2) for side in range(2)]
    ties = (branch, grad_n1_far, input_grad)
    columns = [[], [], []]
    for (at, size), tie in zip(sections_of(mlp_gate.shape[1]), ties):
        part = mlp_weight_grads(
            sides, grad_hiddens[1:], after(acts, tie), *row_pairs, (mlp_gate, mlp_up), at, size)
        part = lax.psum_scatter(
            part, "seq", scatter_dimension=0, axis_index_groups=share, tiled=True)
        for i in range(3):
            columns[i].append(part[:, i * size : (i + 1) * size])
    mlp_down_grad, mlp_gate_grad, mlp_up_grad = [
        jnp.concatenate(parts, axis=1).astype(F32) for parts in columns]

    rows_full = lax.dynamic_update_slice_in_dim(
        jnp.zeros((8, width), F32), vec_rows, x * half, 1)
    vec = jnp.concatenate([grad_gain_one[None], grad_gain_two[None], rows_full], axis=0)
    vec = vec + lay.over_c(vec)
    vec = vec + lay.over_x(vec)
    bit = 1
    while bit < lay.seq:
        vec = vec + lay.over_seq_bit(vec, bit)
        bit *= 2

    own80 = each // 4

    def spread_rows(value, where):
        by_yc = where(value.T)
        by_c = lax.dynamic_index_in_dim(by_yc, c, 1, keepdims=False)
        other_c = lax.dynamic_index_in_dim(by_yc, 1 - c, 1, keepdims=False)
        pair = jnp.concatenate([by_c, lay.over_c(other_c)], axis=2)
        by_y = lax.dynamic_index_in_dim(pair, y, 0, keepdims=False)
        other_y = lax.dynamic_index_in_dim(pair, 1 - y, 0, keepdims=False)
        return jnp.concatenate([by_y, lay.over_y(other_y)], axis=1)

    def all_tokens(value):
        other_y = lay.over_y(value)
        return jnp.concatenate([value, lay.over_c(value), other_y, lay.over_c(other_y)], 0)

    def where_n1(rows):
        split = rows.reshape(nz, 2, 2, 2, own80, two)
        return split.transpose(1, 3, 0, 2, 4, 5).reshape(2, 2, nz * 2 * own80, two)

    def where_mixed(rows):
        split = rows.reshape(2, nz, 2, own80, two)
        return split.transpose(0, 2, 1, 3, 4).reshape(2, 2, nz * own80, two)

    n1_rows = spread_rows(jnp.concatenate([normed_own, normed_x], 0), where_n1)
    mixed_rows = spread_rows(mixed.reshape(two, half), where_mixed)
    branch_all = all_tokens(jnp.concatenate([branch, order_f(branch_x_rel)], 0))
    out_part = dot(mixed_rows, branch_all).astype(BF16).reshape(nz, 2 * own80, half)
    in_y_part = dot(n1_rows, all_tokens(gy)).astype(BF16).reshape(nz, 2 * own80, half)
    done_one = line_sum(lay, jnp.concatenate([in_y_part, out_part], axis=1)).astype(BF16)

    heads = half // BLK
    gate_part = jnp.einsum(
        "thi,thj->hij", conv_low.reshape(two, heads, BLK),
        jnp.concatenate([gip.reshape(two, heads, BLK), gdp.reshape(two, heads, BLK)], 2),
        preferred_element_type=F32).reshape(2, nz, 2, own80, 2 * BLK)
    keep = lax.dynamic_index_in_dim(gate_part, c, 2, keepdims=False)
    away = lax.dynamic_index_in_dim(gate_part, 1 - c, 2, keepdims=False)
    gate_part = keep + lay.over_c(away.astype(BF16)).astype(F32)
    keep = lax.dynamic_index_in_dim(gate_part, y, 0, keepdims=False)
    away = lax.dynamic_index_in_dim(gate_part, 1 - y, 0, keepdims=False)
    gate_part = (keep + lay.over_y(away.astype(BF16)).astype(F32)).astype(BF16)
    in_x_part = dot(n1_rows, all_tokens(gx)).astype(BF16).reshape(nz, 2 * own80, half)
    done_two = line_sum(lay, jnp.concatenate(
        [in_x_part, gate_part.reshape(nz, own80 * 2 * BLK // half, half)], axis=1)).astype(BF16)

    def over_columns(value):
        split = value.reshape(2, own80, half)
        mine = lax.dynamic_index_in_dim(split, x, 0, keepdims=False)
        theirs = lay.over_x(lax.dynamic_index_in_dim(split, 1 - x, 0, keepdims=False))
        return jnp.where(x == 0, jnp.concatenate([mine, theirs], -1),
                         jnp.concatenate([theirs, mine], -1)).astype(F32)

    in_y_grad = over_columns(done_one[: 2 * own80])
    in_x_grad = over_columns(done_two[: 2 * own80])
    def final(z, y, x, c):
        at = ((x * 2 + y) * nz + z) * 2 + c
        s, f = (at // 4, at % 4)
        return (s // 2, s % 2, f // 2, f % 2)

    out_grad = lay.send(done_one[2 * own80 :].reshape(own80, width), final).astype(F32)
    gate_grad = lay.send(done_two[2 * own80 :].reshape(own80, 2 * BLK), final).astype(F32)
    return (output, input_grad, vec, in_y_grad, in_x_grad, gate_grad, out_grad,
            mlp_gate_grad, mlp_up_grad, mlp_down_grad)


def solution(mesh):
    return jax.shard_map(
        local,
        mesh=mesh,
        in_specs=(
            P("fsdp", "seq", None),
            P("fsdp", "seq"),
            P(),
            P(),
            P(None, "fsdp"),
            P(None, "fsdp"),
            P(None, "fsdp"),
            P(None, "fsdp"),
            P(None, "fsdp"),
            P(None, "fsdp"),
            P(None, "fsdp"),
            P("fsdp", "seq", None),
        ),
        out_specs=(
            P("fsdp", "seq", None),
            P("fsdp", "seq", None),
            P(),
            P(("seq", "fsdp"), None),
            P(("seq", "fsdp"), None),
            P(("seq", "fsdp"), None),
            P(("seq", "fsdp"), None),
            P("seq", "fsdp"),
            P("seq", "fsdp"),
            P("seq", "fsdp"),
        ),
        check_vma=False,
    )
```

```python
import functools

import jax
import jax.numpy as jnp
from jax import lax
from jax.experimental import pallas as pl
from jax.experimental.pallas import tpu as pltpu
from jax.sharding import PartitionSpec as P

HEADS = 10
BLK = 256
FBLK = 64
EPS = 1e-06
ALL = ("seq", "fsdp")
F32 = jnp.float32
BF16 = jnp.bfloat16
GELU_C = 0.7978845608028654
GELU_A = 0.044715
VMEM_MAX = 60 * 1024 * 1024
ANY = pl.BlockSpec(memory_space=pl.ANY)
SMALL = pl.CostEstimate(flops=1, bytes_accessed=1, transcendentals=0)


def norm_scale(values):
    inverse = lax.rsqrt(jnp.mean(values * values, axis=-1, keepdims=True) + EPS)
    return (values * inverse, inverse)


def norm_back(grad_normed, scaled, inverse, gain_row):
    grad_gain = jnp.sum(grad_normed * scaled, axis=0)
    inner_term = grad_normed * gain_row
    grad_input = inverse * (
        inner_term - scaled * jnp.mean(inner_term * scaled, axis=-1, keepdims=True)
    )
    return (grad_input, grad_gain)


def gelu_pair(values):
    square = values * values
    t = jnp.tanh(values * (GELU_C + GELU_C * GELU_A * square))
    half = 0.5 + 0.5 * t
    slope = half * (1.0 + (1.0 - t) * values * (GELU_C + 3.0 * GELU_C * GELU_A * square))
    return (values * half, slope)


def dot(left, right):
    return jnp.dot(left, right, preferred_element_type=F32)


def dot_rows(left, right):
    return lax.dot_general(left, right, (((0,), (0,)), ((), ())), preferred_element_type=F32)


def dot_cols(left, right):
    return lax.dot_general(left, right, (((1,), (1,)), ((), ())), preferred_element_type=F32)


class Lay:
    def __init__(self):
        self.seq = lax.axis_size("seq")
        self.nz = self.seq // 2
        seq, fsdp = (lax.axis_index("seq"), lax.axis_index("fsdp"))
        self.z, self.y = (seq // 2, seq % 2)
        self.x, self.c = (fsdp // 2, fsdp % 2)
        self.seq_at = seq

    def pairs(self, target):
        found = []
        for s in range(self.seq):
            for f in range(4):
                z, y, x, c = (s // 2, s % 2, f // 2, f % 2)
                to = target(z, y, x, c)
                if to is not None:
                    found.append((s * 4 + f, ((to[0] * 2 + to[1]) * 2 + to[2]) * 2 + to[3]))
        return found

    def send(self, value, target):
        return lax.ppermute(value, ALL, self.pairs(target))

    def over_c(self, value):
        return self.send(value, lambda z, y, x, c: (z, y, x, 1 - c))

    def over_x(self, value):
        return self.send(value, lambda z, y, x, c: (z, y, 1 - x, c))

    def over_y(self, value):
        return self.send(value, lambda z, y, x, c: (z, 1 - y, x, c))

    def over_seq_bit(self, value, bit):
        def to(z, y, x, c):
            other = (2 * z + y) ^ bit
            return (other // 2, other % 2, x, c)

        return self.send(value, to)

    def over_z(self, value):
        return self.send(value, lambda z, y, x, c: (self.nz - 1 - z, y, x, c))

    def over_seq(self, value, by):
        def to(z, y, x, c):
            other = 2 * z + y + by
            return (other // 2, other % 2, x, c) if 0 <= other < self.seq else None

        return self.send(value, to)


def row_iota(rows, cols):
    return lax.broadcasted_iota(jnp.int32, (rows, cols), 0)


def token_masks(flags_ref, g, rows, cols):
    row = row_iota(rows, cols)
    block = row // FBLK
    offset = row % FBLK
    flagged = jnp.zeros((rows, cols), F32)
    for b in range(rows // FBLK):
        flagged = jnp.where(block == b, flags_ref[g, b], flagged)
    valid = [jnp.where(offset < lag, 1.0 - flagged, 1.0) for lag in range(4)]
    start = jnp.where(offset == 0, flagged, 0.0)
    return start, valid


def neg_expm1(v):
    series = 1.0 + v * (1.0 / 6.0)
    for n in (5.0, 4.0, 3.0, 2.0):
        series = 1.0 + v * (1.0 / n) * series
    return jnp.where(v > -0.25, -v * series, 1.0 - jnp.exp(v))


def shifted_inputs(xl_ref, halo_ref, g):
    ext = jnp.concatenate([halo_ref[g].astype(F32), xl_ref[g].astype(F32)], axis=0)
    pad = halo_ref.shape[1]
    return [ext[pad:] if k == 0 else pltpu.roll(ext, k, 0)[pad:] for k in range(4)]


def mixer_forward(flags_ref, xl_ref, halo_ref, gw_ref, vec_ref, rate_ref,
                  conv_ref, ig_ref, dg_ref, prod_ref, local_ref, sum_ref):
    groups, rows, cols = xl_ref.shape
    row = row_iota(rows, cols)
    for g in range(groups):
        start, valid = token_masks(flags_ref, g, rows, cols)
        lagged = shifted_inputs(xl_ref, halo_ref, g)
        conv = vec_ref[6:7, :] + jnp.zeros((rows, cols), F32)
        for k in range(4):
            conv = conv + vec_ref[2 + k : 3 + k, :] * lagged[k] * valid[k]
        conv_low = conv.astype(BF16)
        conv_ref[g] = conv_low
        prod = jnp.dot(conv_low, gw_ref[...], preferred_element_type=F32)
        ig = jax.nn.sigmoid(prod[:, :cols] + vec_ref[7:8, :])
        dg = jax.nn.sigmoid(prod[:, cols:] + vec_ref[8:9, :])
        ig_ref[g] = ig
        dg_ref[g] = dg
        keep = 1.0 - start
        log_decay = -8.0 * dg * rate_ref[0:1, :]
        p = jnp.exp(log_decay) * keep
        s = jnp.sqrt(keep * neg_expm1(2.0 * log_decay) + start) * ig * conv_low.astype(F32)
        step = 1
        while step < rows:
            inside = row >= step
            p_prev = jnp.where(inside, pltpu.roll(p, step, 0), 1.0)
            s_prev = jnp.where(inside, pltpu.roll(s, step, 0), 0.0)
            s = p * s_prev + s
            p = p * p_prev
            step *= 2
        prod_ref[g] = p
        local_ref[g] = s
        sum_ref[g : g + 1, :] = p[rows - 1 :, :]
        sum_ref[groups + g : groups + g + 1, :] = s[rows - 1 :, :]


def mixer_back_scan(flags_ref, gm_ref, y_ref, dg_ref, prod_ref, local_ref, sin_ref, rate_ref,
                    gy_ref, bprod_ref, blocal_ref, sum_ref):
    groups, rows, cols = gm_ref.shape
    row = row_iota(rows, cols)
    for g in range(groups):
        start, _ = token_masks(flags_ref, g, rows, cols)
        state = local_ref[g] + prod_ref[g] * sin_ref[g : g + 1, :]
        gelu, slope = gelu_pair(y_ref[g])
        gm = gm_ref[g]
        gy_ref[g] = (gm * state * slope).astype(BF16)
        decay = jnp.exp(-8.0 * dg_ref[g] * rate_ref[0:1, :]) * (1.0 - start)
        s = gm * gelu
        p = jnp.where(row == rows - 1, 1.0, pltpu.roll(decay, rows - 1, 0))
        step = 1
        while step < rows:
            inside = row < rows - step
            p_next = jnp.where(inside, pltpu.roll(p, rows - step, 0), 1.0)
            s_next = jnp.where(inside, pltpu.roll(s, rows - step, 0), 0.0)
            s = p * s_next + s
            p = p * p_next
            step *= 2
        bprod_ref[g] = p
        blocal_ref[g] = s
        sum_ref[g : g + 1, :] = decay[:1, :] * p[:1, :]
        sum_ref[groups + g : groups + g + 1, :] = decay[:1, :] * s[:1, :]


def mixer_backward(flags_ref, bprod_ref, blocal_ref, bin_ref, prod_ref, local_ref, sin_ref,
                   ig_ref, dg_ref, conv_ref, xl_ref, halo_ref, gw_ref, vec_ref, rate_ref,
                   gip_ref, gdp_ref, gx_ref, tail_ref, edge_ref, rows_ref):
    groups, rows, cols = xl_ref.shape
    row = row_iota(rows, cols)
    sums = [jnp.zeros((1, cols), F32) for _ in range(8)]
    tail = tail_ref.shape[1]
    pad = edge_ref.shape[1]
    for g in range(groups):
        start, valid = token_masks(flags_ref, g, rows, cols)
        keep = 1.0 - start
        rate = rate_ref[0:1, :]
        state_in = sin_ref[g : g + 1, :]
        state = local_ref[g] + prod_ref[g] * state_in
        prev = jnp.where(row == 0, state_in, pltpu.roll(state, 1, 0))
        sg = blocal_ref[g] + bprod_ref[g] * bin_ref[g : g + 1, :]
        ig, dg = (ig_ref[g], dg_ref[g])
        cf = conv_ref[g].astype(F32)
        log_decay = -8.0 * dg * rate
        decay = jnp.exp(log_decay) * keep
        scale = jnp.sqrt(keep * neg_expm1(2.0 * log_decay) + start)
        gscale = sg * ig * cf
        glog = sg * prev * decay - gscale * keep * jnp.exp(2.0 * log_decay) / scale
        gip = sg * scale * cf * ig * (1.0 - ig)
        gdp = -8.0 * rate * glog * dg * (1.0 - dg)
        gip_low, gdp_low = (gip.astype(BF16), gdp.astype(BF16))
        gip_ref[g] = gip_low
        gdp_ref[g] = gdp_low
        gconv = sg * scale * ig + lax.dot_general(
            jnp.concatenate([gip_low, gdp_low], axis=1), gw_ref[...],
            (((1,), (1,)), ((), ())), preferred_element_type=F32)
        lagged = shifted_inputs(xl_ref, halo_ref, g)
        spread = jnp.zeros((rows + pad, cols), F32)
        for k in range(4):
            masked = gconv * valid[k]
            sums[k] = sums[k] + jnp.sum(masked * lagged[k], axis=0, keepdims=True)
            full = jnp.concatenate(
                [jnp.zeros((pad, cols), F32), vec_ref[2 + k : 3 + k, :] * masked], axis=0)
            spread = spread + (full if k == 0 else pltpu.roll(full, rows + pad - k, 0))
        gx_ref[g] = spread[pad:].astype(BF16)
        tail_ref[g] = spread[pad + rows - tail :]
        edge_ref[g] = spread[:pad]
        sums[4] = sums[4] + jnp.sum(gconv, axis=0, keepdims=True)
        sums[5] = sums[5] + jnp.sum(gip, axis=0, keepdims=True)
        sums[6] = sums[6] + jnp.sum(gdp, axis=0, keepdims=True)
        sums[7] = sums[7] + jnp.sum(-8.0 * dg * glog, axis=0, keepdims=True) * rate_ref[1:2, :]
    rows_ref[...] = jnp.concatenate(sums, axis=0)


def by_head(body, flags, operands, outs):
    def spec(shape, rows_are_channels):
        if rows_are_channels:
            return pl.BlockSpec((BLK, shape[1]), lambda h: (h, 0))
        lead = shape[:-1]
        return pl.BlockSpec(lead + (BLK,), lambda h: (0,) * len(lead) + (h,))

    heads = outs[0].shape[-1] // BLK
    in_specs = [pl.BlockSpec(memory_space=pltpu.SMEM)]
    values = [flags]
    for value, is_gate in operands:
        in_specs.append(spec(value.shape, is_gate))
        values.append(value)
    size = sum(v.size * v.dtype.itemsize for v in values) + sum(
        o.size * o.dtype.itemsize for o in outs)
    return pl.pallas_call(
        body,
        grid=(heads,),
        in_specs=in_specs,
        out_specs=[spec(o.shape, False) for o in outs],
        out_shape=outs,
        compiler_params=pltpu.CompilerParams(vmem_limit_bytes=48 * 1024 * 1024),
        cost_estimate=SMALL,
    )(*values)


def grad_hidden_of(parts, w_down):
    count = len(parts)
    rows, width = parts[0].shape
    total = count * rows
    ff = w_down.shape[1]

    def body(*refs):
        c_refs, (w_ref, out_ref, held, sem) = (refs[:count], refs[count:])

        @pl.when(pl.program_id(0) == 0)
        def _():
            copies = [
                pltpu.make_async_copy(c_refs[i], held.at[pl.ds(i * rows, rows)], sem.at[i])
                for i in range(count)
            ]
            for copy in copies:
                copy.start()
            for copy in copies:
                copy.wait()

        out_ref[...] = dot(held[...], w_ref[...])

    return pl.pallas_call(
        body,
        grid=(pl.cdiv(ff, BLK),),
        in_specs=[ANY] * count + [pl.BlockSpec((width, BLK), lambda j: (0, j))],
        out_specs=pl.BlockSpec((total, BLK), lambda j: (0, j)),
        out_shape=jax.ShapeDtypeStruct((total, ff), F32),
        scratch_shapes=[pltpu.VMEM((total, width), BF16), pltpu.SemaphoreType.DMA((count,))],
        compiler_params=pltpu.CompilerParams(vmem_limit_bytes=VMEM_MAX),
        cost_estimate=SMALL,
    )(*parts, w_down)


def sections_of(total):
    found, at = ([], 0)
    while at < total:
        size = min(768, total - at)
        found.append((at, size))
        at += size
    return found


def mlp_forward(n2_parts, grad_hidden, w_gate, w_up):
    count = len(n2_parts)
    rows, width = n2_parts[0].shape
    total = count * rows
    ff = w_gate.shape[1]
    parts = sections_of(ff)
    widest = parts[0][1]
    far = total // 2

    def body(*refs):
        n_refs = refs[:count]
        gh_ref, wg_ref, wu_ref = refs[count : count + 3]
        hid_ref, gg_ref, gu_ref, far_ref, far_c_ref = refs[count + 3 : count + 8]
        n2_s, gh_s, wg_s, wu_s, acc, sem_n, sem_w = refs[count + 8 :]

        def load(k):
            at, size = parts[k]
            slot = k % 2
            return [
                pltpu.make_async_copy(
                    wg_ref.at[:, pl.ds(at, size)], wg_s.at[slot, :, pl.ds(0, size)], sem_w.at[slot, 0]),
                pltpu.make_async_copy(
                    wu_ref.at[:, pl.ds(at, size)], wu_s.at[slot, :, pl.ds(0, size)], sem_w.at[slot, 1]),
                pltpu.make_async_copy(
                    gh_ref.at[:, pl.ds(at, size)], gh_s.at[slot, :, pl.ds(0, size)], sem_w.at[slot, 2]),
            ]

        first = [
            pltpu.make_async_copy(n_refs[i], n2_s.at[pl.ds(i * rows, rows)], sem_n.at[i])
            for i in range(count)
        ]
        for copy in first + load(0):
            copy.start()
        for copy in first:
            copy.wait()
        for k, (at, size) in enumerate(parts):
            if k + 1 < len(parts):
                for copy in load(k + 1):
                    copy.start()
            for copy in load(k):
                copy.wait()
            slot = k % 2
            wg, wu = (wg_s[slot, :, :size], wu_s[slot, :, :size])
            gelu, slope = gelu_pair(dot(n2_s[...], wg))
            up = dot(n2_s[...], wu)
            gh = gh_s[slot, :, :size]
            hid_ref[:, at : at + size] = (gelu * up).astype(BF16)
            gg = (gh * up * slope).astype(BF16)
            gu = (gh * gelu).astype(BF16)
            gg_ref[:, at : at + size] = gg
            gu_ref[:, at : at + size] = gu

            def far_rows(v):
                return jnp.concatenate([v[rows : 2 * rows], v[3 * rows :]], axis=0)

            part = dot_cols(far_rows(gg), wg) + dot_cols(far_rows(gu), wu)
            if k == 0:
                acc[...] = part
            else:
                acc[...] += part
        far_ref[...] = acc[:rows]
        far_c_ref[...] = acc[rows:].astype(BF16)

    act = jax.ShapeDtypeStruct((total, ff), BF16)
    return pl.pallas_call(
        body,
        in_specs=[ANY] * (count + 3),
        out_shape=[act, act, act, jax.ShapeDtypeStruct((rows, width), F32),
                   jax.ShapeDtypeStruct((rows, width), BF16)],
        scratch_shapes=[
            pltpu.VMEM((total, width), BF16),
            pltpu.VMEM((2, total, widest), F32),
            pltpu.VMEM((2, width, widest), BF16),
            pltpu.VMEM((2, width, widest), BF16),
            pltpu.VMEM((far, width), F32),
            pltpu.SemaphoreType.DMA((count,)),
            pltpu.SemaphoreType.DMA((2, 3)),
        ],
        compiler_params=pltpu.CompilerParams(vmem_limit_bytes=VMEM_MAX),
        cost_estimate=SMALL,
    )(*n2_parts, grad_hidden, w_gate, w_up)


def mlp_rest(hidden, grad_gate, grad_up, w_gate, w_up, w_down, rows):
    total, ff = hidden.shape
    width = w_gate.shape[0]
    block = 512

    def body(hid_ref, gg_ref, gu_ref, wg_ref, wu_ref, wd_ref, gn_ref, gn_c_ref, out_ref, out_c_ref):
        def near(ref):
            return jnp.concatenate([ref[:rows], ref[2 * rows : 3 * rows]], axis=0)

        gn = dot_cols(near(gg_ref), wg_ref[...]) + dot_cols(near(gu_ref), wu_ref[...])
        gn_ref[...] = gn[:rows]
        gn_c_ref[...] = gn[rows:].astype(BF16)
        out = dot_cols(hid_ref[...], wd_ref[...])
        out_ref[...] = out[: total // 2]
        out_c_ref[...] = out[total // 2 :].astype(BF16)

    whole = pl.BlockSpec((total, ff), lambda j: (0, 0))
    weight = pl.BlockSpec((block, ff), lambda j: (j, 0))
    tall = lambda n: pl.BlockSpec((n, block), lambda j: (0, j))
    shape = lambda n, dt: jax.ShapeDtypeStruct((n, width), dt)
    return pl.pallas_call(
        body,
        grid=(width // block,),
        in_specs=[whole] * 3 + [weight] * 3,
        out_specs=[tall(rows), tall(rows), tall(total // 2), tall(total // 2)],
        out_shape=[shape(rows, F32), shape(rows, BF16), shape(total // 2, F32), shape(total // 2, BF16)],
        compiler_params=pltpu.CompilerParams(vmem_limit_bytes=VMEM_MAX),
        cost_estimate=SMALL,
    )(hidden, grad_gate, grad_up, w_gate, w_up, w_down)


def rows_of_tokens(parts, place, rows_out, each):
    tokens, width = parts[0].shape
    half = width // 2
    count = len(parts)

    def body(place_ref, *refs):
        out_ref, turned = (refs[count], refs[count + 1])
        for k in range(count):
            turned[...] = refs[k][...].T
            for i in range(rows_out // each):
                at = pl.multiple_of((2 * i + place_ref[1]) * each, 16)
                out_ref[i * each : (i + 1) * each, k * tokens : (k + 1) * tokens] = turned[pl.ds(at, each), :]

    return pl.pallas_call(
        body,
        grid_spec=pltpu.PrefetchScalarGridSpec(
            num_scalar_prefetch=1,
            grid=(1,),
            in_specs=[pl.BlockSpec((tokens, half), lambda i, place: (0, place[0]))] * count,
            out_specs=pl.BlockSpec((rows_out, count * tokens), lambda i, place: (0, 0)),
            scratch_shapes=[pltpu.VMEM((half, tokens), BF16)],
        ),
        out_shape=jax.ShapeDtypeStruct((rows_out, count * tokens), BF16),
        compiler_params=pltpu.CompilerParams(vmem_limit_bytes=VMEM_MAX),
        cost_estimate=SMALL,
    )(place, *parts)


def mlp_weight_grads(place, n2_parts, given, cot_parts, acts, n2_rows, cot_rows, weights, at, size, each):
    groups, ready = (len(n2_parts), len(given))
    per = len(n2_parts[0])
    tokens, width = n2_parts[0][0].shape
    group = per * tokens
    both = group // 2
    rows = n2_rows[0].shape[0]
    flat_n = [p for g in n2_parts for p in g]
    flat_c = [p for g in cot_parts for p in g]
    lead = [len(flat_n), len(flat_c), ready]

    def body(place_ref, *refs):
        n_refs, refs = (refs[: lead[0]], refs[lead[0] :])
        c_refs, refs = (refs[: lead[1]], refs[lead[1] :])
        h_refs, refs = (refs[: lead[2]], refs[lead[2] :])
        wg_ref, wu_ref, wd_ref, hid_ref, gg_ref, gu_ref, nm, no, cm, co = refs[:10]
        own_ref, rest_ref, n2_s, cot_s, gh_s, acc, sem = refs[10:]

        def load(g, slot):
            found = []
            for i in range(per):
                to = pl.ds(i * tokens, tokens)
                found.append(pltpu.make_async_copy(n_refs[g * per + i], n2_s.at[slot, to], sem.at[slot, i]))
                if g >= ready:
                    found.append(pltpu.make_async_copy(
                        c_refs[(g - ready) * per + i], cot_s.at[slot, to], sem.at[slot, per + i]))
            if g < ready:
                found.append(pltpu.make_async_copy(
                    h_refs[g].at[:, pl.ds(at, size)], gh_s, sem.at[slot, per]))
            return found

        for copy in load(0, 0):
            copy.start()

        def add(g, act, fresh):
            span = slice(g * both, (g + 1) * both)
            for i, (mine, other) in enumerate(((cm, co), (nm, no), (nm, no))):
                part = dot(mine[:, span], act[i][:both]) + dot(other[:, span], act[i][both:])
                if fresh:
                    acc[i] = part
                else:
                    acc[i] += part

        add(0, (hid_ref, gg_ref, gu_ref), True)
        for g in range(groups):
            slot = g % 2
            if g + 1 < groups:
                for copy in load(g + 1, 1 - slot):
                    copy.start()
            for copy in load(g, slot):
                copy.wait()
            gelu, slope = gelu_pair(dot(n2_s[slot], wg_ref[...]))
            up = dot(n2_s[slot], wu_ref[...])
            gh = gh_s[...] if g < ready else dot(cot_s[slot], wd_ref[...])
            add(g + 1, ((gelu * up).astype(BF16), (gh * up * slope).astype(BF16), (gh * gelu).astype(BF16)), False)
        for j in range(rows // each):
            start = pl.multiple_of((place_ref[0] ^ j) * each, 8)
            for i in range(3):
                block = acc[i, pl.ds(start, each), :]
                if j == 0:
                    own_ref[:, i * size : (i + 1) * size] = block
                else:
                    rest_ref[(j - 1) * each : j * each, i * size : (i + 1) * size] = block.astype(BF16)

    index = at // size
    column = lambda n: pl.BlockSpec((n, size), lambda j, place: (0, index))
    whole = pl.BlockSpec(n2_rows[0].shape, lambda j, place: (0, 0))
    return pl.pallas_call(
        body,
        grid_spec=pltpu.PrefetchScalarGridSpec(
            num_scalar_prefetch=1,
            grid=(1,),
            in_specs=[ANY] * sum(lead) + [column(width)] * 3 + [column(group)] * 3 + [whole] * 4,
            out_specs=[pl.BlockSpec((each, 3 * size), lambda j, place: (0, 0)),
                       pl.BlockSpec((rows - each, 3 * size), lambda j, place: (0, 0))],
            scratch_shapes=[
                pltpu.VMEM((2, group, width), BF16),
                pltpu.VMEM((2, group, width), BF16),
                pltpu.VMEM((group, size), F32),
                pltpu.VMEM((3, rows, size), F32),
                pltpu.SemaphoreType.DMA((2, 2 * per)),
            ],
        ),
        out_shape=[jax.ShapeDtypeStruct((each, 3 * size), F32),
                   jax.ShapeDtypeStruct((rows - each, 3 * size), BF16)],
        compiler_params=pltpu.CompilerParams(vmem_limit_bytes=VMEM_MAX),
        cost_estimate=SMALL,
    )(place, *flat_n, *flat_c, *given, *weights, *acts, *n2_rows, *cot_rows)


def rows_by_device(place, parts, starts, block):
    count = len(parts)
    tokens, n = parts[0].shape
    rows = len(starts(0, 0)) * block
    if block % 16:
        turned = jnp.concatenate(parts, axis=0).T

        def taken(dc):
            return jnp.stack([
                jnp.concatenate([
                    lax.dynamic_slice_in_dim(turned, start, block, 0)
                    for start in starts(place[0] ^ dy, place[1] ^ dc)])
                for dy in range(2)])

        return taken(0), taken(1)

    def body(place_ref, *refs):
        keep_ref, send_ref, turned = refs[count:]
        for k in range(count):
            turned[:, k * tokens : (k + 1) * tokens] = refs[k][...].T
        for dy in range(2):
            for dc, ref in ((0, keep_ref), (1, send_ref)):
                for i, start in enumerate(starts(place_ref[0] ^ dy, place_ref[1] ^ dc)):
                    ref[dy, i * block : (i + 1) * block, :] = turned[pl.ds(pl.multiple_of(start, 16), block), :]

    shape = (2, rows, count * tokens)
    return pl.pallas_call(
        body,
        grid_spec=pltpu.PrefetchScalarGridSpec(
            num_scalar_prefetch=1,
            grid=(1,),
            in_specs=[pl.BlockSpec((tokens, n), lambda i, place: (0, 0))] * count,
            out_specs=[pl.BlockSpec(shape, lambda i, place: (0, 0, 0))] * 2,
            scratch_shapes=[pltpu.VMEM((n, count * tokens), BF16)],
        ),
        out_shape=[jax.ShapeDtypeStruct(shape, BF16)] * 2,
        compiler_params=pltpu.CompilerParams(vmem_limit_bytes=VMEM_MAX),
        cost_estimate=SMALL,
    )(place, *parts)


def sum_of_dots(rows, values):
    count = len(rows)

    def body(*refs):
        total = dot(refs[0][...], refs[count][...])
        for k in range(1, count):
            total = total + dot(refs[k][...], refs[count + k][...])
        refs[2 * count][...] = total.astype(BF16)

    return pl.pallas_call(
        body,
        out_shape=jax.ShapeDtypeStruct((rows[0].shape[0], values[0].shape[1]), BF16),
        compiler_params=pltpu.CompilerParams(vmem_limit_bytes=VMEM_MAX),
        cost_estimate=SMALL,
    )(*rows, *values)


def after(value, *others):
    return lax.optimization_barrier((value, others))[0]


def entering(lay, summary, groups, backward):
    prod, state = (summary[:groups], summary[groups : 2 * groups])
    before_p, before_s = (jnp.ones_like(prod), jnp.zeros_like(state))
    mine = lax.axis_index("seq")
    bit = 1
    while bit < lay.seq:
        other = lay.over_seq_bit(jnp.concatenate([prod, state], axis=0), bit)
        other_p, other_s = (other[:groups], other[groups:])
        is_later = (mine & bit) != 0
        take = jnp.logical_not(is_later) if backward else is_later
        before_s = jnp.where(take, before_p * other_s + before_s, before_s)
        before_p = jnp.where(take, before_p * other_p, before_p)
        state = jnp.where(take, prod * other_s + state, other_p * state + other_s)
        prod = prod * other_p
        bit *= 2
    return before_s


def owner_sum(lay, blocks, tie=None):
    nz, z = (lay.nz, lay.z)

    def pick(t):
        return lax.dynamic_index_in_dim(blocks, t, 0, keepdims=False)

    total = pick(z).astype(F32)
    for step in range(1, nz):
        come = lay.send(pick((z + step) % nz), lambda z, y, x, c: ((z + step) % nz, y, x, c))
        total = total + come.astype(F32)
    return total


def local(inputs, block_flags, decay_seed, vectors, in_y, in_x, gate_weight, out_proj,
          mlp_gate, mlp_up, mlp_down, cotangent):
    lay = Lay()
    nz, x, y, z, c = (lay.nz, lay.x, lay.y, lay.z, lay.c)
    tokens, width = inputs.shape[1:]
    half = width // 2
    quarter = width // 4
    first = c == 0

    def order_c(own, other, axis):
        return jnp.where(first, jnp.concatenate([own, other], axis),
                         jnp.concatenate([other, own], axis))

    def order_f(rel):
        b = rel.shape[-1] // 4
        p = [rel[..., i * b : (i + 1) * b] for i in range(4)]
        by_c = jnp.where(first, rel, jnp.concatenate([p[1], p[0], p[3], p[2]], -1))
        return jnp.where(x == 0, by_c, jnp.concatenate([by_c[..., 2 * b :], by_c[..., : 2 * b]], -1))

    cot = cotangent[0]
    cot_y, cot_z = (lay.over_y(cot), lay.over_z(cot))
    halo_raw = lay.over_seq(inputs[0, tokens - 16 :], 1)
    rows_theirs = lax.dynamic_slice_in_dim(gate_weight, (1 - x) * half, half, 0)
    gate_x = lay.over_x(rows_theirs)
    residual = after(inputs[0], rows_theirs).astype(F32)
    scaled_one, inverse_one = norm_scale(residual)
    normed_own = (scaled_one * vectors[0]).astype(BF16)
    normed_x = lay.over_x(normed_own)
    halo_own = (norm_scale(after(halo_raw, normed_own).astype(F32))[0] * vectors[0]).astype(BF16)
    flag_row = jnp.pad(block_flags.astype(BF16), ((0, 0), (0, width - block_flags.shape[1])))
    halo_x = lay.over_x(jnp.concatenate([flag_row, halo_own[1:]], axis=0))
    n_flags = block_flags.shape[1]
    flags = jnp.concatenate(
        [block_flags.astype(F32), halo_x[:1, :n_flags].astype(F32)], axis=0)

    wy, wx = (in_y, in_x)
    wy_c, wx_c = (lay.over_c(in_y), lay.over_c(in_x))
    out_later = after(out_proj, halo_own)
    out_theirs = lax.dynamic_slice_in_dim(out_later, (1 - x) * half, half, 0)
    out_x = lay.over_x(out_theirs)
    out_mine = lax.dynamic_slice_in_dim(out_later, x * half, half, 0)
    rows_mine = lax.dynamic_slice_in_dim(after(gate_weight, out_theirs), x * half, half, 0)
    gate_c, gate_xc = (lay.over_c(rows_mine), lay.over_c(gate_x))
    gates = order_f(jnp.concatenate([rows_mine, gate_c, gate_x, gate_xc], axis=1))
    out_c, out_xc = (lay.over_c(out_mine), lay.over_c(out_x))
    out_rel = jnp.concatenate([out_mine, out_c, out_x, out_xc], axis=1)
    cot_x = lay.over_x(after(cot, out_theirs))

    normed = jnp.concatenate([normed_own, normed_x, halo_own, halo_x], axis=0)
    two = 2 * tokens
    x_all = order_c(dot(normed, wx).astype(BF16), dot(normed, wx_c).astype(BF16), 1)
    x_low = x_all[:two].reshape(2, tokens, half)
    halo = x_all[two:].reshape(2, 16, half)
    vec_half = lax.dynamic_slice_in_dim(vectors, x * half, half, 1)
    base = -5.0 - decay_seed.astype(F32) + vectors[9]
    rates = lax.dynamic_slice_in_dim(
        jnp.stack([jax.nn.softplus(base), jax.nn.sigmoid(base)]), x * half, half, 1)
    shape3 = lambda dt: jax.ShapeDtypeStruct((2, tokens, half), dt)
    summary_shape = jax.ShapeDtypeStruct((4, half), F32)
    conv_low, ig, dg, prods, local_state, summary = by_head(
        mixer_forward, flags,
        [(after(x_low, cot_y), False), (halo, False), (gates, True), (vec_half, False), (rates, False)],
        [shape3(BF16), shape3(F32), shape3(F32), shape3(F32), shape3(F32), summary_shape])
    state_in = entering(lay, summary, 2, False)
    normed_two = after(normed[:two], summary)
    y_pre = order_c(dot(normed_two, wy), dot(normed_two, wy_c), 1).reshape(2, tokens, half)
    state_tied = after(state_in, cot_z)
    cot_xy = lay.over_y(after(cot_x, state_in))
    cot_xz = lay.over_z(after(cot_x, state_in))
    cot_yz = lay.over_y(after(cot_z, state_in))
    cot_xyz = lay.over_y(cot_xz)
    cots = [[cot, cot_x], [cot_y, cot_xy], [cot_z, cot_xz], [cot_yz, cot_xyz]]
    cots_c = [[lay.over_c(part) for part in group] for group in cots]
    state = local_state + prods * state_tied[:, None, :]
    mixed = (state * jax.nn.gelu(y_pre, approximate=True)).astype(BF16)
    part_x_low = dot(mixed[1], out_rel).astype(BF16)
    part_x = lay.over_x(part_x_low)
    gh_main = grad_hidden_of(after(cots[0] + cots_c[0], part_x_low), mlp_down)
    part_own = after(dot(after(mixed[0], part_x_low), out_rel), gh_main, cot_xy)
    swapped = jnp.concatenate([part_x[:, half:], part_x[:, :half]], axis=1)
    mid = residual + order_f(part_own + swapped.astype(F32))

    scaled_two, inverse_two = norm_scale(mid)
    n2 = (scaled_two * vectors[1]).astype(BF16)
    n2_x = lay.over_x(n2)
    n2_c, n2_xc = (lay.over_c(n2), lay.over_c(n2_x))
    n2_z = lay.over_z(n2)
    gh_y = grad_hidden_of(after(cots[1] + cots_c[1], n2), mlp_down)
    place = jnp.stack([lay.seq_at // nz, y]).astype(jnp.int32)
    each = width // lay.seq
    cot_rows = rows_of_tokens(
        after([p for group in cots for p in group], gh_y), place, half // 2, each)
    n2_y = lay.over_y(after(n2, cot_xyz))
    hidden, grad_gate, grad_up, far, far_c = mlp_forward(
        after([n2, n2_x, n2_c, n2_xc], gh_y, cot_rows), gh_main, mlp_gate, mlp_up)
    n2_xy = lay.over_x(after(n2_y, far))
    n2_xz = lay.over_z(n2_x)
    n2_yz = lay.over_y(n2_z)
    n2_xyz = lay.over_y(n2_xz)
    far_sum = (far + lay.over_c(far_c).astype(F32)).astype(BF16)
    arriving = lay.over_x(far_sum)
    near, near_c, out, out_c = mlp_rest(
        after(hidden, far_sum, n2_y, n2_z), grad_gate, grad_up, mlp_gate, mlp_up, mlp_down, tokens)
    near_sum = after(near + lay.over_c(near_c).astype(F32), n2_xz, n2_yz)
    grad_n2 = near_sum + arriving.astype(F32)
    out_sum = out + lay.over_c(out_c).astype(F32)
    n2s = [[n2, n2_x], [n2_y, n2_xy], [n2_z, n2_xz], [n2_yz, n2_xyz]]
    n2s_c = [[n2_c, n2_xc]] + [[lay.over_c(part) for part in group] for group in n2s[1:]]
    acts = (hidden, grad_gate, grad_up)
    low = (lay.z % (nz // 2)).astype(jnp.int32).reshape(1)
    cot_row_pair = (cot_rows, lay.over_c(cot_rows))

    def weight_piece(at, size, n2_row_pair, *ties):
        own, rest = mlp_weight_grads(
            low, [group + group_c for group, group_c in zip(n2s[1:], n2s_c[1:])], [gh_y],
            [group + group_c for group, group_c in zip(cots[2:], cots_c[2:])],
            after(acts, ties), n2_row_pair, cot_row_pair, (mlp_gate, mlp_up, mlp_down), at, size, each)
        blocks = [own] + [rest[j * each : (j + 1) * each] for j in range(nz // 2 - 1)]
        bit = nz // 4
        while bit >= 1:
            gone = blocks[bit] if bit == 1 else jnp.concatenate(
                [b.astype(BF16) for b in blocks[bit : 2 * bit]], axis=0)
            come = lay.over_seq_bit(gone.astype(BF16), 2 * bit)
            blocks = [blocks[j].astype(F32) + come[j * each : (j + 1) * each].astype(F32) for j in range(bit)]
            bit //= 2
        return own, blocks[0]

    grad_mid_norm, grad_gain_two = norm_back(grad_n2, scaled_two, inverse_two, vectors[1])
    grad_mid = cot.astype(F32) + grad_mid_norm
    branch = grad_mid.astype(BF16)
    branch_rel = order_f(branch)
    arriving = lay.over_x(branch_rel)
    n2_rows = rows_of_tokens(
        after([p for group in n2s for p in group], branch_rel), place, half // 2, each)
    n2_row_pair = (n2_rows, lay.over_c(n2_rows))
    cuts = sections_of(mlp_gate.shape[1])
    cuts = cuts[-1:] + cuts[:-1]
    first_own, first_piece = weight_piece(*cuts[0], n2_row_pair, branch_rel)
    arriving = after(arriving, first_own)
    branch_x_rel = jnp.concatenate([arriving[:, half:], arriving[:, :half]], axis=1)
    branch_two = jnp.concatenate([branch, order_f(branch_x_rel)], 0)
    grad_mixed = dot_cols(jnp.concatenate([branch_rel, branch_x_rel], 0), out_rel)
    gy, bprod, blocal, back_summary = by_head(
        mixer_back_scan, flags,
        [(grad_mixed.reshape(2, tokens, half), False), (y_pre, False), (dg, False), (prods, False),
         (local_state, False), (state_in, False), (rates, False)],
        [shape3(BF16), shape3(F32), shape3(F32), summary_shape])
    back_in = entering(lay, back_summary, 2, True)

    own80 = each // 4
    at_yc = jnp.stack([y, c]).astype(jnp.int32)

    def spread(parts, starts):
        keep, away = rows_by_device(at_yc, parts, starts, own80)
        come = lay.over_c(away)
        keep_y, come_y = (lay.over_y(keep[1]), lay.over_y(come[1]))
        return [keep[0], come[0], keep_y, come_y]

    def n1_starts(at_y, at_c):
        return [((2 * i + at_y) * 4 + 2 * j + at_c) * own80 for i in range(nz) for j in range(2)]

    def mixed_starts(at_y, at_c):
        return [((at_y * nz + i) * 2 + at_c) * own80 for i in range(nz)]

    def all_tokens(value, tie):
        other_y = lay.over_y(after(value, tie))
        return [value, lay.over_c(value), other_y, lay.over_c(other_y)]

    n1_rows = spread([normed_own, normed_x], n1_starts)
    mixed_rows = spread([after(mixed, back_summary)[i] for i in range(2)], mixed_starts)

    gip, gdp, gx_main, gx_tail, edge, vec_rows = by_head(
        mixer_backward, flags,
        [(bprod, False), (blocal, False), (back_in, False), (prods, False), (local_state, False),
         (state_in, False), (ig, False), (dg, False), (conv_low, False), (x_low, False),
         (halo, False), (gates, True), (vec_half, False), (rates, False)],
        [shape3(BF16), shape3(BF16), shape3(BF16), jax.ShapeDtypeStruct((2, 16, half), F32),
         jax.ShapeDtypeStruct((2, 8, half), F32), jax.ShapeDtypeStruct((8, half), F32)])
    edge_next = lay.over_seq(edge, -1)
    gx_last = (gx_tail + jnp.pad(edge_next, ((0, 0), (8, 0), (0, 0)))).astype(BF16)
    gx = jnp.concatenate([gx_main[:, : tokens - 16], gx_last], axis=1).reshape(two, half)
    gy = gy.reshape(two, half)

    def own_cols(value, which):
        return lax.dynamic_slice_in_dim(value, which * quarter, quarter, 1)

    gy_o, gy_c, gx_o, gx_c = (
        own_cols(gy, c), own_cols(gy, 1 - c), own_cols(gx, c), own_cols(gx, 1 - c))

    def grad_n1_of(rows):
        return (dot_cols(gy_o[rows], wy) + dot_cols(gy_c[rows], wy_c)
                + dot_cols(gx_o[rows], wx) + dot_cols(gx_c[rows], wx_c))

    grad_n1_far = grad_n1_of(slice(tokens, two)).astype(BF16)
    arriving = lay.over_x(grad_n1_far)
    grad_n1_near = grad_n1_of(slice(0, tokens))
    second_own, second_piece = weight_piece(*cuts[1], n2_row_pair, grad_n1_far)
    grad_n1 = after(grad_n1_near, second_own) + arriving.astype(F32)
    grad_in_norm, grad_gain_one = norm_back(grad_n1, scaled_one, inverse_one, vectors[0])
    input_grad = (grad_mid + grad_in_norm).astype(BF16)[None]

    branch_all = all_tokens(branch_two, edge)
    out_part = sum_of_dots(mixed_rows, branch_all)
    out_sum_z = owner_sum(lay, out_part.reshape(nz, own80, width))
    in_y_part = sum_of_dots(n1_rows, all_tokens(gy, edge))
    in_y_sum = owner_sum(lay, in_y_part.reshape(nz, 2 * own80, half)).astype(BF16)
    heads = half // BLK
    gate_part = jnp.einsum(
        "thi,thj->hij", conv_low.reshape(two, heads, BLK),
        jnp.concatenate([gip.reshape(two, heads, BLK), gdp.reshape(two, heads, BLK)], 2),
        preferred_element_type=F32).reshape(2, nz, 2, own80, 2 * BLK)
    keep = lax.dynamic_index_in_dim(gate_part, c, 2, keepdims=False)
    away = lax.dynamic_index_in_dim(gate_part, 1 - c, 2, keepdims=False)
    gate_part = keep + lay.over_c(away.astype(BF16)).astype(F32)
    keep = lax.dynamic_index_in_dim(gate_part, y, 0, keepdims=False)
    away = lax.dynamic_index_in_dim(gate_part, 1 - y, 0, keepdims=False)
    gate_part = (keep + lay.over_y(away.astype(BF16)).astype(F32)).astype(BF16)
    in_x_part = sum_of_dots(n1_rows, all_tokens(gx, edge))
    in_x_sum = owner_sum(lay, in_x_part.reshape(nz, 2 * own80, half)).astype(BF16)
    gate_sum = owner_sum(lay, gate_part).astype(BF16)

    third_own, third_piece = weight_piece(*cuts[2], n2_row_pair, in_x_part)
    pieces = [second_piece, third_piece, first_piece]
    widths = [cuts[1][1], cuts[2][1], cuts[0][1]]
    mlp_down_grad, mlp_gate_grad, mlp_up_grad = [
        jnp.concatenate([p[:, i * n : (i + 1) * n] for p, n in zip(pieces, widths)], axis=1)
        for i in range(3)]

    def over_columns(value):
        split = value.reshape(2, own80, half)
        mine = lax.dynamic_index_in_dim(split, x, 0, keepdims=False)
        theirs = lay.over_x(lax.dynamic_index_in_dim(split, 1 - x, 0, keepdims=False))
        return jnp.where(x == 0, jnp.concatenate([mine, theirs], -1),
                         jnp.concatenate([theirs, mine], -1)).astype(F32)

    in_y_grad = over_columns(in_y_sum)
    in_x_grad = over_columns(in_x_sum)

    def final(z, y, x, c):
        at = ((x * 2 + y) * nz + z) * 2 + c
        s, f = (at // 4, at % 4)
        return (s // 2, s % 2, f // 2, f % 2)

    out_grad = lay.send(out_sum_z.astype(BF16), final).astype(F32)
    gate_grad = lay.send(gate_sum, final).astype(F32)
    out_arriving = lay.over_x(after(out_sum[tokens:].astype(BF16), input_grad))
    output = (mid + out_sum[:tokens] + out_arriving.astype(F32)).astype(BF16)[None]

    rows_full = lax.dynamic_update_slice_in_dim(
        jnp.zeros((8, width), F32), vec_rows, x * half, 1)
    vec = jnp.concatenate([grad_gain_one[None], grad_gain_two[None], rows_full], axis=0)
    vec = vec + lay.over_c(vec)
    vec = vec + lay.over_x(vec)
    bit = 1
    while bit < lay.seq:
        vec = vec + lay.over_seq_bit(vec, bit)
        bit *= 2

    return (output, input_grad, vec, in_y_grad, in_x_grad, gate_grad, out_grad,
            mlp_gate_grad, mlp_up_grad, mlp_down_grad)


def solution(mesh):
    return jax.shard_map(
        local,
        mesh=mesh,
        in_specs=(
            P("fsdp", "seq", None),
            P("fsdp", "seq"),
            P(),
            P(),
            P(None, "fsdp"),
            P(None, "fsdp"),
            P(None, "fsdp"),
            P(None, "fsdp"),
            P(None, "fsdp"),
            P(None, "fsdp"),
            P(None, "fsdp"),
            P("fsdp", "seq", None),
        ),
        out_specs=(
            P("fsdp", "seq", None),
            P("fsdp", "seq", None),
            P(),
            P(("seq", "fsdp"), None),
            P(("seq", "fsdp"), None),
            P(("seq", "fsdp"), None),
            P(("seq", "fsdp"), None),
            P("seq", "fsdp"),
            P("seq", "fsdp"),
            P("seq", "fsdp"),
        ),
        check_vma=False,
    )
```

```python
import functools

import jax
import jax.numpy as jnp
from jax import lax
from jax.experimental import pallas as pl
from jax.experimental.pallas import tpu as pltpu
from jax.sharding import PartitionSpec as P

HEADS = 10
BLK = 256
FBLK = 64
EPS = 1e-06
ALL = ("seq", "fsdp")
F32 = jnp.float32
BF16 = jnp.bfloat16
GELU_C = 0.7978845608028654
GELU_A = 0.044715
VMEM_MAX = 60 * 1024 * 1024
ANY = pl.BlockSpec(memory_space=pl.ANY)


def work(us):
    return pl.CostEstimate(flops=us, bytes_accessed=us, transcendentals=0)


def norm_scale(values):
    inverse = lax.rsqrt(jnp.mean(values * values, axis=-1, keepdims=True) + EPS)
    return (values * inverse, inverse)


def norm_back(grad_normed, scaled, inverse, gain_row):
    grad_gain = jnp.sum(grad_normed * scaled, axis=0)
    inner_term = grad_normed * gain_row
    grad_input = inverse * (
        inner_term - scaled * jnp.mean(inner_term * scaled, axis=-1, keepdims=True)
    )
    return (grad_input, grad_gain)


def gelu_pair(values):
    square = values * values
    t = jnp.tanh(values * (GELU_C + GELU_C * GELU_A * square))
    half = 0.5 + 0.5 * t
    slope = half * (1.0 + (1.0 - t) * values * (GELU_C + 3.0 * GELU_C * GELU_A * square))
    return (values * half, slope)


def dot(left, right):
    return jnp.dot(left, right, preferred_element_type=F32)


def dot_rows(left, right):
    return lax.dot_general(left, right, (((0,), (0,)), ((), ())), preferred_element_type=F32)


def dot_cols(left, right):
    return lax.dot_general(left, right, (((1,), (1,)), ((), ())), preferred_element_type=F32)


class Lay:
    def __init__(self):
        self.seq = lax.axis_size("seq")
        self.nz = self.seq // 2
        seq, fsdp = (lax.axis_index("seq"), lax.axis_index("fsdp"))
        self.z, self.y = (seq // 2, seq % 2)
        self.x, self.c = (fsdp // 2, fsdp % 2)
        self.seq_at = seq

    def pairs(self, target):
        found = []
        for s in range(self.seq):
            for f in range(4):
                z, y, x, c = (s // 2, s % 2, f // 2, f % 2)
                to = target(z, y, x, c)
                if to is not None:
                    found.append((s * 4 + f, ((to[0] * 2 + to[1]) * 2 + to[2]) * 2 + to[3]))
        return found

    def send(self, value, target):
        return lax.ppermute(value, ALL, self.pairs(target))

    def over_c(self, value):
        return self.send(value, lambda z, y, x, c: (z, y, x, 1 - c))

    def over_x(self, value):
        return self.send(value, lambda z, y, x, c: (z, y, 1 - x, c))

    def over_y(self, value):
        return self.send(value, lambda z, y, x, c: (z, 1 - y, x, c))

    def over_seq_bit(self, value, bit):
        def to(z, y, x, c):
            other = (2 * z + y) ^ bit
            return (other // 2, other % 2, x, c)

        return self.send(value, to)

    def over_z(self, value):
        return self.send(value, lambda z, y, x, c: (self.nz - 1 - z, y, x, c))

    def over_seq(self, value, by):
        def to(z, y, x, c):
            other = 2 * z + y + by
            return (other // 2, other % 2, x, c) if 0 <= other < self.seq else None

        return self.send(value, to)


def row_iota(rows, cols):
    return lax.broadcasted_iota(jnp.int32, (rows, cols), 0)


def token_masks(flags_ref, g, rows, cols):
    row = row_iota(rows, cols)
    block = row // FBLK
    offset = row % FBLK
    flagged = jnp.zeros((rows, cols), F32)
    for b in range(rows // FBLK):
        flagged = jnp.where(block == b, flags_ref[g, b], flagged)
    valid = [jnp.where(offset < lag, 1.0 - flagged, 1.0) for lag in range(4)]
    start = jnp.where(offset == 0, flagged, 0.0)
    return start, valid


def neg_expm1(v):
    series = 1.0 + v * (1.0 / 6.0)
    for n in (5.0, 4.0, 3.0, 2.0):
        series = 1.0 + v * (1.0 / n) * series
    return jnp.where(v > -0.25, -v * series, 1.0 - jnp.exp(v))


def shifted_inputs(xl_ref, halo_ref, g):
    ext = jnp.concatenate([halo_ref[g].astype(F32), xl_ref[g].astype(F32)], axis=0)
    pad = halo_ref.shape[1]
    return [ext[pad:] if k == 0 else pltpu.roll(ext, k, 0)[pad:] for k in range(4)]


def mixer_forward(flags_ref, xl_ref, halo_ref, gw_ref, vec_ref, rate_ref,
                  conv_ref, ig_ref, dg_ref, prod_ref, local_ref, sum_ref):
    groups, rows, cols = xl_ref.shape
    row = row_iota(rows, cols)
    for g in range(groups):
        start, valid = token_masks(flags_ref, g, rows, cols)
        lagged = shifted_inputs(xl_ref, halo_ref, g)
        conv = vec_ref[6:7, :] + jnp.zeros((rows, cols), F32)
        for k in range(4):
            conv = conv + vec_ref[2 + k : 3 + k, :] * lagged[k] * valid[k]
        conv_low = conv.astype(BF16)
        conv_ref[g] = conv_low
        prod = jnp.dot(conv_low, gw_ref[...], preferred_element_type=F32)
        ig = jax.nn.sigmoid(prod[:, :cols] + vec_ref[7:8, :])
        dg = jax.nn.sigmoid(prod[:, cols:] + vec_ref[8:9, :])
        ig_ref[g] = ig
        dg_ref[g] = dg
        keep = 1.0 - start
        log_decay = -8.0 * dg * rate_ref[0:1, :]
        p = jnp.exp(log_decay) * keep
        s = jnp.sqrt(keep * neg_expm1(2.0 * log_decay) + start) * ig * conv_low.astype(F32)
        step = 1
        while step < rows:
            inside = row >= step
            p_prev = jnp.where(inside, pltpu.roll(p, step, 0), 1.0)
            s_prev = jnp.where(inside, pltpu.roll(s, step, 0), 0.0)
            s = p * s_prev + s
            p = p * p_prev
            step *= 2
        prod_ref[g] = p
        local_ref[g] = s
        sum_ref[g : g + 1, :] = p[rows - 1 :, :]
        sum_ref[groups + g : groups + g + 1, :] = s[rows - 1 :, :]


def mixer_back_scan(flags_ref, gm_ref, y_ref, dg_ref, prod_ref, local_ref, sin_ref, rate_ref,
                    gy_ref, bprod_ref, blocal_ref, sum_ref):
    groups, rows, cols = gm_ref.shape
    row = row_iota(rows, cols)
    for g in range(groups):
        start, _ = token_masks(flags_ref, g, rows, cols)
        state = local_ref[g] + prod_ref[g] * sin_ref[g : g + 1, :]
        gelu, slope = gelu_pair(y_ref[g])
        gm = gm_ref[g]
        gy_ref[g] = (gm * state * slope).astype(BF16)
        decay = jnp.exp(-8.0 * dg_ref[g] * rate_ref[0:1, :]) * (1.0 - start)
        s = gm * gelu
        p = jnp.where(row == rows - 1, 1.0, pltpu.roll(decay, rows - 1, 0))
        step = 1
        while step < rows:
            inside = row < rows - step
            p_next = jnp.where(inside, pltpu.roll(p, rows - step, 0), 1.0)
            s_next = jnp.where(inside, pltpu.roll(s, rows - step, 0), 0.0)
            s = p * s_next + s
            p = p * p_next
            step *= 2
        bprod_ref[g] = p
        blocal_ref[g] = s
        sum_ref[g : g + 1, :] = decay[:1, :] * p[:1, :]
        sum_ref[groups + g : groups + g + 1, :] = decay[:1, :] * s[:1, :]


def mixer_backward(flags_ref, bprod_ref, blocal_ref, bin_ref, prod_ref, local_ref, sin_ref,
                   ig_ref, dg_ref, conv_ref, xl_ref, halo_ref, gw_ref, vec_ref, rate_ref,
                   gip_ref, gdp_ref, gx_ref, tail_ref, edge_ref, rows_ref):
    groups, rows, cols = xl_ref.shape
    row = row_iota(rows, cols)
    sums = [jnp.zeros((1, cols), F32) for _ in range(8)]
    tail = tail_ref.shape[1]
    pad = edge_ref.shape[1]
    for g in range(groups):
        start, valid = token_masks(flags_ref, g, rows, cols)
        keep = 1.0 - start
        rate = rate_ref[0:1, :]
        state_in = sin_ref[g : g + 1, :]
        state = local_ref[g] + prod_ref[g] * state_in
        prev = jnp.where(row == 0, state_in, pltpu.roll(state, 1, 0))
        sg = blocal_ref[g] + bprod_ref[g] * bin_ref[g : g + 1, :]
        ig, dg = (ig_ref[g], dg_ref[g])
        cf = conv_ref[g].astype(F32)
        log_decay = -8.0 * dg * rate
        decay = jnp.exp(log_decay) * keep
        scale = jnp.sqrt(keep * neg_expm1(2.0 * log_decay) + start)
        gscale = sg * ig * cf
        glog = sg * prev * decay - gscale * keep * jnp.exp(2.0 * log_decay) / scale
        gip = sg * scale * cf * ig * (1.0 - ig)
        gdp = -8.0 * rate * glog * dg * (1.0 - dg)
        gip_low, gdp_low = (gip.astype(BF16), gdp.astype(BF16))
        gip_ref[g] = gip_low
        gdp_ref[g] = gdp_low
        gconv = sg * scale * ig + lax.dot_general(
            jnp.concatenate([gip_low, gdp_low], axis=1), gw_ref[...],
            (((1,), (1,)), ((), ())), preferred_element_type=F32)
        lagged = shifted_inputs(xl_ref, halo_ref, g)
        spread = jnp.zeros((rows + pad, cols), F32)
        for k in range(4):
            masked = gconv * valid[k]
            sums[k] = sums[k] + jnp.sum(masked * lagged[k], axis=0, keepdims=True)
            full = jnp.concatenate(
                [jnp.zeros((pad, cols), F32), vec_ref[2 + k : 3 + k, :] * masked], axis=0)
            spread = spread + (full if k == 0 else pltpu.roll(full, rows + pad - k, 0))
        gx_ref[g] = spread[pad:].astype(BF16)
        tail_ref[g] = spread[pad + rows - tail :]
        edge_ref[g] = spread[:pad]
        sums[4] = sums[4] + jnp.sum(gconv, axis=0, keepdims=True)
        sums[5] = sums[5] + jnp.sum(gip, axis=0, keepdims=True)
        sums[6] = sums[6] + jnp.sum(gdp, axis=0, keepdims=True)
        sums[7] = sums[7] + jnp.sum(-8.0 * dg * glog, axis=0, keepdims=True) * rate_ref[1:2, :]
    rows_ref[...] = jnp.concatenate(sums, axis=0)


def by_head(body, flags, operands, outs):
    def spec(shape, rows_are_channels):
        if rows_are_channels:
            return pl.BlockSpec((BLK, shape[1]), lambda h: (h, 0))
        lead = shape[:-1]
        return pl.BlockSpec(lead + (BLK,), lambda h: (0,) * len(lead) + (h,))

    heads = outs[0].shape[-1] // BLK
    in_specs = [pl.BlockSpec(memory_space=pltpu.SMEM)]
    values = [flags]
    for value, is_gate in operands:
        in_specs.append(spec(value.shape, is_gate))
        values.append(value)
    size = sum(v.size * v.dtype.itemsize for v in values) + sum(
        o.size * o.dtype.itemsize for o in outs)
    return pl.pallas_call(
        body,
        grid=(heads,),
        in_specs=in_specs,
        out_specs=[spec(o.shape, False) for o in outs],
        out_shape=outs,
        compiler_params=pltpu.CompilerParams(vmem_limit_bytes=48 * 1024 * 1024),
        cost_estimate=work(7),
    )(*values)


def grad_hidden_of(parts, w_down):
    count = len(parts)
    rows, width = parts[0].shape
    total = count * rows
    ff = w_down.shape[1]

    def body(*refs):
        c_refs, (w_ref, out_ref, held, sem) = (refs[:count], refs[count:])

        @pl.when(pl.program_id(0) == 0)
        def _():
            copies = [
                pltpu.make_async_copy(c_refs[i], held.at[pl.ds(i * rows, rows)], sem.at[i])
                for i in range(count)
            ]
            for copy in copies:
                copy.start()
            for copy in copies:
                copy.wait()

        out_ref[...] = dot(held[...], w_ref[...])

    return pl.pallas_call(
        body,
        grid=(pl.cdiv(ff, BLK),),
        in_specs=[ANY] * count + [pl.BlockSpec((width, BLK), lambda j: (0, j))],
        out_specs=pl.BlockSpec((total, BLK), lambda j: (0, j)),
        out_shape=jax.ShapeDtypeStruct((total, ff), F32),
        scratch_shapes=[pltpu.VMEM((total, width), BF16), pltpu.SemaphoreType.DMA((count,))],
        compiler_params=pltpu.CompilerParams(vmem_limit_bytes=VMEM_MAX),
        cost_estimate=work(5 + total // 64),
    )(*parts, w_down)


def sections_of(total):
    found, at = ([], 0)
    while at < total:
        size = min(768, total - at)
        found.append((at, size))
        at += size
    return found


def mlp_forward(n2_parts, grad_hidden, w_gate, w_up):
    count = len(n2_parts)
    rows, width = n2_parts[0].shape
    total = count * rows
    ff = w_gate.shape[1]
    parts = sections_of(ff)
    widest = parts[0][1]
    far = total // 2

    def body(*refs):
        n_refs = refs[:count]
        gh_ref, wg_ref, wu_ref = refs[count : count + 3]
        hid_ref, gg_ref, gu_ref, far_ref, far_c_ref = refs[count + 3 : count + 8]
        n2_s, gh_s, wg_s, wu_s, acc, sem_n, sem_w = refs[count + 8 :]

        def load(k):
            at, size = parts[k]
            slot = k % 2
            return [
                pltpu.make_async_copy(
                    wg_ref.at[:, pl.ds(at, size)], wg_s.at[slot, :, pl.ds(0, size)], sem_w.at[slot, 0]),
                pltpu.make_async_copy(
                    wu_ref.at[:, pl.ds(at, size)], wu_s.at[slot, :, pl.ds(0, size)], sem_w.at[slot, 1]),
                pltpu.make_async_copy(
                    gh_ref.at[:, pl.ds(at, size)], gh_s.at[slot, :, pl.ds(0, size)], sem_w.at[slot, 2]),
            ]

        first = [
            pltpu.make_async_copy(n_refs[i], n2_s.at[pl.ds(i * rows, rows)], sem_n.at[i])
            for i in range(count)
        ]
        for copy in first + load(0):
            copy.start()
        for copy in first:
            copy.wait()
        for k, (at, size) in enumerate(parts):
            if k + 1 < len(parts):
                for copy in load(k + 1):
                    copy.start()
            for copy in load(k):
                copy.wait()
            slot = k % 2
            wg, wu = (wg_s[slot, :, :size], wu_s[slot, :, :size])
            gelu, slope = gelu_pair(dot(n2_s[...], wg))
            up = dot(n2_s[...], wu)
            gh = gh_s[slot, :, :size]
            hid_ref[:, at : at + size] = (gelu * up).astype(BF16)
            gg = (gh * up * slope).astype(BF16)
            gu = (gh * gelu).astype(BF16)
            gg_ref[:, at : at + size] = gg
            gu_ref[:, at : at + size] = gu

            def far_rows(v):
                return jnp.concatenate([v[rows : 2 * rows], v[3 * rows :]], axis=0)

            part = dot_cols(far_rows(gg), wg) + dot_cols(far_rows(gu), wu)
            if k == 0:
                acc[...] = part
            else:
                acc[...] += part
        far_ref[...] = acc[:rows]
        far_c_ref[...] = acc[rows:].astype(BF16)

    act = jax.ShapeDtypeStruct((total, ff), BF16)
    return pl.pallas_call(
        body,
        in_specs=[ANY] * (count + 3),
        out_shape=[act, act, act, jax.ShapeDtypeStruct((rows, width), F32),
                   jax.ShapeDtypeStruct((rows, width), BF16)],
        scratch_shapes=[
            pltpu.VMEM((total, width), BF16),
            pltpu.VMEM((2, total, widest), F32),
            pltpu.VMEM((2, width, widest), BF16),
            pltpu.VMEM((2, width, widest), BF16),
            pltpu.VMEM((far, width), F32),
            pltpu.SemaphoreType.DMA((count,)),
            pltpu.SemaphoreType.DMA((2, 3)),
        ],
        compiler_params=pltpu.CompilerParams(vmem_limit_bytes=VMEM_MAX),
        cost_estimate=work(23),
    )(*n2_parts, grad_hidden, w_gate, w_up)


def mlp_rest(hidden, grad_gate, grad_up, w_gate, w_up, w_down, rows):
    total, ff = hidden.shape
    width = w_gate.shape[0]
    block = 512

    def body(hid_ref, gg_ref, gu_ref, wg_ref, wu_ref, wd_ref, gn_ref, gn_c_ref, out_ref, out_c_ref):
        def near(ref):
            return jnp.concatenate([ref[:rows], ref[2 * rows : 3 * rows]], axis=0)

        gn = dot_cols(near(gg_ref), wg_ref[...]) + dot_cols(near(gu_ref), wu_ref[...])
        gn_ref[...] = gn[:rows]
        gn_c_ref[...] = gn[rows:].astype(BF16)
        out = dot_cols(hid_ref[...], wd_ref[...])
        out_ref[...] = out[: total // 2]
        out_c_ref[...] = out[total // 2 :].astype(BF16)

    whole = pl.BlockSpec((total, ff), lambda j: (0, 0))
    weight = pl.BlockSpec((block, ff), lambda j: (j, 0))
    tall = lambda n: pl.BlockSpec((n, block), lambda j: (0, j))
    shape = lambda n, dt: jax.ShapeDtypeStruct((n, width), dt)
    return pl.pallas_call(
        body,
        grid=(width // block,),
        in_specs=[whole] * 3 + [weight] * 3,
        out_specs=[tall(rows), tall(rows), tall(total // 2), tall(total // 2)],
        out_shape=[shape(rows, F32), shape(rows, BF16), shape(total // 2, F32), shape(total // 2, BF16)],
        compiler_params=pltpu.CompilerParams(vmem_limit_bytes=VMEM_MAX),
        cost_estimate=work(19),
    )(hidden, grad_gate, grad_up, w_gate, w_up, w_down)


def rows_of_tokens(place, parts, rows_out, each):
    tokens, width = parts[0].shape
    half = width // 2
    count = len(parts)

    def body(place_ref, *refs):
        out_ref, turned = (refs[count], refs[count + 1])
        for k in range(count):
            turned[...] = refs[k][...].T
            for i in range(rows_out // each):
                at = pl.multiple_of((2 * i + place_ref[2]) * each, 16)
                out_ref[i * each : (i + 1) * each, k * tokens : (k + 1) * tokens] = turned[pl.ds(at, each), :]

    return pl.pallas_call(
        body,
        grid_spec=pltpu.PrefetchScalarGridSpec(
            num_scalar_prefetch=1,
            grid=(1,),
            in_specs=[pl.BlockSpec((tokens, half), lambda i, place: (0, place[1]))] * count,
            out_specs=pl.BlockSpec((rows_out, count * tokens), lambda i, place: (0, 0)),
            scratch_shapes=[pltpu.VMEM((half, tokens), BF16)],
        ),
        out_shape=jax.ShapeDtypeStruct((rows_out, count * tokens), BF16),
        compiler_params=pltpu.CompilerParams(vmem_limit_bytes=VMEM_MAX),
        cost_estimate=work(5),
    )(place, *parts)


def mlp_weight_grads(place, n2_parts, first_hidden, cot_parts, acts, n2_rows, cot_rows, weights, at, size, each):
    groups = len(n2_parts)
    per = len(n2_parts[0])
    tokens, width = n2_parts[0][0].shape
    group = per * tokens
    both = group // 2
    rows = n2_rows[0].shape[0]
    flat_n = [p for g in n2_parts for p in g]
    flat_c = [p for g in cot_parts for p in g]
    total, total_c = (len(flat_n), len(flat_c))

    def body(place_ref, *refs):
        n_refs, c_refs, refs = (refs[:total], refs[total : total + total_c], refs[total + total_c :])
        gh_ref, wg_ref, wu_ref, wd_ref, hid_ref, gg_ref, gu_ref, nm, no, cm, co = refs[:11]
        own_ref, rest_ref, n2_s, cot_s, acc, sem = refs[11:]

        def load(g, slot):
            found = []
            for i in range(per):
                to = pl.ds(i * tokens, tokens)
                found.append(pltpu.make_async_copy(n_refs[g * per + i], n2_s.at[slot, to], sem.at[slot, i]))
                if g > 0:
                    found.append(pltpu.make_async_copy(
                        c_refs[(g - 1) * per + i], cot_s.at[slot, to], sem.at[slot, per + i]))
            return found

        for copy in load(0, 0) + load(1, 1):
            copy.start()

        def add(g, act, fresh):
            start = g * both if isinstance(g, int) else pl.multiple_of(g * both, both)
            for i, (mine, other) in enumerate(((cm, co), (nm, no), (nm, no))):
                part = dot(mine[:, pl.ds(start, both)], act[i][:both]) + dot(
                    other[:, pl.ds(start, both)], act[i][both:])
                if fresh:
                    acc[i] = part
                else:
                    acc[i] += part

        def recompute(g, slot, gh):
            gelu, slope = gelu_pair(dot(n2_s[slot], wg_ref[...]))
            up = dot(n2_s[slot], wu_ref[...])
            add(g + 1, ((gelu * up).astype(BF16), (gh * up * slope).astype(BF16), (gh * gelu).astype(BF16)), False)

        add(0, (hid_ref, gg_ref, gu_ref), True)
        for copy in load(0, 0):
            copy.wait()
        recompute(0, 0, gh_ref[...])

        def step(g, carry):
            slot = lax.rem(g, 2)
            for k in range(2, groups):
                @pl.when(g + 1 == k)
                def _():
                    for copy in load(k, k % 2):
                        copy.start()

            for copy in load(1, slot):
                copy.wait()
            recompute(g, slot, dot(cot_s[slot], wd_ref[...]))
            return carry

        lax.fori_loop(1, groups, step, 0)
        for j in range(rows // each):
            start = pl.multiple_of((place_ref[0] ^ j) * each, 8)
            for i in range(3):
                block = acc[i, pl.ds(start, each), :]
                if j == 0:
                    own_ref[:, i * size : (i + 1) * size] = block
                else:
                    rest_ref[(j - 1) * each : j * each, i * size : (i + 1) * size] = block.astype(BF16)

    index = at // size
    column = lambda n: pl.BlockSpec((n, size), lambda j, place: (0, index))
    whole = pl.BlockSpec(n2_rows[0].shape, lambda j, place: (0, 0))
    return pl.pallas_call(
        body,
        grid_spec=pltpu.PrefetchScalarGridSpec(
            num_scalar_prefetch=1,
            grid=(1,),
            in_specs=[ANY] * (total + total_c) + [column(group)] + [column(width)] * 3 + [column(group)] * 3
            + [whole] * 4,
            out_specs=[pl.BlockSpec((each, 3 * size), lambda j, place: (0, 0)),
                       pl.BlockSpec((rows - each, 3 * size), lambda j, place: (0, 0))],
            scratch_shapes=[
                pltpu.VMEM((2, group, width), BF16),
                pltpu.VMEM((2, group, width), BF16),
                pltpu.VMEM((3, rows, size), F32),
                pltpu.SemaphoreType.DMA((2, 2 * per)),
            ],
        ),
        out_shape=[jax.ShapeDtypeStruct((each, 3 * size), F32),
                   jax.ShapeDtypeStruct((rows - each, 3 * size), BF16)],
        compiler_params=pltpu.CompilerParams(vmem_limit_bytes=VMEM_MAX),
        cost_estimate=work(35 * size // 768),
    )(place, *flat_n, *flat_c, first_hidden, *weights, *acts, *n2_rows, *cot_rows)


def rows_by_device(place, parts, starts, block):
    columns, count = (len(parts), len(parts[0]))
    tokens, n = parts[0][0].shape
    rows = len(starts(0, 0)) * block
    flat = [block_of for column in parts for block_of in column]
    if block % 16:
        turned = [jnp.concatenate(column, axis=0).T for column in parts]
        turned = turned[0] if columns == 1 else jnp.where(
            place[2] == 0, jnp.concatenate(turned), jnp.concatenate(turned[::-1]))

        def taken(dc):
            return jnp.stack([
                jnp.concatenate([
                    lax.dynamic_slice_in_dim(turned, start, block, 0)
                    for start in starts(place[0] ^ dy, place[1] ^ dc)])
                for dy in range(2)])

        kept, sent = (taken(0), taken(1))
        return kept[0], kept[1], sent[0], sent[1]

    def body(place_ref, *refs):
        keep_ref, keep_y_ref, send_ref, send_y_ref, turned = refs[len(flat):]
        for h in range(columns):
            base = 0 if columns == 1 else pl.multiple_of((place_ref[2] ^ h) * n, 16)
            for k in range(count):
                turned[pl.ds(base, n), k * tokens : (k + 1) * tokens] = refs[h * count + k][...].T
        for dy, dc, ref in ((0, 0, keep_ref), (1, 0, keep_y_ref), (0, 1, send_ref), (1, 1, send_y_ref)):
            for i, start in enumerate(starts(place_ref[0] ^ dy, place_ref[1] ^ dc)):
                ref[i * block : (i + 1) * block, :] = turned[pl.ds(pl.multiple_of(start, 16), block), :]

    shape = (rows, count * tokens)
    return pl.pallas_call(
        body,
        grid_spec=pltpu.PrefetchScalarGridSpec(
            num_scalar_prefetch=1,
            grid=(1,),
            in_specs=[pl.BlockSpec((tokens, n), lambda i, place: (0, 0))] * len(flat),
            out_specs=[pl.BlockSpec(shape, lambda i, place: (0, 0))] * 4,
            scratch_shapes=[pltpu.VMEM((columns * n, count * tokens), BF16)],
        ),
        out_shape=[jax.ShapeDtypeStruct(shape, BF16)] * 4,
        compiler_params=pltpu.CompilerParams(vmem_limit_bytes=VMEM_MAX),
        cost_estimate=work(3),
    )(place, *flat)


def joined_columns(pairs):
    rows = pairs[0][0].shape[0]
    widths = [a.shape[1] // 3 for a, _ in pairs]
    total = sum(widths)
    step = rows // 4 if rows % 64 == 0 else rows
    flat = [term for pair in pairs for term in pair]

    def body(*refs):
        for i in range(3):
            at = 0
            for k, n in enumerate(widths):
                span = slice(i * n, (i + 1) * n)
                refs[len(flat) + i][:, at : at + n] = refs[2 * k][:, span].astype(F32) + refs[
                    2 * k + 1][:, span].astype(F32)
                at += n

    return pl.pallas_call(
        body,
        grid=(rows // step,),
        in_specs=[pl.BlockSpec((step, term.shape[1]), lambda j: (j, 0)) for term in flat],
        out_specs=[pl.BlockSpec((step, total), lambda j: (j, 0))] * 3,
        out_shape=[jax.ShapeDtypeStruct((rows, total), F32)] * 3,
        compiler_params=pltpu.CompilerParams(vmem_limit_bytes=VMEM_MAX),
        cost_estimate=work(5),
    )(*flat)


def gate_weight_grad(conv, grad_in, grad_decay):
    tokens, n = conv.shape

    def body(conv_ref, in_ref, decay_ref, out_ref):
        turned = conv_ref[...].T
        out_ref[:, :BLK] = dot(turned, in_ref[...])
        out_ref[:, BLK:] = dot(turned, decay_ref[...])

    spec = pl.BlockSpec((tokens, BLK), lambda h: (0, h))
    return pl.pallas_call(
        body,
        grid=(n // BLK,),
        in_specs=[spec] * 3,
        out_specs=pl.BlockSpec((BLK, 2 * BLK), lambda h: (h, 0)),
        out_shape=jax.ShapeDtypeStruct((n, 2 * BLK), F32),
        compiler_params=pltpu.CompilerParams(vmem_limit_bytes=VMEM_MAX),
        cost_estimate=work(3),
    )(conv, grad_in, grad_decay)


def sum_of_dots(rows, values):
    count = len(rows)

    def body(*refs):
        total = dot(refs[0][...], refs[count][...])
        for k in range(1, count):
            total = total + dot(refs[k][...], refs[count + k][...])
        refs[2 * count][...] = total.astype(BF16)

    return pl.pallas_call(
        body,
        out_shape=jax.ShapeDtypeStruct((rows[0].shape[0], values[0].shape[1]), BF16),
        compiler_params=pltpu.CompilerParams(vmem_limit_bytes=VMEM_MAX),
        cost_estimate=work(5),
    )(*rows, *values)


def after(value, *others):
    return lax.optimization_barrier((value, others))[0]


class Live:
    def cut(self):
        names = sorted(vars(self))
        for name, value in zip(names, lax.optimization_barrier([getattr(self, n) for n in names])):
            setattr(self, name, value)

    def hold(self, **values):
        for name, value in values.items():
            setattr(self, name, value)
        self.cut()


def seq_bits(lay):
    found, bit = ([], 1)
    while bit < lay.seq:
        found.append(bit)
        bit *= 2
    return found


def scan_start(summary, groups):
    prod, state = (summary[:groups], summary[groups : 2 * groups])
    return (prod, state, jnp.ones_like(prod), jnp.zeros_like(state))


def scan_join(lay, held, other, bit, backward):
    prod, state, before_p, before_s = held
    groups = prod.shape[0]
    other_p, other_s = (other[:groups], other[groups:])
    is_later = (lay.seq_at & bit) != 0
    take = jnp.logical_not(is_later) if backward else is_later
    before_s = jnp.where(take, before_p * other_s + before_s, before_s)
    before_p = jnp.where(take, before_p * other_p, before_p)
    state = jnp.where(take, prod * other_s + state, other_p * state + other_s)
    return (prod * other_p, state, before_p, before_s)


def local(inputs, block_flags, decay_seed, vectors, in_y, in_x, gate_weight, out_proj,
          mlp_gate, mlp_up, mlp_down, cotangent):
    lay = Lay()
    nz, x, y, z, c = (lay.nz, lay.x, lay.y, lay.z, lay.c)
    tokens, width = inputs.shape[1:]
    half, quarter, two = (width // 2, width // 4, 2 * tokens)
    each = width // lay.seq
    own80 = each // 4
    bits = seq_bits(lay)
    place = jnp.stack([z % (nz // 2), lay.seq_at // nz, y]).astype(jnp.int32)
    at_yc = jnp.stack([y, c, x]).astype(jnp.int32)
    live = Live()

    def order_c(own, other, axis):
        return jnp.where(c == 0, jnp.concatenate([own, other], axis),
                         jnp.concatenate([other, own], axis))

    def order_f(rel):
        b = rel.shape[-1] // 4
        p = [rel[..., i * b : (i + 1) * b] for i in range(4)]
        by_c = jnp.where(c == 0, rel, jnp.concatenate([p[1], p[0], p[3], p[2]], -1))
        return jnp.where(x == 0, by_c, jnp.concatenate([by_c[..., 2 * b :], by_c[..., : 2 * b]], -1))

    def owner_parts(blocks):
        pick = lambda t: lax.dynamic_index_in_dim(blocks, t, 0, keepdims=False)
        come = [
            lay.send(pick((z + step) % nz), lambda z, y, x, c: ((z + step) % nz, y, x, c))
            for step in range(1, nz)
        ]
        return pick(z), come

    def total_of(own, come):
        total = own.astype(F32)
        for part in come:
            total = total + part.astype(F32)
        return total.astype(BF16)

    def half_of(value, which, n, axis):
        return lax.dynamic_slice_in_dim(value, which * n, n, axis)

    cot = cotangent[0]
    cut = tokens // 2
    gate_away, inputs, gate_weight, out_proj, vectors, decay_seed, block_flags = lax.optimization_barrier(
        (half_of(gate_weight, 1 - x, half, 0), inputs, gate_weight, out_proj, vectors, decay_seed, block_flags))
    halo_raw = lay.over_seq(inputs[0, tokens - 16 :], 1)
    gate_x = lay.over_x(gate_away)
    wx_c, wy_c = (lay.over_c(in_x), lay.over_c(in_y))
    scaled_one, inverse_one = norm_scale(inputs[0].astype(F32))
    live.hold(n1=(scaled_one * vectors[0]).astype(BF16), inv1=inverse_one, halo_raw=halo_raw,
              params=(gate_weight, out_proj, vectors, decay_seed, block_flags))

    gate_weight, out_proj, vectors, decay_seed, block_flags = live.params
    n1_x = lay.over_x(live.n1)
    halo_own = (norm_scale(live.halo_raw.astype(F32))[0] * vectors[0]).astype(BF16)
    n_flags = block_flags.shape[1]
    flag_row = jnp.pad(block_flags.astype(BF16), ((0, 0), (0, width - n_flags)))
    halo_x = lay.over_x(jnp.concatenate([flag_row, halo_own[1:]], axis=0))
    gate_own = half_of(gate_weight, x, half, 0)
    gate_c = lay.over_c(gate_own)
    cot_z = lay.over_z(after(cot, live.n1))
    cot_y = lay.over_y(after(cot, live.n1))
    base = -5.0 - decay_seed.astype(F32) + vectors[9]
    del live.params, live.halo_raw
    live.hold(
        n1_x=n1_x, halo_x=halo_x, halo_own=halo_own, gate_x=gate_x, gate_c=gate_c, wx_c=wx_c, cot_y=cot_y,
        flags=jnp.concatenate([block_flags.astype(F32), halo_x[:1, :n_flags].astype(F32)], axis=0),
        gate_own=gate_own, out_away=half_of(out_proj, 2 * (1 - x) + y, quarter, 0),
        out_mine=half_of(out_proj, x, half, 0), vec=half_of(vectors, x, half, 1), gain_two=vectors[1],
        gain_one=vectors[0],
        rates=half_of(jnp.stack([jax.nn.softplus(base), jax.nn.sigmoid(base)]), x, half, 1))

    out_a = lay.over_x(live.out_away)
    gates = order_f(jnp.concatenate(
        [live.gate_own, live.gate_c, live.gate_x, lay.over_c(live.gate_x)], axis=1))
    normed = jnp.concatenate([live.n1, live.n1_x, live.halo_own, live.halo_x], axis=0)
    x_all = order_c(dot(normed, in_x).astype(BF16), dot(normed, live.wx_c).astype(BF16), 1)
    x_low = x_all[:two].reshape(2, tokens, half)
    halo = x_all[two:].reshape(2, 16, half)
    shape3 = lambda dt: jax.ShapeDtypeStruct((2, tokens, half), dt)
    summary_shape = jax.ShapeDtypeStruct((4, half), F32)
    conv_low, ig, dg, prods, local_state, summary = by_head(
        mixer_forward, live.flags,
        [(x_low, False), (halo, False), (gates, True), (live.vec, False), (live.rates, False)],
        [shape3(BF16), shape3(F32), shape3(F32), shape3(F32), shape3(F32), summary_shape])
    out_c = lay.over_c(live.out_mine)
    del live.gate_x, live.gate_own, live.gate_c, live.halo_own, live.halo_x
    live.hold(x_low=x_low, halo=halo, gates=gates, conv_low=conv_low, ig=ig, dg=dg, prods=prods,
              local_state=local_state, scan=scan_start(summary, 2), out_c=out_c, normed=normed[:two], wy_c=wy_c, out_a=out_a,
              cot_z=cot_z)
    del live.out_away

    def n1_starts(at_y, at_c):
        return [((2 * i + at_y) * 4 + 2 * j + at_c) * own80 for i in range(nz) for j in range(2)]

    for bit in bits:
        come = lay.over_seq_bit(jnp.concatenate(live.scan[:2], axis=0), bit)
        live.scan = scan_join(lay, live.scan, come, bit, False)
        if bit == 1:
            live.cut()
            out_b = lay.over_y(live.out_a)
            cot_x = lay.over_x(after(cot, live.scan))
    out_x = jnp.where(y == 0, jnp.concatenate([live.out_a, out_b], 0), jnp.concatenate([out_b, live.out_a], 0))
    y_pre = order_c(dot(live.normed, in_y), dot(live.normed, live.wy_c), 1).reshape(2, tokens, half)
    n1_own, n1_away, sent, sent_y = rows_by_device(at_yc, [[live.n1, live.n1_x]], n1_starts, own80)
    state_in = live.scan[3]
    del live.scan, live.out_a
    live.hold(state_in=state_in, y_pre=y_pre, out_left=jnp.concatenate([live.out_mine, live.out_c], axis=1),
              out_x=out_x, cot_x=cot_x, n1_own=n1_own, n1_away=n1_away, n1_c=lay.over_c(sent), n1_away_c=lay.over_c(sent_y))
    del live.out_mine, live.out_c

    n1_y = lay.over_y(live.n1_away)
    state = live.local_state + live.prods * live.state_in[:, None, :]
    mixed = (state * jax.nn.gelu(live.y_pre, approximate=True)).astype(BF16)
    mixed_two = mixed.reshape(two, half)
    out_right = jnp.concatenate([live.out_x, lay.over_c(live.out_x)], axis=1)
    part = jnp.concatenate([dot(mixed_two, live.out_left), dot(mixed_two, out_right)], axis=1)
    del live.out_x
    live.hold(mixed=mixed, part_own=part[:tokens], part_x=part[tokens:].astype(BF16), out_right=out_right, n1_y=n1_y)

    part_x = lay.over_x(live.part_x)
    cot_xy = lay.over_y(live.cot_x)
    gh_main = grad_hidden_of([cot, live.cot_x, lay.over_c(cot), lay.over_c(live.cot_x)], mlp_down)
    live.hold(part_x=part_x, gh_main=gh_main, cot_xy=cot_xy)

    swapped = jnp.concatenate([live.part_x[:, half:], live.part_x[:, :half]], axis=1)
    mid = inputs[0].astype(F32) + order_f(live.part_own + swapped.astype(F32))
    scaled_two, inverse_two = norm_scale(mid)
    del live.part_x, live.part_own
    live.hold(mid=mid, inv2=inverse_two, n2=(scaled_two * live.gain_two).astype(BF16))

    n2_x = lay.over_x(live.n2)
    n2_y = lay.over_y(live.n2)
    n2_z_top = lay.over_z(live.n2[:cut])
    n2_c = lay.over_c(live.n2)
    pair = [live.cot_y, live.cot_xy]
    gh_y = grad_hidden_of(pair + [lay.over_c(p) for p in pair], mlp_down)
    live.hold(n2_x=n2_x, n2_c=n2_c, n2_y=n2_y, n2_z_top=n2_z_top, gh_y=gh_y)

    live.hold(n2_xc=lay.over_c(live.n2_x))
    cot_xz = lay.over_x(live.cot_z)
    n2_xy = lay.over_y(live.n2_x)
    n2_z_low = lay.over_z(live.n2[cut:])
    hidden, grad_gate, grad_up, far, far_c = mlp_forward(
        [live.n2, live.n2_x, live.n2_c, live.n2_xc], live.gh_main, mlp_gate, mlp_up)
    del live.gh_main, live.n2_c
    live.hold(acts=(hidden, grad_gate, grad_up), far=far, far_c=far_c, cot_xz=cot_xz, n2_xy=n2_xy,
              n2_z_low=n2_z_low)
    live.hold(far=(live.far + lay.over_c(live.far_c).astype(F32)).astype(BF16),
              n2_z=jnp.concatenate([live.n2_z_top, live.n2_z_low], axis=0))

    arriving = lay.over_x(live.far)
    n2_yz = lay.over_y(live.n2_z)
    n2_xz_top = lay.over_z(live.n2_x[:cut])
    near, near_c, out, out_c = mlp_rest(*live.acts, mlp_gate, mlp_up, mlp_down, tokens)
    del live.far, live.far_c, live.n2_z_top, live.n2_z_low
    live.hold(arriving=arriving, near=near, near_c=near_c, out=out, out_c=lay.over_c(out_c), n2_yz=n2_yz, n2_xz_top=n2_xz_top)

    grad_n2 = live.near + lay.over_c(live.near_c).astype(F32) + live.arriving.astype(F32)
    grad_mid_norm, grad_gain_two = norm_back(grad_n2, live.mid * live.inv2, live.inv2, live.gain_two)
    grad_mid = cot.astype(F32) + grad_mid_norm
    branch = grad_mid.astype(BF16)
    del live.near, live.near_c, live.arriving
    live.hold(grad_gain_two=grad_gain_two, grad_mid=grad_mid, branch=branch, branch_rel=order_f(branch))

    arriving = lay.over_x(live.branch_rel)
    n2_xz_low = lay.over_z(live.n2_x[cut:])
    cot_yz = lay.over_y(live.cot_z)
    live.hold(arriving=arriving, n2_xz_low=n2_xz_low, cot_yz=cot_yz, out_sum=live.out + live.out_c.astype(F32),
              n2_y_c=lay.over_c(live.n2_y),
              n2_xy_c=lay.over_c(live.n2_xy))

    n1_yc = lay.over_y(live.n1_away_c)
    cot_z_c, cot_xz_c = (lay.over_c(live.cot_z), lay.over_c(live.cot_xz))
    branch_x_rel = jnp.concatenate([live.arriving[:, half:], live.arriving[:, :half]], axis=1)
    both_rel = jnp.concatenate([live.branch_rel, branch_x_rel], 0)
    grad_mixed = dot_cols(both_rel[:, :half], live.out_left) + dot_cols(both_rel[:, half:], live.out_right)
    gy, bprod, blocal, back_summary = by_head(
        mixer_back_scan, live.flags,
        [(grad_mixed.reshape(2, tokens, half), False), (live.y_pre, False), (live.dg, False),
         (live.prods, False), (live.local_state, False), (live.state_in, False), (live.rates, False)],
        [shape3(BF16), shape3(F32), shape3(F32), summary_shape])
    del live.arriving, live.branch_rel, live.y_pre
    live.hold(gy=gy.reshape(two, half), bprod=bprod, blocal=blocal, scan=scan_start(back_summary, 2),
              branch_x_rel=branch_x_rel, n1_yc=n1_yc, cot_z_c=cot_z_c, cot_xz_c=cot_xz_c)

    n2_xyz = lay.over_x(live.n2_yz)
    own_cols = lambda value, which: half_of(value, which, quarter, 1)
    part_y = dot_cols(own_cols(live.gy, c), in_y) + dot_cols(own_cols(live.gy, 1 - c), live.wy_c)
    for bit in bits:
        come = lay.over_seq_bit(jnp.concatenate(live.scan[:2], axis=0), bit)
        live.scan = scan_join(lay, live.scan, come, bit, True)
        if bit == 1:
            live.cut()
            cot_xyz = lay.over_y(live.cot_xz)
            n2_z_c, n2_yz_c, cot_yz_c = (lay.over_c(live.n2_z), lay.over_c(live.n2_yz), lay.over_c(live.cot_yz))
    back_in = live.scan[3]
    del live.scan
    live.hold(back_in=back_in, cot_xyz=cot_xyz, n2_xyz=n2_xyz, part_y=part_y, n2_z_c=n2_z_c, n2_yz_c=n2_yz_c,
              cot_yz_c=cot_yz_c)

    gip, gdp, gx_main, gx_tail, edge, vec_rows = by_head(
        mixer_backward, live.flags,
        [(live.bprod, False), (live.blocal, False), (live.back_in, False), (live.prods, False),
         (live.local_state, False), (live.state_in, False), (live.ig, False), (live.dg, False),
         (live.conv_low, False), (live.x_low, False), (live.halo, False), (live.gates, True),
         (live.vec, False), (live.rates, False)],
        [shape3(BF16), shape3(BF16), shape3(BF16), jax.ShapeDtypeStruct((2, 16, half), F32),
         jax.ShapeDtypeStruct((2, 8, half), F32), jax.ShapeDtypeStruct((8, half), F32)])
    for name in ("bprod", "blocal", "back_in", "prods", "local_state", "state_in", "ig", "dg", "x_low", "halo",
                 "gates", "vec", "rates", "flags"):
        delattr(live, name)
    live.hold(gip=gip, gdp=gdp, gx_main=gx_main, gx_tail=gx_tail, edge=edge, vec_rows=vec_rows)

    edge_next = lay.over_seq(live.edge, -1)
    mixed_x = lay.over_x(jnp.concatenate([live.mixed[1], live.mixed[0]], axis=0))
    n2_xz = jnp.concatenate([live.n2_xz_top, live.n2_xz_low], axis=0)
    n2_xz_c, n2_xyz_c, cot_xyz_c = (lay.over_c(n2_xz), lay.over_c(live.n2_xyz), lay.over_c(live.cot_xyz))
    live.n2s = [[live.n2, live.n2_x], [live.n2_y, live.n2_xy], [live.n2_z, n2_xz], [live.n2_yz, live.n2_xyz]]
    live.cots = [cot, live.cot_x, live.cot_y, live.cot_xy, live.cot_z, live.cot_xz, live.cot_yz, live.cot_xyz]
    n2_rows = rows_of_tokens(place, [p for group in live.n2s for p in group], half // 2, each)
    cot_rows = rows_of_tokens(place, live.cots, half // 2, each)
    del live.edge
    live.hold(edge_next=edge_next, n2_rows=n2_rows, cot_rows=cot_rows,
              n2s_c=[[live.n2_y_c, live.n2_xy_c], [live.n2_z_c, n2_xz_c], [live.n2_yz_c, n2_xyz_c]],
              cots_c=[live.cot_z_c, live.cot_xz_c, live.cot_yz_c, cot_xyz_c], mixed_x=mixed_x)

    gx_last = (live.gx_tail + jnp.pad(live.edge_next, ((0, 0), (8, 0), (0, 0)))).astype(BF16)
    gx = jnp.concatenate([live.gx_main[:, : tokens - 16], gx_last], axis=1).reshape(two, half)
    gx_o, gx_c = (own_cols(gx, c), own_cols(gx, 1 - c))
    part_n1 = live.part_y + dot_cols(gx_o, in_x) + dot_cols(gx_c, live.wx_c)
    del live.gx_main, live.gx_tail, live.edge_next, live.part_y
    live.hold(gx=gx, n1_near=part_n1[:tokens], n1_far=part_n1[tokens:].astype(BF16),
              n2_rows_c=lay.over_c(live.n2_rows), cot_rows_c=lay.over_c(live.cot_rows))

    cuts = sections_of(mlp_gate.shape[1])
    cuts = cuts[-1:] + cuts[:-1]

    def weight_piece(at, size):
        return mlp_weight_grads(
            place, [a + b for a, b in zip(live.n2s[1:], live.n2s_c)], live.gh_y,
            [live.cots[4:6] + live.cots_c[:2], live.cots[6:] + live.cots_c[2:]], live.acts,
            (live.n2_rows, live.n2_rows_c), (live.cot_rows, live.cot_rows_c), (mlp_gate, mlp_up, mlp_down),
            at, size, each)

    def piece_sum(own, rest):
        blocks = [own] + [rest[j * each : (j + 1) * each] for j in range(nz // 2 - 1)]
        bit = nz // 4
        while bit >= 1:
            gone = blocks[bit] if bit == 1 else jnp.concatenate(
                [b.astype(BF16) for b in blocks[bit : 2 * bit]], axis=0)
            come = lay.over_seq_bit(gone.astype(BF16), 2 * bit)
            blocks = [(blocks[j], come[j * each : (j + 1) * each]) for j in range(bit)]
            if bit > 1:
                blocks = [a.astype(F32) + b.astype(F32) for a, b in blocks]
            bit //= 2
        return blocks[0]

    arriving = lay.over_x(live.n1_far)
    gy_y = lay.over_y(live.gy)
    live.gy_c = lay.over_c(live.gy)
    live.hold(piece_a=weight_piece(*cuts[0]), arriving=arriving, gy_y=gy_y)

    grad_n1 = live.n1_near + live.arriving.astype(F32)
    scaled_one = inputs[0].astype(F32) * live.inv1
    grad_in_norm, grad_gain_one = norm_back(grad_n1, scaled_one, live.inv1, live.gain_one)
    input_grad = (live.grad_mid + grad_in_norm).astype(BF16)[None]
    rows_full = lax.dynamic_update_slice_in_dim(
        jnp.zeros((8, width), F32), live.vec_rows, x * half, 1)
    sums = jnp.concatenate([grad_gain_one[None], live.grad_gain_two[None], rows_full], axis=0)
    sums = sums + lay.over_c(sums)
    del live.n1_near, live.n1_far, live.arriving, live.vec_rows, live.grad_gain_two, live.grad_mid
    live.hold(sums=sums, gy_yc=lay.over_c(live.gy_y))

    def over_columns(value):
        split = value.reshape(2, own80, half)
        mine = lax.dynamic_index_in_dim(split, x, 0, keepdims=False)
        theirs = lay.over_x(lax.dynamic_index_in_dim(split, 1 - x, 0, keepdims=False))
        return jnp.where(x == 0, jnp.concatenate([mine, theirs], -1),
                         jnp.concatenate([theirs, mine], -1)).astype(F32)

    sums = live.sums + lay.over_x(live.sums)
    sums = sums + lay.over_seq_bit(sums, 1)
    n1_all = [live.n1_own, live.n1_c, live.n1_y, live.n1_yc]
    in_y_part = sum_of_dots(n1_all, [live.gy, live.gy_c, live.gy_y, live.gy_yc])
    branch_far = half_of(order_f(live.branch_x_rel), x, half, 1)
    branch_near = half_of(live.branch, x, half, 1)
    del live.gy, live.gy_c, live.gy_y, live.gy_yc, live.branch_x_rel
    live.hold(in_y_part=in_y_part, sums=sums, branch_two=jnp.concatenate([branch_near, branch_far], axis=0))

    sum_a = piece_sum(*live.piece_a)
    in_y_own, in_y_come = owner_parts(live.in_y_part.reshape(nz, 2 * own80, half))
    gx_y = lay.over_y(live.gx)
    branch_two_y = lay.over_y(live.branch_two)
    piece_b = weight_piece(*cuts[1])
    del live.piece_a
    live.hold(piece_b=piece_b, sum_a=sum_a, gx_y=gx_y, branch_two_y=branch_two_y, in_y_own=in_y_own,
              in_y_come=in_y_come[:-1], in_y_part=live.in_y_part)

    in_y_last = owner_parts(live.in_y_part.reshape(nz, 2 * own80, half))[1][-1:]
    sum_b = piece_sum(*live.piece_b)
    mixed_own, mixed_away, sent, sent_y = rows_by_device(
        at_yc, [[live.mixed[0], live.mixed[1]], [live.mixed_x[:tokens], live.mixed_x[tokens:]]], n1_starts, own80)
    in_x_part = sum_of_dots(n1_all, [live.gx, lay.over_c(live.gx), live.gx_y, lay.over_c(live.gx_y)])
    gate_part = gate_weight_grad(
        live.conv_low.reshape(two, half), live.gip.reshape(two, half), live.gdp.reshape(two, half)
    ).reshape(2, nz, 2, own80, 2 * BLK)
    pick = lambda value, at, axis: lax.dynamic_index_in_dim(value, at, axis, keepdims=False)
    gate_part = pick(gate_part, c, 2) + lay.over_c(pick(gate_part, 1 - c, 2).astype(BF16)).astype(F32)
    gate_y = lay.over_y(pick(gate_part, 1 - y, 0).astype(BF16))
    del live.mixed, live.mixed_x, live.conv_low, live.gip, live.gdp, live.in_y_part, live.piece_b
    live.hold(in_x_part=in_x_part, gate_keep=pick(gate_part, y, 0), gate_y=gate_y, sum_b=sum_b,
              in_y_total=total_of(live.in_y_own, live.in_y_come + in_y_last),
              mixed_own=mixed_own, mixed_away=mixed_away, mixed_c=lay.over_c(sent), mixed_away_c=lay.over_c(sent_y),
              branch_c=lay.over_c(live.branch_two), branch_yc=lay.over_c(live.branch_two_y))
    del live.in_y_own, live.in_y_come

    mixed_y = (lay.over_y(live.mixed_away), lay.over_y(live.mixed_away_c))
    in_y_grad = over_columns(live.in_y_total)
    gate_part = (live.gate_keep + live.gate_y.astype(F32)).astype(BF16)
    del live.gate_keep, live.gate_y, live.mixed_away, live.mixed_away_c, live.in_y_total
    live.hold(in_x_part=jnp.concatenate(
        [live.in_x_part.reshape(nz, 2 * own80, half), gate_part.reshape(nz, own80 * 2 * BLK // half, half)], axis=1),
        mixed_y=mixed_y, in_y_grad=in_y_grad)

    live.hold(out_part=sum_of_dots(
        [live.mixed_own, live.mixed_c, *live.mixed_y],
        [live.branch_two, live.branch_c, live.branch_two_y, live.branch_yc]))
    del live.mixed_own, live.mixed_c, live.mixed_y

    in_x_own, in_x_come = owner_parts(live.in_x_part)
    out_arriving = lay.over_x(live.out_sum[tokens:].astype(BF16))
    piece_c = weight_piece(*cuts[2])
    del live.in_x_part
    live.hold(piece_c=piece_c, in_x_own=in_x_own, in_x_come=in_x_come, out_arriving=out_arriving)

    sum_c = piece_sum(*live.piece_c)
    out_own, out_come = owner_parts(live.out_part.reshape(nz, 2 * own80, half))
    live.hold(sum_c=sum_c, out_own=out_own, out_come=out_come,
              in_x_total=total_of(live.in_x_own, live.in_x_come),
              output=(live.mid + live.out_sum[:tokens] + live.out_arriving.astype(F32)).astype(BF16)[None])

    sums = live.sums
    for bit in bits[1:]:
        sums = sums + lay.over_seq_bit(sums, bit)
    mlp_down_grad, mlp_gate_grad, mlp_up_grad = joined_columns([live.sum_b, live.sum_c, live.sum_a])

    def final(z, y, x, c):
        at = ((x * 2 + y) * nz + z) * 2 + c
        s, f = (at // 4, at % 4)
        return (s // 2, s % 2, f // 2, f % 2)

    in_x_grad = over_columns(live.in_x_total[: 2 * own80])
    out_grad = over_columns(total_of(live.out_own, live.out_come))
    gate_grad = lay.send(live.in_x_total[2 * own80 :].reshape(own80, 2 * BLK), final).astype(F32)
    return (live.output, input_grad, sums, live.in_y_grad, in_x_grad, gate_grad, out_grad,
            mlp_gate_grad, mlp_up_grad, mlp_down_grad)


def solution(mesh):
    return jax.shard_map(
        local,
        mesh=mesh,
        in_specs=(
            P("fsdp", "seq", None),
            P("fsdp", "seq"),
            P(),
            P(),
            P(None, "fsdp"),
            P(None, "fsdp"),
            P(None, "fsdp"),
            P(None, "fsdp"),
            P(None, "fsdp"),
            P(None, "fsdp"),
            P(None, "fsdp"),
            P("fsdp", "seq", None),
        ),
        out_specs=(
            P("fsdp", "seq", None),
            P("fsdp", "seq", None),
            P(),
            P(("seq", "fsdp"), None),
            P(("seq", "fsdp"), None),
            P(("seq", "fsdp"), None),
            P(("seq", "fsdp"), None),
            P("seq", "fsdp"),
            P("seq", "fsdp"),
            P("seq", "fsdp"),
        ),
        check_vma=False,
    )
```

```python
import functools

import jax
import jax.numpy as jnp
from jax import lax
from jax.experimental import pallas as pl
from jax.experimental.pallas import tpu as pltpu
from jax.sharding import PartitionSpec as P

HEADS = 10
BLK = 256
FBLK = 64
EPS = 1e-06
ALL = ("seq", "fsdp")
F32 = jnp.float32
BF16 = jnp.bfloat16
GELU_C = 0.7978845608028654
GELU_A = 0.044715
VMEM_MAX = 60 * 1024 * 1024
ANY = pl.BlockSpec(memory_space=pl.ANY)


def work(us):
    scale = 1000 if us >= 10 else 0
    return pl.CostEstimate(flops=1 + us * scale * 900000, bytes_accessed=1 + us * scale * 2000, transcendentals=0)


def norm_scale(values):
    inverse = lax.rsqrt(jnp.mean(values * values, axis=-1, keepdims=True) + EPS)
    return (values * inverse, inverse)


def norm_back(grad_normed, scaled, inverse, gain_row):
    grad_gain = jnp.sum(grad_normed * scaled, axis=0)
    inner_term = grad_normed * gain_row
    grad_input = inverse * (
        inner_term - scaled * jnp.mean(inner_term * scaled, axis=-1, keepdims=True)
    )
    return (grad_input, grad_gain)


def gelu_pair(values):
    square = values * values
    t = jnp.tanh(values * (GELU_C + GELU_C * GELU_A * square))
    half = 0.5 + 0.5 * t
    slope = half * (1.0 + (1.0 - t) * values * (GELU_C + 3.0 * GELU_C * GELU_A * square))
    return (values * half, slope)


def dot(left, right):
    return jnp.dot(left, right, preferred_element_type=F32)


def dot_rows(left, right):
    return lax.dot_general(left, right, (((0,), (0,)), ((), ())), preferred_element_type=F32)


def dot_cols(left, right):
    return lax.dot_general(left, right, (((1,), (1,)), ((), ())), preferred_element_type=F32)


class Lay:
    def __init__(self):
        self.seq = lax.axis_size("seq")
        self.nz = self.seq // 2
        seq, fsdp = (lax.axis_index("seq"), lax.axis_index("fsdp"))
        self.z, self.y = (seq // 2, seq % 2)
        self.x, self.c = (fsdp // 2, fsdp % 2)
        self.seq_at = seq

    def pairs(self, target):
        found = []
        for s in range(self.seq):
            for f in range(4):
                z, y, x, c = (s // 2, s % 2, f // 2, f % 2)
                to = target(z, y, x, c)
                if to is not None:
                    found.append((s * 4 + f, ((to[0] * 2 + to[1]) * 2 + to[2]) * 2 + to[3]))
        return found

    def send(self, value, target):
        return lax.ppermute(value, ALL, self.pairs(target))

    def over_c(self, value):
        return self.send(value, lambda z, y, x, c: (z, y, x, 1 - c))

    def over_x(self, value):
        return self.send(value, lambda z, y, x, c: (z, y, 1 - x, c))

    def over_y(self, value):
        return self.send(value, lambda z, y, x, c: (z, 1 - y, x, c))

    def over_seq_bit(self, value, bit):
        def to(z, y, x, c):
            other = (2 * z + y) ^ bit
            return (other // 2, other % 2, x, c)

        return self.send(value, to)

    def over_z(self, value):
        return self.send(value, lambda z, y, x, c: (self.nz - 1 - z, y, x, c))

    def over_seq(self, value, by):
        def to(z, y, x, c):
            other = 2 * z + y + by
            return (other // 2, other % 2, x, c) if 0 <= other < self.seq else None

        return self.send(value, to)


def row_iota(rows, cols):
    return lax.broadcasted_iota(jnp.int32, (rows, cols), 0)


def token_masks(flags_ref, g, rows, cols):
    row = row_iota(rows, cols)
    block = row // FBLK
    offset = row % FBLK
    flagged = jnp.zeros((rows, cols), F32)
    for b in range(rows // FBLK):
        flagged = jnp.where(block == b, flags_ref[g, b], flagged)
    valid = [jnp.where(offset < lag, 1.0 - flagged, 1.0) for lag in range(4)]
    start = jnp.where(offset == 0, flagged, 0.0)
    return start, valid


def neg_expm1(v):
    series = 1.0 + v * (1.0 / 6.0)
    for n in (5.0, 4.0, 3.0, 2.0):
        series = 1.0 + v * (1.0 / n) * series
    return jnp.where(v > -0.25, -v * series, 1.0 - jnp.exp(v))


def shifted_inputs(xl_ref, halo_ref, g):
    ext = jnp.concatenate([halo_ref[g].astype(F32), xl_ref[g].astype(F32)], axis=0)
    pad = halo_ref.shape[1]
    return [ext[pad:] if k == 0 else pltpu.roll(ext, k, 0)[pad:] for k in range(4)]


def mixer_forward(flags_ref, xl_ref, halo_ref, gw_ref, vec_ref, rate_ref,
                  conv_ref, ig_ref, dg_ref, prod_ref, local_ref, sum_ref):
    groups, rows, cols = xl_ref.shape
    row = row_iota(rows, cols)
    for g in range(groups):
        start, valid = token_masks(flags_ref, g, rows, cols)
        lagged = shifted_inputs(xl_ref, halo_ref, g)
        conv = vec_ref[6:7, :] + jnp.zeros((rows, cols), F32)
        for k in range(4):
            conv = conv + vec_ref[2 + k : 3 + k, :] * lagged[k] * valid[k]
        conv_low = conv.astype(BF16)
        conv_ref[g] = conv_low
        prod = jnp.dot(conv_low, gw_ref[...], preferred_element_type=F32)
        ig = jax.nn.sigmoid(prod[:, :cols] + vec_ref[7:8, :])
        dg = jax.nn.sigmoid(prod[:, cols:] + vec_ref[8:9, :])
        ig_ref[g] = ig
        dg_ref[g] = dg
        keep = 1.0 - start
        log_decay = -8.0 * dg * rate_ref[0:1, :]
        p = jnp.exp(log_decay) * keep
        s = jnp.sqrt(keep * neg_expm1(2.0 * log_decay) + start) * ig * conv_low.astype(F32)
        step = 1
        while step < rows:
            inside = row >= step
            p_prev = jnp.where(inside, pltpu.roll(p, step, 0), 1.0)
            s_prev = jnp.where(inside, pltpu.roll(s, step, 0), 0.0)
            s = p * s_prev + s
            p = p * p_prev
            step *= 2
        prod_ref[g] = p
        local_ref[g] = s
        sum_ref[g : g + 1, :] = p[rows - 1 :, :]
        sum_ref[groups + g : groups + g + 1, :] = s[rows - 1 :, :]


def mixer_back_scan(flags_ref, gm_ref, y_ref, dg_ref, prod_ref, local_ref, sin_ref, rate_ref,
                    gy_ref, bprod_ref, blocal_ref, sum_ref):
    groups, rows, cols = gm_ref.shape
    row = row_iota(rows, cols)
    for g in range(groups):
        start, _ = token_masks(flags_ref, g, rows, cols)
        state = local_ref[g] + prod_ref[g] * sin_ref[g : g + 1, :]
        gelu, slope = gelu_pair(y_ref[g])
        gm = gm_ref[g]
        gy_ref[g] = (gm * state * slope).astype(BF16)
        decay = jnp.exp(-8.0 * dg_ref[g] * rate_ref[0:1, :]) * (1.0 - start)
        s = gm * gelu
        p = jnp.where(row == rows - 1, 1.0, pltpu.roll(decay, rows - 1, 0))
        step = 1
        while step < rows:
            inside = row < rows - step
            p_next = jnp.where(inside, pltpu.roll(p, rows - step, 0), 1.0)
            s_next = jnp.where(inside, pltpu.roll(s, rows - step, 0), 0.0)
            s = p * s_next + s
            p = p * p_next
            step *= 2
        bprod_ref[g] = p
        blocal_ref[g] = s
        sum_ref[g : g + 1, :] = decay[:1, :] * p[:1, :]
        sum_ref[groups + g : groups + g + 1, :] = decay[:1, :] * s[:1, :]


def mixer_backward(flags_ref, bprod_ref, blocal_ref, bin_ref, prod_ref, local_ref, sin_ref,
                   ig_ref, dg_ref, conv_ref, xl_ref, halo_ref, gw_ref, vec_ref, rate_ref,
                   gip_ref, gdp_ref, gx_ref, tail_ref, edge_ref, rows_ref):
    groups, rows, cols = xl_ref.shape
    row = row_iota(rows, cols)
    sums = [jnp.zeros((1, cols), F32) for _ in range(8)]
    tail = tail_ref.shape[1]
    pad = edge_ref.shape[1]
    for g in range(groups):
        start, valid = token_masks(flags_ref, g, rows, cols)
        keep = 1.0 - start
        rate = rate_ref[0:1, :]
        state_in = sin_ref[g : g + 1, :]
        state = local_ref[g] + prod_ref[g] * state_in
        prev = jnp.where(row == 0, state_in, pltpu.roll(state, 1, 0))
        sg = blocal_ref[g] + bprod_ref[g] * bin_ref[g : g + 1, :]
        ig, dg = (ig_ref[g], dg_ref[g])
        cf = conv_ref[g].astype(F32)
        log_decay = -8.0 * dg * rate
        decay = jnp.exp(log_decay) * keep
        scale = jnp.sqrt(keep * neg_expm1(2.0 * log_decay) + start)
        gscale = sg * ig * cf
        glog = sg * prev * decay - gscale * keep * jnp.exp(2.0 * log_decay) / scale
        gip = sg * scale * cf * ig * (1.0 - ig)
        gdp = -8.0 * rate * glog * dg * (1.0 - dg)
        gip_low, gdp_low = (gip.astype(BF16), gdp.astype(BF16))
        gip_ref[g] = gip_low
        gdp_ref[g] = gdp_low
        gconv = sg * scale * ig + lax.dot_general(
            jnp.concatenate([gip_low, gdp_low], axis=1), gw_ref[...],
            (((1,), (1,)), ((), ())), preferred_element_type=F32)
        lagged = shifted_inputs(xl_ref, halo_ref, g)
        spread = jnp.zeros((rows + pad, cols), F32)
        for k in range(4):
            masked = gconv * valid[k]
            sums[k] = sums[k] + jnp.sum(masked * lagged[k], axis=0, keepdims=True)
            full = jnp.concatenate(
                [jnp.zeros((pad, cols), F32), vec_ref[2 + k : 3 + k, :] * masked], axis=0)
            spread = spread + (full if k == 0 else pltpu.roll(full, rows + pad - k, 0))
        gx_ref[g] = spread[pad:].astype(BF16)
        tail_ref[g] = spread[pad + rows - tail :]
        edge_ref[g] = spread[:pad]
        sums[4] = sums[4] + jnp.sum(gconv, axis=0, keepdims=True)
        sums[5] = sums[5] + jnp.sum(gip, axis=0, keepdims=True)
        sums[6] = sums[6] + jnp.sum(gdp, axis=0, keepdims=True)
        sums[7] = sums[7] + jnp.sum(-8.0 * dg * glog, axis=0, keepdims=True) * rate_ref[1:2, :]
    rows_ref[...] = jnp.concatenate(sums, axis=0)


def by_head(body, flags, operands, outs):
    def spec(shape, rows_are_channels):
        if rows_are_channels:
            return pl.BlockSpec((BLK, shape[1]), lambda h: (h, 0))
        lead = shape[:-1]
        return pl.BlockSpec(lead + (BLK,), lambda h: (0,) * len(lead) + (h,))

    heads = outs[0].shape[-1] // BLK
    in_specs = [pl.BlockSpec(memory_space=pltpu.SMEM)]
    values = [flags]
    for value, is_gate in operands:
        in_specs.append(spec(value.shape, is_gate))
        values.append(value)
    size = sum(v.size * v.dtype.itemsize for v in values) + sum(
        o.size * o.dtype.itemsize for o in outs)
    return pl.pallas_call(
        body,
        grid=(heads,),
        in_specs=in_specs,
        out_specs=[spec(o.shape, False) for o in outs],
        out_shape=outs,
        compiler_params=pltpu.CompilerParams(vmem_limit_bytes=48 * 1024 * 1024),
        cost_estimate=work(7),
    )(*values)


def grad_hidden_of(parts, w_down):
    count = len(parts)
    rows, width = parts[0].shape
    total = count * rows
    ff = w_down.shape[1]

    def body(*refs):
        c_refs, (w_ref, out_ref, held, sem) = (refs[:count], refs[count:])

        @pl.when(pl.program_id(0) == 0)
        def _():
            copies = [
                pltpu.make_async_copy(c_refs[i], held.at[pl.ds(i * rows, rows)], sem.at[i])
                for i in range(count)
            ]
            for copy in copies:
                copy.start()
            for copy in copies:
                copy.wait()

        out_ref[...] = dot(held[...], w_ref[...])

    return pl.pallas_call(
        body,
        grid=(pl.cdiv(ff, BLK),),
        in_specs=[ANY] * count + [pl.BlockSpec((width, BLK), lambda j: (0, j))],
        out_specs=pl.BlockSpec((total, BLK), lambda j: (0, j)),
        out_shape=jax.ShapeDtypeStruct((total, ff), F32),
        scratch_shapes=[pltpu.VMEM((total, width), BF16), pltpu.SemaphoreType.DMA((count,))],
        compiler_params=pltpu.CompilerParams(vmem_limit_bytes=VMEM_MAX),
        cost_estimate=work(5 + total // 64),
    )(*parts, w_down)


def sections_of(total):
    found, at = ([], 0)
    while at < total:
        size = min(768, total - at)
        found.append((at, size))
        at += size
    return found


def mlp_forward(n2_parts, grad_hidden, w_gate, w_up):
    count = len(n2_parts)
    rows, width = n2_parts[0].shape
    total = count * rows
    ff = w_gate.shape[1]
    parts = sections_of(ff)
    widest = parts[0][1]
    far = total // 2

    def body(*refs):
        n_refs = refs[:count]
        gh_ref, wg_ref, wu_ref = refs[count : count + 3]
        hid_ref, gg_ref, gu_ref, far_ref, far_c_ref = refs[count + 3 : count + 8]
        n2_s, gh_s, wg_s, wu_s, acc, sem_n, sem_w = refs[count + 8 :]

        def load(k):
            at, size = parts[k]
            slot = k % 2
            return [
                pltpu.make_async_copy(
                    wg_ref.at[:, pl.ds(at, size)], wg_s.at[slot, :, pl.ds(0, size)], sem_w.at[slot, 0]),
                pltpu.make_async_copy(
                    wu_ref.at[:, pl.ds(at, size)], wu_s.at[slot, :, pl.ds(0, size)], sem_w.at[slot, 1]),
                pltpu.make_async_copy(
                    gh_ref.at[:, pl.ds(at, size)], gh_s.at[slot, :, pl.ds(0, size)], sem_w.at[slot, 2]),
            ]

        first = [
            pltpu.make_async_copy(n_refs[i], n2_s.at[pl.ds(i * rows, rows)], sem_n.at[i])
            for i in range(count)
        ]
        for copy in first + load(0):
            copy.start()
        for copy in first:
            copy.wait()
        for k, (at, size) in enumerate(parts):
            if k + 1 < len(parts):
                for copy in load(k + 1):
                    copy.start()
            for copy in load(k):
                copy.wait()
            slot = k % 2
            wg, wu = (wg_s[slot, :, :size], wu_s[slot, :, :size])
            gelu, slope = gelu_pair(dot(n2_s[...], wg))
            up = dot(n2_s[...], wu)
            gh = gh_s[slot, :, :size]
            hid_ref[:, at : at + size] = (gelu * up).astype(BF16)
            gg = (gh * up * slope).astype(BF16)
            gu = (gh * gelu).astype(BF16)
            gg_ref[:, at : at + size] = gg
            gu_ref[:, at : at + size] = gu

            def far_rows(v):
                return jnp.concatenate([v[rows : 2 * rows], v[3 * rows :]], axis=0)

            part = dot_cols(far_rows(gg), wg) + dot_cols(far_rows(gu), wu)
            if k == 0:
                acc[...] = part
            else:
                acc[...] += part
        far_ref[...] = acc[:rows]
        far_c_ref[...] = acc[rows:].astype(BF16)

    act = jax.ShapeDtypeStruct((total, ff), BF16)
    return pl.pallas_call(
        body,
        in_specs=[ANY] * (count + 3),
        out_shape=[act, act, act, jax.ShapeDtypeStruct((rows, width), F32),
                   jax.ShapeDtypeStruct((rows, width), BF16)],
        scratch_shapes=[
            pltpu.VMEM((total, width), BF16),
            pltpu.VMEM((2, total, widest), F32),
            pltpu.VMEM((2, width, widest), BF16),
            pltpu.VMEM((2, width, widest), BF16),
            pltpu.VMEM((far, width), F32),
            pltpu.SemaphoreType.DMA((count,)),
            pltpu.SemaphoreType.DMA((2, 3)),
        ],
        compiler_params=pltpu.CompilerParams(vmem_limit_bytes=VMEM_MAX),
        cost_estimate=work(23),
    )(*n2_parts, grad_hidden, w_gate, w_up)


def mlp_rest(hidden, grad_gate, grad_up, w_gate, w_up, w_down, rows):
    total, ff = hidden.shape
    width = w_gate.shape[0]
    block = 512

    def body(hid_ref, gg_ref, gu_ref, wg_ref, wu_ref, wd_ref, gn_ref, gn_c_ref, out_ref, out_c_ref):
        def near(ref):
            return jnp.concatenate([ref[:rows], ref[2 * rows : 3 * rows]], axis=0)

        gn = dot_cols(near(gg_ref), wg_ref[...]) + dot_cols(near(gu_ref), wu_ref[...])
        gn_ref[...] = gn[:rows]
        gn_c_ref[...] = gn[rows:].astype(BF16)
        out = dot_cols(hid_ref[...], wd_ref[...])
        out_ref[...] = out[: total // 2]
        out_c_ref[...] = out[total // 2 :].astype(BF16)

    whole = pl.BlockSpec((total, ff), lambda j: (0, 0))
    weight = pl.BlockSpec((block, ff), lambda j: (j, 0))
    tall = lambda n: pl.BlockSpec((n, block), lambda j: (0, j))
    shape = lambda n, dt: jax.ShapeDtypeStruct((n, width), dt)
    return pl.pallas_call(
        body,
        grid=(width // block,),
        in_specs=[whole] * 3 + [weight] * 3,
        out_specs=[tall(rows), tall(rows), tall(total // 2), tall(total // 2)],
        out_shape=[shape(rows, F32), shape(rows, BF16), shape(total // 2, F32), shape(total // 2, BF16)],
        compiler_params=pltpu.CompilerParams(vmem_limit_bytes=VMEM_MAX),
        cost_estimate=work(19),
    )(hidden, grad_gate, grad_up, w_gate, w_up, w_down)


def rows_of_tokens(place, parts, rows_out, each):
    tokens, width = parts[0].shape
    half = width // 2
    count = len(parts)

    def body(place_ref, *refs):
        out_ref, turned = (refs[count], refs[count + 1])
        for k in range(count):
            turned[...] = refs[k][...].T
            for i in range(rows_out // each):
                at = pl.multiple_of((2 * i + place_ref[2]) * each, 16)
                out_ref[i * each : (i + 1) * each, k * tokens : (k + 1) * tokens] = turned[pl.ds(at, each), :]

    return pl.pallas_call(
        body,
        grid_spec=pltpu.PrefetchScalarGridSpec(
            num_scalar_prefetch=1,
            grid=(1,),
            in_specs=[pl.BlockSpec((tokens, half), lambda i, place: (0, place[1]))] * count,
            out_specs=pl.BlockSpec((rows_out, count * tokens), lambda i, place: (0, 0)),
            scratch_shapes=[pltpu.VMEM((half, tokens), BF16)],
        ),
        out_shape=jax.ShapeDtypeStruct((rows_out, count * tokens), BF16),
        compiler_params=pltpu.CompilerParams(vmem_limit_bytes=VMEM_MAX),
        cost_estimate=work(5),
    )(place, *parts)


def mlp_weight_grads(place, n2_parts, first_hidden, cot_parts, acts, n2_rows, cot_rows, weights, at, size, each):
    groups = len(n2_parts)
    per = len(n2_parts[0])
    tokens, width = n2_parts[0][0].shape
    group = per * tokens
    both = group // 2
    rows = n2_rows[0].shape[0]
    flat_n = [p for g in n2_parts for p in g]
    flat_c = [p for g in cot_parts for p in g]
    total, total_c = (len(flat_n), len(flat_c))

    def body(place_ref, *refs):
        n_refs, c_refs, refs = (refs[:total], refs[total : total + total_c], refs[total + total_c :])
        gh_ref, wg_ref, wu_ref, wd_ref, hid_ref, gg_ref, gu_ref, nm, no, cm, co = refs[:11]
        own_ref, rest_ref, n2_s, cot_s, acc, sem = refs[11:]

        def load(g, slot):
            found = []
            for i in range(per):
                to = pl.ds(i * tokens, tokens)
                found.append(pltpu.make_async_copy(n_refs[g * per + i], n2_s.at[slot, to], sem.at[slot, i]))
                if g > 0:
                    found.append(pltpu.make_async_copy(
                        c_refs[(g - 1) * per + i], cot_s.at[slot, to], sem.at[slot, per + i]))
            return found

        for copy in load(0, 0) + load(1, 1):
            copy.start()

        def add(g, act, fresh):
            start = g * both if isinstance(g, int) else pl.multiple_of(g * both, both)
            for i, (mine, other) in enumerate(((cm, co), (nm, no), (nm, no))):
                part = dot(mine[:, pl.ds(start, both)], act[i][:both]) + dot(
                    other[:, pl.ds(start, both)], act[i][both:])
                if fresh:
                    acc[i] = part
                else:
                    acc[i] += part

        def recompute(g, slot, gh):
            gelu, slope = gelu_pair(dot(n2_s[slot], wg_ref[...]))
            up = dot(n2_s[slot], wu_ref[...])
            add(g + 1, ((gelu * up).astype(BF16), (gh * up * slope).astype(BF16), (gh * gelu).astype(BF16)), False)

        add(0, (hid_ref, gg_ref, gu_ref), True)
        for copy in load(0, 0):
            copy.wait()
        recompute(0, 0, gh_ref[...])

        def step(g, carry):
            slot = lax.rem(g, 2)
            for k in range(2, groups):
                @pl.when(g + 1 == k)
                def _():
                    for copy in load(k, k % 2):
                        copy.start()

            for copy in load(1, slot):
                copy.wait()
            recompute(g, slot, dot(cot_s[slot], wd_ref[...]))
            return carry

        lax.fori_loop(1, groups, step, 0)
        for j in range(rows // each):
            start = pl.multiple_of((place_ref[0] ^ j) * each, 8)
            for i in range(3):
                block = acc[i, pl.ds(start, each), :]
                if j == 0:
                    own_ref[:, i * size : (i + 1) * size] = block
                else:
                    rest_ref[(j - 1) * each : j * each, i * size : (i + 1) * size] = block.astype(BF16)

    index = at // size
    column = lambda n: pl.BlockSpec((n, size), lambda j, place: (0, index))
    whole = pl.BlockSpec(n2_rows[0].shape, lambda j, place: (0, 0))
    return pl.pallas_call(
        body,
        grid_spec=pltpu.PrefetchScalarGridSpec(
            num_scalar_prefetch=1,
            grid=(1,),
            in_specs=[ANY] * (total + total_c) + [column(group)] + [column(width)] * 3 + [column(group)] * 3
            + [whole] * 4,
            out_specs=[pl.BlockSpec((each, 3 * size), lambda j, place: (0, 0)),
                       pl.BlockSpec((rows - each, 3 * size), lambda j, place: (0, 0))],
            scratch_shapes=[
                pltpu.VMEM((2, group, width), BF16),
                pltpu.VMEM((2, group, width), BF16),
                pltpu.VMEM((3, rows, size), F32),
                pltpu.SemaphoreType.DMA((2, 2 * per)),
            ],
        ),
        out_shape=[jax.ShapeDtypeStruct((each, 3 * size), F32),
                   jax.ShapeDtypeStruct((rows - each, 3 * size), BF16)],
        compiler_params=pltpu.CompilerParams(vmem_limit_bytes=VMEM_MAX),
        cost_estimate=work(35 * size // 768),
    )(place, *flat_n, *flat_c, first_hidden, *weights, *acts, *n2_rows, *cot_rows)


def rows_by_device(place, parts, starts, block):
    columns, count = (len(parts), len(parts[0]))
    tokens, n = parts[0][0].shape
    rows = len(starts(0, 0)) * block
    flat = [block_of for column in parts for block_of in column]
    if block % 16:
        turned = [jnp.concatenate(column, axis=0).T for column in parts]
        turned = turned[0] if columns == 1 else jnp.where(
            place[2] == 0, jnp.concatenate(turned), jnp.concatenate(turned[::-1]))

        def taken(dc):
            return jnp.stack([
                jnp.concatenate([
                    lax.dynamic_slice_in_dim(turned, start, block, 0)
                    for start in starts(place[0] ^ dy, place[1] ^ dc)])
                for dy in range(2)])

        kept, sent = (taken(0), taken(1))
        return kept[0], sent[0], jnp.concatenate([kept[1], sent[1]], axis=0)

    def body(place_ref, *refs):
        keep_ref, send_ref, y_ref, turned = refs[len(flat):]
        for h in range(columns):
            base = 0 if columns == 1 else pl.multiple_of((place_ref[2] ^ h) * n, 16)
            for k in range(count):
                turned[pl.ds(base, n), k * tokens : (k + 1) * tokens] = refs[h * count + k][...].T
        for dy, dc, ref, at in ((0, 0, keep_ref, 0), (0, 1, send_ref, 0), (1, 0, y_ref, 0), (1, 1, y_ref, rows)):
            for i, start in enumerate(starts(place_ref[0] ^ dy, place_ref[1] ^ dc)):
                ref[at + i * block : at + (i + 1) * block, :] = turned[pl.ds(pl.multiple_of(start, 16), block), :]

    shape = (rows, count * tokens)
    return pl.pallas_call(
        body,
        grid_spec=pltpu.PrefetchScalarGridSpec(
            num_scalar_prefetch=1,
            grid=(1,),
            in_specs=[pl.BlockSpec((tokens, n), lambda i, place: (0, 0))] * len(flat),
            out_specs=[pl.BlockSpec((n_rows, shape[1]), lambda i, place: (0, 0)) for n_rows in (rows, rows, 2 * rows)],
            scratch_shapes=[pltpu.VMEM((columns * n, count * tokens), BF16)],
        ),
        out_shape=[jax.ShapeDtypeStruct((n_rows, shape[1]), BF16) for n_rows in (rows, rows, 2 * rows)],
        compiler_params=pltpu.CompilerParams(vmem_limit_bytes=VMEM_MAX),
        cost_estimate=work(3),
    )(place, *flat)


def joined_columns(pairs):
    rows = pairs[0][0].shape[0]
    widths = [a.shape[1] // 3 for a, _ in pairs]
    total = sum(widths)
    step = rows // 4 if rows % 64 == 0 else rows
    flat = [term for pair in pairs for term in pair]

    def body(*refs):
        for i in range(3):
            at = 0
            for k, n in enumerate(widths):
                span = slice(i * n, (i + 1) * n)
                refs[len(flat) + i][:, at : at + n] = refs[2 * k][:, span].astype(F32) + refs[
                    2 * k + 1][:, span].astype(F32)
                at += n

    return pl.pallas_call(
        body,
        grid=(rows // step,),
        in_specs=[pl.BlockSpec((step, term.shape[1]), lambda j: (j, 0)) for term in flat],
        out_specs=[pl.BlockSpec((step, total), lambda j: (j, 0))] * 3,
        out_shape=[jax.ShapeDtypeStruct((rows, total), F32)] * 3,
        compiler_params=pltpu.CompilerParams(vmem_limit_bytes=VMEM_MAX),
        cost_estimate=work(5),
    )(*flat)


def gate_weight_grad(conv, grad_in, grad_decay):
    tokens, n = conv.shape

    def body(conv_ref, in_ref, decay_ref, out_ref):
        turned = conv_ref[...].T
        out_ref[:, :BLK] = dot(turned, in_ref[...])
        out_ref[:, BLK:] = dot(turned, decay_ref[...])

    spec = pl.BlockSpec((tokens, BLK), lambda h: (0, h))
    return pl.pallas_call(
        body,
        grid=(n // BLK,),
        in_specs=[spec] * 3,
        out_specs=pl.BlockSpec((BLK, 2 * BLK), lambda h: (h, 0)),
        out_shape=jax.ShapeDtypeStruct((n, 2 * BLK), F32),
        compiler_params=pltpu.CompilerParams(vmem_limit_bytes=VMEM_MAX),
        cost_estimate=work(3),
    )(conv, grad_in, grad_decay)


def sum_of_dots(rows, values):
    count = len(rows)

    def body(*refs):
        total = dot(refs[0][...], refs[count][...])
        for k in range(1, count):
            total = total + dot(refs[k][...], refs[count + k][...])
        refs[2 * count][...] = total.astype(BF16)

    return pl.pallas_call(
        body,
        out_shape=jax.ShapeDtypeStruct((rows[0].shape[0], values[0].shape[1]), BF16),
        compiler_params=pltpu.CompilerParams(vmem_limit_bytes=VMEM_MAX),
        cost_estimate=work(5),
    )(*rows, *values)


def after(value, *others):
    return lax.optimization_barrier((value, others))[0]


class Live:
    def cut(self):
        names = sorted(vars(self))
        for name, value in zip(names, lax.optimization_barrier([getattr(self, n) for n in names])):
            setattr(self, name, value)

    def hold(self, **values):
        for name, value in values.items():
            setattr(self, name, value)
        self.cut()


def seq_bits(lay):
    found, bit = ([], 1)
    while bit < lay.seq:
        found.append(bit)
        bit *= 2
    return found


def scan_start(summary, groups):
    prod, state = (summary[:groups], summary[groups : 2 * groups])
    return (prod, state, jnp.ones_like(prod), jnp.zeros_like(state))


def scan_join(lay, held, other, bit, backward):
    prod, state, before_p, before_s = held
    groups = prod.shape[0]
    other_p, other_s = (other[:groups], other[groups:])
    is_later = (lay.seq_at & bit) != 0
    take = jnp.logical_not(is_later) if backward else is_later
    before_s = jnp.where(take, before_p * other_s + before_s, before_s)
    before_p = jnp.where(take, before_p * other_p, before_p)
    state = jnp.where(take, prod * other_s + state, other_p * state + other_s)
    return (prod * other_p, state, before_p, before_s)


def local(inputs, block_flags, decay_seed, vectors, in_y, in_x, gate_weight, out_proj,
          mlp_gate, mlp_up, mlp_down, cotangent):
    lay = Lay()
    nz, x, y, z, c = (lay.nz, lay.x, lay.y, lay.z, lay.c)
    tokens, width = inputs.shape[1:]
    half, quarter, two = (width // 2, width // 4, 2 * tokens)
    each = width // lay.seq
    own80 = each // 4
    bits = seq_bits(lay)
    place = jnp.stack([z % (nz // 2), lay.seq_at // nz, y]).astype(jnp.int32)
    at_yc = jnp.stack([y, c, x]).astype(jnp.int32)
    live = Live()

    def order_c(own, other, axis):
        return jnp.where(c == 0, jnp.concatenate([own, other], axis),
                         jnp.concatenate([other, own], axis))

    def order_f(rel):
        b = rel.shape[-1] // 4
        p = [rel[..., i * b : (i + 1) * b] for i in range(4)]
        by_c = jnp.where(c == 0, rel, jnp.concatenate([p[1], p[0], p[3], p[2]], -1))
        return jnp.where(x == 0, by_c, jnp.concatenate([by_c[..., 2 * b :], by_c[..., : 2 * b]], -1))

    def owner_parts(blocks):
        pick = lambda t: lax.dynamic_index_in_dim(blocks, t, 0, keepdims=False)
        come = [
            lay.send(pick((z + step) % nz), lambda z, y, x, c: ((z + step) % nz, y, x, c))
            for step in range(1, nz)
        ]
        return pick(z), come

    def total_of(own, come):
        total = own.astype(F32)
        for part in come:
            total = total + part.astype(F32)
        return total.astype(BF16)

    def half_of(value, which, n, axis):
        return lax.dynamic_slice_in_dim(value, which * n, n, axis)

    cot = cotangent[0]
    cut = tokens // 2
    gate_away, inputs, gate_weight, out_proj, vectors, decay_seed, block_flags = lax.optimization_barrier(
        (half_of(gate_weight, 1 - x, half, 0), inputs, gate_weight, out_proj, vectors, decay_seed, block_flags))
    halo_raw = lay.over_seq(inputs[0, tokens - 16 :], 1)
    gate_x = lay.over_x(gate_away)
    wx_c, wy_c = (lay.over_c(in_x), lay.over_c(in_y))
    scaled_one, inverse_one = norm_scale(inputs[0].astype(F32))
    live.hold(n1=(scaled_one * vectors[0]).astype(BF16), inv1=inverse_one, halo_raw=halo_raw,
              params=(gate_weight, out_proj, vectors, decay_seed, block_flags))

    gate_weight, out_proj, vectors, decay_seed, block_flags = live.params
    n1_x = lay.over_x(live.n1)
    halo_own = (norm_scale(live.halo_raw.astype(F32))[0] * vectors[0]).astype(BF16)
    n_flags = block_flags.shape[1]
    flag_row = jnp.pad(block_flags.astype(BF16), ((0, 0), (0, width - n_flags)))
    halo_x = lay.over_x(jnp.concatenate([flag_row, halo_own[1:]], axis=0))
    gate_own = half_of(gate_weight, x, half, 0)
    gate_c = lay.over_c(gate_own)
    cot_z = lay.over_z(after(cot, live.n1))
    cot_y = lay.over_y(after(cot, live.n1))
    base = -5.0 - decay_seed.astype(F32) + vectors[9]
    del live.params, live.halo_raw
    live.hold(
        n1_x=n1_x, halo_x=halo_x, halo_own=halo_own, gate_x=gate_x, gate_c=gate_c, wx_c=wx_c, cot_y=cot_y,
        flags=jnp.concatenate([block_flags.astype(F32), halo_x[:1, :n_flags].astype(F32)], axis=0),
        gate_own=gate_own, out_away=half_of(out_proj, 2 * (1 - x) + y, quarter, 0),
        out_mine=half_of(out_proj, x, half, 0), vec=half_of(vectors, x, half, 1), gain_two=vectors[1],
        gain_one=vectors[0],
        rates=half_of(jnp.stack([jax.nn.softplus(base), jax.nn.sigmoid(base)]), x, half, 1))

    out_a = lay.over_x(live.out_away)
    gates = order_f(jnp.concatenate(
        [live.gate_own, live.gate_c, live.gate_x, lay.over_c(live.gate_x)], axis=1))
    normed = jnp.concatenate([live.n1, live.n1_x, live.halo_own, live.halo_x], axis=0)
    x_all = order_c(dot(normed, in_x).astype(BF16), dot(normed, live.wx_c).astype(BF16), 1)
    x_low = x_all[:two].reshape(2, tokens, half)
    halo = x_all[two:].reshape(2, 16, half)
    shape3 = lambda dt: jax.ShapeDtypeStruct((2, tokens, half), dt)
    summary_shape = jax.ShapeDtypeStruct((4, half), F32)
    conv_low, ig, dg, prods, local_state, summary = by_head(
        mixer_forward, live.flags,
        [(x_low, False), (halo, False), (gates, True), (live.vec, False), (live.rates, False)],
        [shape3(BF16), shape3(F32), shape3(F32), shape3(F32), shape3(F32), summary_shape])
    out_c = lay.over_c(live.out_mine)
    del live.gate_x, live.gate_own, live.gate_c, live.halo_own, live.halo_x
    live.hold(x_low=x_low, halo=halo, gates=gates, conv_low=conv_low, ig=ig, dg=dg, prods=prods,
              local_state=local_state, scan=scan_start(summary, 2), out_c=out_c, normed=normed[:two], wy_c=wy_c, out_a=out_a,
              cot_z=cot_z)
    del live.out_away

    def n1_starts(at_y, at_c):
        return [((2 * i + at_y) * 4 + 2 * j + at_c) * own80 for i in range(nz) for j in range(2)]

    for bit in bits:
        come = lay.over_seq_bit(jnp.concatenate(live.scan[:2], axis=0), bit)
        live.scan = scan_join(lay, live.scan, come, bit, False)
        if bit == 1:
            live.cut()
            out_b = lay.over_y(live.out_a)
            cot_x = lay.over_x(after(cot, live.scan))
    out_x = jnp.where(y == 0, jnp.concatenate([live.out_a, out_b], 0), jnp.concatenate([out_b, live.out_a], 0))
    y_pre = order_c(dot(live.normed, in_y), dot(live.normed, live.wy_c), 1).reshape(2, tokens, half)
    n1_own, sent, n1_away = rows_by_device(at_yc, [[live.n1, live.n1_x]], n1_starts, own80)
    state_in = live.scan[3]
    del live.scan, live.out_a
    live.hold(state_in=state_in, y_pre=y_pre, out_left=jnp.concatenate([live.out_mine, live.out_c], axis=1),
              out_x=out_x, cot_x=cot_x, n1_own=n1_own, n1_away=n1_away, n1_c=lay.over_c(sent))
    del live.out_mine, live.out_c

    n1_y = lay.over_y(live.n1_away[: live.n1_own.shape[0]])
    state = live.local_state + live.prods * live.state_in[:, None, :]
    mixed = (state * jax.nn.gelu(live.y_pre, approximate=True)).astype(BF16)
    mixed_two = mixed.reshape(two, half)
    out_right = jnp.concatenate([live.out_x, lay.over_c(live.out_x)], axis=1)
    part = jnp.concatenate([dot(mixed_two, live.out_left), dot(mixed_two, out_right)], axis=1)
    del live.out_x
    live.hold(mixed=mixed, part_own=part[:tokens], part_x=part[tokens:].astype(BF16), out_right=out_right, n1_y=n1_y)

    part_x = lay.over_x(live.part_x)
    cot_xy = lay.over_y(live.cot_x)
    gh_main = grad_hidden_of([cot, live.cot_x, lay.over_c(cot), lay.over_c(live.cot_x)], mlp_down)
    live.hold(part_x=part_x, gh_main=gh_main, cot_xy=cot_xy)

    swapped = jnp.concatenate([live.part_x[:, half:], live.part_x[:, :half]], axis=1)
    mid = inputs[0].astype(F32) + order_f(live.part_own + swapped.astype(F32))
    scaled_two, inverse_two = norm_scale(mid)
    del live.part_x, live.part_own
    live.hold(mid=mid, inv2=inverse_two, n2=(scaled_two * live.gain_two).astype(BF16))

    n2_x = lay.over_x(live.n2)
    n2_y = lay.over_y(live.n2)
    n2_z_top = lay.over_z(live.n2[:cut])
    n2_c = lay.over_c(live.n2)
    pair = [live.cot_y, live.cot_xy]
    gh_y = grad_hidden_of(pair + [lay.over_c(p) for p in pair], mlp_down)
    live.hold(n2_x=n2_x, n2_c=n2_c, n2_y=n2_y, n2_z_top=n2_z_top, gh_y=gh_y)

    live.hold(n2_xc=lay.over_c(live.n2_x), n2_low=live.n2[cut:], n2_x_top=live.n2_x[:cut], n2_x_low=live.n2_x[cut:])
    cot_xz = lay.over_x(live.cot_z)
    n2_xy = lay.over_y(live.n2_x)
    n2_z_low = lay.over_z(live.n2_low)
    hidden, grad_gate, grad_up, far, far_c = mlp_forward(
        [live.n2, live.n2_x, live.n2_c, live.n2_xc], live.gh_main, mlp_gate, mlp_up)
    del live.gh_main, live.n2_c
    live.hold(acts=(hidden, grad_gate, grad_up), far=far, far_c=far_c, cot_xz=cot_xz, n2_xy=n2_xy,
              n2_z_low=n2_z_low)
    live.hold(far=(live.far + lay.over_c(live.far_c).astype(F32)).astype(BF16),
              n2_z=jnp.concatenate([live.n2_z_top, live.n2_z_low], axis=0))

    arriving = lay.over_x(live.far)
    n2_yz = lay.over_y(live.n2_z)
    n2_xz_top = lay.over_z(live.n2_x_top)
    near, near_c, out, out_c = mlp_rest(*live.acts, mlp_gate, mlp_up, mlp_down, tokens)
    del live.far, live.far_c, live.n2_z_top, live.n2_z_low
    live.hold(arriving=arriving, near=near, near_c=near_c, out=out, out_c=out_c, n2_yz=n2_yz, n2_xz_top=n2_xz_top)

    out_c = lay.over_c(live.out_c)
    grad_n2 = live.near + lay.over_c(live.near_c).astype(F32) + live.arriving.astype(F32)
    grad_mid_norm, grad_gain_two = norm_back(grad_n2, live.mid * live.inv2, live.inv2, live.gain_two)
    grad_mid = cot.astype(F32) + grad_mid_norm
    branch = grad_mid.astype(BF16)
    live.out_c = out_c
    del live.near, live.near_c, live.arriving
    live.hold(grad_gain_two=grad_gain_two, grad_mid=grad_mid, branch=branch, branch_rel=order_f(branch))

    arriving = lay.over_x(live.branch_rel)
    n2_xz_low = lay.over_z(live.n2_x_low)
    cot_yz = lay.over_y(live.cot_z)
    live.hold(arriving=arriving, n2_xz_low=n2_xz_low, cot_yz=cot_yz, out_sum=live.out + live.out_c.astype(F32),
              n2_y_c=lay.over_c(live.n2_y),
              n2_xy_c=lay.over_c(live.n2_xy))

    rows_each = live.n1_own.shape[0]
    n1_yc = lay.over_y(live.n1_away[rows_each:])
    cot_z_c, cot_xz_c = (lay.over_c(live.cot_z), lay.over_c(live.cot_xz))
    branch_x_rel = jnp.concatenate([live.arriving[:, half:], live.arriving[:, :half]], axis=1)
    both_rel = jnp.concatenate([live.branch_rel, branch_x_rel], 0)
    grad_mixed = dot_cols(both_rel[:, :half], live.out_left) + dot_cols(both_rel[:, half:], live.out_right)
    gy, bprod, blocal, back_summary = by_head(
        mixer_back_scan, live.flags,
        [(grad_mixed.reshape(2, tokens, half), False), (live.y_pre, False), (live.dg, False),
         (live.prods, False), (live.local_state, False), (live.state_in, False), (live.rates, False)],
        [shape3(BF16), shape3(F32), shape3(F32), summary_shape])
    del live.arriving, live.branch_rel, live.y_pre
    live.hold(gy=gy.reshape(two, half), bprod=bprod, blocal=blocal, scan=scan_start(back_summary, 2),
              branch_x_rel=branch_x_rel, n1_yc=n1_yc, cot_z_c=cot_z_c, cot_xz_c=cot_xz_c)

    n2_xyz = lay.over_x(live.n2_yz)
    own_cols = lambda value, which: half_of(value, which, quarter, 1)
    part_y = dot_cols(own_cols(live.gy, c), in_y) + dot_cols(own_cols(live.gy, 1 - c), live.wy_c)
    for bit in bits:
        come = lay.over_seq_bit(jnp.concatenate(live.scan[:2], axis=0), bit)
        live.scan = scan_join(lay, live.scan, come, bit, True)
        if bit == 1:
            live.cut()
            cot_xyz = lay.over_y(live.cot_xz)
            n2_z_c, n2_yz_c, cot_yz_c = (lay.over_c(live.n2_z), lay.over_c(live.n2_yz), lay.over_c(live.cot_yz))
    back_in = live.scan[3]
    del live.scan
    live.n1_yc = lay.over_c(live.n1_yc)
    live.hold(back_in=back_in, cot_xyz=cot_xyz, n2_xyz=n2_xyz, part_y=part_y, n2_z_c=n2_z_c, n2_yz_c=n2_yz_c,
              cot_yz_c=cot_yz_c)

    gip, gdp, gx_main, gx_tail, edge, vec_rows = by_head(
        mixer_backward, live.flags,
        [(live.bprod, False), (live.blocal, False), (live.back_in, False), (live.prods, False),
         (live.local_state, False), (live.state_in, False), (live.ig, False), (live.dg, False),
         (live.conv_low, False), (live.x_low, False), (live.halo, False), (live.gates, True),
         (live.vec, False), (live.rates, False)],
        [shape3(BF16), shape3(BF16), shape3(BF16), jax.ShapeDtypeStruct((2, 16, half), F32),
         jax.ShapeDtypeStruct((2, 8, half), F32), jax.ShapeDtypeStruct((8, half), F32)])
    for name in ("bprod", "blocal", "back_in", "prods", "local_state", "state_in", "ig", "dg", "x_low", "halo",
                 "gates", "vec", "rates", "flags"):
        delattr(live, name)
    live.hold(gip=gip, gdp=gdp, gx_main=gx_main, gx_tail=gx_tail, edge=edge, vec_rows=vec_rows)

    edge_next = lay.over_seq(live.edge, -1)
    mixed_x = lay.over_x(jnp.concatenate([live.mixed[1], live.mixed[0]], axis=0))
    n2_xz = jnp.concatenate([live.n2_xz_top, live.n2_xz_low], axis=0)
    n2_xz_c, n2_xyz_c, cot_xyz_c = (lay.over_c(n2_xz), lay.over_c(live.n2_xyz), lay.over_c(live.cot_xyz))
    live.n2s = [[live.n2, live.n2_x], [live.n2_y, live.n2_xy], [live.n2_z, n2_xz], [live.n2_yz, live.n2_xyz]]
    live.cots = [cot, live.cot_x, live.cot_y, live.cot_xy, live.cot_z, live.cot_xz, live.cot_yz, live.cot_xyz]
    n2_rows = rows_of_tokens(place, [p for group in live.n2s for p in group], half // 2, each)
    cot_rows = rows_of_tokens(place, live.cots, half // 2, each)
    del live.edge
    live.hold(edge_next=edge_next, n2_rows=n2_rows, cot_rows=cot_rows,
              n2s_c=[[live.n2_y_c, live.n2_xy_c], [live.n2_z_c, n2_xz_c], [live.n2_yz_c, n2_xyz_c]],
              cots_c=[live.cot_z_c, live.cot_xz_c, live.cot_yz_c, cot_xyz_c], mixed_x=mixed_x)

    gx_last = (live.gx_tail + jnp.pad(live.edge_next, ((0, 0), (8, 0), (0, 0)))).astype(BF16)
    gx = jnp.concatenate([live.gx_main[:, : tokens - 16], gx_last], axis=1).reshape(two, half)
    gx_o, gx_c = (own_cols(gx, c), own_cols(gx, 1 - c))
    part_n1 = live.part_y + dot_cols(gx_o, in_x) + dot_cols(gx_c, live.wx_c)
    del live.gx_main, live.gx_tail, live.edge_next, live.part_y
    live.hold(gx=gx, n1_near=part_n1[:tokens], n1_far=part_n1[tokens:].astype(BF16),
              n2_rows_c=lay.over_c(live.n2_rows), cot_rows_c=lay.over_c(live.cot_rows))

    cuts = sections_of(mlp_gate.shape[1])
    cuts = cuts[-1:] + cuts[:-1]

    def weight_piece(at, size):
        return mlp_weight_grads(
            place, [a + b for a, b in zip(live.n2s[1:], live.n2s_c)], live.gh_y,
            [live.cots[4:6] + live.cots_c[:2], live.cots[6:] + live.cots_c[2:]], live.acts,
            (live.n2_rows, live.n2_rows_c), (live.cot_rows, live.cot_rows_c), (mlp_gate, mlp_up, mlp_down),
            at, size, each)

    def piece_sum(own, rest):
        blocks = [own] + [rest[j * each : (j + 1) * each] for j in range(nz // 2 - 1)]
        bit = nz // 4
        while bit >= 1:
            gone = blocks[bit] if bit == 1 else jnp.concatenate(
                [b.astype(BF16) for b in blocks[bit : 2 * bit]], axis=0)
            come = lay.over_seq_bit(gone.astype(BF16), 2 * bit)
            blocks = [(blocks[j], come[j * each : (j + 1) * each]) for j in range(bit)]
            if bit > 1:
                blocks = [a.astype(F32) + b.astype(F32) for a, b in blocks]
            bit //= 2
        return blocks[0]

    arriving = lay.over_x(live.n1_far)
    gy_y = lay.over_y(live.gy)
    live.gy_c = lay.over_c(live.gy)
    live.hold(piece_a=weight_piece(*cuts[0]), arriving=arriving, gy_y=gy_y)

    grad_n1 = live.n1_near + live.arriving.astype(F32)
    scaled_one = inputs[0].astype(F32) * live.inv1
    grad_in_norm, grad_gain_one = norm_back(grad_n1, scaled_one, live.inv1, live.gain_one)
    input_grad = (live.grad_mid + grad_in_norm).astype(BF16)[None]
    rows_full = lax.dynamic_update_slice_in_dim(
        jnp.zeros((8, width), F32), live.vec_rows, x * half, 1)
    sums = jnp.concatenate([grad_gain_one[None], live.grad_gain_two[None], rows_full], axis=0)
    sums = sums + lay.over_c(sums)
    del live.n1_near, live.n1_far, live.arriving, live.vec_rows, live.grad_gain_two, live.grad_mid
    branch_far = half_of(order_f(live.branch_x_rel), x, half, 1)
    branch_near = half_of(live.branch, x, half, 1)
    del live.branch_x_rel
    live.hold(sums=sums, gy_yc=lay.over_c(live.gy_y), branch_two=jnp.concatenate([branch_near, branch_far], axis=0))

    def over_columns(value):
        split = value.reshape(2, own80, half)
        mine = lax.dynamic_index_in_dim(split, x, 0, keepdims=False)
        theirs = lay.over_x(lax.dynamic_index_in_dim(split, 1 - x, 0, keepdims=False))
        return jnp.where(x == 0, jnp.concatenate([mine, theirs], -1),
                         jnp.concatenate([theirs, mine], -1)).astype(F32)

    sums = live.sums + lay.over_x(live.sums)
    sums = sums + lay.over_seq_bit(sums, 1)
    branch_two_y = lay.over_y(live.branch_two)
    sum_a = piece_sum(*live.piece_a)
    n1_all = [live.n1_own, live.n1_c, live.n1_y, live.n1_yc]
    in_y_part = sum_of_dots(n1_all, [live.gy, live.gy_c, live.gy_y, live.gy_yc])
    gate_part = gate_weight_grad(
        live.conv_low.reshape(two, half), live.gip.reshape(two, half), live.gdp.reshape(two, half)
    ).reshape(2, nz, 2, own80, 2 * BLK)
    pick = lambda value, at, axis: lax.dynamic_index_in_dim(value, at, axis, keepdims=False)
    gate_part = pick(gate_part, c, 2) + lay.over_c(pick(gate_part, 1 - c, 2).astype(BF16)).astype(F32)
    gate_y = lay.over_y(pick(gate_part, 1 - y, 0).astype(BF16))
    mixed_own, sent, mixed_away = rows_by_device(
        at_yc, [[live.mixed[0], live.mixed[1]], [live.mixed_x[:tokens], live.mixed_x[tokens:]]], n1_starts, own80)
    del live.gy, live.gy_c, live.gy_y, live.gy_yc, live.mixed, live.mixed_x, live.conv_low, live.gip, live.gdp
    live.hold(in_y_part=in_y_part, sums=sums, sum_a=sum_a, branch_two_y=branch_two_y, gate_keep=pick(gate_part, y, 0), gate_y=gate_y,
              mixed_own=mixed_own, mixed_away=mixed_away, mixed_c=lay.over_c(sent),
              gx_c=lay.over_c(live.gx), branch_c=lay.over_c(live.branch_two))

    in_y_own, in_y_come = owner_parts(live.in_y_part.reshape(nz, 2 * own80, half))
    gx_y = lay.over_y(live.gx)
    mixed_y = lay.over_y(live.mixed_away)
    piece_b = weight_piece(*cuts[1])
    del live.piece_a, live.mixed_away
    del live.in_y_part
    live.hold(piece_b=piece_b, gx_y=gx_y, mixed_y=mixed_y, in_y_own=in_y_own, in_y_come=in_y_come)

    sum_b = piece_sum(*live.piece_b)
    in_x_part = sum_of_dots(n1_all, [live.gx, live.gx_c, live.gx_y, lay.over_c(live.gx_y)])
    out_part = sum_of_dots(
        [live.mixed_own, live.mixed_c, live.mixed_y[:rows_each], lay.over_c(live.mixed_y[rows_each:])],
        [live.branch_two, live.branch_c, live.branch_two_y, lay.over_c(live.branch_two_y)])
    gate_part = (live.gate_keep + live.gate_y.astype(F32)).astype(BF16)
    del live.piece_b, live.gate_keep, live.gate_y, live.mixed_own, live.mixed_c, live.mixed_y
    live.hold(in_x_part=jnp.concatenate(
        [in_x_part.reshape(nz, 2 * own80, half), gate_part.reshape(nz, own80 * 2 * BLK // half, half)], axis=1),
        out_part=out_part, sum_b=sum_b, in_y_total=total_of(live.in_y_own, live.in_y_come),
        out_far=live.out_sum[tokens:].astype(BF16))
    del live.in_y_own, live.in_y_come

    in_x_own, in_x_come = owner_parts(live.in_x_part)
    out_arriving = lay.over_x(live.out_far)
    sums = live.sums
    sums_z = lay.over_seq_bit(sums, 2)
    piece_c = weight_piece(*cuts[2])
    del live.in_x_part
    live.hold(piece_c=piece_c, in_x_own=in_x_own, in_x_come=in_x_come, out_arriving=out_arriving, sums=sums + sums_z)

    sum_c = piece_sum(*live.piece_c)
    sums = live.sums
    for bit in bits[2:]:
        sums = sums + lay.over_seq_bit(sums, bit)
    in_y_grad = over_columns(live.in_y_total)
    live.hold(sum_c=sum_c, sums=sums, in_x_total=total_of(live.in_x_own, live.in_x_come), in_y_grad=in_y_grad,
              output=(live.mid + live.out_sum[:tokens] + live.out_arriving.astype(F32)).astype(BF16)[None])

    out_own, out_come = owner_parts(live.out_part.reshape(nz, 2 * own80, half))
    in_x_grad = over_columns(live.in_x_total[: 2 * own80])
    mlp_grads = joined_columns([live.sum_b, live.sum_c, live.sum_a])
    live.hold(out_own=out_own, out_come=out_come, mlp_grads=mlp_grads, in_x_grad=in_x_grad)
    mlp_down_grad, mlp_gate_grad, mlp_up_grad = live.mlp_grads

    def final(z, y, x, c):
        at = ((x * 2 + y) * nz + z) * 2 + c
        s, f = (at // 4, at % 4)
        return (s // 2, s % 2, f // 2, f % 2)

    out_grad = over_columns(total_of(live.out_own, live.out_come))
    gate_grad = lay.send(live.in_x_total[2 * own80 :].reshape(own80, 2 * BLK), final).astype(F32)
    return (live.output, input_grad, live.sums, live.in_y_grad, live.in_x_grad, gate_grad, out_grad,
            mlp_gate_grad, mlp_up_grad, mlp_down_grad)


def solution(mesh):
    return jax.shard_map(
        local,
        mesh=mesh,
        in_specs=(
            P("fsdp", "seq", None),
            P("fsdp", "seq"),
            P(),
            P(),
            P(None, "fsdp"),
            P(None, "fsdp"),
            P(None, "fsdp"),
            P(None, "fsdp"),
            P(None, "fsdp"),
            P(None, "fsdp"),
            P(None, "fsdp"),
            P("fsdp", "seq", None),
        ),
        out_specs=(
            P("fsdp", "seq", None),
            P("fsdp", "seq", None),
            P(),
            P(("seq", "fsdp"), None),
            P(("seq", "fsdp"), None),
            P(("seq", "fsdp"), None),
            P(("seq", "fsdp"), None),
            P("seq", "fsdp"),
            P("seq", "fsdp"),
            P("seq", "fsdp"),
        ),
        check_vma=False,
    )
```

```python
import functools

import jax
import jax.numpy as jnp
from jax import lax
from jax.experimental import pallas as pl
from jax.experimental.pallas import tpu as pltpu
from jax.sharding import PartitionSpec as P

HEADS = 10
BLK = 256
FBLK = 64
EPS = 1e-06
ALL = ("seq", "fsdp")
F32 = jnp.float32
BF16 = jnp.bfloat16
GELU_C = 0.7978845608028654
GELU_A = 0.044715
VMEM_MAX = 60 * 1024 * 1024
ANY = pl.BlockSpec(memory_space=pl.ANY)


def work(us):
    scale = 1000 if us >= 10 else 0
    return pl.CostEstimate(flops=1 + us * scale * 900000, bytes_accessed=1 + us * scale * 2000, transcendentals=0)


def norm_scale(values):
    inverse = lax.rsqrt(jnp.mean(values * values, axis=-1, keepdims=True) + EPS)
    return (values * inverse, inverse)


def norm_back(grad_normed, scaled, inverse, gain_row):
    grad_gain = jnp.sum(grad_normed * scaled, axis=0)
    inner_term = grad_normed * gain_row
    grad_input = inverse * (
        inner_term - scaled * jnp.mean(inner_term * scaled, axis=-1, keepdims=True)
    )
    return (grad_input, grad_gain)


def gelu_pair(values):
    square = values * values
    t = jnp.tanh(values * (GELU_C + GELU_C * GELU_A * square))
    half = 0.5 + 0.5 * t
    slope = half * (1.0 + (1.0 - t) * values * (GELU_C + 3.0 * GELU_C * GELU_A * square))
    return (values * half, slope)


def dot(left, right):
    return jnp.dot(left, right, preferred_element_type=F32)


def dot_rows(left, right):
    return lax.dot_general(left, right, (((0,), (0,)), ((), ())), preferred_element_type=F32)


def dot_cols(left, right):
    return lax.dot_general(left, right, (((1,), (1,)), ((), ())), preferred_element_type=F32)


class Lay:
    def __init__(self):
        self.seq = lax.axis_size("seq")
        self.nz = self.seq // 2
        seq, fsdp = (lax.axis_index("seq"), lax.axis_index("fsdp"))
        self.z, self.y = (seq // 2, seq % 2)
        self.x, self.c = (fsdp // 2, fsdp % 2)
        self.seq_at = seq

    def pairs(self, target):
        found = []
        for s in range(self.seq):
            for f in range(4):
                z, y, x, c = (s // 2, s % 2, f // 2, f % 2)
                to = target(z, y, x, c)
                if to is not None:
                    found.append((s * 4 + f, ((to[0] * 2 + to[1]) * 2 + to[2]) * 2 + to[3]))
        return found

    def send(self, value, target):
        return lax.ppermute(value, ALL, self.pairs(target))

    def over_c(self, value):
        return self.send(value, lambda z, y, x, c: (z, y, x, 1 - c))

    def over_x(self, value):
        return self.send(value, lambda z, y, x, c: (z, y, 1 - x, c))

    def over_y(self, value):
        return self.send(value, lambda z, y, x, c: (z, 1 - y, x, c))

    def over_seq_bit(self, value, bit):
        def to(z, y, x, c):
            other = (2 * z + y) ^ bit
            return (other // 2, other % 2, x, c)

        return self.send(value, to)

    def over_z(self, value):
        return self.send(value, lambda z, y, x, c: (self.nz - 1 - z, y, x, c))

    def over_seq(self, value, by):
        def to(z, y, x, c):
            other = 2 * z + y + by
            return (other // 2, other % 2, x, c) if 0 <= other < self.seq else None

        return self.send(value, to)


def row_iota(rows, cols):
    return lax.broadcasted_iota(jnp.int32, (rows, cols), 0)


def token_masks(flags_ref, g, rows, cols):
    row = row_iota(rows, cols)
    block = row // FBLK
    offset = row % FBLK
    flagged = jnp.zeros((rows, cols), F32)
    for b in range(rows // FBLK):
        flagged = jnp.where(block == b, flags_ref[g, b], flagged)
    valid = [jnp.where(offset < lag, 1.0 - flagged, 1.0) for lag in range(4)]
    start = jnp.where(offset == 0, flagged, 0.0)
    return start, valid


def neg_expm1(v):
    series = 1.0 + v * (1.0 / 6.0)
    for n in (5.0, 4.0, 3.0, 2.0):
        series = 1.0 + v * (1.0 / n) * series
    return jnp.where(v > -0.25, -v * series, 1.0 - jnp.exp(v))


def shifted_inputs(xl_ref, halo_ref, g):
    ext = jnp.concatenate([halo_ref[g].astype(F32), xl_ref[g].astype(F32)], axis=0)
    pad = halo_ref.shape[1]
    return [ext[pad:] if k == 0 else pltpu.roll(ext, k, 0)[pad:] for k in range(4)]


def mixer_forward(flags_ref, xl_ref, halo_ref, gw_ref, vec_ref, rate_ref,
                  conv_ref, ig_ref, dg_ref, prod_ref, local_ref, sum_ref):
    groups, rows, cols = xl_ref.shape
    row = row_iota(rows, cols)
    for g in range(groups):
        start, valid = token_masks(flags_ref, g, rows, cols)
        lagged = shifted_inputs(xl_ref, halo_ref, g)
        conv = vec_ref[6:7, :] + jnp.zeros((rows, cols), F32)
        for k in range(4):
            conv = conv + vec_ref[2 + k : 3 + k, :] * lagged[k] * valid[k]
        conv_low = conv.astype(BF16)
        conv_ref[g] = conv_low
        prod = jnp.dot(conv_low, gw_ref[...], preferred_element_type=F32)
        ig = jax.nn.sigmoid(prod[:, :cols] + vec_ref[7:8, :])
        dg = jax.nn.sigmoid(prod[:, cols:] + vec_ref[8:9, :])
        ig_ref[g] = ig
        dg_ref[g] = dg
        keep = 1.0 - start
        log_decay = -8.0 * dg * rate_ref[0:1, :]
        p = jnp.exp(log_decay) * keep
        s = jnp.sqrt(keep * neg_expm1(2.0 * log_decay) + start) * ig * conv_low.astype(F32)
        step = 1
        while step < rows:
            inside = row >= step
            p_prev = jnp.where(inside, pltpu.roll(p, step, 0), 1.0)
            s_prev = jnp.where(inside, pltpu.roll(s, step, 0), 0.0)
            s = p * s_prev + s
            p = p * p_prev
            step *= 2
        prod_ref[g] = p
        local_ref[g] = s
        sum_ref[g : g + 1, :] = p[rows - 1 :, :]
        sum_ref[groups + g : groups + g + 1, :] = s[rows - 1 :, :]


def mixer_back_scan(flags_ref, gm_ref, y_ref, dg_ref, prod_ref, local_ref, sin_ref, rate_ref,
                    gy_ref, bprod_ref, blocal_ref, sum_ref):
    groups, rows, cols = gm_ref.shape
    row = row_iota(rows, cols)
    for g in range(groups):
        start, _ = token_masks(flags_ref, g, rows, cols)
        state = local_ref[g] + prod_ref[g] * sin_ref[g : g + 1, :]
        gelu, slope = gelu_pair(y_ref[g])
        gm = gm_ref[g]
        gy_ref[g] = (gm * state * slope).astype(BF16)
        decay = jnp.exp(-8.0 * dg_ref[g] * rate_ref[0:1, :]) * (1.0 - start)
        s = gm * gelu
        p = jnp.where(row == rows - 1, 1.0, pltpu.roll(decay, rows - 1, 0))
        step = 1
        while step < rows:
            inside = row < rows - step
            p_next = jnp.where(inside, pltpu.roll(p, rows - step, 0), 1.0)
            s_next = jnp.where(inside, pltpu.roll(s, rows - step, 0), 0.0)
            s = p * s_next + s
            p = p * p_next
            step *= 2
        bprod_ref[g] = p
        blocal_ref[g] = s
        sum_ref[g : g + 1, :] = decay[:1, :] * p[:1, :]
        sum_ref[groups + g : groups + g + 1, :] = decay[:1, :] * s[:1, :]


def mixer_backward(flags_ref, bprod_ref, blocal_ref, bin_ref, prod_ref, local_ref, sin_ref,
                   ig_ref, dg_ref, conv_ref, xl_ref, halo_ref, gw_ref, vec_ref, rate_ref,
                   gip_ref, gdp_ref, gx_ref, tail_ref, edge_ref, rows_ref):
    groups, rows, cols = xl_ref.shape
    row = row_iota(rows, cols)
    sums = [jnp.zeros((1, cols), F32) for _ in range(8)]
    tail = tail_ref.shape[1]
    pad = edge_ref.shape[1]
    for g in range(groups):
        start, valid = token_masks(flags_ref, g, rows, cols)
        keep = 1.0 - start
        rate = rate_ref[0:1, :]
        state_in = sin_ref[g : g + 1, :]
        state = local_ref[g] + prod_ref[g] * state_in
        prev = jnp.where(row == 0, state_in, pltpu.roll(state, 1, 0))
        sg = blocal_ref[g] + bprod_ref[g] * bin_ref[g : g + 1, :]
        ig, dg = (ig_ref[g], dg_ref[g])
        cf = conv_ref[g].astype(F32)
        log_decay = -8.0 * dg * rate
        decay = jnp.exp(log_decay) * keep
        scale = jnp.sqrt(keep * neg_expm1(2.0 * log_decay) + start)
        gscale = sg * ig * cf
        glog = sg * prev * decay - gscale * keep * jnp.exp(2.0 * log_decay) / scale
        gip = sg * scale * cf * ig * (1.0 - ig)
        gdp = -8.0 * rate * glog * dg * (1.0 - dg)
        gip_low, gdp_low = (gip.astype(BF16), gdp.astype(BF16))
        gip_ref[g] = gip_low
        gdp_ref[g] = gdp_low
        gconv = sg * scale * ig + lax.dot_general(
            jnp.concatenate([gip_low, gdp_low], axis=1), gw_ref[...],
            (((1,), (1,)), ((), ())), preferred_element_type=F32)
        lagged = shifted_inputs(xl_ref, halo_ref, g)
        spread = jnp.zeros((rows + pad, cols), F32)
        for k in range(4):
            masked = gconv * valid[k]
            sums[k] = sums[k] + jnp.sum(masked * lagged[k], axis=0, keepdims=True)
            full = jnp.concatenate(
                [jnp.zeros((pad, cols), F32), vec_ref[2 + k : 3 + k, :] * masked], axis=0)
            spread = spread + (full if k == 0 else pltpu.roll(full, rows + pad - k, 0))
        gx_ref[g] = spread[pad:].astype(BF16)
        tail_ref[g] = spread[pad + rows - tail :]
        edge_ref[g] = spread[:pad]
        sums[4] = sums[4] + jnp.sum(gconv, axis=0, keepdims=True)
        sums[5] = sums[5] + jnp.sum(gip, axis=0, keepdims=True)
        sums[6] = sums[6] + jnp.sum(gdp, axis=0, keepdims=True)
        sums[7] = sums[7] + jnp.sum(-8.0 * dg * glog, axis=0, keepdims=True) * rate_ref[1:2, :]
    rows_ref[...] = jnp.concatenate(sums, axis=0)


def by_head(body, flags, operands, outs):
    def spec(shape, rows_are_channels):
        if rows_are_channels:
            return pl.BlockSpec((BLK, shape[1]), lambda h: (h, 0))
        lead = shape[:-1]
        return pl.BlockSpec(lead + (BLK,), lambda h: (0,) * len(lead) + (h,))

    heads = outs[0].shape[-1] // BLK
    in_specs = [pl.BlockSpec(memory_space=pltpu.SMEM)]
    values = [flags]
    for value, is_gate in operands:
        in_specs.append(spec(value.shape, is_gate))
        values.append(value)
    size = sum(v.size * v.dtype.itemsize for v in values) + sum(
        o.size * o.dtype.itemsize for o in outs)
    return pl.pallas_call(
        body,
        grid=(heads,),
        in_specs=in_specs,
        out_specs=[spec(o.shape, False) for o in outs],
        out_shape=outs,
        compiler_params=pltpu.CompilerParams(vmem_limit_bytes=48 * 1024 * 1024),
        cost_estimate=work(7),
    )(*values)


def grad_hidden_of(parts, w_down):
    count = len(parts)
    rows, width = parts[0].shape
    total = count * rows
    ff = w_down.shape[1]

    def body(*refs):
        c_refs, (w_ref, out_ref, held, sem) = (refs[:count], refs[count:])

        @pl.when(pl.program_id(0) == 0)
        def _():
            copies = [
                pltpu.make_async_copy(c_refs[i], held.at[pl.ds(i * rows, rows)], sem.at[i])
                for i in range(count)
            ]
            for copy in copies:
                copy.start()
            for copy in copies:
                copy.wait()

        out_ref[...] = dot(held[...], w_ref[...])

    return pl.pallas_call(
        body,
        grid=(pl.cdiv(ff, BLK),),
        in_specs=[ANY] * count + [pl.BlockSpec((width, BLK), lambda j: (0, j))],
        out_specs=pl.BlockSpec((total, BLK), lambda j: (0, j)),
        out_shape=jax.ShapeDtypeStruct((total, ff), F32),
        scratch_shapes=[pltpu.VMEM((total, width), BF16), pltpu.SemaphoreType.DMA((count,))],
        compiler_params=pltpu.CompilerParams(vmem_limit_bytes=VMEM_MAX),
        cost_estimate=work(5 + total // 64),
    )(*parts, w_down)


def sections_of(total):
    found, at = ([], 0)
    while at < total:
        size = min(768, total - at)
        found.append((at, size))
        at += size
    return found


def mlp_forward(n2_parts, grad_hidden, w_gate, w_up):
    count = len(n2_parts)
    rows, width = n2_parts[0].shape
    total = count * rows
    ff = w_gate.shape[1]
    parts = sections_of(ff)
    widest = parts[0][1]
    far = total // 2

    def body(*refs):
        n_refs = refs[:count]
        gh_ref, wg_ref, wu_ref = refs[count : count + 3]
        hid_ref, gg_ref, gu_ref, far_ref, far_c_ref = refs[count + 3 : count + 8]
        n2_s, gh_s, wg_s, wu_s, acc, sem_n, sem_w = refs[count + 8 :]

        def load(k):
            at, size = parts[k]
            slot = k % 2
            return [
                pltpu.make_async_copy(
                    wg_ref.at[:, pl.ds(at, size)], wg_s.at[slot, :, pl.ds(0, size)], sem_w.at[slot, 0]),
                pltpu.make_async_copy(
                    wu_ref.at[:, pl.ds(at, size)], wu_s.at[slot, :, pl.ds(0, size)], sem_w.at[slot, 1]),
                pltpu.make_async_copy(
                    gh_ref.at[:, pl.ds(at, size)], gh_s.at[slot, :, pl.ds(0, size)], sem_w.at[slot, 2]),
            ]

        first = [
            pltpu.make_async_copy(n_refs[i], n2_s.at[pl.ds(i * rows, rows)], sem_n.at[i])
            for i in range(count)
        ]
        for copy in first + load(0):
            copy.start()
        for copy in first:
            copy.wait()
        for k, (at, size) in enumerate(parts):
            if k + 1 < len(parts):
                for copy in load(k + 1):
                    copy.start()
            for copy in load(k):
                copy.wait()
            slot = k % 2
            wg, wu = (wg_s[slot, :, :size], wu_s[slot, :, :size])
            gelu, slope = gelu_pair(dot(n2_s[...], wg))
            up = dot(n2_s[...], wu)
            gh = gh_s[slot, :, :size]
            hid_ref[:, at : at + size] = (gelu * up).astype(BF16)
            gg = (gh * up * slope).astype(BF16)
            gu = (gh * gelu).astype(BF16)
            gg_ref[:, at : at + size] = gg
            gu_ref[:, at : at + size] = gu

            def far_rows(v):
                return jnp.concatenate([v[rows : 2 * rows], v[3 * rows :]], axis=0)

            part = dot_cols(far_rows(gg), wg) + dot_cols(far_rows(gu), wu)
            if k == 0:
                acc[...] = part
            else:
                acc[...] += part
        far_ref[...] = acc[:rows]
        far_c_ref[...] = acc[rows:].astype(BF16)

    act = jax.ShapeDtypeStruct((total, ff), BF16)
    return pl.pallas_call(
        body,
        in_specs=[ANY] * (count + 3),
        out_shape=[act, act, act, jax.ShapeDtypeStruct((rows, width), F32),
                   jax.ShapeDtypeStruct((rows, width), BF16)],
        scratch_shapes=[
            pltpu.VMEM((total, width), BF16),
            pltpu.VMEM((2, total, widest), F32),
            pltpu.VMEM((2, width, widest), BF16),
            pltpu.VMEM((2, width, widest), BF16),
            pltpu.VMEM((far, width), F32),
            pltpu.SemaphoreType.DMA((count,)),
            pltpu.SemaphoreType.DMA((2, 3)),
        ],
        compiler_params=pltpu.CompilerParams(vmem_limit_bytes=VMEM_MAX),
        cost_estimate=work(23),
    )(*n2_parts, grad_hidden, w_gate, w_up)


def mlp_rest(hidden, grad_gate, grad_up, w_gate, w_up, w_down, rows):
    total, ff = hidden.shape
    width = w_gate.shape[0]
    block = 512

    def body(hid_ref, gg_ref, gu_ref, wg_ref, wu_ref, wd_ref, gn_ref, gn_c_ref, out_ref, out_c_ref):
        def near(ref):
            return jnp.concatenate([ref[:rows], ref[2 * rows : 3 * rows]], axis=0)

        gn = dot_cols(near(gg_ref), wg_ref[...]) + dot_cols(near(gu_ref), wu_ref[...])
        gn_ref[...] = gn[:rows]
        gn_c_ref[...] = gn[rows:].astype(BF16)
        out = dot_cols(hid_ref[...], wd_ref[...])
        out_ref[...] = out[: total // 2]
        out_c_ref[...] = out[total // 2 :].astype(BF16)

    whole = pl.BlockSpec((total, ff), lambda j: (0, 0))
    weight = pl.BlockSpec((block, ff), lambda j: (j, 0))
    tall = lambda n: pl.BlockSpec((n, block), lambda j: (0, j))
    shape = lambda n, dt: jax.ShapeDtypeStruct((n, width), dt)
    return pl.pallas_call(
        body,
        grid=(width // block,),
        in_specs=[whole] * 3 + [weight] * 3,
        out_specs=[tall(rows), tall(rows), tall(total // 2), tall(total // 2)],
        out_shape=[shape(rows, F32), shape(rows, BF16), shape(total // 2, F32), shape(total // 2, BF16)],
        compiler_params=pltpu.CompilerParams(vmem_limit_bytes=VMEM_MAX),
        cost_estimate=work(19),
    )(hidden, grad_gate, grad_up, w_gate, w_up, w_down)


def rows_of_tokens(place, parts, rows_out, each):
    tokens, width = parts[0].shape
    half = width // 2
    count = len(parts)

    def body(place_ref, *refs):
        out_ref, turned = (refs[count], refs[count + 1])
        for k in range(count):
            turned[...] = refs[k][...].T
            for i in range(rows_out // each):
                at = pl.multiple_of((2 * i + place_ref[2]) * each, 16)
                out_ref[i * each : (i + 1) * each, k * tokens : (k + 1) * tokens] = turned[pl.ds(at, each), :]

    return pl.pallas_call(
        body,
        grid_spec=pltpu.PrefetchScalarGridSpec(
            num_scalar_prefetch=1,
            grid=(1,),
            in_specs=[pl.BlockSpec((tokens, half), lambda i, place: (0, place[1]))] * count,
            out_specs=pl.BlockSpec((rows_out, count * tokens), lambda i, place: (0, 0)),
            scratch_shapes=[pltpu.VMEM((half, tokens), BF16)],
        ),
        out_shape=jax.ShapeDtypeStruct((rows_out, count * tokens), BF16),
        compiler_params=pltpu.CompilerParams(vmem_limit_bytes=VMEM_MAX),
        cost_estimate=work(5),
    )(place, *parts)


def mlp_weight_grads(place, n2_parts, first_hidden, cot_parts, acts, n2_rows, cot_rows, weights, at, size, each):
    groups = len(n2_parts)
    per = len(n2_parts[0])
    tokens, width = n2_parts[0][0].shape
    group = per * tokens
    both = group // 2
    rows = n2_rows[0].shape[0]
    flat_n = [p for g in n2_parts for p in g]
    flat_c = [p for g in cot_parts for p in g]
    total, total_c = (len(flat_n), len(flat_c))

    def body(place_ref, *refs):
        n_refs, c_refs, refs = (refs[:total], refs[total : total + total_c], refs[total + total_c :])
        gh_ref, wg_ref, wu_ref, wd_ref, hid_ref, gg_ref, gu_ref = refs[:7]
        n_rows, c_rows = (refs[7:11], refs[11:15])
        own_ref, rest_ref, n2_s, cot_s, acc, sem = refs[15:]

        def load(g, slot):
            found = []
            for i in range(per):
                to = pl.ds(i * tokens, tokens)
                found.append(pltpu.make_async_copy(n_refs[g * per + i], n2_s.at[slot, to], sem.at[slot, i]))
                if g > 0:
                    found.append(pltpu.make_async_copy(
                        c_refs[(g - 1) * per + i], cot_s.at[slot, to], sem.at[slot, per + i]))
            return found

        for copy in load(0, 0) + load(1, 1):
            copy.start()

        def add(g, act, fresh):
            fixed = isinstance(g, int)
            start = g * both if fixed else pl.multiple_of((g - 2) * both, both)
            for i, four in enumerate((c_rows, n_rows, n_rows)):
                mine, other = four[:2] if fixed else four[2:]
                part = dot(mine[:, pl.ds(start, both)], act[i][:both]) + dot(
                    other[:, pl.ds(start, both)], act[i][both:])
                if fresh:
                    acc[i] = part
                else:
                    acc[i] += part

        def recompute(g, slot, gh):
            gelu, slope = gelu_pair(dot(n2_s[slot], wg_ref[...]))
            up = dot(n2_s[slot], wu_ref[...])
            add(g + 1, ((gelu * up).astype(BF16), (gh * up * slope).astype(BF16), (gh * gelu).astype(BF16)), False)

        add(0, (hid_ref, gg_ref, gu_ref), True)
        for copy in load(0, 0):
            copy.wait()
        recompute(0, 0, gh_ref[...])

        def step(g, carry):
            slot = lax.rem(g, 2)
            for k in range(2, groups):
                @pl.when(g + 1 == k)
                def _():
                    for copy in load(k, k % 2):
                        copy.start()

            for copy in load(1, slot):
                copy.wait()
            recompute(g, slot, dot(cot_s[slot], wd_ref[...]))
            return carry

        lax.fori_loop(1, groups, step, 0)
        for j in range(rows // each):
            start = pl.multiple_of((place_ref[0] ^ j) * each, 8)
            for i in range(3):
                block = acc[i, pl.ds(start, each), :]
                if j == 0:
                    own_ref[:, i * size : (i + 1) * size] = block
                else:
                    rest_ref[(j - 1) * each : j * each, i * size : (i + 1) * size] = block.astype(BF16)

    index = at // size
    column = lambda n: pl.BlockSpec((n, size), lambda j, place: (0, index))
    whole = pl.BlockSpec(n2_rows[0].shape, lambda j, place: (0, 0))
    return pl.pallas_call(
        body,
        grid_spec=pltpu.PrefetchScalarGridSpec(
            num_scalar_prefetch=1,
            grid=(1,),
            in_specs=[ANY] * (total + total_c) + [column(group)] + [column(width)] * 3 + [column(group)] * 3
            + [whole] * 8,
            out_specs=[pl.BlockSpec((each, 3 * size), lambda j, place: (0, 0)),
                       pl.BlockSpec((rows - each, 3 * size), lambda j, place: (0, 0))],
            scratch_shapes=[
                pltpu.VMEM((2, group, width), BF16),
                pltpu.VMEM((2, group, width), BF16),
                pltpu.VMEM((3, rows, size), F32),
                pltpu.SemaphoreType.DMA((2, 2 * per)),
            ],
        ),
        out_shape=[jax.ShapeDtypeStruct((each, 3 * size), F32),
                   jax.ShapeDtypeStruct((rows - each, 3 * size), BF16)],
        compiler_params=pltpu.CompilerParams(vmem_limit_bytes=VMEM_MAX),
        cost_estimate=work(35 * size // 768),
    )(place, *flat_n, *flat_c, first_hidden, *weights, *acts, *n2_rows, *cot_rows)


def rows_by_device(place, parts, starts, block):
    columns, count = (len(parts), len(parts[0]))
    tokens, n = parts[0][0].shape
    rows = len(starts(0, 0)) * block
    flat = [block_of for column in parts for block_of in column]
    if block % 16:
        turned = [jnp.concatenate(column, axis=0).T for column in parts]
        turned = turned[0] if columns == 1 else jnp.where(
            place[2] == 0, jnp.concatenate(turned), jnp.concatenate(turned[::-1]))

        def taken(dc):
            return jnp.stack([
                jnp.concatenate([
                    lax.dynamic_slice_in_dim(turned, start, block, 0)
                    for start in starts(place[0] ^ dy, place[1] ^ dc)])
                for dy in range(2)])

        kept, sent = (taken(0), taken(1))
        return kept[0], sent[0], jnp.concatenate([kept[1], sent[1]], axis=0)

    def body(place_ref, *refs):
        keep_ref, send_ref, y_ref, turned = refs[len(flat):]
        for h in range(columns):
            base = 0 if columns == 1 else pl.multiple_of((place_ref[2] ^ h) * n, 16)
            for k in range(count):
                turned[pl.ds(base, n), k * tokens : (k + 1) * tokens] = refs[h * count + k][...].T
        for dy, dc, ref, at in ((0, 0, keep_ref, 0), (0, 1, send_ref, 0), (1, 0, y_ref, 0), (1, 1, y_ref, rows)):
            for i, start in enumerate(starts(place_ref[0] ^ dy, place_ref[1] ^ dc)):
                ref[at + i * block : at + (i + 1) * block, :] = turned[pl.ds(pl.multiple_of(start, 16), block), :]

    shape = (rows, count * tokens)
    return pl.pallas_call(
        body,
        grid_spec=pltpu.PrefetchScalarGridSpec(
            num_scalar_prefetch=1,
            grid=(1,),
            in_specs=[pl.BlockSpec((tokens, n), lambda i, place: (0, 0))] * len(flat),
            out_specs=[pl.BlockSpec((n_rows, shape[1]), lambda i, place: (0, 0)) for n_rows in (rows, rows, 2 * rows)],
            scratch_shapes=[pltpu.VMEM((columns * n, count * tokens), BF16)],
        ),
        out_shape=[jax.ShapeDtypeStruct((n_rows, shape[1]), BF16) for n_rows in (rows, rows, 2 * rows)],
        compiler_params=pltpu.CompilerParams(vmem_limit_bytes=VMEM_MAX),
        cost_estimate=work(3),
    )(place, *flat)


def joined_columns(pairs):
    rows = pairs[0][0].shape[0]
    widths = [a.shape[1] // 3 for a, _ in pairs]
    total = sum(widths)
    step = rows // 4 if rows % 64 == 0 else rows
    flat = [term for pair in pairs for term in pair]

    def body(*refs):
        for i in range(3):
            at = 0
            for k, n in enumerate(widths):
                span = slice(i * n, (i + 1) * n)
                refs[len(flat) + i][:, at : at + n] = refs[2 * k][:, span].astype(F32) + refs[
                    2 * k + 1][:, span].astype(F32)
                at += n

    return pl.pallas_call(
        body,
        grid=(rows // step,),
        in_specs=[pl.BlockSpec((step, term.shape[1]), lambda j: (j, 0)) for term in flat],
        out_specs=[pl.BlockSpec((step, total), lambda j: (j, 0))] * 3,
        out_shape=[jax.ShapeDtypeStruct((rows, total), F32)] * 3,
        compiler_params=pltpu.CompilerParams(vmem_limit_bytes=VMEM_MAX),
        cost_estimate=work(5),
    )(*flat)


def gate_weight_grad(place, conv, grad_in, grad_decay, block):
    tokens, n = conv.shape
    count = n // block // 2
    if block % 16:
        by_head = lambda v: v.reshape(tokens, n // BLK, BLK)
        blocks = jnp.einsum(
            "thi,thj->hij", by_head(conv), jnp.concatenate([by_head(grad_in), by_head(grad_decay)], 2),
            preferred_element_type=F32).reshape(count, 2, block, 2 * BLK)
        mine, theirs = [
            lax.dynamic_index_in_dim(blocks, core, 1, keepdims=False).reshape(n // 2, 2 * BLK)
            for core in (place[1], 1 - place[1])]
        return mine, theirs.astype(BF16)

    def body(place_ref, conv_ref, in_ref, decay_ref, keep_ref, away_ref, whole):
        for h in range(n // BLK):
            cols = slice(h * BLK, (h + 1) * BLK)
            turned = conv_ref[:, cols].T
            whole[cols, :BLK] = dot(turned, in_ref[:, cols])
            whole[cols, BLK:] = dot(turned, decay_ref[:, cols])
        for i in range(count):
            at = pl.multiple_of((2 * i + place_ref[1]) * block, 16)
            keep_ref[i * block : (i + 1) * block, :] = whole[pl.ds(at, block), :]
            at = pl.multiple_of((2 * i + 1 - place_ref[1]) * block, 16)
            away_ref[i * block : (i + 1) * block, :] = whole[pl.ds(at, block), :].astype(BF16)

    spec = pl.BlockSpec((tokens, n), lambda h, place: (0, 0))
    out = pl.BlockSpec((n // 2, 2 * BLK), lambda h, place: (0, 0))
    return pl.pallas_call(
        body,
        grid_spec=pltpu.PrefetchScalarGridSpec(
            num_scalar_prefetch=1,
            grid=(1,),
            in_specs=[spec] * 3,
            out_specs=[out, out],
            scratch_shapes=[pltpu.VMEM((n, 2 * BLK), F32)],
        ),
        out_shape=[jax.ShapeDtypeStruct((n // 2, 2 * BLK), F32), jax.ShapeDtypeStruct((n // 2, 2 * BLK), BF16)],
        compiler_params=pltpu.CompilerParams(vmem_limit_bytes=VMEM_MAX),
        cost_estimate=work(3),
    )(place, conv, grad_in, grad_decay)


def sum_of_dots(rows, values):
    count = len(rows)

    def body(*refs):
        total = dot(refs[0][...], refs[count][...])
        for k in range(1, count):
            total = total + dot(refs[k][...], refs[count + k][...])
        refs[2 * count][...] = total.astype(BF16)

    return pl.pallas_call(
        body,
        out_shape=jax.ShapeDtypeStruct((rows[0].shape[0], values[0].shape[1]), BF16),
        compiler_params=pltpu.CompilerParams(vmem_limit_bytes=VMEM_MAX),
        cost_estimate=work(5),
    )(*rows, *values)


def after(value, *others):
    return lax.optimization_barrier((value, others))[0]


class Live:
    def cut(self):
        names = sorted(vars(self))
        for name, value in zip(names, lax.optimization_barrier([getattr(self, n) for n in names])):
            setattr(self, name, value)

    def hold(self, **values):
        for name, value in values.items():
            setattr(self, name, value)
        self.cut()


def seq_bits(lay):
    found, bit = ([], 1)
    while bit < lay.seq:
        found.append(bit)
        bit *= 2
    return found


def scan_start(summary, groups):
    prod, state = (summary[:groups], summary[groups : 2 * groups])
    return (prod, state, jnp.ones_like(prod), jnp.zeros_like(state))


def scan_join(lay, held, other, bit, backward):
    prod, state, before_p, before_s = held
    groups = prod.shape[0]
    other_p, other_s = (other[:groups], other[groups:])
    is_later = (lay.seq_at & bit) != 0
    take = jnp.logical_not(is_later) if backward else is_later
    before_s = jnp.where(take, before_p * other_s + before_s, before_s)
    before_p = jnp.where(take, before_p * other_p, before_p)
    state = jnp.where(take, prod * other_s + state, other_p * state + other_s)
    return (prod * other_p, state, before_p, before_s)


def local(inputs, block_flags, decay_seed, vectors, in_y, in_x, gate_weight, out_proj,
          mlp_gate, mlp_up, mlp_down, cotangent):
    lay = Lay()
    nz, x, y, z, c = (lay.nz, lay.x, lay.y, lay.z, lay.c)
    tokens, width = inputs.shape[1:]
    half, quarter, two = (width // 2, width // 4, 2 * tokens)
    each = width // lay.seq
    own80 = each // 4
    bits = seq_bits(lay)
    place = jnp.stack([z % (nz // 2), lay.seq_at // nz, y]).astype(jnp.int32)
    at_yc = jnp.stack([y, c, x]).astype(jnp.int32)
    live = Live()

    def order_c(own, other, axis):
        return jnp.where(c == 0, jnp.concatenate([own, other], axis),
                         jnp.concatenate([other, own], axis))

    def order_f(rel):
        b = rel.shape[-1] // 4
        p = [rel[..., i * b : (i + 1) * b] for i in range(4)]
        by_c = jnp.where(c == 0, rel, jnp.concatenate([p[1], p[0], p[3], p[2]], -1))
        return jnp.where(x == 0, by_c, jnp.concatenate([by_c[..., 2 * b :], by_c[..., : 2 * b]], -1))

    def owner_parts(blocks):
        pick = lambda t: lax.dynamic_index_in_dim(blocks, t, 0, keepdims=False)
        come = [
            lay.send(pick((z + step) % nz), lambda z, y, x, c: ((z + step) % nz, y, x, c))
            for step in range(1, nz)
        ]
        return pick(z), come

    def total_of(own, come):
        total = own.astype(F32)
        for part in come:
            total = total + part.astype(F32)
        return total.astype(BF16)

    def half_of(value, which, n, axis):
        return lax.dynamic_slice_in_dim(value, which * n, n, axis)

    cot = cotangent[0]
    cut = tokens // 2
    gate_away, inputs, gate_weight, out_proj, vectors, decay_seed, block_flags = lax.optimization_barrier(
        (half_of(gate_weight, 1 - x, half, 0), inputs, gate_weight, out_proj, vectors, decay_seed, block_flags))
    halo_raw = lay.over_seq(inputs[0, tokens - 16 :], 1)
    gate_x = lay.over_x(gate_away)
    wx_c = lay.over_c(in_x)
    scaled_one, inverse_one = norm_scale(inputs[0].astype(F32))
    live.hold(n1=(scaled_one * vectors[0]).astype(BF16), inv1=inverse_one, halo_raw=halo_raw, cot_top=cot[:cut],
              cot_low=cot[cut:], wx_c=wx_c,
              params=(gate_weight, out_proj, vectors, decay_seed, block_flags))

    gate_weight, out_proj, vectors, decay_seed, block_flags = live.params
    n1_x = lay.over_x(live.n1)
    halo_own = (norm_scale(live.halo_raw.astype(F32))[0] * vectors[0]).astype(BF16)
    n_flags = block_flags.shape[1]
    flag_row = jnp.pad(block_flags.astype(BF16), ((0, 0), (0, width - n_flags)))
    halo_x = lay.over_x(jnp.concatenate([flag_row, halo_own[1:]], axis=0))
    gate_own = half_of(gate_weight, x, half, 0)
    gate_c = lay.over_c(gate_own)
    cot_z_top = lay.over_z(live.cot_top)
    base = -5.0 - decay_seed.astype(F32) + vectors[9]
    del live.params, live.halo_raw, live.cot_top
    live.hold(
        n1_x=n1_x, halo_x=halo_x, halo_own=halo_own, gate_x=gate_x, gate_c=gate_c, cot_z_top=cot_z_top,
        flags=jnp.concatenate([block_flags.astype(F32), halo_x[:1, :n_flags].astype(F32)], axis=0),
        gate_own=gate_own, out_away=half_of(out_proj, 2 * (1 - x) + y, quarter, 0),
        out_mine=half_of(out_proj, x, half, 0), vec=half_of(vectors, x, half, 1), gain_two=vectors[1],
        gain_one=vectors[0],
        rates=half_of(jnp.stack([jax.nn.softplus(base), jax.nn.sigmoid(base)]), x, half, 1))

    out_a = lay.over_x(live.out_away)
    cot_z_low, cot_y = (lay.over_z(live.cot_low), lay.over_y(after(cot, live.n1_x)))
    wy_c = lay.over_c(after(in_y, live.n1_x))
    gates = order_f(jnp.concatenate(
        [live.gate_own, live.gate_c, live.gate_x, lay.over_c(live.gate_x)], axis=1))
    normed = jnp.concatenate([live.n1, live.n1_x, live.halo_own, live.halo_x], axis=0)
    x_all = order_c(dot(normed, in_x).astype(BF16), dot(normed, live.wx_c).astype(BF16), 1)
    x_low = x_all[:two].reshape(2, tokens, half)
    halo = x_all[two:].reshape(2, 16, half)
    shape3 = lambda dt: jax.ShapeDtypeStruct((2, tokens, half), dt)
    summary_shape = jax.ShapeDtypeStruct((4, half), F32)
    conv_low, ig, dg, prods, local_state, summary = by_head(
        mixer_forward, live.flags,
        [(x_low, False), (halo, False), (gates, True), (live.vec, False), (live.rates, False)],
        [shape3(BF16), shape3(F32), shape3(F32), shape3(F32), shape3(F32), summary_shape])
    del live.gate_x, live.gate_own, live.gate_c, live.halo_own, live.halo_x
    live.hold(x_low=x_low, halo=halo, gates=gates, conv_low=conv_low, ig=ig, dg=dg, prods=prods,
              local_state=local_state, scan=scan_start(summary, 2), cot_y=cot_y, normed=normed[:two], wy_c=wy_c, out_a=out_a,
              cot_z_low=cot_z_low)
    del live.cot_low
    del live.out_away

    def n1_starts(at_y, at_c):
        return [((2 * i + at_y) * 4 + 2 * j + at_c) * own80 for i in range(nz) for j in range(2)]

    for bit in bits:
        come = lay.over_seq_bit(jnp.concatenate(live.scan[:2], axis=0), bit)
        live.scan = scan_join(lay, live.scan, come, bit, False)
        if bit == 1:
            live.cut()
            out_b = lay.over_y(live.out_a)
            out_c = lay.over_c(live.out_mine)
            cot_x = lay.over_x(after(cot, live.scan))
    out_x = jnp.where(y == 0, jnp.concatenate([live.out_a, out_b], 0), jnp.concatenate([out_b, live.out_a], 0))
    y_pre = order_c(dot(live.normed, in_y), dot(live.normed, live.wy_c), 1).reshape(2, tokens, half)
    n1_own, sent, n1_away = rows_by_device(at_yc, [[live.n1, live.n1_x]], n1_starts, own80)
    state_in = live.scan[3]
    del live.scan, live.out_a
    live.hold(state_in=state_in, y_pre=y_pre, out_left=jnp.concatenate([live.out_mine, out_c], axis=1),
              cot_z=jnp.concatenate([live.cot_z_top, live.cot_z_low], axis=0),
              out_x=out_x, cot_x=cot_x, n1_own=n1_own, n1_away=n1_away, n1_c=lay.over_c(sent))
    del live.out_mine, live.cot_z_top, live.cot_z_low

    n1_y = lay.over_y(live.n1_away[: live.n1_own.shape[0]])
    state = live.local_state + live.prods * live.state_in[:, None, :]
    mixed = (state * jax.nn.gelu(live.y_pre, approximate=True)).astype(BF16)
    mixed_two = mixed.reshape(two, half)
    out_right = jnp.concatenate([live.out_x, lay.over_c(live.out_x)], axis=1)
    part = jnp.concatenate([dot(mixed_two, live.out_left), dot(mixed_two, out_right)], axis=1)
    del live.out_x
    live.hold(mixed=mixed, part_own=part[:tokens], part_x=part[tokens:].astype(BF16), out_right=out_right, n1_y=n1_y)

    part_x = lay.over_x(live.part_x)
    cot_xy = lay.over_y(live.cot_x)
    gh_main = grad_hidden_of([cot, live.cot_x, lay.over_c(cot), lay.over_c(live.cot_x)], mlp_down)
    live.hold(part_x=part_x, gh_main=gh_main, cot_xy=cot_xy)

    swapped = jnp.concatenate([live.part_x[:, half:], live.part_x[:, :half]], axis=1)
    mid = inputs[0].astype(F32) + order_f(live.part_own + swapped.astype(F32))
    scaled_two, inverse_two = norm_scale(mid)
    del live.part_x, live.part_own
    live.hold(mid=mid, inv2=inverse_two, n2=(scaled_two * live.gain_two).astype(BF16))

    n2_x = lay.over_x(live.n2)
    n2_y = lay.over_y(live.n2)
    n2_z_top = lay.over_z(live.n2[:cut])
    n2_c = lay.over_c(live.n2)
    pair = [live.cot_y, live.cot_xy]
    gh_y = grad_hidden_of(pair + [lay.over_c(p) for p in pair], mlp_down)
    live.hold(n2_x=n2_x, n2_c=n2_c, n2_y=n2_y, n2_z_top=n2_z_top, gh_y=gh_y)

    live.hold(n2_xc=lay.over_c(live.n2_x), n2_low=live.n2[cut:], n2_x_top=live.n2_x[:cut], n2_x_low=live.n2_x[cut:])
    cot_xz = lay.over_x(live.cot_z)
    n2_xy = lay.over_y(live.n2_x)
    n2_z_low = lay.over_z(live.n2_low)
    hidden, grad_gate, grad_up, far, far_c = mlp_forward(
        [live.n2, live.n2_x, live.n2_c, live.n2_xc], live.gh_main, mlp_gate, mlp_up)
    del live.gh_main, live.n2_c
    live.hold(acts=(hidden, grad_gate, grad_up), far=far, far_c=far_c, cot_xz=cot_xz, n2_xy=n2_xy,
              n2_z_low=n2_z_low)
    live.hold(far=(live.far + lay.over_c(live.far_c).astype(F32)).astype(BF16),
              n2_z=jnp.concatenate([live.n2_z_top, live.n2_z_low], axis=0))

    arriving = lay.over_x(live.far)
    n2_yz, n2_y_c, n2_xy_c = (lay.over_y(live.n2_z), lay.over_c(live.n2_y), lay.over_c(live.n2_xy))
    n2_xz_top = lay.over_z(live.n2_x_top)
    near, near_c, out, out_c = mlp_rest(*live.acts, mlp_gate, mlp_up, mlp_down, tokens)
    del live.far, live.far_c, live.n2_z_top, live.n2_z_low
    live.hold(arriving=arriving, near=near, near_c=near_c, out=out, out_c=out_c, n2_yz=n2_yz, n2_y_c=n2_y_c, n2_xy_c=n2_xy_c, n2_xz_top=n2_xz_top)

    out_c = lay.over_c(live.out_c)
    grad_n2 = live.near + lay.over_c(live.near_c).astype(F32) + live.arriving.astype(F32)
    grad_mid_norm, grad_gain_two = norm_back(grad_n2, live.mid * live.inv2, live.inv2, live.gain_two)
    grad_mid = cot.astype(F32) + grad_mid_norm
    branch = grad_mid.astype(BF16)
    live.out_c = out_c
    del live.near, live.near_c, live.arriving
    live.hold(grad_gain_two=grad_gain_two, grad_mid=grad_mid, branch=branch, branch_rel=order_f(branch))

    arriving = lay.over_x(live.branch_rel)
    n2_xz_low = lay.over_z(live.n2_x_low)
    cot_yz = lay.over_y(live.cot_z)
    live.hold(arriving=arriving, n2_xz_low=n2_xz_low, cot_yz=cot_yz, out_sum=live.out + live.out_c.astype(F32),
              n2_z_c=lay.over_c(live.n2_z), cot_z_c=lay.over_c(live.cot_z),
              n2_rows_ahead=rows_of_tokens(place, [live.n2, live.n2_x, live.n2_y, live.n2_xy], half // 2, each),
              cot_rows_ahead=rows_of_tokens(place, [cot, live.cot_x, live.cot_y, live.cot_xy], half // 2, each))

    rows_each = live.n1_own.shape[0]
    n1_yc = lay.over_y(live.n1_away[rows_each:])
    cot_xz_c, n2_yz_c = (lay.over_c(live.cot_xz), lay.over_c(live.n2_yz))
    mixed_xa = lay.over_x(live.mixed[1])
    branch_x_rel = jnp.concatenate([live.arriving[:, half:], live.arriving[:, :half]], axis=1)
    both_rel = jnp.concatenate([live.branch_rel, branch_x_rel], 0)
    grad_mixed = dot_cols(both_rel[:, :half], live.out_left) + dot_cols(both_rel[:, half:], live.out_right)
    gy, bprod, blocal, back_summary = by_head(
        mixer_back_scan, live.flags,
        [(grad_mixed.reshape(2, tokens, half), False), (live.y_pre, False), (live.dg, False),
         (live.prods, False), (live.local_state, False), (live.state_in, False), (live.rates, False)],
        [shape3(BF16), shape3(F32), shape3(F32), summary_shape])
    del live.arriving, live.branch_rel, live.y_pre
    live.hold(gy=gy.reshape(two, half), bprod=bprod, blocal=blocal, scan=scan_start(back_summary, 2),
              branch_x_rel=branch_x_rel, n1_yc=n1_yc, cot_xz_c=cot_xz_c, n2_yz_c=n2_yz_c,
              mixed_xa=mixed_xa, mixed_b=live.mixed[0])

    n2_xyz = lay.over_x(live.n2_yz)
    own_cols = lambda value, which: half_of(value, which, quarter, 1)
    part_y = dot_cols(own_cols(live.gy, c), in_y) + dot_cols(own_cols(live.gy, 1 - c), live.wy_c)
    for bit in bits:
        come = lay.over_seq_bit(jnp.concatenate(live.scan[:2], axis=0), bit)
        live.scan = scan_join(lay, live.scan, come, bit, True)
        if bit == 1:
            live.cut()
            cot_xyz = lay.over_y(live.cot_xz)
            cot_yz_c = lay.over_c(live.cot_yz)
    back_in = live.scan[3]
    del live.scan
    live.hold(back_in=back_in, cot_xyz=cot_xyz, n2_xyz=n2_xyz, part_y=part_y, cot_yz_c=cot_yz_c)

    live.ahead_c = (lay.over_c(live.n2_rows_ahead), lay.over_c(live.cot_rows_ahead))
    live.n1_yc = lay.over_c(live.n1_yc)
    gip, gdp, gx_main, gx_tail, edge, vec_rows = by_head(
        mixer_backward, live.flags,
        [(live.bprod, False), (live.blocal, False), (live.back_in, False), (live.prods, False),
         (live.local_state, False), (live.state_in, False), (live.ig, False), (live.dg, False),
         (live.conv_low, False), (live.x_low, False), (live.halo, False), (live.gates, True),
         (live.vec, False), (live.rates, False)],
        [shape3(BF16), shape3(BF16), shape3(BF16), jax.ShapeDtypeStruct((2, 16, half), F32),
         jax.ShapeDtypeStruct((2, 8, half), F32), jax.ShapeDtypeStruct((8, half), F32)])
    for name in ("bprod", "blocal", "back_in", "prods", "local_state", "state_in", "ig", "dg", "x_low", "halo",
                 "gates", "vec", "rates", "flags"):
        delattr(live, name)
    live.hold(gip=gip, gdp=gdp, gx_main=gx_main, gx_tail=gx_tail, edge=edge, vec_rows=vec_rows)

    edge_next = lay.over_seq(live.edge, -1)
    mixed_xb = lay.over_x(live.mixed_b)
    n2_xz = jnp.concatenate([live.n2_xz_top, live.n2_xz_low], axis=0)
    n2_xz_c, n2_xyz_c, cot_xyz_c = (lay.over_c(n2_xz), lay.over_c(live.n2_xyz), lay.over_c(live.cot_xyz))
    live.n2s = [[live.n2, live.n2_x], [live.n2_y, live.n2_xy], [live.n2_z, n2_xz], [live.n2_yz, live.n2_xyz]]
    live.cots = [cot, live.cot_x, live.cot_y, live.cot_xy, live.cot_z, live.cot_xz, live.cot_yz, live.cot_xyz]
    n2_rows = rows_of_tokens(place, [p for group in live.n2s[2:] for p in group], half // 2, each)
    cot_rows = rows_of_tokens(place, live.cots[4:], half // 2, each)
    del live.edge
    live.hold(edge_next=edge_next, n2_rows=n2_rows, cot_rows=cot_rows,
              n2s_c=[[live.n2_y_c, live.n2_xy_c], [live.n2_z_c, n2_xz_c], [live.n2_yz_c, n2_xyz_c]],
              cots_c=[live.cot_z_c, live.cot_xz_c, live.cot_yz_c, cot_xyz_c], mixed_xb=mixed_xb)

    gx_last = (live.gx_tail + jnp.pad(live.edge_next, ((0, 0), (8, 0), (0, 0)))).astype(BF16)
    gx = jnp.concatenate([live.gx_main[:, : tokens - 16], gx_last], axis=1).reshape(two, half)
    gx_o, gx_c = (own_cols(gx, c), own_cols(gx, 1 - c))
    part_n1 = live.part_y + dot_cols(gx_o, in_x) + dot_cols(gx_c, live.wx_c)
    del live.gx_main, live.gx_tail, live.edge_next, live.part_y
    live.hold(gx=gx, n1_near=part_n1[:tokens], n1_far=part_n1[tokens:].astype(BF16),
              n2_rows_c=lay.over_c(live.n2_rows), cot_rows_c=lay.over_c(live.cot_rows))

    cuts = sections_of(mlp_gate.shape[1])
    cuts = cuts[-1:] + cuts[:-1]

    def weight_piece(at, size):
        return mlp_weight_grads(
            place, [a + b for a, b in zip(live.n2s[1:], live.n2s_c)], live.gh_y,
            [live.cots[4:6] + live.cots_c[:2], live.cots[6:] + live.cots_c[2:]], live.acts,
            (live.n2_rows_ahead, live.ahead_c[0], live.n2_rows, live.n2_rows_c),
            (live.cot_rows_ahead, live.ahead_c[1], live.cot_rows, live.cot_rows_c),
            (mlp_gate, mlp_up, mlp_down), at, size, each)

    def piece_sum(own, rest):
        blocks = [own] + [rest[j * each : (j + 1) * each] for j in range(nz // 2 - 1)]
        bit = nz // 4
        while bit >= 1:
            gone = blocks[bit] if bit == 1 else jnp.concatenate(
                [b.astype(BF16) for b in blocks[bit : 2 * bit]], axis=0)
            come = lay.over_seq_bit(gone.astype(BF16), 2 * bit)
            blocks = [(blocks[j], come[j * each : (j + 1) * each]) for j in range(bit)]
            if bit > 1:
                blocks = [a.astype(F32) + b.astype(F32) for a, b in blocks]
            bit //= 2
        return blocks[0]

    arriving = lay.over_x(live.n1_far)
    gy_y = lay.over_y(live.gy)
    live.gy_c = lay.over_c(live.gy)
    live.hold(piece_a=weight_piece(*cuts[0]), arriving=arriving, gy_y=gy_y)

    grad_n1 = live.n1_near + live.arriving.astype(F32)
    scaled_one = inputs[0].astype(F32) * live.inv1
    grad_in_norm, grad_gain_one = norm_back(grad_n1, scaled_one, live.inv1, live.gain_one)
    input_grad = (live.grad_mid + grad_in_norm).astype(BF16)[None]
    rows_full = lax.dynamic_update_slice_in_dim(
        jnp.zeros((8, width), F32), live.vec_rows, x * half, 1)
    sums = jnp.concatenate([grad_gain_one[None], live.grad_gain_two[None], rows_full], axis=0)
    sums = sums + lay.over_c(sums)
    del live.n1_near, live.n1_far, live.arriving, live.vec_rows, live.grad_gain_two, live.grad_mid
    branch_far = half_of(order_f(live.branch_x_rel), x, half, 1)
    branch_near = half_of(live.branch, x, half, 1)
    del live.branch_x_rel
    live.hold(sums=sums, gy_yc=lay.over_c(live.gy_y), branch_two=jnp.concatenate([branch_near, branch_far], axis=0))

    def over_columns(value):
        split = value.reshape(2, own80, half)
        mine = lax.dynamic_index_in_dim(split, x, 0, keepdims=False)
        theirs = lay.over_x(lax.dynamic_index_in_dim(split, 1 - x, 0, keepdims=False))
        return jnp.where(x == 0, jnp.concatenate([mine, theirs], -1),
                         jnp.concatenate([theirs, mine], -1)).astype(F32)

    sums = live.sums + lay.over_x(live.sums)
    branch_two_y = lay.over_y(live.branch_two)
    sum_a = piece_sum(*live.piece_a)
    n1_all = [live.n1_own, live.n1_c, live.n1_y, live.n1_yc]
    in_y_part = sum_of_dots(n1_all, [live.gy, live.gy_c, live.gy_y, live.gy_yc])
    gate_part, gate_away = gate_weight_grad(
        at_yc, live.conv_low.reshape(two, half), live.gip.reshape(two, half), live.gdp.reshape(two, half), own80)
    gate_part = (gate_part + lay.over_c(gate_away).astype(F32)).reshape(2, nz, own80, 2 * BLK)
    pick = lambda value, at, axis: lax.dynamic_index_in_dim(value, at, axis, keepdims=False)
    gate_y = lay.over_y(pick(gate_part, 1 - y, 0).astype(BF16))
    mixed_own, sent, mixed_away = rows_by_device(
        at_yc, [[live.mixed[0], live.mixed[1]], [live.mixed_xa, live.mixed_xb]], n1_starts, own80)
    del live.gy, live.gy_c, live.gy_y, live.gy_yc, live.mixed, live.mixed_xa, live.mixed_xb, live.conv_low, live.gip, live.gdp
    live.hold(in_y_part=in_y_part, sums=sums, sum_a=sum_a, branch_two_y=branch_two_y, gate_keep=pick(gate_part, y, 0), gate_y=gate_y,
              mixed_own=mixed_own, mixed_away=mixed_away, mixed_c=lay.over_c(sent),
              gx_c=lay.over_c(live.gx), branch_c=lay.over_c(live.branch_two))

    in_y_own, in_y_come = owner_parts(live.in_y_part.reshape(nz, 2 * own80, half))
    gx_y = lay.over_y(live.gx)
    mixed_y = lay.over_y(live.mixed_away)
    piece_b = weight_piece(*cuts[1])
    del live.piece_a, live.mixed_away
    del live.in_y_part
    live.hold(piece_b=piece_b, gx_y=gx_y, mixed_y=mixed_y, in_y_own=in_y_own, in_y_come=in_y_come)

    sum_b = piece_sum(*live.piece_b)
    sums = live.sums
    for bit in bits[:1]:
        sums = sums + lay.over_seq_bit(sums, bit)
    in_x_part = sum_of_dots(n1_all, [live.gx, live.gx_c, live.gx_y, lay.over_c(live.gx_y)])
    out_part = sum_of_dots(
        [live.mixed_own, live.mixed_c, live.mixed_y[:rows_each], lay.over_c(live.mixed_y[rows_each:])],
        [live.branch_two, live.branch_c, live.branch_two_y, lay.over_c(live.branch_two_y)])
    gate_part = (live.gate_keep + live.gate_y.astype(F32)).astype(BF16)
    del live.piece_b, live.gate_keep, live.gate_y, live.mixed_own, live.mixed_c, live.mixed_y
    live.hold(in_x_part=jnp.concatenate(
        [in_x_part.reshape(nz, 2 * own80, half), gate_part.reshape(nz, own80 * 2 * BLK // half, half)], axis=1),
        out_part=out_part, sum_b=sum_b, sums=sums, in_y_total=total_of(live.in_y_own, live.in_y_come),
        out_far=live.out_sum[tokens:].astype(BF16))
    del live.in_y_own, live.in_y_come

    in_x_own, in_x_come = owner_parts(live.in_x_part)
    out_own, out_come = owner_parts(live.out_part.reshape(nz, 2 * own80, half))
    out_arriving = lay.over_x(live.out_far)
    piece_c = weight_piece(*cuts[2])
    del live.in_x_part
    live.hold(piece_c=piece_c, in_x_own=in_x_own, in_x_come=in_x_come, out_arriving=out_arriving,
              out_come=out_come[:1])

    sum_c = piece_sum(*live.piece_c)
    out_own, out_come = owner_parts(live.out_part.reshape(nz, 2 * own80, half))
    in_x_own, in_x_come, in_y_total = after((live.in_x_own, live.in_x_come, live.in_y_total), out_come[1])
    in_x_total = total_of(in_x_own, in_x_come)
    sums_z = lay.over_seq_bit(live.sums, 2)
    live.hold(sum_c=sum_c, sums_z=sums_z, out_total=total_of(out_own, live.out_come + out_come[1:]),
              in_y_grad=over_columns(in_y_total), in_x_grad=over_columns(in_x_total[: 2 * own80]),
              gate_total=in_x_total[2 * own80 :].reshape(own80, 2 * BLK),
              output=(live.mid + after(live.out_sum, out_come[1])[:tokens] + live.out_arriving.astype(F32)
                      ).astype(BF16)[None])

    sums = live.sums + live.sums_z
    for bit in bits[2:]:
        sums = sums + lay.over_seq_bit(sums, bit)
    mlp_down_grad, mlp_gate_grad, mlp_up_grad = joined_columns([live.sum_b, live.sum_c, live.sum_a])

    def final(z, y, x, c):
        at = ((x * 2 + y) * nz + z) * 2 + c
        s, f = (at // 4, at % 4)
        return (s // 2, s % 2, f // 2, f % 2)

    out_grad = over_columns(live.out_total)
    gate_grad = lay.send(live.gate_total, final).astype(F32)
    return (live.output, input_grad, sums, live.in_y_grad, live.in_x_grad, gate_grad, out_grad,
            mlp_gate_grad, mlp_up_grad, mlp_down_grad)


def solution(mesh):
    return jax.shard_map(
        local,
        mesh=mesh,
        in_specs=(
            P("fsdp", "seq", None),
            P("fsdp", "seq"),
            P(),
            P(),
            P(None, "fsdp"),
            P(None, "fsdp"),
            P(None, "fsdp"),
            P(None, "fsdp"),
            P(None, "fsdp"),
            P(None, "fsdp"),
            P(None, "fsdp"),
            P("fsdp", "seq", None),
        ),
        out_specs=(
            P("fsdp", "seq", None),
            P("fsdp", "seq", None),
            P(),
            P(("seq", "fsdp"), None),
            P(("seq", "fsdp"), None),
            P(("seq", "fsdp"), None),
            P(("seq", "fsdp"), None),
            P("seq", "fsdp"),
            P("seq", "fsdp"),
            P("seq", "fsdp"),
        ),
        check_vma=False,
    )
```

```python
import functools

import jax
import jax.numpy as jnp
from jax import lax
from jax.experimental import pallas as pl
from jax.experimental.pallas import tpu as pltpu
from jax.sharding import PartitionSpec as P

HEADS = 10
BLK = 256
FBLK = 64
EPS = 1e-06
ALL = ("seq", "fsdp")
F32 = jnp.float32
BF16 = jnp.bfloat16
GELU_C = 0.7978845608028654
GELU_A = 0.044715
VMEM_MAX = 60 * 1024 * 1024
ANY = pl.BlockSpec(memory_space=pl.ANY)


def work(us):
    scale = 1000 if us >= 10 else 0
    return pl.CostEstimate(flops=1 + us * scale * 900000, bytes_accessed=1 + us * scale * 2000, transcendentals=0)


def norm_scale(values):
    inverse = lax.rsqrt(jnp.mean(values * values, axis=-1, keepdims=True) + EPS)
    return (values * inverse, inverse)


def norm_back(grad_normed, scaled, inverse, gain_row):
    grad_gain = jnp.sum(grad_normed * scaled, axis=0)
    inner_term = grad_normed * gain_row
    grad_input = inverse * (
        inner_term - scaled * jnp.mean(inner_term * scaled, axis=-1, keepdims=True)
    )
    return (grad_input, grad_gain)


def gelu_pair(values):
    square = values * values
    t = jnp.tanh(values * (GELU_C + GELU_C * GELU_A * square))
    half = 0.5 + 0.5 * t
    slope = half * (1.0 + (1.0 - t) * values * (GELU_C + 3.0 * GELU_C * GELU_A * square))
    return (values * half, slope)


def dot(left, right):
    return jnp.dot(left, right, preferred_element_type=F32)


def dot_rows(left, right):
    return lax.dot_general(left, right, (((0,), (0,)), ((), ())), preferred_element_type=F32)


def dot_cols(left, right):
    return lax.dot_general(left, right, (((1,), (1,)), ((), ())), preferred_element_type=F32)


class Lay:
    def __init__(self):
        self.seq = lax.axis_size("seq")
        self.nz = self.seq // 2
        seq, fsdp = (lax.axis_index("seq"), lax.axis_index("fsdp"))
        self.z, self.y = (seq // 2, seq % 2)
        self.x, self.c = (fsdp // 2, fsdp % 2)
        self.seq_at = seq

    def pairs(self, target):
        found = []
        for s in range(self.seq):
            for f in range(4):
                z, y, x, c = (s // 2, s % 2, f // 2, f % 2)
                to = target(z, y, x, c)
                if to is not None:
                    found.append((s * 4 + f, ((to[0] * 2 + to[1]) * 2 + to[2]) * 2 + to[3]))
        return found

    def send(self, value, target):
        return lax.ppermute(value, ALL, self.pairs(target))

    def over_c(self, value):
        return self.send(value, lambda z, y, x, c: (z, y, x, 1 - c))

    def over_x(self, value):
        return self.send(value, lambda z, y, x, c: (z, y, 1 - x, c))

    def over_y(self, value):
        return self.send(value, lambda z, y, x, c: (z, 1 - y, x, c))

    def over_seq_bit(self, value, bit):
        def to(z, y, x, c):
            other = (2 * z + y) ^ bit
            return (other // 2, other % 2, x, c)

        return self.send(value, to)

    def over_z(self, value):
        return self.send(value, lambda z, y, x, c: (self.nz - 1 - z, y, x, c))

    def over_seq(self, value, by):
        def to(z, y, x, c):
            other = 2 * z + y + by
            return (other // 2, other % 2, x, c) if 0 <= other < self.seq else None

        return self.send(value, to)


def row_iota(rows, cols):
    return lax.broadcasted_iota(jnp.int32, (rows, cols), 0)


def token_masks(flags_ref, g, rows, cols):
    row = row_iota(rows, cols)
    block = row // FBLK
    offset = row % FBLK
    flagged = jnp.zeros((rows, cols), F32)
    for b in range(rows // FBLK):
        flagged = jnp.where(block == b, flags_ref[g, b], flagged)
    valid = [jnp.where(offset < lag, 1.0 - flagged, 1.0) for lag in range(4)]
    start = jnp.where(offset == 0, flagged, 0.0)
    return start, valid


def neg_expm1(v):
    series = 1.0 + v * (1.0 / 6.0)
    for n in (5.0, 4.0, 3.0, 2.0):
        series = 1.0 + v * (1.0 / n) * series
    return jnp.where(v > -0.25, -v * series, 1.0 - jnp.exp(v))


def shifted_inputs(xl_ref, halo_ref, g):
    ext = jnp.concatenate([halo_ref[g].astype(F32), xl_ref[g].astype(F32)], axis=0)
    pad = halo_ref.shape[1]
    return [ext[pad:] if k == 0 else pltpu.roll(ext, k, 0)[pad:] for k in range(4)]


def mixer_forward(flags_ref, xl_ref, halo_ref, gw_ref, vec_ref, rate_ref,
                  conv_ref, ig_ref, dg_ref, prod_ref, local_ref, sum_ref):
    groups, rows, cols = xl_ref.shape
    row = row_iota(rows, cols)
    for g in range(groups):
        start, valid = token_masks(flags_ref, g, rows, cols)
        lagged = shifted_inputs(xl_ref, halo_ref, g)
        conv = vec_ref[6:7, :] + jnp.zeros((rows, cols), F32)
        for k in range(4):
            conv = conv + vec_ref[2 + k : 3 + k, :] * lagged[k] * valid[k]
        conv_low = conv.astype(BF16)
        conv_ref[g] = conv_low
        prod = jnp.dot(conv_low, gw_ref[...], preferred_element_type=F32)
        ig = jax.nn.sigmoid(prod[:, :cols] + vec_ref[7:8, :])
        dg = jax.nn.sigmoid(prod[:, cols:] + vec_ref[8:9, :])
        ig_ref[g] = ig
        dg_ref[g] = dg
        keep = 1.0 - start
        log_decay = -8.0 * dg * rate_ref[0:1, :]
        p = jnp.exp(log_decay) * keep
        s = jnp.sqrt(keep * neg_expm1(2.0 * log_decay) + start) * ig * conv_low.astype(F32)
        step = 1
        while step < rows:
            inside = row >= step
            p_prev = jnp.where(inside, pltpu.roll(p, step, 0), 1.0)
            s_prev = jnp.where(inside, pltpu.roll(s, step, 0), 0.0)
            s = p * s_prev + s
            p = p * p_prev
            step *= 2
        prod_ref[g] = p
        local_ref[g] = s
        sum_ref[g : g + 1, :] = p[rows - 1 :, :]
        sum_ref[groups + g : groups + g + 1, :] = s[rows - 1 :, :]


def mixer_back_scan(flags_ref, gm_ref, y_ref, dg_ref, prod_ref, local_ref, sin_ref, rate_ref,
                    gy_ref, bprod_ref, blocal_ref, sum_ref):
    groups, rows, cols = gm_ref.shape
    row = row_iota(rows, cols)
    for g in range(groups):
        start, _ = token_masks(flags_ref, g, rows, cols)
        state = local_ref[g] + prod_ref[g] * sin_ref[g : g + 1, :]
        gelu, slope = gelu_pair(y_ref[g])
        gm = gm_ref[g]
        gy_ref[g] = (gm * state * slope).astype(BF16)
        decay = jnp.exp(-8.0 * dg_ref[g] * rate_ref[0:1, :]) * (1.0 - start)
        s = gm * gelu
        p = jnp.where(row == rows - 1, 1.0, pltpu.roll(decay, rows - 1, 0))
        step = 1
        while step < rows:
            inside = row < rows - step
            p_next = jnp.where(inside, pltpu.roll(p, rows - step, 0), 1.0)
            s_next = jnp.where(inside, pltpu.roll(s, rows - step, 0), 0.0)
            s = p * s_next + s
            p = p * p_next
            step *= 2
        bprod_ref[g] = p
        blocal_ref[g] = s
        sum_ref[g : g + 1, :] = decay[:1, :] * p[:1, :]
        sum_ref[groups + g : groups + g + 1, :] = decay[:1, :] * s[:1, :]


def mixer_backward(flags_ref, bprod_ref, blocal_ref, bin_ref, prod_ref, local_ref, sin_ref,
                   ig_ref, dg_ref, conv_ref, xl_ref, halo_ref, gw_ref, vec_ref, rate_ref,
                   gip_ref, gdp_ref, gx_ref, tail_ref, edge_ref, rows_ref):
    groups, rows, cols = xl_ref.shape
    row = row_iota(rows, cols)
    sums = [jnp.zeros((1, cols), F32) for _ in range(8)]
    tail = tail_ref.shape[1]
    pad = edge_ref.shape[1]
    for g in range(groups):
        start, valid = token_masks(flags_ref, g, rows, cols)
        keep = 1.0 - start
        rate = rate_ref[0:1, :]
        state_in = sin_ref[g : g + 1, :]
        state = local_ref[g] + prod_ref[g] * state_in
        prev = jnp.where(row == 0, state_in, pltpu.roll(state, 1, 0))
        sg = blocal_ref[g] + bprod_ref[g] * bin_ref[g : g + 1, :]
        ig, dg = (ig_ref[g], dg_ref[g])
        cf = conv_ref[g].astype(F32)
        log_decay = -8.0 * dg * rate
        decay = jnp.exp(log_decay) * keep
        scale = jnp.sqrt(keep * neg_expm1(2.0 * log_decay) + start)
        gscale = sg * ig * cf
        glog = sg * prev * decay - gscale * keep * jnp.exp(2.0 * log_decay) / scale
        gip = sg * scale * cf * ig * (1.0 - ig)
        gdp = -8.0 * rate * glog * dg * (1.0 - dg)
        gip_low, gdp_low = (gip.astype(BF16), gdp.astype(BF16))
        gip_ref[g] = gip_low
        gdp_ref[g] = gdp_low
        gconv = sg * scale * ig + lax.dot_general(
            jnp.concatenate([gip_low, gdp_low], axis=1), gw_ref[...],
            (((1,), (1,)), ((), ())), preferred_element_type=F32)
        lagged = shifted_inputs(xl_ref, halo_ref, g)
        spread = jnp.zeros((rows + pad, cols), F32)
        for k in range(4):
            masked = gconv * valid[k]
            sums[k] = sums[k] + jnp.sum(masked * lagged[k], axis=0, keepdims=True)
            full = jnp.concatenate(
                [jnp.zeros((pad, cols), F32), vec_ref[2 + k : 3 + k, :] * masked], axis=0)
            spread = spread + (full if k == 0 else pltpu.roll(full, rows + pad - k, 0))
        gx_ref[g] = spread[pad:].astype(BF16)
        tail_ref[g] = spread[pad + rows - tail :]
        edge_ref[g] = spread[:pad]
        sums[4] = sums[4] + jnp.sum(gconv, axis=0, keepdims=True)
        sums[5] = sums[5] + jnp.sum(gip, axis=0, keepdims=True)
        sums[6] = sums[6] + jnp.sum(gdp, axis=0, keepdims=True)
        sums[7] = sums[7] + jnp.sum(-8.0 * dg * glog, axis=0, keepdims=True) * rate_ref[1:2, :]
    rows_ref[...] = jnp.concatenate(sums, axis=0)


def by_head(body, flags, operands, outs):
    def spec(shape, rows_are_channels):
        if rows_are_channels:
            return pl.BlockSpec((BLK, shape[1]), lambda h: (h, 0))
        lead = shape[:-1]
        return pl.BlockSpec(lead + (BLK,), lambda h: (0,) * len(lead) + (h,))

    heads = outs[0].shape[-1] // BLK
    in_specs = [pl.BlockSpec(memory_space=pltpu.SMEM)]
    values = [flags]
    for value, is_gate in operands:
        in_specs.append(spec(value.shape, is_gate))
        values.append(value)
    size = sum(v.size * v.dtype.itemsize for v in values) + sum(
        o.size * o.dtype.itemsize for o in outs)
    return pl.pallas_call(
        body,
        grid=(heads,),
        in_specs=in_specs,
        out_specs=[spec(o.shape, False) for o in outs],
        out_shape=outs,
        compiler_params=pltpu.CompilerParams(vmem_limit_bytes=48 * 1024 * 1024),
        cost_estimate=work(7),
    )(*values)


def grad_hidden_of(parts, w_down):
    count = len(parts)
    rows, width = parts[0].shape
    total = count * rows
    ff = w_down.shape[1]

    def body(*refs):
        c_refs, (w_ref, out_ref, held, sem) = (refs[:count], refs[count:])

        @pl.when(pl.program_id(0) == 0)
        def _():
            copies = [
                pltpu.make_async_copy(c_refs[i], held.at[pl.ds(i * rows, rows)], sem.at[i])
                for i in range(count)
            ]
            for copy in copies:
                copy.start()
            for copy in copies:
                copy.wait()

        out_ref[...] = dot(held[...], w_ref[...])

    return pl.pallas_call(
        body,
        grid=(pl.cdiv(ff, BLK),),
        in_specs=[ANY] * count + [pl.BlockSpec((width, BLK), lambda j: (0, j))],
        out_specs=pl.BlockSpec((total, BLK), lambda j: (0, j)),
        out_shape=jax.ShapeDtypeStruct((total, ff), F32),
        scratch_shapes=[pltpu.VMEM((total, width), BF16), pltpu.SemaphoreType.DMA((count,))],
        compiler_params=pltpu.CompilerParams(vmem_limit_bytes=VMEM_MAX),
        cost_estimate=work(5 + total // 64),
    )(*parts, w_down)


def sections_of(total):
    found, at = ([], 0)
    while at < total:
        size = min(768, total - at)
        found.append((at, size))
        at += size
    return found


def mlp_forward(n2_parts, grad_hidden, w_gate, w_up):
    count = len(n2_parts)
    rows, width = n2_parts[0].shape
    total = count * rows
    ff = w_gate.shape[1]
    parts = sections_of(ff)
    widest = parts[0][1]
    far = total // 2

    def body(*refs):
        n_refs = refs[:count]
        gh_ref, wg_ref, wu_ref = refs[count : count + 3]
        hid_ref, gg_ref, gu_ref, far_ref, far_c_ref = refs[count + 3 : count + 8]
        n2_s, gh_s, wg_s, wu_s, acc, sem_n, sem_w = refs[count + 8 :]

        def load(k):
            at, size = parts[k]
            slot = k % 2
            return [
                pltpu.make_async_copy(
                    wg_ref.at[:, pl.ds(at, size)], wg_s.at[slot, :, pl.ds(0, size)], sem_w.at[slot, 0]),
                pltpu.make_async_copy(
                    wu_ref.at[:, pl.ds(at, size)], wu_s.at[slot, :, pl.ds(0, size)], sem_w.at[slot, 1]),
                pltpu.make_async_copy(
                    gh_ref.at[:, pl.ds(at, size)], gh_s.at[slot, :, pl.ds(0, size)], sem_w.at[slot, 2]),
            ]

        first = [
            pltpu.make_async_copy(n_refs[i], n2_s.at[pl.ds(i * rows, rows)], sem_n.at[i])
            for i in range(count)
        ]
        for copy in first + load(0):
            copy.start()
        for copy in first:
            copy.wait()
        for k, (at, size) in enumerate(parts):
            if k + 1 < len(parts):
                for copy in load(k + 1):
                    copy.start()
            for copy in load(k):
                copy.wait()
            slot = k % 2
            wg, wu = (wg_s[slot, :, :size], wu_s[slot, :, :size])
            gelu, slope = gelu_pair(dot(n2_s[...], wg))
            up = dot(n2_s[...], wu)
            gh = gh_s[slot, :, :size]
            hid_ref[:, at : at + size] = (gelu * up).astype(BF16)
            gg = (gh * up * slope).astype(BF16)
            gu = (gh * gelu).astype(BF16)
            gg_ref[:, at : at + size] = gg
            gu_ref[:, at : at + size] = gu

            def far_rows(v):
                return jnp.concatenate([v[rows : 2 * rows], v[3 * rows :]], axis=0)

            part = dot_cols(far_rows(gg), wg) + dot_cols(far_rows(gu), wu)
            if k == 0:
                acc[...] = part
            else:
                acc[...] += part
        far_ref[...] = acc[:rows]
        far_c_ref[...] = acc[rows:].astype(BF16)

    act = jax.ShapeDtypeStruct((total, ff), BF16)
    return pl.pallas_call(
        body,
        in_specs=[ANY] * (count + 3),
        out_shape=[act, act, act, jax.ShapeDtypeStruct((rows, width), F32),
                   jax.ShapeDtypeStruct((rows, width), BF16)],
        scratch_shapes=[
            pltpu.VMEM((total, width), BF16),
            pltpu.VMEM((2, total, widest), F32),
            pltpu.VMEM((2, width, widest), BF16),
            pltpu.VMEM((2, width, widest), BF16),
            pltpu.VMEM((far, width), F32),
            pltpu.SemaphoreType.DMA((count,)),
            pltpu.SemaphoreType.DMA((2, 3)),
        ],
        compiler_params=pltpu.CompilerParams(vmem_limit_bytes=VMEM_MAX),
        cost_estimate=work(23),
    )(*n2_parts, grad_hidden, w_gate, w_up)


def mlp_rest(hidden, grad_gate, grad_up, w_gate, w_up, w_down, rows):
    total, ff = hidden.shape
    width = w_gate.shape[0]
    block = 512

    def body(hid_ref, gg_ref, gu_ref, wg_ref, wu_ref, wd_ref, gn_ref, gn_c_ref, out_ref, out_c_ref):
        def near(ref):
            return jnp.concatenate([ref[:rows], ref[2 * rows : 3 * rows]], axis=0)

        gn = dot_cols(near(gg_ref), wg_ref[...]) + dot_cols(near(gu_ref), wu_ref[...])
        gn_ref[...] = gn[:rows]
        gn_c_ref[...] = gn[rows:].astype(BF16)
        out = dot_cols(hid_ref[...], wd_ref[...])
        out_ref[...] = out[: total // 2]
        out_c_ref[...] = out[total // 2 :].astype(BF16)

    whole = pl.BlockSpec((total, ff), lambda j: (0, 0))
    weight = pl.BlockSpec((block, ff), lambda j: (j, 0))
    tall = lambda n: pl.BlockSpec((n, block), lambda j: (0, j))
    shape = lambda n, dt: jax.ShapeDtypeStruct((n, width), dt)
    return pl.pallas_call(
        body,
        grid=(width // block,),
        in_specs=[whole] * 3 + [weight] * 3,
        out_specs=[tall(rows), tall(rows), tall(total // 2), tall(total // 2)],
        out_shape=[shape(rows, F32), shape(rows, BF16), shape(total // 2, F32), shape(total // 2, BF16)],
        compiler_params=pltpu.CompilerParams(vmem_limit_bytes=VMEM_MAX),
        cost_estimate=work(19),
    )(hidden, grad_gate, grad_up, w_gate, w_up, w_down)


def rows_of_tokens(place, parts, rows_out, each):
    tokens, width = parts[0].shape
    half = width // 2
    count = len(parts)

    def body(place_ref, *refs):
        out_ref, turned = (refs[count], refs[count + 1])
        for k in range(count):
            turned[...] = refs[k][...].T
            for i in range(rows_out // each):
                at = pl.multiple_of((2 * i + place_ref[2]) * each, 16)
                out_ref[i * each : (i + 1) * each, k * tokens : (k + 1) * tokens] = turned[pl.ds(at, each), :]

    return pl.pallas_call(
        body,
        grid_spec=pltpu.PrefetchScalarGridSpec(
            num_scalar_prefetch=1,
            grid=(1,),
            in_specs=[pl.BlockSpec((tokens, half), lambda i, place: (0, place[1]))] * count,
            out_specs=pl.BlockSpec((rows_out, count * tokens), lambda i, place: (0, 0)),
            scratch_shapes=[pltpu.VMEM((half, tokens), BF16)],
        ),
        out_shape=jax.ShapeDtypeStruct((rows_out, count * tokens), BF16),
        compiler_params=pltpu.CompilerParams(vmem_limit_bytes=VMEM_MAX),
        cost_estimate=work(5),
    )(place, *parts)


def mlp_weight_grads(place, n2_parts, first_hidden, cot_parts, acts, n2_rows, cot_rows, weights, at, size, each):
    groups = len(n2_parts)
    per = len(n2_parts[0])
    tokens, width = n2_parts[0][0].shape
    group = per * tokens
    both = group // 2
    rows = n2_rows[0].shape[0]
    flat_n = [p for g in n2_parts for p in g]
    flat_c = [p for g in cot_parts for p in g]
    total, total_c = (len(flat_n), len(flat_c))

    def body(place_ref, *refs):
        n_refs, c_refs, refs = (refs[:total], refs[total : total + total_c], refs[total + total_c :])
        gh_ref, wg_ref, wu_ref, wd_ref, hid_ref, gg_ref, gu_ref = refs[:7]
        n_rows, c_rows = (refs[7:11], refs[11:15])
        own_ref, rest_ref, n2_s, cot_s, acc, sem = refs[15:]

        def load(g, slot):
            found = []
            for i in range(per):
                to = pl.ds(i * tokens, tokens)
                found.append(pltpu.make_async_copy(n_refs[g * per + i], n2_s.at[slot, to], sem.at[slot, i]))
                if g > 0:
                    found.append(pltpu.make_async_copy(
                        c_refs[(g - 1) * per + i], cot_s.at[slot, to], sem.at[slot, per + i]))
            return found

        for copy in load(0, 0) + load(1, 1):
            copy.start()

        def add(g, act, fresh):
            fixed = isinstance(g, int)
            start = g * both if fixed else pl.multiple_of((g - 2) * both, both)
            for i, four in enumerate((c_rows, n_rows, n_rows)):
                mine, other = four[:2] if fixed else four[2:]
                part = dot(mine[:, pl.ds(start, both)], act[i][:both]) + dot(
                    other[:, pl.ds(start, both)], act[i][both:])
                if fresh:
                    acc[i] = part
                else:
                    acc[i] += part

        def recompute(g, slot, gh):
            gelu, slope = gelu_pair(dot(n2_s[slot], wg_ref[...]))
            up = dot(n2_s[slot], wu_ref[...])
            add(g + 1, ((gelu * up).astype(BF16), (gh * up * slope).astype(BF16), (gh * gelu).astype(BF16)), False)

        add(0, (hid_ref, gg_ref, gu_ref), True)
        for copy in load(0, 0):
            copy.wait()
        recompute(0, 0, gh_ref[...])

        def step(g, carry):
            slot = lax.rem(g, 2)
            for k in range(2, groups):
                @pl.when(g + 1 == k)
                def _():
                    for copy in load(k, k % 2):
                        copy.start()

            for copy in load(1, slot):
                copy.wait()
            recompute(g, slot, dot(cot_s[slot], wd_ref[...]))
            return carry

        lax.fori_loop(1, groups, step, 0)
        for j in range(rows // each):
            start = pl.multiple_of((place_ref[0] ^ j) * each, 8)
            for i in range(3):
                block = acc[i, pl.ds(start, each), :]
                if j == 0:
                    own_ref[:, i * size : (i + 1) * size] = block
                else:
                    rest_ref[(j - 1) * each : j * each, i * size : (i + 1) * size] = block.astype(BF16)

    index = at // size
    column = lambda n: pl.BlockSpec((n, size), lambda j, place: (0, index))
    whole = pl.BlockSpec(n2_rows[0].shape, lambda j, place: (0, 0))
    return pl.pallas_call(
        body,
        grid_spec=pltpu.PrefetchScalarGridSpec(
            num_scalar_prefetch=1,
            grid=(1,),
            in_specs=[ANY] * (total + total_c) + [column(group)] + [column(width)] * 3 + [column(group)] * 3
            + [whole] * 8,
            out_specs=[pl.BlockSpec((each, 3 * size), lambda j, place: (0, 0)),
                       pl.BlockSpec((rows - each, 3 * size), lambda j, place: (0, 0))],
            scratch_shapes=[
                pltpu.VMEM((2, group, width), BF16),
                pltpu.VMEM((2, group, width), BF16),
                pltpu.VMEM((3, rows, size), F32),
                pltpu.SemaphoreType.DMA((2, 2 * per)),
            ],
        ),
        out_shape=[jax.ShapeDtypeStruct((each, 3 * size), F32),
                   jax.ShapeDtypeStruct((rows - each, 3 * size), BF16)],
        compiler_params=pltpu.CompilerParams(vmem_limit_bytes=VMEM_MAX),
        cost_estimate=work(35 * size // 768),
    )(place, *flat_n, *flat_c, first_hidden, *weights, *acts, *n2_rows, *cot_rows)


def rows_by_device(place, parts, starts, block):
    columns, count = (len(parts), len(parts[0]))
    tokens, n = parts[0][0].shape
    rows = len(starts(0, 0)) * block
    flat = [block_of for column in parts for block_of in column]
    if block % 16:
        turned = [jnp.concatenate(column, axis=0).T for column in parts]
        turned = turned[0] if columns == 1 else jnp.where(
            place[2] == 0, jnp.concatenate(turned), jnp.concatenate(turned[::-1]))

        def taken(dc):
            return jnp.stack([
                jnp.concatenate([
                    lax.dynamic_slice_in_dim(turned, start, block, 0)
                    for start in starts(place[0] ^ dy, place[1] ^ dc)])
                for dy in range(2)])

        kept, sent = (taken(0), taken(1))
        return kept[0], sent[0], jnp.concatenate([kept[1], sent[1]], axis=0)

    def body(place_ref, *refs):
        keep_ref, send_ref, y_ref, turned = refs[len(flat):]
        for h in range(columns):
            base = 0 if columns == 1 else pl.multiple_of((place_ref[2] ^ h) * n, 16)
            for k in range(count):
                turned[pl.ds(base, n), k * tokens : (k + 1) * tokens] = refs[h * count + k][...].T
        for dy, dc, ref, at in ((0, 0, keep_ref, 0), (0, 1, send_ref, 0), (1, 0, y_ref, 0), (1, 1, y_ref, rows)):
            for i, start in enumerate(starts(place_ref[0] ^ dy, place_ref[1] ^ dc)):
                ref[at + i * block : at + (i + 1) * block, :] = turned[pl.ds(pl.multiple_of(start, 16), block), :]

    shape = (rows, count * tokens)
    return pl.pallas_call(
        body,
        grid_spec=pltpu.PrefetchScalarGridSpec(
            num_scalar_prefetch=1,
            grid=(1,),
            in_specs=[pl.BlockSpec((tokens, n), lambda i, place: (0, 0))] * len(flat),
            out_specs=[pl.BlockSpec((n_rows, shape[1]), lambda i, place: (0, 0)) for n_rows in (rows, rows, 2 * rows)],
            scratch_shapes=[pltpu.VMEM((columns * n, count * tokens), BF16)],
        ),
        out_shape=[jax.ShapeDtypeStruct((n_rows, shape[1]), BF16) for n_rows in (rows, rows, 2 * rows)],
        compiler_params=pltpu.CompilerParams(vmem_limit_bytes=VMEM_MAX),
        cost_estimate=work(3),
    )(place, *flat)


def joined_columns(pairs):
    rows = pairs[0][0].shape[0]
    widths = [a.shape[1] // 3 for a, _ in pairs]
    total = sum(widths)
    step = rows // 4 if rows % 64 == 0 else rows
    flat = [term for pair in pairs for term in pair]

    def body(*refs):
        for i in range(3):
            at = 0
            for k, n in enumerate(widths):
                span = slice(i * n, (i + 1) * n)
                refs[len(flat) + i][:, at : at + n] = refs[2 * k][:, span].astype(F32) + refs[
                    2 * k + 1][:, span].astype(F32)
                at += n

    return pl.pallas_call(
        body,
        grid=(rows // step,),
        in_specs=[pl.BlockSpec((step, term.shape[1]), lambda j: (j, 0)) for term in flat],
        out_specs=[pl.BlockSpec((step, total), lambda j: (j, 0))] * 3,
        out_shape=[jax.ShapeDtypeStruct((rows, total), F32)] * 3,
        compiler_params=pltpu.CompilerParams(vmem_limit_bytes=VMEM_MAX),
        cost_estimate=work(5),
    )(*flat)


def gate_weight_grad(place, conv, grad_in, grad_decay, block):
    tokens, n = conv.shape
    count = n // block // 2
    if block % 16:
        by_head = lambda v: v.reshape(tokens, n // BLK, BLK)
        blocks = jnp.einsum(
            "thi,thj->hij", by_head(conv), jnp.concatenate([by_head(grad_in), by_head(grad_decay)], 2),
            preferred_element_type=F32).reshape(count, 2, block, 2 * BLK)
        mine, theirs = [
            lax.dynamic_index_in_dim(blocks, core, 1, keepdims=False).reshape(n // 2, 2 * BLK)
            for core in (place[1], 1 - place[1])]
        return mine, theirs.astype(BF16)

    def body(place_ref, conv_ref, in_ref, decay_ref, keep_ref, away_ref, whole):
        for h in range(n // BLK):
            cols = slice(h * BLK, (h + 1) * BLK)
            turned = conv_ref[:, cols].T
            whole[cols, :BLK] = dot(turned, in_ref[:, cols])
            whole[cols, BLK:] = dot(turned, decay_ref[:, cols])
        for i in range(count):
            at = pl.multiple_of((2 * i + place_ref[1]) * block, 16)
            keep_ref[i * block : (i + 1) * block, :] = whole[pl.ds(at, block), :]
            at = pl.multiple_of((2 * i + 1 - place_ref[1]) * block, 16)
            away_ref[i * block : (i + 1) * block, :] = whole[pl.ds(at, block), :].astype(BF16)

    spec = pl.BlockSpec((tokens, n), lambda h, place: (0, 0))
    out = pl.BlockSpec((n // 2, 2 * BLK), lambda h, place: (0, 0))
    return pl.pallas_call(
        body,
        grid_spec=pltpu.PrefetchScalarGridSpec(
            num_scalar_prefetch=1,
            grid=(1,),
            in_specs=[spec] * 3,
            out_specs=[out, out],
            scratch_shapes=[pltpu.VMEM((n, 2 * BLK), F32)],
        ),
        out_shape=[jax.ShapeDtypeStruct((n // 2, 2 * BLK), F32), jax.ShapeDtypeStruct((n // 2, 2 * BLK), BF16)],
        compiler_params=pltpu.CompilerParams(vmem_limit_bytes=VMEM_MAX),
        cost_estimate=work(3),
    )(place, conv, grad_in, grad_decay)


def sum_of_dots(rows, values):
    count = len(rows)

    def body(*refs):
        total = dot(refs[0][...], refs[count][...])
        for k in range(1, count):
            total = total + dot(refs[k][...], refs[count + k][...])
        refs[2 * count][...] = total.astype(BF16)

    return pl.pallas_call(
        body,
        out_shape=jax.ShapeDtypeStruct((rows[0].shape[0], values[0].shape[1]), BF16),
        compiler_params=pltpu.CompilerParams(vmem_limit_bytes=VMEM_MAX),
        cost_estimate=work(5),
    )(*rows, *values)


def after(value, *others):
    return lax.optimization_barrier((value, others))[0]


class Live:
    def cut(self):
        names = sorted(vars(self))
        for name, value in zip(names, lax.optimization_barrier([getattr(self, n) for n in names])):
            setattr(self, name, value)

    def hold(self, **values):
        for name, value in values.items():
            setattr(self, name, value)
        self.cut()


def seq_bits(lay):
    found, bit = ([], 1)
    while bit < lay.seq:
        found.append(bit)
        bit *= 2
    return found


def scan_start(summary, groups):
    prod, state = (summary[:groups], summary[groups : 2 * groups])
    return (prod, state, jnp.ones_like(prod), jnp.zeros_like(state))


def scan_join(lay, held, other, bit, backward):
    prod, state, before_p, before_s = held
    groups = prod.shape[0]
    other_p, other_s = (other[:groups], other[groups:])
    is_later = (lay.seq_at & bit) != 0
    take = jnp.logical_not(is_later) if backward else is_later
    before_s = jnp.where(take, before_p * other_s + before_s, before_s)
    before_p = jnp.where(take, before_p * other_p, before_p)
    state = jnp.where(take, prod * other_s + state, other_p * state + other_s)
    return (prod * other_p, state, before_p, before_s)


def local(inputs, block_flags, decay_seed, vectors, in_y, in_x, gate_weight, out_proj,
          mlp_gate, mlp_up, mlp_down, cotangent):
    lay = Lay()
    nz, x, y, z, c = (lay.nz, lay.x, lay.y, lay.z, lay.c)
    tokens, width = inputs.shape[1:]
    half, quarter, two = (width // 2, width // 4, 2 * tokens)
    each = width // lay.seq
    own80 = each // 4
    bits = seq_bits(lay)
    place = jnp.stack([z % (nz // 2), lay.seq_at // nz, y]).astype(jnp.int32)
    at_yc = jnp.stack([y, c, x]).astype(jnp.int32)
    live = Live()

    def order_c(own, other, axis):
        return jnp.where(c == 0, jnp.concatenate([own, other], axis),
                         jnp.concatenate([other, own], axis))

    def order_f(rel):
        b = rel.shape[-1] // 4
        p = [rel[..., i * b : (i + 1) * b] for i in range(4)]
        by_c = jnp.where(c == 0, rel, jnp.concatenate([p[1], p[0], p[3], p[2]], -1))
        return jnp.where(x == 0, by_c, jnp.concatenate([by_c[..., 2 * b :], by_c[..., : 2 * b]], -1))

    def owner_parts(blocks):
        pick = lambda t: lax.dynamic_index_in_dim(blocks, t, 0, keepdims=False)
        come = [
            lay.send(pick((z + step) % nz), lambda z, y, x, c: ((z + step) % nz, y, x, c))
            for step in range(1, nz)
        ]
        return pick(z), come

    def total_of(own, come):
        total = own.astype(F32)
        for part in come:
            total = total + part.astype(F32)
        return total.astype(BF16)

    def half_of(value, which, n, axis):
        return lax.dynamic_slice_in_dim(value, which * n, n, axis)

    cot = cotangent[0]
    cut = tokens // 2
    gate_away, inputs, gate_weight, out_proj, vectors, decay_seed, block_flags = lax.optimization_barrier(
        (half_of(gate_weight, 1 - x, half, 0), inputs, gate_weight, out_proj, vectors, decay_seed, block_flags))
    halo_raw = lay.over_seq(inputs[0, tokens - 16 :], 1)
    gate_x = lay.over_x(gate_away)
    wx_c = lay.over_c(in_x)
    scaled_one, inverse_one = norm_scale(inputs[0].astype(F32))
    live.hold(n1=(scaled_one * vectors[0]).astype(BF16), inv1=inverse_one, halo_raw=halo_raw, cot_top=cot[:cut],
              cot_low=cot[cut:], wx_c=wx_c,
              params=(gate_weight, out_proj, vectors, decay_seed, block_flags))

    gate_weight, out_proj, vectors, decay_seed, block_flags = live.params
    n1_x = lay.over_x(live.n1)
    halo_own = (norm_scale(live.halo_raw.astype(F32))[0] * vectors[0]).astype(BF16)
    n_flags = block_flags.shape[1]
    flag_row = jnp.pad(block_flags.astype(BF16), ((0, 0), (0, width - n_flags)))
    halo_x = lay.over_x(jnp.concatenate([flag_row, halo_own[1:]], axis=0))
    gate_own = half_of(gate_weight, x, half, 0)
    gate_c = lay.over_c(gate_own)
    cot_z_top = lay.over_z(live.cot_top)
    base = -5.0 - decay_seed.astype(F32) + vectors[9]
    del live.params, live.halo_raw, live.cot_top
    live.hold(
        n1_x=n1_x, halo_x=halo_x, halo_own=halo_own, gate_x=gate_x, gate_c=gate_c, cot_z_top=cot_z_top,
        flags=jnp.concatenate([block_flags.astype(F32), halo_x[:1, :n_flags].astype(F32)], axis=0),
        gate_own=gate_own, out_away=half_of(out_proj, 2 * (1 - x) + y, quarter, 0),
        out_mine=half_of(out_proj, x, half, 0), vec=half_of(vectors, x, half, 1), gain_two=vectors[1],
        gain_one=vectors[0],
        rates=half_of(jnp.stack([jax.nn.softplus(base), jax.nn.sigmoid(base)]), x, half, 1))

    out_a = lay.over_x(live.out_away)
    cot_z_low, cot_y = (lay.over_z(live.cot_low), lay.over_y(after(cot, live.n1_x)))
    wy_c = lay.over_c(after(in_y, live.n1_x))
    gates = order_f(jnp.concatenate(
        [live.gate_own, live.gate_c, live.gate_x, lay.over_c(live.gate_x)], axis=1))
    normed = jnp.concatenate([live.n1, live.n1_x, live.halo_own, live.halo_x], axis=0)
    x_all = order_c(dot(normed, in_x).astype(BF16), dot(normed, live.wx_c).astype(BF16), 1)
    x_low = x_all[:two].reshape(2, tokens, half)
    halo = x_all[two:].reshape(2, 16, half)
    shape3 = lambda dt: jax.ShapeDtypeStruct((2, tokens, half), dt)
    summary_shape = jax.ShapeDtypeStruct((4, half), F32)
    conv_low, ig, dg, prods, local_state, summary = by_head(
        mixer_forward, live.flags,
        [(x_low, False), (halo, False), (gates, True), (live.vec, False), (live.rates, False)],
        [shape3(BF16), shape3(F32), shape3(F32), shape3(F32), shape3(F32), summary_shape])
    del live.gate_x, live.gate_own, live.gate_c, live.halo_own, live.halo_x
    live.hold(x_low=x_low, halo=halo, gates=gates, conv_low=conv_low, ig=ig, dg=dg, prods=prods,
              local_state=local_state, scan=scan_start(summary, 2), cot_y=cot_y, normed=normed[:two], wy_c=wy_c, out_a=out_a,
              cot_z_low=cot_z_low)
    del live.cot_low
    del live.out_away

    def n1_starts(at_y, at_c):
        return [((2 * i + at_y) * 4 + 2 * j + at_c) * own80 for i in range(nz) for j in range(2)]

    for bit in bits:
        come = lay.over_seq_bit(jnp.concatenate(live.scan[:2], axis=0), bit)
        live.scan = scan_join(lay, live.scan, come, bit, False)
        if bit == 1:
            live.cut()
            out_b = lay.over_y(live.out_a)
            out_c = lay.over_c(live.out_mine)
            cot_x = lay.over_x(after(cot, live.scan))
    out_x = jnp.where(y == 0, jnp.concatenate([live.out_a, out_b], 0), jnp.concatenate([out_b, live.out_a], 0))
    y_pre = order_c(dot(live.normed, in_y), dot(live.normed, live.wy_c), 1).reshape(2, tokens, half)
    n1_own, sent, n1_away = rows_by_device(at_yc, [[live.n1, live.n1_x]], n1_starts, own80)
    state_in = live.scan[3]
    del live.scan, live.out_a
    live.hold(state_in=state_in, y_pre=y_pre, out_left=jnp.concatenate([live.out_mine, out_c], axis=1),
              cot_z=jnp.concatenate([live.cot_z_top, live.cot_z_low], axis=0),
              out_x=out_x, cot_x=cot_x, n1_own=n1_own, n1_away=n1_away, n1_c=lay.over_c(sent))
    del live.out_mine, live.cot_z_top, live.cot_z_low

    n1_y = lay.over_y(live.n1_away[: live.n1_own.shape[0]])
    state = live.local_state + live.prods * live.state_in[:, None, :]
    mixed = (state * jax.nn.gelu(live.y_pre, approximate=True)).astype(BF16)
    mixed_two = mixed.reshape(two, half)
    out_right = jnp.concatenate([live.out_x, lay.over_c(live.out_x)], axis=1)
    part = jnp.concatenate([dot(mixed_two, live.out_left), dot(mixed_two, out_right)], axis=1)
    del live.out_x
    live.hold(mixed=mixed, part_own=part[:tokens], part_x=part[tokens:].astype(BF16), out_right=out_right, n1_y=n1_y)

    part_x = lay.over_x(live.part_x)
    cot_xy = lay.over_y(live.cot_x)
    gh_main = grad_hidden_of([cot, live.cot_x, lay.over_c(cot), lay.over_c(live.cot_x)], mlp_down)
    live.hold(part_x=part_x, gh_main=gh_main, cot_xy=cot_xy)

    swapped = jnp.concatenate([live.part_x[:, half:], live.part_x[:, :half]], axis=1)
    mid = inputs[0].astype(F32) + order_f(live.part_own + swapped.astype(F32))
    scaled_two, inverse_two = norm_scale(mid)
    del live.part_x, live.part_own
    live.hold(mid=mid, inv2=inverse_two, n2=(scaled_two * live.gain_two).astype(BF16))

    n2_x = lay.over_x(live.n2)
    n2_y = lay.over_y(live.n2)
    n2_z_top = lay.over_z(live.n2[:cut])
    n2_c = lay.over_c(live.n2)
    pair = [live.cot_y, live.cot_xy]
    gh_y = grad_hidden_of(pair + [lay.over_c(p) for p in pair], mlp_down)
    live.hold(n2_x=n2_x, n2_c=n2_c, n2_y=n2_y, n2_z_top=n2_z_top, gh_y=gh_y)

    live.hold(n2_xc=lay.over_c(live.n2_x), n2_low=live.n2[cut:], n2_x_top=live.n2_x[:cut], n2_x_low=live.n2_x[cut:])
    cot_xz = lay.over_x(live.cot_z)
    n2_xy = lay.over_y(live.n2_x)
    n2_z_low = lay.over_z(live.n2_low)
    hidden, grad_gate, grad_up, far, far_c = mlp_forward(
        [live.n2, live.n2_x, live.n2_c, live.n2_xc], live.gh_main, mlp_gate, mlp_up)
    del live.gh_main, live.n2_c
    live.hold(acts=(hidden, grad_gate, grad_up), far=far, far_c=far_c, cot_xz=cot_xz, n2_xy=n2_xy,
              n2_z_low=n2_z_low)
    live.hold(far=(live.far + lay.over_c(live.far_c).astype(F32)).astype(BF16),
              n2_z=jnp.concatenate([live.n2_z_top, live.n2_z_low], axis=0))

    arriving = lay.over_x(live.far)
    n2_yz, n2_y_c, n2_xy_c = (lay.over_y(live.n2_z), lay.over_c(live.n2_y), lay.over_c(live.n2_xy))
    n2_xz_top = lay.over_z(live.n2_x_top)
    near, near_c, out, out_c = mlp_rest(*live.acts, mlp_gate, mlp_up, mlp_down, tokens)
    del live.far, live.far_c, live.n2_z_top, live.n2_z_low
    live.hold(arriving=arriving, near=near, near_c=near_c, out=out, out_c=out_c, n2_yz=n2_yz, n2_y_c=n2_y_c, n2_xy_c=n2_xy_c, n2_xz_top=n2_xz_top)

    out_c = lay.over_c(live.out_c)
    grad_n2 = live.near + lay.over_c(live.near_c).astype(F32) + live.arriving.astype(F32)
    grad_mid_norm, grad_gain_two = norm_back(grad_n2, live.mid * live.inv2, live.inv2, live.gain_two)
    grad_mid = cot.astype(F32) + grad_mid_norm
    branch = grad_mid.astype(BF16)
    live.out_c = out_c
    del live.near, live.near_c, live.arriving
    live.hold(grad_gain_two=grad_gain_two, grad_mid=grad_mid, branch=branch, branch_rel=order_f(branch))

    arriving = lay.over_x(live.branch_rel)
    n2_xz_low = lay.over_z(live.n2_x_low)
    cot_yz = lay.over_y(live.cot_z)
    live.hold(arriving=arriving, n2_xz_low=n2_xz_low, cot_yz=cot_yz, out_sum=live.out + live.out_c.astype(F32),
              n2_z_c=lay.over_c(live.n2_z), cot_z_c=lay.over_c(live.cot_z),
              n2_rows_ahead=rows_of_tokens(place, [live.n2, live.n2_x, live.n2_y, live.n2_xy], half // 2, each),
              cot_rows_ahead=rows_of_tokens(place, [cot, live.cot_x, live.cot_y, live.cot_xy], half // 2, each))

    rows_each = live.n1_own.shape[0]
    n1_yc = lay.over_y(live.n1_away[rows_each:])
    cot_xz_c, n2_yz_c = (lay.over_c(live.cot_xz), lay.over_c(live.n2_yz))
    mixed_xa = lay.over_x(live.mixed[1])
    branch_x_rel = jnp.concatenate([live.arriving[:, half:], live.arriving[:, :half]], axis=1)
    both_rel = jnp.concatenate([live.branch_rel, branch_x_rel], 0)
    grad_mixed = dot_cols(both_rel[:, :half], live.out_left) + dot_cols(both_rel[:, half:], live.out_right)
    gy, bprod, blocal, back_summary = by_head(
        mixer_back_scan, live.flags,
        [(grad_mixed.reshape(2, tokens, half), False), (live.y_pre, False), (live.dg, False),
         (live.prods, False), (live.local_state, False), (live.state_in, False), (live.rates, False)],
        [shape3(BF16), shape3(F32), shape3(F32), summary_shape])
    del live.arriving, live.branch_rel, live.y_pre
    live.hold(gy=gy.reshape(two, half), bprod=bprod, blocal=blocal, scan=scan_start(back_summary, 2),
              branch_x_rel=branch_x_rel, n1_yc=n1_yc, cot_xz_c=cot_xz_c, n2_yz_c=n2_yz_c,
              mixed_xa=mixed_xa, mixed_b=live.mixed[0])

    n2_xyz = lay.over_x(live.n2_yz)
    own_cols = lambda value, which: half_of(value, which, quarter, 1)
    part_y = dot_cols(own_cols(live.gy, c), in_y) + dot_cols(own_cols(live.gy, 1 - c), live.wy_c)
    for bit in bits:
        come = lay.over_seq_bit(jnp.concatenate(live.scan[:2], axis=0), bit)
        live.scan = scan_join(lay, live.scan, come, bit, True)
        if bit == 1:
            live.cut()
            cot_xyz = lay.over_y(live.cot_xz)
            cot_yz_c = lay.over_c(live.cot_yz)
    back_in = live.scan[3]
    del live.scan
    live.hold(back_in=back_in, cot_xyz=cot_xyz, n2_xyz=n2_xyz, part_y=part_y, cot_yz_c=cot_yz_c)

    live.ahead_c = (lay.over_c(live.n2_rows_ahead), lay.over_c(live.cot_rows_ahead))
    live.n1_yc = lay.over_c(live.n1_yc)
    gip, gdp, gx_main, gx_tail, edge, vec_rows = by_head(
        mixer_backward, live.flags,
        [(live.bprod, False), (live.blocal, False), (live.back_in, False), (live.prods, False),
         (live.local_state, False), (live.state_in, False), (live.ig, False), (live.dg, False),
         (live.conv_low, False), (live.x_low, False), (live.halo, False), (live.gates, True),
         (live.vec, False), (live.rates, False)],
        [shape3(BF16), shape3(BF16), shape3(BF16), jax.ShapeDtypeStruct((2, 16, half), F32),
         jax.ShapeDtypeStruct((2, 8, half), F32), jax.ShapeDtypeStruct((8, half), F32)])
    for name in ("bprod", "blocal", "back_in", "prods", "local_state", "state_in", "ig", "dg", "x_low", "halo",
                 "gates", "vec", "rates", "flags"):
        delattr(live, name)
    live.hold(gip=gip, gdp=gdp, gx_main=gx_main, gx_tail=gx_tail, edge=edge, vec_rows=vec_rows)

    edge_next = lay.over_seq(live.edge, -1)
    mixed_xb = lay.over_x(live.mixed_b)
    n2_xz = jnp.concatenate([live.n2_xz_top, live.n2_xz_low], axis=0)
    n2_xz_c, n2_xyz_c, cot_xyz_c = (lay.over_c(n2_xz), lay.over_c(live.n2_xyz), lay.over_c(live.cot_xyz))
    live.n2s = [[live.n2, live.n2_x], [live.n2_y, live.n2_xy], [live.n2_z, n2_xz], [live.n2_yz, live.n2_xyz]]
    live.cots = [cot, live.cot_x, live.cot_y, live.cot_xy, live.cot_z, live.cot_xz, live.cot_yz, live.cot_xyz]
    n2_rows = rows_of_tokens(place, [p for group in live.n2s[2:] for p in group], half // 2, each)
    cot_rows = rows_of_tokens(place, live.cots[4:], half // 2, each)
    del live.edge
    live.hold(edge_next=edge_next, n2_rows=n2_rows, cot_rows=cot_rows,
              n2s_c=[[live.n2_y_c, live.n2_xy_c], [live.n2_z_c, n2_xz_c], [live.n2_yz_c, n2_xyz_c]],
              cots_c=[live.cot_z_c, live.cot_xz_c, live.cot_yz_c, cot_xyz_c], mixed_xb=mixed_xb)

    gx_last = (live.gx_tail + jnp.pad(live.edge_next, ((0, 0), (8, 0), (0, 0)))).astype(BF16)
    gx = jnp.concatenate([live.gx_main[:, : tokens - 16], gx_last], axis=1).reshape(two, half)
    gx_o, gx_c = (own_cols(gx, c), own_cols(gx, 1 - c))
    part_n1 = live.part_y + dot_cols(gx_o, in_x) + dot_cols(gx_c, live.wx_c)
    del live.gx_main, live.gx_tail, live.edge_next, live.part_y
    live.hold(gx=gx, n1_near=part_n1[:tokens], n1_far=part_n1[tokens:].astype(BF16),
              n2_rows_c=lay.over_c(live.n2_rows), cot_rows_c=lay.over_c(live.cot_rows))

    cuts = sections_of(mlp_gate.shape[1])

    def weight_piece(at, size):
        return mlp_weight_grads(
            place, [a + b for a, b in zip(live.n2s[1:], live.n2s_c)], live.gh_y,
            [live.cots[4:6] + live.cots_c[:2], live.cots[6:] + live.cots_c[2:]], live.acts,
            (live.n2_rows_ahead, live.ahead_c[0], live.n2_rows, live.n2_rows_c),
            (live.cot_rows_ahead, live.ahead_c[1], live.cot_rows, live.cot_rows_c),
            (mlp_gate, mlp_up, mlp_down), at, size, each)

    def piece_sum(own, rest):
        blocks = [own] + [rest[j * each : (j + 1) * each] for j in range(nz // 2 - 1)]
        bit = nz // 4
        while bit >= 1:
            gone = blocks[bit] if bit == 1 else jnp.concatenate(
                [b.astype(BF16) for b in blocks[bit : 2 * bit]], axis=0)
            come = lay.over_seq_bit(gone.astype(BF16), 2 * bit)
            blocks = [(blocks[j], come[j * each : (j + 1) * each]) for j in range(bit)]
            if bit > 1:
                blocks = [a.astype(F32) + b.astype(F32) for a, b in blocks]
            bit //= 2
        return blocks[0]

    arriving = lay.over_x(live.n1_far)
    gy_y = lay.over_y(live.gy)
    live.gy_c = lay.over_c(live.gy)
    live.hold(piece_a=weight_piece(*cuts[0]), arriving=arriving, gy_y=gy_y)

    grad_n1 = live.n1_near + live.arriving.astype(F32)
    scaled_one = inputs[0].astype(F32) * live.inv1
    grad_in_norm, grad_gain_one = norm_back(grad_n1, scaled_one, live.inv1, live.gain_one)
    input_grad = (live.grad_mid + grad_in_norm).astype(BF16)[None]
    rows_full = lax.dynamic_update_slice_in_dim(
        jnp.zeros((8, width), F32), live.vec_rows, x * half, 1)
    sums = jnp.concatenate([grad_gain_one[None], live.grad_gain_two[None], rows_full], axis=0)
    sums = sums + lay.over_c(sums)
    del live.n1_near, live.n1_far, live.arriving, live.vec_rows, live.grad_gain_two, live.grad_mid
    branch_far = half_of(order_f(live.branch_x_rel), x, half, 1)
    branch_near = half_of(live.branch, x, half, 1)
    del live.branch_x_rel
    live.hold(sums=sums, gy_yc=lay.over_c(live.gy_y), branch_two=jnp.concatenate([branch_near, branch_far], axis=0))

    def over_columns(value):
        split = value.reshape(2, own80, half)
        mine = lax.dynamic_index_in_dim(split, x, 0, keepdims=False)
        theirs = lay.over_x(lax.dynamic_index_in_dim(split, 1 - x, 0, keepdims=False))
        return jnp.where(x == 0, jnp.concatenate([mine, theirs], -1),
                         jnp.concatenate([theirs, mine], -1)).astype(F32)

    sums = live.sums + lay.over_x(live.sums)
    branch_two_y = lay.over_y(live.branch_two)
    sum_a = piece_sum(*live.piece_a)
    n1_all = [live.n1_own, live.n1_c, live.n1_y, live.n1_yc]
    in_y_part = sum_of_dots(n1_all, [live.gy, live.gy_c, live.gy_y, live.gy_yc])
    gate_part, gate_away = gate_weight_grad(
        at_yc, live.conv_low.reshape(two, half), live.gip.reshape(two, half), live.gdp.reshape(two, half), own80)
    gate_part = (gate_part + lay.over_c(gate_away).astype(F32)).reshape(2, nz, own80, 2 * BLK)
    pick = lambda value, at, axis: lax.dynamic_index_in_dim(value, at, axis, keepdims=False)
    gate_y = lay.over_y(pick(gate_part, 1 - y, 0).astype(BF16))
    mixed_own, sent, mixed_away = rows_by_device(
        at_yc, [[live.mixed[0], live.mixed[1]], [live.mixed_xa, live.mixed_xb]], n1_starts, own80)
    del live.gy, live.gy_c, live.gy_y, live.gy_yc, live.mixed, live.mixed_xa, live.mixed_xb, live.conv_low, live.gip, live.gdp
    live.hold(in_y_part=in_y_part, sums=sums, sum_a=sum_a, branch_two_y=branch_two_y, gate_keep=pick(gate_part, y, 0), gate_y=gate_y,
              mixed_own=mixed_own, mixed_away=mixed_away, mixed_c=lay.over_c(sent),
              gx_c=lay.over_c(live.gx), branch_c=lay.over_c(live.branch_two))

    in_y_own, in_y_come = owner_parts(live.in_y_part.reshape(nz, 2 * own80, half))
    gx_y = lay.over_y(live.gx)
    mixed_y = lay.over_y(live.mixed_away)
    piece_b = weight_piece(*cuts[1])
    del live.piece_a, live.mixed_away
    del live.in_y_part
    live.hold(piece_b=piece_b, gx_y=gx_y, mixed_y=mixed_y, in_y_own=in_y_own, in_y_come=in_y_come)

    sum_b = piece_sum(*live.piece_b)
    sums = live.sums
    for bit in bits[:1]:
        sums = sums + lay.over_seq_bit(sums, bit)
    in_x_part = sum_of_dots(n1_all, [live.gx, live.gx_c, live.gx_y, lay.over_c(live.gx_y)])
    out_part = sum_of_dots(
        [live.mixed_own, live.mixed_c, live.mixed_y[:rows_each], lay.over_c(live.mixed_y[rows_each:])],
        [live.branch_two, live.branch_c, live.branch_two_y, lay.over_c(live.branch_two_y)])
    gate_part = (live.gate_keep + live.gate_y.astype(F32)).astype(BF16)
    del live.piece_b, live.gate_keep, live.gate_y, live.mixed_own, live.mixed_c, live.mixed_y
    live.hold(in_x_part=jnp.concatenate(
        [in_x_part.reshape(nz, 2 * own80, half), gate_part.reshape(nz, own80 * 2 * BLK // half, half)], axis=1),
        out_part=out_part, sum_b=sum_b, sums=sums, in_y_total=total_of(live.in_y_own, live.in_y_come),
        out_far=live.out_sum[tokens:].astype(BF16))
    del live.in_y_own, live.in_y_come

    in_x_own, in_x_come = owner_parts(live.in_x_part)
    out_arriving = lay.over_x(live.out_far)
    sums_z = lay.over_seq_bit(live.sums, 2)
    piece_c = weight_piece(*cuts[2])
    del live.in_x_part
    live.hold(piece_c=piece_c, in_x_own=in_x_own, in_x_come=in_x_come, out_arriving=out_arriving,
              sums=live.sums + sums_z)

    sum_c = piece_sum(*live.piece_c)
    out_own, out_come = owner_parts(live.out_part.reshape(nz, 2 * own80, half))
    in_x_own, in_x_come, in_y_total = after((live.in_x_own, live.in_x_come, live.in_y_total), out_come[1])
    in_x_total = total_of(in_x_own, in_x_come)
    live.hold(sum_c=sum_c, out_total=total_of(out_own, out_come),
              in_y_grad=over_columns(in_y_total), in_x_grad=over_columns(in_x_total[: 2 * own80]),
              gate_total=in_x_total[2 * own80 :].reshape(own80, 2 * BLK),
              output=(live.mid + after(live.out_sum, out_come[1])[:tokens] + live.out_arriving.astype(F32)
                      ).astype(BF16)[None])

    sums = live.sums
    for bit in bits[2:]:
        sums = sums + lay.over_seq_bit(sums, bit)
    mlp_down_grad, mlp_gate_grad, mlp_up_grad = joined_columns([live.sum_a, live.sum_b, live.sum_c])

    def final(z, y, x, c):
        at = ((x * 2 + y) * nz + z) * 2 + c
        s, f = (at // 4, at % 4)
        return (s // 2, s % 2, f // 2, f % 2)

    out_grad = over_columns(live.out_total)
    gate_grad = lay.send(live.gate_total, final).astype(F32)
    return (live.output, input_grad, sums, live.in_y_grad, live.in_x_grad, gate_grad, out_grad,
            mlp_gate_grad, mlp_up_grad, mlp_down_grad)


def solution(mesh):
    return jax.shard_map(
        local,
        mesh=mesh,
        in_specs=(
            P("fsdp", "seq", None),
            P("fsdp", "seq"),
            P(),
            P(),
            P(None, "fsdp"),
            P(None, "fsdp"),
            P(None, "fsdp"),
            P(None, "fsdp"),
            P(None, "fsdp"),
            P(None, "fsdp"),
            P(None, "fsdp"),
            P("fsdp", "seq", None),
        ),
        out_specs=(
            P("fsdp", "seq", None),
            P("fsdp", "seq", None),
            P(),
            P(("seq", "fsdp"), None),
            P(("seq", "fsdp"), None),
            P(("seq", "fsdp"), None),
            P(("seq", "fsdp"), None),
            P("seq", "fsdp"),
            P("seq", "fsdp"),
            P("seq", "fsdp"),
        ),
        check_vma=False,
    )
```

```python
import functools

import jax
import jax.numpy as jnp
from jax import lax
from jax.experimental import pallas as pl
from jax.experimental.pallas import tpu as pltpu
from jax.sharding import PartitionSpec as P

HEADS = 10
BLK = 256
FBLK = 64
EPS = 1e-06
ALL = ("seq", "fsdp")
F32 = jnp.float32
BF16 = jnp.bfloat16
GELU_C = 0.7978845608028654
GELU_A = 0.044715
VMEM_MAX = 60 * 1024 * 1024
ANY = pl.BlockSpec(memory_space=pl.ANY)


def work(us):
    scale = 1000 if us >= 10 else 0
    return pl.CostEstimate(flops=1 + us * scale * 900000, bytes_accessed=1 + us * scale * 2000, transcendentals=0)


def norm_scale(values):
    inverse = lax.rsqrt(jnp.mean(values * values, axis=-1, keepdims=True) + EPS)
    return (values * inverse, inverse)


def norm_back(grad_normed, scaled, inverse, gain_row):
    grad_gain = jnp.sum(grad_normed * scaled, axis=0)
    inner_term = grad_normed * gain_row
    grad_input = inverse * (
        inner_term - scaled * jnp.mean(inner_term * scaled, axis=-1, keepdims=True)
    )
    return (grad_input, grad_gain)


def gelu_pair(values):
    square = values * values
    t = jnp.tanh(values * (GELU_C + GELU_C * GELU_A * square))
    half = 0.5 + 0.5 * t
    slope = half * (1.0 + (1.0 - t) * values * (GELU_C + 3.0 * GELU_C * GELU_A * square))
    return (values * half, slope)


def dot(left, right):
    return jnp.dot(left, right, preferred_element_type=F32)


def dot_rows(left, right):
    return lax.dot_general(left, right, (((0,), (0,)), ((), ())), preferred_element_type=F32)


def dot_cols(left, right):
    return lax.dot_general(left, right, (((1,), (1,)), ((), ())), preferred_element_type=F32)


class Lay:
    def __init__(self):
        self.seq = lax.axis_size("seq")
        self.nz = self.seq // 2
        seq, fsdp = (lax.axis_index("seq"), lax.axis_index("fsdp"))
        self.z, self.y = (seq // 2, seq % 2)
        self.x, self.c = (fsdp // 2, fsdp % 2)
        self.seq_at = seq

    def pairs(self, target):
        found = []
        for s in range(self.seq):
            for f in range(4):
                z, y, x, c = (s // 2, s % 2, f // 2, f % 2)
                to = target(z, y, x, c)
                if to is not None:
                    found.append((s * 4 + f, ((to[0] * 2 + to[1]) * 2 + to[2]) * 2 + to[3]))
        return found

    def send(self, value, target):
        return lax.ppermute(value, ALL, self.pairs(target))

    def over_c(self, value):
        return self.send(value, lambda z, y, x, c: (z, y, x, 1 - c))

    def over_x(self, value):
        return self.send(value, lambda z, y, x, c: (z, y, 1 - x, c))

    def over_y(self, value):
        return self.send(value, lambda z, y, x, c: (z, 1 - y, x, c))

    def over_seq_bit(self, value, bit):
        def to(z, y, x, c):
            other = (2 * z + y) ^ bit
            return (other // 2, other % 2, x, c)

        return self.send(value, to)

    def over_z(self, value):
        return self.send(value, lambda z, y, x, c: (self.nz - 1 - z, y, x, c))

    def over_seq(self, value, by):
        def to(z, y, x, c):
            other = 2 * z + y + by
            return (other // 2, other % 2, x, c) if 0 <= other < self.seq else None

        return self.send(value, to)


def row_iota(rows, cols):
    return lax.broadcasted_iota(jnp.int32, (rows, cols), 0)


def token_masks(flags_ref, g, rows, cols):
    row = row_iota(rows, cols)
    block = row // FBLK
    offset = row % FBLK
    flagged = jnp.zeros((rows, cols), F32)
    for b in range(rows // FBLK):
        flagged = jnp.where(block == b, flags_ref[g, b], flagged)
    valid = [jnp.where(offset < lag, 1.0 - flagged, 1.0) for lag in range(4)]
    start = jnp.where(offset == 0, flagged, 0.0)
    return start, valid


def neg_expm1(v):
    series = 1.0 + v * (1.0 / 6.0)
    for n in (5.0, 4.0, 3.0, 2.0):
        series = 1.0 + v * (1.0 / n) * series
    return jnp.where(v > -0.25, -v * series, 1.0 - jnp.exp(v))


def shifted_inputs(xl_ref, halo_ref, g):
    ext = jnp.concatenate([halo_ref[g].astype(F32), xl_ref[g].astype(F32)], axis=0)
    pad = halo_ref.shape[1]
    return [ext[pad:] if k == 0 else pltpu.roll(ext, k, 0)[pad:] for k in range(4)]


def mixer_forward(flags_ref, xl_ref, halo_ref, gw_ref, vec_ref, rate_ref,
                  conv_ref, ig_ref, dg_ref, prod_ref, local_ref, sum_ref):
    groups, rows, cols = xl_ref.shape
    row = row_iota(rows, cols)
    for g in range(groups):
        start, valid = token_masks(flags_ref, g, rows, cols)
        lagged = shifted_inputs(xl_ref, halo_ref, g)
        conv = vec_ref[6:7, :] + jnp.zeros((rows, cols), F32)
        for k in range(4):
            conv = conv + vec_ref[2 + k : 3 + k, :] * lagged[k] * valid[k]
        conv_low = conv.astype(BF16)
        conv_ref[g] = conv_low
        prod = jnp.dot(conv_low, gw_ref[...], preferred_element_type=F32)
        ig = jax.nn.sigmoid(prod[:, :cols] + vec_ref[7:8, :])
        dg = jax.nn.sigmoid(prod[:, cols:] + vec_ref[8:9, :])
        ig_ref[g] = ig
        dg_ref[g] = dg
        keep = 1.0 - start
        log_decay = -8.0 * dg * rate_ref[0:1, :]
        p = jnp.exp(log_decay) * keep
        s = jnp.sqrt(keep * neg_expm1(2.0 * log_decay) + start) * ig * conv_low.astype(F32)
        step = 1
        while step < rows:
            inside = row >= step
            p_prev = jnp.where(inside, pltpu.roll(p, step, 0), 1.0)
            s_prev = jnp.where(inside, pltpu.roll(s, step, 0), 0.0)
            s = p * s_prev + s
            p = p * p_prev
            step *= 2
        prod_ref[g] = p
        local_ref[g] = s
        sum_ref[g : g + 1, :] = p[rows - 1 :, :]
        sum_ref[groups + g : groups + g + 1, :] = s[rows - 1 :, :]


def mixer_back_scan(flags_ref, gm_ref, y_ref, dg_ref, prod_ref, local_ref, sin_ref, rate_ref,
                    gy_ref, bprod_ref, blocal_ref, sum_ref):
    groups, rows, cols = gm_ref.shape
    row = row_iota(rows, cols)
    for g in range(groups):
        start, _ = token_masks(flags_ref, g, rows, cols)
        state = local_ref[g] + prod_ref[g] * sin_ref[g : g + 1, :]
        gelu, slope = gelu_pair(y_ref[g])
        gm = gm_ref[g]
        gy_ref[g] = (gm * state * slope).astype(BF16)
        decay = jnp.exp(-8.0 * dg_ref[g] * rate_ref[0:1, :]) * (1.0 - start)
        s = gm * gelu
        p = jnp.where(row == rows - 1, 1.0, pltpu.roll(decay, rows - 1, 0))
        step = 1
        while step < rows:
            inside = row < rows - step
            p_next = jnp.where(inside, pltpu.roll(p, rows - step, 0), 1.0)
            s_next = jnp.where(inside, pltpu.roll(s, rows - step, 0), 0.0)
            s = p * s_next + s
            p = p * p_next
            step *= 2
        bprod_ref[g] = p
        blocal_ref[g] = s
        sum_ref[g : g + 1, :] = decay[:1, :] * p[:1, :]
        sum_ref[groups + g : groups + g + 1, :] = decay[:1, :] * s[:1, :]


def mixer_backward(flags_ref, bprod_ref, blocal_ref, bin_ref, prod_ref, local_ref, sin_ref,
                   ig_ref, dg_ref, conv_ref, xl_ref, halo_ref, gw_ref, vec_ref, rate_ref,
                   gip_ref, gdp_ref, gx_ref, tail_ref, edge_ref, rows_ref):
    groups, rows, cols = xl_ref.shape
    row = row_iota(rows, cols)
    sums = [jnp.zeros((1, cols), F32) for _ in range(8)]
    tail = tail_ref.shape[1]
    pad = edge_ref.shape[1]
    for g in range(groups):
        start, valid = token_masks(flags_ref, g, rows, cols)
        keep = 1.0 - start
        rate = rate_ref[0:1, :]
        state_in = sin_ref[g : g + 1, :]
        state = local_ref[g] + prod_ref[g] * state_in
        prev = jnp.where(row == 0, state_in, pltpu.roll(state, 1, 0))
        sg = blocal_ref[g] + bprod_ref[g] * bin_ref[g : g + 1, :]
        ig, dg = (ig_ref[g], dg_ref[g])
        cf = conv_ref[g].astype(F32)
        log_decay = -8.0 * dg * rate
        decay = jnp.exp(log_decay) * keep
        scale = jnp.sqrt(keep * neg_expm1(2.0 * log_decay) + start)
        gscale = sg * ig * cf
        glog = sg * prev * decay - gscale * keep * jnp.exp(2.0 * log_decay) / scale
        gip = sg * scale * cf * ig * (1.0 - ig)
        gdp = -8.0 * rate * glog * dg * (1.0 - dg)
        gip_low, gdp_low = (gip.astype(BF16), gdp.astype(BF16))
        gip_ref[g] = gip_low
        gdp_ref[g] = gdp_low
        gconv = sg * scale * ig + lax.dot_general(
            jnp.concatenate([gip_low, gdp_low], axis=1), gw_ref[...],
            (((1,), (1,)), ((), ())), preferred_element_type=F32)
        lagged = shifted_inputs(xl_ref, halo_ref, g)
        spread = jnp.zeros((rows + pad, cols), F32)
        for k in range(4):
            masked = gconv * valid[k]
            sums[k] = sums[k] + jnp.sum(masked * lagged[k], axis=0, keepdims=True)
            full = jnp.concatenate(
                [jnp.zeros((pad, cols), F32), vec_ref[2 + k : 3 + k, :] * masked], axis=0)
            spread = spread + (full if k == 0 else pltpu.roll(full, rows + pad - k, 0))
        gx_ref[g] = spread[pad:].astype(BF16)
        tail_ref[g] = spread[pad + rows - tail :]
        edge_ref[g] = spread[:pad]
        sums[4] = sums[4] + jnp.sum(gconv, axis=0, keepdims=True)
        sums[5] = sums[5] + jnp.sum(gip, axis=0, keepdims=True)
        sums[6] = sums[6] + jnp.sum(gdp, axis=0, keepdims=True)
        sums[7] = sums[7] + jnp.sum(-8.0 * dg * glog, axis=0, keepdims=True) * rate_ref[1:2, :]
    rows_ref[...] = jnp.concatenate(sums, axis=0)


def by_head(body, flags, operands, outs):
    def spec(shape, rows_are_channels):
        if rows_are_channels:
            return pl.BlockSpec((BLK, shape[1]), lambda h: (h, 0))
        lead = shape[:-1]
        return pl.BlockSpec(lead + (BLK,), lambda h: (0,) * len(lead) + (h,))

    heads = outs[0].shape[-1] // BLK
    in_specs = [pl.BlockSpec(memory_space=pltpu.SMEM)]
    values = [flags]
    for value, is_gate in operands:
        in_specs.append(spec(value.shape, is_gate))
        values.append(value)
    size = sum(v.size * v.dtype.itemsize for v in values) + sum(
        o.size * o.dtype.itemsize for o in outs)
    return pl.pallas_call(
        body,
        grid=(heads,),
        in_specs=in_specs,
        out_specs=[spec(o.shape, False) for o in outs],
        out_shape=outs,
        compiler_params=pltpu.CompilerParams(vmem_limit_bytes=48 * 1024 * 1024),
        cost_estimate=work(7),
    )(*values)


def grad_hidden_of(parts, w_down):
    count = len(parts)
    rows, width = parts[0].shape
    total = count * rows
    ff = w_down.shape[1]

    def body(*refs):
        c_refs, (w_ref, out_ref, held, sem) = (refs[:count], refs[count:])

        @pl.when(pl.program_id(0) == 0)
        def _():
            copies = [
                pltpu.make_async_copy(c_refs[i], held.at[pl.ds(i * rows, rows)], sem.at[i])
                for i in range(count)
            ]
            for copy in copies:
                copy.start()
            for copy in copies:
                copy.wait()

        out_ref[...] = dot(held[...], w_ref[...])

    return pl.pallas_call(
        body,
        grid=(pl.cdiv(ff, BLK),),
        in_specs=[ANY] * count + [pl.BlockSpec((width, BLK), lambda j: (0, j))],
        out_specs=pl.BlockSpec((total, BLK), lambda j: (0, j)),
        out_shape=jax.ShapeDtypeStruct((total, ff), F32),
        scratch_shapes=[pltpu.VMEM((total, width), BF16), pltpu.SemaphoreType.DMA((count,))],
        compiler_params=pltpu.CompilerParams(vmem_limit_bytes=VMEM_MAX),
        cost_estimate=work(5 + total // 64),
    )(*parts, w_down)


def sections_of(total):
    found, at = ([], 0)
    while at < total:
        size = min(768, total - at)
        found.append((at, size))
        at += size
    return found


def mlp_forward(n2_parts, grad_hidden, w_gate, w_up):
    count = len(n2_parts)
    rows, width = n2_parts[0].shape
    total = count * rows
    ff = w_gate.shape[1]
    parts = sections_of(ff)
    widest = parts[0][1]
    far = total // 2

    def body(*refs):
        n_refs = refs[:count]
        gh_ref, wg_ref, wu_ref = refs[count : count + 3]
        hid_ref, gg_ref, gu_ref, far_ref, far_c_ref = refs[count + 3 : count + 8]
        n2_s, gh_s, wg_s, wu_s, acc, sem_n, sem_w = refs[count + 8 :]

        def load(k):
            at, size = parts[k]
            slot = k % 2
            return [
                pltpu.make_async_copy(
                    wg_ref.at[:, pl.ds(at, size)], wg_s.at[slot, :, pl.ds(0, size)], sem_w.at[slot, 0]),
                pltpu.make_async_copy(
                    wu_ref.at[:, pl.ds(at, size)], wu_s.at[slot, :, pl.ds(0, size)], sem_w.at[slot, 1]),
                pltpu.make_async_copy(
                    gh_ref.at[:, pl.ds(at, size)], gh_s.at[slot, :, pl.ds(0, size)], sem_w.at[slot, 2]),
            ]

        first = [
            pltpu.make_async_copy(n_refs[i], n2_s.at[pl.ds(i * rows, rows)], sem_n.at[i])
            for i in range(count)
        ]
        for copy in first + load(0):
            copy.start()
        for copy in first:
            copy.wait()
        for k, (at, size) in enumerate(parts):
            if k + 1 < len(parts):
                for copy in load(k + 1):
                    copy.start()
            for copy in load(k):
                copy.wait()
            slot = k % 2
            wg, wu = (wg_s[slot, :, :size], wu_s[slot, :, :size])
            gelu, slope = gelu_pair(dot(n2_s[...], wg))
            up = dot(n2_s[...], wu)
            gh = gh_s[slot, :, :size]
            hid_ref[:, at : at + size] = (gelu * up).astype(BF16)
            gg = (gh * up * slope).astype(BF16)
            gu = (gh * gelu).astype(BF16)
            gg_ref[:, at : at + size] = gg
            gu_ref[:, at : at + size] = gu

            def far_rows(v):
                return jnp.concatenate([v[rows : 2 * rows], v[3 * rows :]], axis=0)

            part = dot_cols(far_rows(gg), wg) + dot_cols(far_rows(gu), wu)
            if k == 0:
                acc[...] = part
            else:
                acc[...] += part
        far_ref[...] = acc[:rows]
        far_c_ref[...] = acc[rows:].astype(BF16)

    act = jax.ShapeDtypeStruct((total, ff), BF16)
    return pl.pallas_call(
        body,
        in_specs=[ANY] * (count + 3),
        out_shape=[act, act, act, jax.ShapeDtypeStruct((rows, width), F32),
                   jax.ShapeDtypeStruct((rows, width), BF16)],
        scratch_shapes=[
            pltpu.VMEM((total, width), BF16),
            pltpu.VMEM((2, total, widest), F32),
            pltpu.VMEM((2, width, widest), BF16),
            pltpu.VMEM((2, width, widest), BF16),
            pltpu.VMEM((far, width), F32),
            pltpu.SemaphoreType.DMA((count,)),
            pltpu.SemaphoreType.DMA((2, 3)),
        ],
        compiler_params=pltpu.CompilerParams(vmem_limit_bytes=VMEM_MAX),
        cost_estimate=work(23),
    )(*n2_parts, grad_hidden, w_gate, w_up)


def mlp_rest(hidden, grad_gate, grad_up, w_gate, w_up, w_down, rows):
    total, ff = hidden.shape
    width = w_gate.shape[0]
    block = 512

    def body(hid_ref, gg_ref, gu_ref, wg_ref, wu_ref, wd_ref, gn_ref, gn_c_ref, out_ref, out_c_ref):
        def near(ref):
            return jnp.concatenate([ref[:rows], ref[2 * rows : 3 * rows]], axis=0)

        gn = dot_cols(near(gg_ref), wg_ref[...]) + dot_cols(near(gu_ref), wu_ref[...])
        gn_ref[...] = gn[:rows]
        gn_c_ref[...] = gn[rows:].astype(BF16)
        out = dot_cols(hid_ref[...], wd_ref[...])
        out_ref[...] = out[: total // 2]
        out_c_ref[...] = out[total // 2 :].astype(BF16)

    whole = pl.BlockSpec((total, ff), lambda j: (0, 0))
    weight = pl.BlockSpec((block, ff), lambda j: (j, 0))
    tall = lambda n: pl.BlockSpec((n, block), lambda j: (0, j))
    shape = lambda n, dt: jax.ShapeDtypeStruct((n, width), dt)
    return pl.pallas_call(
        body,
        grid=(width // block,),
        in_specs=[whole] * 3 + [weight] * 3,
        out_specs=[tall(rows), tall(rows), tall(total // 2), tall(total // 2)],
        out_shape=[shape(rows, F32), shape(rows, BF16), shape(total // 2, F32), shape(total // 2, BF16)],
        compiler_params=pltpu.CompilerParams(vmem_limit_bytes=VMEM_MAX),
        cost_estimate=work(19),
    )(hidden, grad_gate, grad_up, w_gate, w_up, w_down)


def rows_of_tokens(place, parts, rows_out, each):
    tokens, width = parts[0].shape
    half = width // 2
    count = len(parts)

    def body(place_ref, *refs):
        out_ref, turned = (refs[count], refs[count + 1])
        for k in range(count):
            turned[...] = refs[k][...].T
            for i in range(rows_out // each):
                at = pl.multiple_of((2 * i + place_ref[2]) * each, 16)
                out_ref[i * each : (i + 1) * each, k * tokens : (k + 1) * tokens] = turned[pl.ds(at, each), :]

    return pl.pallas_call(
        body,
        grid_spec=pltpu.PrefetchScalarGridSpec(
            num_scalar_prefetch=1,
            grid=(1,),
            in_specs=[pl.BlockSpec((tokens, half), lambda i, place: (0, place[1]))] * count,
            out_specs=pl.BlockSpec((rows_out, count * tokens), lambda i, place: (0, 0)),
            scratch_shapes=[pltpu.VMEM((half, tokens), BF16)],
        ),
        out_shape=jax.ShapeDtypeStruct((rows_out, count * tokens), BF16),
        compiler_params=pltpu.CompilerParams(vmem_limit_bytes=VMEM_MAX),
        cost_estimate=work(5),
    )(place, *parts)


def mlp_weight_grads(place, n2_parts, first_hidden, cot_parts, acts, n2_rows, cot_rows, weights, at, size, each):
    groups = len(n2_parts)
    per = len(n2_parts[0])
    tokens, width = n2_parts[0][0].shape
    group = per * tokens
    both = group // 2
    rows = n2_rows[0].shape[0]
    flat_n = [p for g in n2_parts for p in g]
    flat_c = [p for g in cot_parts for p in g]
    total, total_c = (len(flat_n), len(flat_c))

    def body(place_ref, *refs):
        n_refs, c_refs, refs = (refs[:total], refs[total : total + total_c], refs[total + total_c :])
        gh_ref, wg_ref, wu_ref, wd_ref, hid_ref, gg_ref, gu_ref = refs[:7]
        n_rows, c_rows = (refs[7:11], refs[11:15])
        own_ref, rest_ref, n2_s, cot_s, acc, sem = refs[15:]

        def load(g, slot):
            found = []
            for i in range(per):
                to = pl.ds(i * tokens, tokens)
                found.append(pltpu.make_async_copy(n_refs[g * per + i], n2_s.at[slot, to], sem.at[slot, i]))
                if g > 0:
                    found.append(pltpu.make_async_copy(
                        c_refs[(g - 1) * per + i], cot_s.at[slot, to], sem.at[slot, per + i]))
            return found

        for copy in load(0, 0) + load(1, 1):
            copy.start()

        def add(g, act, fresh):
            fixed = isinstance(g, int)
            start = g * both if fixed else pl.multiple_of((g - 2) * both, both)
            for i, four in enumerate((c_rows, n_rows, n_rows)):
                mine, other = four[:2] if fixed else four[2:]
                part = dot(mine[:, pl.ds(start, both)], act[i][:both]) + dot(
                    other[:, pl.ds(start, both)], act[i][both:])
                if fresh:
                    acc[i] = part
                else:
                    acc[i] += part

        def recompute(g, slot, gh):
            gelu, slope = gelu_pair(dot(n2_s[slot], wg_ref[...]))
            up = dot(n2_s[slot], wu_ref[...])
            add(g + 1, ((gelu * up).astype(BF16), (gh * up * slope).astype(BF16), (gh * gelu).astype(BF16)), False)

        add(0, (hid_ref, gg_ref, gu_ref), True)
        for copy in load(0, 0):
            copy.wait()
        recompute(0, 0, gh_ref[...])

        def step(g, carry):
            slot = lax.rem(g, 2)
            for k in range(2, groups):
                @pl.when(g + 1 == k)
                def _():
                    for copy in load(k, k % 2):
                        copy.start()

            for copy in load(1, slot):
                copy.wait()
            recompute(g, slot, dot(cot_s[slot], wd_ref[...]))
            return carry

        lax.fori_loop(1, groups, step, 0)
        for j in range(rows // each):
            start = pl.multiple_of((place_ref[0] ^ j) * each, 8)
            for i in range(3):
                block = acc[i, pl.ds(start, each), :]
                if j == 0:
                    own_ref[:, i * size : (i + 1) * size] = block
                else:
                    rest_ref[(j - 1) * each : j * each, i * size : (i + 1) * size] = block.astype(BF16)

    index = at // size
    column = lambda n: pl.BlockSpec((n, size), lambda j, place: (0, index))
    whole = pl.BlockSpec(n2_rows[0].shape, lambda j, place: (0, 0))
    return pl.pallas_call(
        body,
        grid_spec=pltpu.PrefetchScalarGridSpec(
            num_scalar_prefetch=1,
            grid=(1,),
            in_specs=[ANY] * (total + total_c) + [column(group)] + [column(width)] * 3 + [column(group)] * 3
            + [whole] * 8,
            out_specs=[pl.BlockSpec((each, 3 * size), lambda j, place: (0, 0)),
                       pl.BlockSpec((rows - each, 3 * size), lambda j, place: (0, 0))],
            scratch_shapes=[
                pltpu.VMEM((2, group, width), BF16),
                pltpu.VMEM((2, group, width), BF16),
                pltpu.VMEM((3, rows, size), F32),
                pltpu.SemaphoreType.DMA((2, 2 * per)),
            ],
        ),
        out_shape=[jax.ShapeDtypeStruct((each, 3 * size), F32),
                   jax.ShapeDtypeStruct((rows - each, 3 * size), BF16)],
        compiler_params=pltpu.CompilerParams(vmem_limit_bytes=VMEM_MAX),
        cost_estimate=work(35 * size // 768),
    )(place, *flat_n, *flat_c, first_hidden, *weights, *acts, *n2_rows, *cot_rows)


def rows_by_device(place, parts, starts, block):
    columns, count = (len(parts), len(parts[0]))
    tokens, n = parts[0][0].shape
    rows = len(starts(0, 0)) * block
    flat = [block_of for column in parts for block_of in column]
    if block % 16:
        turned = [jnp.concatenate(column, axis=0).T for column in parts]
        turned = turned[0] if columns == 1 else jnp.where(
            place[2] == 0, jnp.concatenate(turned), jnp.concatenate(turned[::-1]))

        def taken(dc):
            return jnp.stack([
                jnp.concatenate([
                    lax.dynamic_slice_in_dim(turned, start, block, 0)
                    for start in starts(place[0] ^ dy, place[1] ^ dc)])
                for dy in range(2)])

        kept, sent = (taken(0), taken(1))
        return kept[0], sent[0], jnp.concatenate([kept[1], sent[1]], axis=0)

    def body(place_ref, *refs):
        keep_ref, send_ref, y_ref, turned = refs[len(flat):]
        for h in range(columns):
            base = 0 if columns == 1 else pl.multiple_of((place_ref[2] ^ h) * n, 16)
            for k in range(count):
                turned[pl.ds(base, n), k * tokens : (k + 1) * tokens] = refs[h * count + k][...].T
        for dy, dc, ref, at in ((0, 0, keep_ref, 0), (0, 1, send_ref, 0), (1, 0, y_ref, 0), (1, 1, y_ref, rows)):
            for i, start in enumerate(starts(place_ref[0] ^ dy, place_ref[1] ^ dc)):
                ref[at + i * block : at + (i + 1) * block, :] = turned[pl.ds(pl.multiple_of(start, 16), block), :]

    shape = (rows, count * tokens)
    return pl.pallas_call(
        body,
        grid_spec=pltpu.PrefetchScalarGridSpec(
            num_scalar_prefetch=1,
            grid=(1,),
            in_specs=[pl.BlockSpec((tokens, n), lambda i, place: (0, 0))] * len(flat),
            out_specs=[pl.BlockSpec((n_rows, shape[1]), lambda i, place: (0, 0)) for n_rows in (rows, rows, 2 * rows)],
            scratch_shapes=[pltpu.VMEM((columns * n, count * tokens), BF16)],
        ),
        out_shape=[jax.ShapeDtypeStruct((n_rows, shape[1]), BF16) for n_rows in (rows, rows, 2 * rows)],
        compiler_params=pltpu.CompilerParams(vmem_limit_bytes=VMEM_MAX),
        cost_estimate=work(3),
    )(place, *flat)


def joined_columns(pairs, total, before=None):
    rows = pairs[0][0].shape[0]
    widths = [a.shape[1] // 3 for a, _ in pairs]
    span = sum(widths)
    step = rows // 4 if rows % 64 == 0 else rows
    flat = [term for pair in pairs for term in pair]
    kept = [] if before is None else list(before)
    index = 0 if before is None else total // span - 1

    def body(*refs):
        refs = refs[len(kept) :]
        for i in range(3):
            at = 0
            for k, n in enumerate(widths):
                cols = slice(i * n, (i + 1) * n)
                refs[len(flat) + i][:, at : at + n] = refs[2 * k][:, cols].astype(F32) + refs[
                    2 * k + 1][:, cols].astype(F32)
                at += n

    return pl.pallas_call(
        body,
        grid=(rows // step,),
        in_specs=[ANY] * len(kept) + [pl.BlockSpec((step, term.shape[1]), lambda j: (j, 0)) for term in flat],
        out_specs=[pl.BlockSpec((step, span), lambda j: (j, index))] * 3,
        out_shape=[jax.ShapeDtypeStruct((rows, total), F32)] * 3,
        input_output_aliases={i: i for i in range(len(kept))},
        compiler_params=pltpu.CompilerParams(vmem_limit_bytes=VMEM_MAX),
        cost_estimate=work(5 if kept else 10),
    )(*kept, *flat)


def gate_weight_grad(place, conv, grad_in, grad_decay, block):
    tokens, n = conv.shape
    count = n // block // 2
    if block % 16:
        by_head = lambda v: v.reshape(tokens, n // BLK, BLK)
        blocks = jnp.einsum(
            "thi,thj->hij", by_head(conv), jnp.concatenate([by_head(grad_in), by_head(grad_decay)], 2),
            preferred_element_type=F32).reshape(count, 2, block, 2 * BLK)
        mine, theirs = [
            lax.dynamic_index_in_dim(blocks, core, 1, keepdims=False).reshape(n // 2, 2 * BLK)
            for core in (place[1], 1 - place[1])]
        return mine, theirs.astype(BF16)

    def body(place_ref, conv_ref, in_ref, decay_ref, keep_ref, away_ref, whole):
        for h in range(n // BLK):
            cols = slice(h * BLK, (h + 1) * BLK)
            turned = conv_ref[:, cols].T
            whole[cols, :BLK] = dot(turned, in_ref[:, cols])
            whole[cols, BLK:] = dot(turned, decay_ref[:, cols])
        for i in range(count):
            at = pl.multiple_of((2 * i + place_ref[1]) * block, 16)
            keep_ref[i * block : (i + 1) * block, :] = whole[pl.ds(at, block), :]
            at = pl.multiple_of((2 * i + 1 - place_ref[1]) * block, 16)
            away_ref[i * block : (i + 1) * block, :] = whole[pl.ds(at, block), :].astype(BF16)

    spec = pl.BlockSpec((tokens, n), lambda h, place: (0, 0))
    out = pl.BlockSpec((n // 2, 2 * BLK), lambda h, place: (0, 0))
    return pl.pallas_call(
        body,
        grid_spec=pltpu.PrefetchScalarGridSpec(
            num_scalar_prefetch=1,
            grid=(1,),
            in_specs=[spec] * 3,
            out_specs=[out, out],
            scratch_shapes=[pltpu.VMEM((n, 2 * BLK), F32)],
        ),
        out_shape=[jax.ShapeDtypeStruct((n // 2, 2 * BLK), F32), jax.ShapeDtypeStruct((n // 2, 2 * BLK), BF16)],
        compiler_params=pltpu.CompilerParams(vmem_limit_bytes=VMEM_MAX),
        cost_estimate=work(3),
    )(place, conv, grad_in, grad_decay)


def sum_of_dots(rows, values):
    count = len(rows)

    def body(*refs):
        total = dot(refs[0][...], refs[count][...])
        for k in range(1, count):
            total = total + dot(refs[k][...], refs[count + k][...])
        refs[2 * count][...] = total.astype(BF16)

    return pl.pallas_call(
        body,
        out_shape=jax.ShapeDtypeStruct((rows[0].shape[0], values[0].shape[1]), BF16),
        compiler_params=pltpu.CompilerParams(vmem_limit_bytes=VMEM_MAX),
        cost_estimate=work(5),
    )(*rows, *values)


def after(value, *others):
    return lax.optimization_barrier((value, others))[0]


class Live:
    def cut(self):
        names = sorted(vars(self))
        for name, value in zip(names, lax.optimization_barrier([getattr(self, n) for n in names])):
            setattr(self, name, value)

    def hold(self, **values):
        for name, value in values.items():
            setattr(self, name, value)
        self.cut()


def seq_bits(lay):
    found, bit = ([], 1)
    while bit < lay.seq:
        found.append(bit)
        bit *= 2
    return found


def scan_start(summary, groups):
    prod, state = (summary[:groups], summary[groups : 2 * groups])
    return (prod, state, jnp.ones_like(prod), jnp.zeros_like(state))


def scan_join(lay, held, other, bit, backward):
    prod, state, before_p, before_s = held
    groups = prod.shape[0]
    other_p, other_s = (other[:groups], other[groups:])
    is_later = (lay.seq_at & bit) != 0
    take = jnp.logical_not(is_later) if backward else is_later
    before_s = jnp.where(take, before_p * other_s + before_s, before_s)
    before_p = jnp.where(take, before_p * other_p, before_p)
    state = jnp.where(take, prod * other_s + state, other_p * state + other_s)
    return (prod * other_p, state, before_p, before_s)


def local(inputs, block_flags, decay_seed, vectors, in_y, in_x, gate_weight, out_proj,
          mlp_gate, mlp_up, mlp_down, cotangent):
    lay = Lay()
    nz, x, y, z, c = (lay.nz, lay.x, lay.y, lay.z, lay.c)
    tokens, width = inputs.shape[1:]
    half, quarter, two = (width // 2, width // 4, 2 * tokens)
    each = width // lay.seq
    own80 = each // 4
    bits = seq_bits(lay)
    place = jnp.stack([z % (nz // 2), lay.seq_at // nz, y]).astype(jnp.int32)
    at_yc = jnp.stack([y, c, x]).astype(jnp.int32)
    live = Live()

    def order_c(own, other, axis):
        return jnp.where(c == 0, jnp.concatenate([own, other], axis),
                         jnp.concatenate([other, own], axis))

    def order_f(rel):
        b = rel.shape[-1] // 4
        p = [rel[..., i * b : (i + 1) * b] for i in range(4)]
        by_c = jnp.where(c == 0, rel, jnp.concatenate([p[1], p[0], p[3], p[2]], -1))
        return jnp.where(x == 0, by_c, jnp.concatenate([by_c[..., 2 * b :], by_c[..., : 2 * b]], -1))

    def owner_parts(blocks):
        pick = lambda t: lax.dynamic_index_in_dim(blocks, t, 0, keepdims=False)
        come = [
            lay.send(pick((z + step) % nz), lambda z, y, x, c: ((z + step) % nz, y, x, c))
            for step in range(1, nz)
        ]
        return pick(z), come

    def total_of(own, come):
        total = own.astype(F32)
        for part in come:
            total = total + part.astype(F32)
        return total.astype(BF16)

    def half_of(value, which, n, axis):
        return lax.dynamic_slice_in_dim(value, which * n, n, axis)

    cot = cotangent[0]
    cut = tokens // 2
    gate_away, inputs, gate_weight, out_proj, vectors, decay_seed, block_flags = lax.optimization_barrier(
        (half_of(gate_weight, 1 - x, half, 0), inputs, gate_weight, out_proj, vectors, decay_seed, block_flags))
    halo_raw = lay.over_seq(inputs[0, tokens - 16 :], 1)
    gate_x = lay.over_x(gate_away)
    wx_c = lay.over_c(in_x)
    scaled_one, inverse_one = norm_scale(inputs[0].astype(F32))
    live.hold(n1=(scaled_one * vectors[0]).astype(BF16), inv1=inverse_one, halo_raw=halo_raw, cot_top=cot[:cut],
              cot_low=cot[cut:], wx_c=wx_c,
              params=(gate_weight, out_proj, vectors, decay_seed, block_flags))

    gate_weight, out_proj, vectors, decay_seed, block_flags = live.params
    n1_x = lay.over_x(live.n1)
    halo_own = (norm_scale(live.halo_raw.astype(F32))[0] * vectors[0]).astype(BF16)
    n_flags = block_flags.shape[1]
    flag_row = jnp.pad(block_flags.astype(BF16), ((0, 0), (0, width - n_flags)))
    halo_x = lay.over_x(jnp.concatenate([flag_row, halo_own[1:]], axis=0))
    gate_own = half_of(gate_weight, x, half, 0)
    gate_c = lay.over_c(gate_own)
    cot_z_top = lay.over_z(live.cot_top)
    base = -5.0 - decay_seed.astype(F32) + vectors[9]
    del live.params, live.halo_raw, live.cot_top
    live.hold(
        n1_x=n1_x, halo_x=halo_x, halo_own=halo_own, gate_x=gate_x, gate_c=gate_c, cot_z_top=cot_z_top,
        flags=jnp.concatenate([block_flags.astype(F32), halo_x[:1, :n_flags].astype(F32)], axis=0),
        gate_own=gate_own, out_away=half_of(out_proj, 2 * (1 - x) + y, quarter, 0),
        out_mine=half_of(out_proj, x, half, 0), vec=half_of(vectors, x, half, 1), gain_two=vectors[1],
        gain_one=vectors[0],
        rates=half_of(jnp.stack([jax.nn.softplus(base), jax.nn.sigmoid(base)]), x, half, 1))

    out_a = lay.over_x(live.out_away)
    cot_z_low, cot_y = (lay.over_z(live.cot_low), lay.over_y(after(cot, live.n1_x)))
    wy_c = lay.over_c(after(in_y, live.n1_x))
    gates = order_f(jnp.concatenate(
        [live.gate_own, live.gate_c, live.gate_x, lay.over_c(live.gate_x)], axis=1))
    normed = jnp.concatenate([live.n1, live.n1_x, live.halo_own, live.halo_x], axis=0)
    x_all = order_c(dot(normed, in_x).astype(BF16), dot(normed, live.wx_c).astype(BF16), 1)
    x_low = x_all[:two].reshape(2, tokens, half)
    halo = x_all[two:].reshape(2, 16, half)
    shape3 = lambda dt: jax.ShapeDtypeStruct((2, tokens, half), dt)
    summary_shape = jax.ShapeDtypeStruct((4, half), F32)
    conv_low, ig, dg, prods, local_state, summary = by_head(
        mixer_forward, live.flags,
        [(x_low, False), (halo, False), (gates, True), (live.vec, False), (live.rates, False)],
        [shape3(BF16), shape3(F32), shape3(F32), shape3(F32), shape3(F32), summary_shape])
    del live.gate_x, live.gate_own, live.gate_c, live.halo_own, live.halo_x
    live.hold(x_low=x_low, halo=halo, gates=gates, conv_low=conv_low, ig=ig, dg=dg, prods=prods,
              local_state=local_state, scan=scan_start(summary, 2), cot_y=cot_y, normed=normed[:two], wy_c=wy_c, out_a=out_a,
              cot_z_low=cot_z_low)
    del live.cot_low
    del live.out_away

    def n1_starts(at_y, at_c):
        return [((2 * i + at_y) * 4 + 2 * j + at_c) * own80 for i in range(nz) for j in range(2)]

    for bit in bits:
        come = lay.over_seq_bit(jnp.concatenate(live.scan[:2], axis=0), bit)
        live.scan = scan_join(lay, live.scan, come, bit, False)
        if bit == 1:
            live.cut()
            out_b = lay.over_y(live.out_a)
            out_c = lay.over_c(live.out_mine)
            cot_x = lay.over_x(after(cot, live.scan))
    out_x = jnp.where(y == 0, jnp.concatenate([live.out_a, out_b], 0), jnp.concatenate([out_b, live.out_a], 0))
    y_pre = order_c(dot(live.normed, in_y), dot(live.normed, live.wy_c), 1).reshape(2, tokens, half)
    n1_own, sent, n1_away = rows_by_device(at_yc, [[live.n1, live.n1_x]], n1_starts, own80)
    state_in = live.scan[3]
    del live.scan, live.out_a
    live.hold(state_in=state_in, y_pre=y_pre, out_left=jnp.concatenate([live.out_mine, out_c], axis=1),
              cot_z=jnp.concatenate([live.cot_z_top, live.cot_z_low], axis=0),
              out_x=out_x, cot_x=cot_x, n1_own=n1_own, n1_away=n1_away, n1_c=lay.over_c(sent))
    del live.out_mine, live.cot_z_top, live.cot_z_low

    n1_y = lay.over_y(live.n1_away[: live.n1_own.shape[0]])
    state = live.local_state + live.prods * live.state_in[:, None, :]
    mixed = (state * jax.nn.gelu(live.y_pre, approximate=True)).astype(BF16)
    mixed_two = mixed.reshape(two, half)
    out_right = jnp.concatenate([live.out_x, lay.over_c(live.out_x)], axis=1)
    part = jnp.concatenate([dot(mixed_two, live.out_left), dot(mixed_two, out_right)], axis=1)
    del live.out_x
    live.hold(mixed=mixed, part_own=part[:tokens], part_x=part[tokens:].astype(BF16), out_right=out_right, n1_y=n1_y)

    part_x = lay.over_x(live.part_x)
    cot_xy = lay.over_y(live.cot_x)
    gh_main = grad_hidden_of([cot, live.cot_x, lay.over_c(cot), lay.over_c(live.cot_x)], mlp_down)
    live.hold(part_x=part_x, gh_main=gh_main, cot_xy=cot_xy)

    swapped = jnp.concatenate([live.part_x[:, half:], live.part_x[:, :half]], axis=1)
    mid = inputs[0].astype(F32) + order_f(live.part_own + swapped.astype(F32))
    scaled_two, inverse_two = norm_scale(mid)
    del live.part_x, live.part_own
    live.hold(mid=mid, inv2=inverse_two, n2=(scaled_two * live.gain_two).astype(BF16))

    n2_x = lay.over_x(live.n2)
    n2_y = lay.over_y(live.n2)
    n2_z_top = lay.over_z(live.n2[:cut])
    n2_c = lay.over_c(live.n2)
    pair = [live.cot_y, live.cot_xy]
    gh_y = grad_hidden_of(pair + [lay.over_c(p) for p in pair], mlp_down)
    live.hold(n2_x=n2_x, n2_c=n2_c, n2_y=n2_y, n2_z_top=n2_z_top, gh_y=gh_y)

    live.hold(n2_xc=lay.over_c(live.n2_x), n2_low=live.n2[cut:], n2_x_top=live.n2_x[:cut], n2_x_low=live.n2_x[cut:])
    cot_xz = lay.over_x(live.cot_z)
    n2_xy = lay.over_y(live.n2_x)
    n2_z_low = lay.over_z(live.n2_low)
    hidden, grad_gate, grad_up, far, far_c = mlp_forward(
        [live.n2, live.n2_x, live.n2_c, live.n2_xc], live.gh_main, mlp_gate, mlp_up)
    del live.gh_main, live.n2_c
    live.hold(acts=(hidden, grad_gate, grad_up), far=far, far_c=far_c, cot_xz=cot_xz, n2_xy=n2_xy,
              n2_z_low=n2_z_low)
    live.hold(far=(live.far + lay.over_c(live.far_c).astype(F32)).astype(BF16),
              n2_z=jnp.concatenate([live.n2_z_top, live.n2_z_low], axis=0))

    arriving = lay.over_x(live.far)
    n2_yz, n2_y_c, n2_xy_c = (lay.over_y(live.n2_z), lay.over_c(live.n2_y), lay.over_c(live.n2_xy))
    n2_xz_top = lay.over_z(live.n2_x_top)
    near, near_c, out, out_c = mlp_rest(*live.acts, mlp_gate, mlp_up, mlp_down, tokens)
    del live.far, live.far_c, live.n2_z_top, live.n2_z_low
    live.hold(arriving=arriving, near=near, near_c=near_c, out=out, out_c=out_c, n2_yz=n2_yz, n2_y_c=n2_y_c, n2_xy_c=n2_xy_c, n2_xz_top=n2_xz_top)

    out_c = lay.over_c(live.out_c)
    grad_n2 = live.near + lay.over_c(live.near_c).astype(F32) + live.arriving.astype(F32)
    grad_mid_norm, grad_gain_two = norm_back(grad_n2, live.mid * live.inv2, live.inv2, live.gain_two)
    grad_mid = cot.astype(F32) + grad_mid_norm
    branch = grad_mid.astype(BF16)
    live.out_c = out_c
    del live.near, live.near_c, live.arriving
    live.hold(grad_gain_two=grad_gain_two, grad_mid=grad_mid, branch=branch, branch_rel=order_f(branch))

    arriving = lay.over_x(live.branch_rel)
    n2_xz_low = lay.over_z(live.n2_x_low)
    cot_yz = lay.over_y(live.cot_z)
    live.hold(arriving=arriving, n2_xz_low=n2_xz_low, cot_yz=cot_yz, out_sum=live.out + live.out_c.astype(F32),
              n2_z_c=lay.over_c(live.n2_z), cot_z_c=lay.over_c(live.cot_z),
              n2_rows_ahead=rows_of_tokens(place, [live.n2, live.n2_x, live.n2_y, live.n2_xy], half // 2, each),
              cot_rows_ahead=rows_of_tokens(place, [cot, live.cot_x, live.cot_y, live.cot_xy], half // 2, each))

    rows_each = live.n1_own.shape[0]
    n1_yc = lay.over_y(live.n1_away[rows_each:])
    cot_xz_c, n2_yz_c = (lay.over_c(live.cot_xz), lay.over_c(live.n2_yz))
    mixed_xa = lay.over_x(live.mixed[1])
    branch_x_rel = jnp.concatenate([live.arriving[:, half:], live.arriving[:, :half]], axis=1)
    both_rel = jnp.concatenate([live.branch_rel, branch_x_rel], 0)
    grad_mixed = dot_cols(both_rel[:, :half], live.out_left) + dot_cols(both_rel[:, half:], live.out_right)
    gy, bprod, blocal, back_summary = by_head(
        mixer_back_scan, live.flags,
        [(grad_mixed.reshape(2, tokens, half), False), (live.y_pre, False), (live.dg, False),
         (live.prods, False), (live.local_state, False), (live.state_in, False), (live.rates, False)],
        [shape3(BF16), shape3(F32), shape3(F32), summary_shape])
    del live.arriving, live.branch_rel, live.y_pre
    live.hold(gy=gy.reshape(two, half), bprod=bprod, blocal=blocal, scan=scan_start(back_summary, 2),
              branch_x_rel=branch_x_rel, n1_yc=n1_yc, cot_xz_c=cot_xz_c, n2_yz_c=n2_yz_c,
              mixed_xa=mixed_xa, mixed_b=live.mixed[0])

    n2_xyz = lay.over_x(live.n2_yz)
    own_cols = lambda value, which: half_of(value, which, quarter, 1)
    part_y = dot_cols(own_cols(live.gy, c), in_y) + dot_cols(own_cols(live.gy, 1 - c), live.wy_c)
    for bit in bits:
        come = lay.over_seq_bit(jnp.concatenate(live.scan[:2], axis=0), bit)
        live.scan = scan_join(lay, live.scan, come, bit, True)
        if bit == 1:
            live.cut()
            cot_xyz = lay.over_y(live.cot_xz)
            cot_yz_c = lay.over_c(live.cot_yz)
    back_in = live.scan[3]
    del live.scan
    live.hold(back_in=back_in, cot_xyz=cot_xyz, n2_xyz=n2_xyz, part_y=part_y, cot_yz_c=cot_yz_c)

    live.ahead_c = (lay.over_c(live.n2_rows_ahead), lay.over_c(live.cot_rows_ahead))
    live.n1_yc = lay.over_c(live.n1_yc)
    gip, gdp, gx_main, gx_tail, edge, vec_rows = by_head(
        mixer_backward, live.flags,
        [(live.bprod, False), (live.blocal, False), (live.back_in, False), (live.prods, False),
         (live.local_state, False), (live.state_in, False), (live.ig, False), (live.dg, False),
         (live.conv_low, False), (live.x_low, False), (live.halo, False), (live.gates, True),
         (live.vec, False), (live.rates, False)],
        [shape3(BF16), shape3(BF16), shape3(BF16), jax.ShapeDtypeStruct((2, 16, half), F32),
         jax.ShapeDtypeStruct((2, 8, half), F32), jax.ShapeDtypeStruct((8, half), F32)])
    for name in ("bprod", "blocal", "back_in", "prods", "local_state", "state_in", "ig", "dg", "x_low", "halo",
                 "gates", "vec", "rates", "flags"):
        delattr(live, name)
    live.hold(gip=gip, gdp=gdp, gx_main=gx_main, gx_tail=gx_tail, edge=edge, vec_rows=vec_rows)

    edge_next = lay.over_seq(live.edge, -1)
    mixed_xb = lay.over_x(live.mixed_b)
    n2_xz = jnp.concatenate([live.n2_xz_top, live.n2_xz_low], axis=0)
    n2_xz_c, n2_xyz_c, cot_xyz_c = (lay.over_c(n2_xz), lay.over_c(live.n2_xyz), lay.over_c(live.cot_xyz))
    live.n2s = [[live.n2, live.n2_x], [live.n2_y, live.n2_xy], [live.n2_z, n2_xz], [live.n2_yz, live.n2_xyz]]
    live.cots = [cot, live.cot_x, live.cot_y, live.cot_xy, live.cot_z, live.cot_xz, live.cot_yz, live.cot_xyz]
    n2_rows = rows_of_tokens(place, [p for group in live.n2s[2:] for p in group], half // 2, each)
    cot_rows = rows_of_tokens(place, live.cots[4:], half // 2, each)
    del live.edge
    live.hold(edge_next=edge_next, n2_rows=n2_rows, cot_rows=cot_rows,
              n2s_c=[[live.n2_y_c, live.n2_xy_c], [live.n2_z_c, n2_xz_c], [live.n2_yz_c, n2_xyz_c]],
              cots_c=[live.cot_z_c, live.cot_xz_c, live.cot_yz_c, cot_xyz_c], mixed_xb=mixed_xb)

    gx_last = (live.gx_tail + jnp.pad(live.edge_next, ((0, 0), (8, 0), (0, 0)))).astype(BF16)
    gx = jnp.concatenate([live.gx_main[:, : tokens - 16], gx_last], axis=1).reshape(two, half)
    gx_o, gx_c = (own_cols(gx, c), own_cols(gx, 1 - c))
    part_n1 = live.part_y + dot_cols(gx_o, in_x) + dot_cols(gx_c, live.wx_c)
    del live.gx_main, live.gx_tail, live.edge_next, live.part_y
    live.hold(gx=gx, n1_near=part_n1[:tokens], n1_far=part_n1[tokens:].astype(BF16),
              n2_rows_c=lay.over_c(live.n2_rows), cot_rows_c=lay.over_c(live.cot_rows))

    cuts = sections_of(mlp_gate.shape[1])

    def weight_piece(at, size):
        return mlp_weight_grads(
            place, [a + b for a, b in zip(live.n2s[1:], live.n2s_c)], live.gh_y,
            [live.cots[4:6] + live.cots_c[:2], live.cots[6:] + live.cots_c[2:]], live.acts,
            (live.n2_rows_ahead, live.ahead_c[0], live.n2_rows, live.n2_rows_c),
            (live.cot_rows_ahead, live.ahead_c[1], live.cot_rows, live.cot_rows_c),
            (mlp_gate, mlp_up, mlp_down), at, size, each)

    def piece_sum(own, rest):
        blocks = [own] + [rest[j * each : (j + 1) * each] for j in range(nz // 2 - 1)]
        bit = nz // 4
        while bit >= 1:
            gone = blocks[bit] if bit == 1 else jnp.concatenate(
                [b.astype(BF16) for b in blocks[bit : 2 * bit]], axis=0)
            come = lay.over_seq_bit(gone.astype(BF16), 2 * bit)
            blocks = [(blocks[j], come[j * each : (j + 1) * each]) for j in range(bit)]
            if bit > 1:
                blocks = [a.astype(F32) + b.astype(F32) for a, b in blocks]
            bit //= 2
        return blocks[0]

    arriving = lay.over_x(live.n1_far)
    gy_y = lay.over_y(live.gy)
    live.gy_c = lay.over_c(live.gy)
    live.hold(piece_a=weight_piece(*cuts[0]), arriving=arriving, gy_y=gy_y)

    grad_n1 = live.n1_near + live.arriving.astype(F32)
    scaled_one = inputs[0].astype(F32) * live.inv1
    grad_in_norm, grad_gain_one = norm_back(grad_n1, scaled_one, live.inv1, live.gain_one)
    input_grad = (live.grad_mid + grad_in_norm).astype(BF16)[None]
    rows_full = lax.dynamic_update_slice_in_dim(
        jnp.zeros((8, width), F32), live.vec_rows, x * half, 1)
    sums = jnp.concatenate([grad_gain_one[None], live.grad_gain_two[None], rows_full], axis=0)
    sums = sums + lay.over_c(sums)
    del live.n1_near, live.n1_far, live.arriving, live.vec_rows, live.grad_gain_two, live.grad_mid
    branch_far = half_of(order_f(live.branch_x_rel), x, half, 1)
    branch_near = half_of(live.branch, x, half, 1)
    del live.branch_x_rel
    live.hold(sums=sums, gy_yc=lay.over_c(live.gy_y), branch_two=jnp.concatenate([branch_near, branch_far], axis=0))

    def over_columns(value):
        split = value.reshape(2, own80, half)
        mine = lax.dynamic_index_in_dim(split, x, 0, keepdims=False)
        theirs = lay.over_x(lax.dynamic_index_in_dim(split, 1 - x, 0, keepdims=False))
        return jnp.where(x == 0, jnp.concatenate([mine, theirs], -1),
                         jnp.concatenate([theirs, mine], -1)).astype(F32)

    sums = live.sums + lay.over_x(live.sums)
    branch_two_y = lay.over_y(live.branch_two)
    sum_a = piece_sum(*live.piece_a)
    n1_all = [live.n1_own, live.n1_c, live.n1_y, live.n1_yc]
    in_y_part = sum_of_dots(n1_all, [live.gy, live.gy_c, live.gy_y, live.gy_yc])
    gate_part, gate_away = gate_weight_grad(
        at_yc, live.conv_low.reshape(two, half), live.gip.reshape(two, half), live.gdp.reshape(two, half), own80)
    gate_part = (gate_part + lay.over_c(gate_away).astype(F32)).reshape(2, nz, own80, 2 * BLK)
    pick = lambda value, at, axis: lax.dynamic_index_in_dim(value, at, axis, keepdims=False)
    gate_y = lay.over_y(pick(gate_part, 1 - y, 0).astype(BF16))
    mixed_own, sent, mixed_away = rows_by_device(
        at_yc, [[live.mixed[0], live.mixed[1]], [live.mixed_xa, live.mixed_xb]], n1_starts, own80)
    del live.gy, live.gy_c, live.gy_y, live.gy_yc, live.mixed, live.mixed_xa, live.mixed_xb, live.conv_low, live.gip, live.gdp
    live.hold(in_y_part=in_y_part, sums=sums, sum_a=sum_a, branch_two_y=branch_two_y, gate_keep=pick(gate_part, y, 0), gate_y=gate_y,
              mixed_own=mixed_own, mixed_away=mixed_away, mixed_c=lay.over_c(sent),
              gx_c=lay.over_c(live.gx), branch_c=lay.over_c(live.branch_two))

    in_y_own, in_y_come = owner_parts(live.in_y_part.reshape(nz, 2 * own80, half))
    gx_y = lay.over_y(live.gx)
    mixed_y = lay.over_y(live.mixed_away)
    piece_b = weight_piece(*cuts[1])
    del live.piece_a, live.mixed_away
    del live.in_y_part
    live.hold(piece_b=piece_b, gx_y=gx_y, mixed_y=mixed_y, in_y_own=in_y_own, in_y_come=in_y_come)

    sum_b = piece_sum(*live.piece_b)
    sums = live.sums
    for bit in bits[:1]:
        sums = sums + lay.over_seq_bit(sums, bit)
    in_x_part = sum_of_dots(n1_all, [live.gx, live.gx_c, live.gx_y, lay.over_c(live.gx_y)])
    out_part = sum_of_dots(
        [live.mixed_own, live.mixed_c, live.mixed_y[:rows_each], lay.over_c(live.mixed_y[rows_each:])],
        [live.branch_two, live.branch_c, live.branch_two_y, lay.over_c(live.branch_two_y)])
    gate_part = (live.gate_keep + live.gate_y.astype(F32)).astype(BF16)
    del live.piece_b, live.gate_keep, live.gate_y, live.mixed_own, live.mixed_c, live.mixed_y
    live.hold(in_x_part=jnp.concatenate(
        [in_x_part.reshape(nz, 2 * own80, half), gate_part.reshape(nz, own80 * 2 * BLK // half, half)], axis=1),
        out_part=out_part, sum_b=sum_b, sums=sums, in_y_total=total_of(live.in_y_own, live.in_y_come),
        out_far=live.out_sum[tokens:].astype(BF16))
    del live.in_y_own, live.in_y_come

    in_x_own, in_x_come = owner_parts(live.in_x_part)
    out_arriving = lay.over_x(live.out_far)
    sums_z = lay.over_seq_bit(live.sums, 2)
    piece_c = weight_piece(*cuts[2])
    del live.in_x_part
    live.hold(piece_c=piece_c, in_x_own=in_x_own, in_x_come=in_x_come, out_arriving=out_arriving,
              sums=live.sums + sums_z)

    sum_c = piece_sum(*live.piece_c)
    out_own, out_come = owner_parts(live.out_part.reshape(nz, 2 * own80, half))
    in_x_own, in_x_come, in_y_total = after((live.in_x_own, live.in_x_come, live.in_y_total), out_come[1])
    in_x_total = total_of(in_x_own, in_x_come)
    mlp_grads = joined_columns([live.sum_a, live.sum_b], mlp_gate.shape[1])
    live.hold(sum_c=sum_c, mlp_grads=mlp_grads, out_total=total_of(out_own, out_come),
              in_y_grad=over_columns(in_y_total), in_x_grad=over_columns(in_x_total[: 2 * own80]),
              gate_total=in_x_total[2 * own80 :].reshape(own80, 2 * BLK),
              output=(live.mid + after(live.out_sum, out_come[1])[:tokens] + live.out_arriving.astype(F32)
                      ).astype(BF16)[None])

    sums = live.sums
    for bit in bits[2:]:
        sums = sums + lay.over_seq_bit(sums, bit)
    mlp_down_grad, mlp_gate_grad, mlp_up_grad = joined_columns(
        [live.sum_c], mlp_gate.shape[1], live.mlp_grads)

    def final(z, y, x, c):
        at = ((x * 2 + y) * nz + z) * 2 + c
        s, f = (at // 4, at % 4)
        return (s // 2, s % 2, f // 2, f % 2)

    out_grad = over_columns(live.out_total)
    gate_grad = lay.send(live.gate_total, final).astype(F32)
    return (live.output, input_grad, sums, live.in_y_grad, live.in_x_grad, gate_grad, out_grad,
            mlp_gate_grad, mlp_up_grad, mlp_down_grad)


def solution(mesh):
    return jax.shard_map(
        local,
        mesh=mesh,
        in_specs=(
            P("fsdp", "seq", None),
            P("fsdp", "seq"),
            P(),
            P(),
            P(None, "fsdp"),
            P(None, "fsdp"),
            P(None, "fsdp"),
            P(None, "fsdp"),
            P(None, "fsdp"),
            P(None, "fsdp"),
            P(None, "fsdp"),
            P("fsdp", "seq", None),
        ),
        out_specs=(
            P("fsdp", "seq", None),
            P("fsdp", "seq", None),
            P(),
            P(("seq", "fsdp"), None),
            P(("seq", "fsdp"), None),
            P(("seq", "fsdp"), None),
            P(("seq", "fsdp"), None),
            P("seq", "fsdp"),
            P("seq", "fsdp"),
            P("seq", "fsdp"),
        ),
        check_vma=False,
    )
```

```python
import functools

import jax
import jax.numpy as jnp
from jax import lax
from jax.experimental import pallas as pl
from jax.experimental.pallas import tpu as pltpu
from jax.sharding import PartitionSpec as P

HEADS = 10
BLK = 256
FBLK = 64
EPS = 1e-06
ALL = ("seq", "fsdp")
F32 = jnp.float32
BF16 = jnp.bfloat16
GELU_C = 0.7978845608028654
GELU_A = 0.044715
VMEM_MAX = 60 * 1024 * 1024
ANY = pl.BlockSpec(memory_space=pl.ANY)


def work(us):
    scale = 1000 if us >= 10 else 0
    return pl.CostEstimate(flops=1 + us * scale * 900000, bytes_accessed=1 + us * scale * 2000, transcendentals=0)


def norm_scale(values):
    inverse = lax.rsqrt(jnp.mean(values * values, axis=-1, keepdims=True) + EPS)
    return (values * inverse, inverse)


def norm_back(grad_normed, scaled, inverse, gain_row):
    grad_gain = jnp.sum(grad_normed * scaled, axis=0)
    inner_term = grad_normed * gain_row
    grad_input = inverse * (
        inner_term - scaled * jnp.mean(inner_term * scaled, axis=-1, keepdims=True)
    )
    return (grad_input, grad_gain)


def gelu_pair(values):
    square = values * values
    t = jnp.tanh(values * (GELU_C + GELU_C * GELU_A * square))
    half = 0.5 + 0.5 * t
    slope = half * (1.0 + (1.0 - t) * values * (GELU_C + 3.0 * GELU_C * GELU_A * square))
    return (values * half, slope)


def dot(left, right):
    return jnp.dot(left, right, preferred_element_type=F32)


def dot_rows(left, right):
    return lax.dot_general(left, right, (((0,), (0,)), ((), ())), preferred_element_type=F32)


def dot_cols(left, right):
    return lax.dot_general(left, right, (((1,), (1,)), ((), ())), preferred_element_type=F32)


class Lay:
    def __init__(self):
        self.seq = lax.axis_size("seq")
        self.nz = self.seq // 2
        seq, fsdp = (lax.axis_index("seq"), lax.axis_index("fsdp"))
        self.z, self.y = (seq // 2, seq % 2)
        self.x, self.c = (fsdp // 2, fsdp % 2)
        self.seq_at = seq

    def pairs(self, target):
        found = []
        for s in range(self.seq):
            for f in range(4):
                z, y, x, c = (s // 2, s % 2, f // 2, f % 2)
                to = target(z, y, x, c)
                if to is not None:
                    found.append((s * 4 + f, ((to[0] * 2 + to[1]) * 2 + to[2]) * 2 + to[3]))
        return found

    def send(self, value, target):
        return lax.ppermute(value, ALL, self.pairs(target))

    def over_c(self, value):
        return self.send(value, lambda z, y, x, c: (z, y, x, 1 - c))

    def over_x(self, value):
        return self.send(value, lambda z, y, x, c: (z, y, 1 - x, c))

    def over_y(self, value):
        return self.send(value, lambda z, y, x, c: (z, 1 - y, x, c))

    def over_seq_bit(self, value, bit):
        def to(z, y, x, c):
            other = (2 * z + y) ^ bit
            return (other // 2, other % 2, x, c)

        return self.send(value, to)

    def over_z(self, value):
        return self.send(value, lambda z, y, x, c: (self.nz - 1 - z, y, x, c))

    def over_seq(self, value, by):
        def to(z, y, x, c):
            other = 2 * z + y + by
            return (other // 2, other % 2, x, c) if 0 <= other < self.seq else None

        return self.send(value, to)


def row_iota(rows, cols):
    return lax.broadcasted_iota(jnp.int32, (rows, cols), 0)


def token_masks(flags_ref, g, rows, cols):
    row = row_iota(rows, cols)
    block = row // FBLK
    offset = row % FBLK
    flagged = jnp.zeros((rows, cols), F32)
    for b in range(rows // FBLK):
        flagged = jnp.where(block == b, flags_ref[g, b], flagged)
    valid = [jnp.where(offset < lag, 1.0 - flagged, 1.0) for lag in range(4)]
    start = jnp.where(offset == 0, flagged, 0.0)
    return start, valid


def neg_expm1(v):
    series = 1.0 + v * (1.0 / 6.0)
    for n in (5.0, 4.0, 3.0, 2.0):
        series = 1.0 + v * (1.0 / n) * series
    return jnp.where(v > -0.25, -v * series, 1.0 - jnp.exp(v))


def shifted_inputs(xl_ref, halo_ref, g):
    ext = jnp.concatenate([halo_ref[g].astype(F32), xl_ref[g].astype(F32)], axis=0)
    pad = halo_ref.shape[1]
    return [ext[pad:] if k == 0 else pltpu.roll(ext, k, 0)[pad:] for k in range(4)]


def mixer_forward(flags_ref, xl_ref, halo_ref, gw_ref, vec_ref, rate_ref,
                  conv_ref, ig_ref, dg_ref, prod_ref, local_ref, sum_ref):
    groups, rows, cols = xl_ref.shape
    row = row_iota(rows, cols)
    for g in range(groups):
        start, valid = token_masks(flags_ref, g, rows, cols)
        lagged = shifted_inputs(xl_ref, halo_ref, g)
        conv = vec_ref[6:7, :] + jnp.zeros((rows, cols), F32)
        for k in range(4):
            conv = conv + vec_ref[2 + k : 3 + k, :] * lagged[k] * valid[k]
        conv_low = conv.astype(BF16)
        conv_ref[g] = conv_low
        prod = jnp.dot(conv_low, gw_ref[...], preferred_element_type=F32)
        ig = jax.nn.sigmoid(prod[:, :cols] + vec_ref[7:8, :])
        dg = jax.nn.sigmoid(prod[:, cols:] + vec_ref[8:9, :])
        ig_ref[g] = ig
        dg_ref[g] = dg
        keep = 1.0 - start
        log_decay = -8.0 * dg * rate_ref[0:1, :]
        p = jnp.exp(log_decay) * keep
        s = jnp.sqrt(keep * neg_expm1(2.0 * log_decay) + start) * ig * conv_low.astype(F32)
        step = 1
        while step < rows:
            inside = row >= step
            p_prev = jnp.where(inside, pltpu.roll(p, step, 0), 1.0)
            s_prev = jnp.where(inside, pltpu.roll(s, step, 0), 0.0)
            s = p * s_prev + s
            p = p * p_prev
            step *= 2
        prod_ref[g] = p
        local_ref[g] = s
        sum_ref[g : g + 1, :] = p[rows - 1 :, :]
        sum_ref[groups + g : groups + g + 1, :] = s[rows - 1 :, :]


def mixer_back_scan(flags_ref, gm_ref, y_ref, dg_ref, prod_ref, local_ref, sin_ref, rate_ref,
                    gy_ref, bprod_ref, blocal_ref, sum_ref):
    groups, rows, cols = gm_ref.shape
    row = row_iota(rows, cols)
    for g in range(groups):
        start, _ = token_masks(flags_ref, g, rows, cols)
        state = local_ref[g] + prod_ref[g] * sin_ref[g : g + 1, :]
        gelu, slope = gelu_pair(y_ref[g])
        gm = gm_ref[g]
        gy_ref[g] = (gm * state * slope).astype(BF16)
        decay = jnp.exp(-8.0 * dg_ref[g] * rate_ref[0:1, :]) * (1.0 - start)
        s = gm * gelu
        p = jnp.where(row == rows - 1, 1.0, pltpu.roll(decay, rows - 1, 0))
        step = 1
        while step < rows:
            inside = row < rows - step
            p_next = jnp.where(inside, pltpu.roll(p, rows - step, 0), 1.0)
            s_next = jnp.where(inside, pltpu.roll(s, rows - step, 0), 0.0)
            s = p * s_next + s
            p = p * p_next
            step *= 2
        bprod_ref[g] = p
        blocal_ref[g] = s
        sum_ref[g : g + 1, :] = decay[:1, :] * p[:1, :]
        sum_ref[groups + g : groups + g + 1, :] = decay[:1, :] * s[:1, :]


def mixer_backward(flags_ref, bprod_ref, blocal_ref, bin_ref, prod_ref, local_ref, sin_ref,
                   ig_ref, dg_ref, conv_ref, xl_ref, halo_ref, gw_ref, vec_ref, rate_ref,
                   gip_ref, gdp_ref, gx_ref, tail_ref, edge_ref, rows_ref):
    groups, rows, cols = xl_ref.shape
    row = row_iota(rows, cols)
    sums = [jnp.zeros((1, cols), F32) for _ in range(8)]
    tail = tail_ref.shape[1]
    pad = edge_ref.shape[1]
    for g in range(groups):
        start, valid = token_masks(flags_ref, g, rows, cols)
        keep = 1.0 - start
        rate = rate_ref[0:1, :]
        state_in = sin_ref[g : g + 1, :]
        state = local_ref[g] + prod_ref[g] * state_in
        prev = jnp.where(row == 0, state_in, pltpu.roll(state, 1, 0))
        sg = blocal_ref[g] + bprod_ref[g] * bin_ref[g : g + 1, :]
        ig, dg = (ig_ref[g], dg_ref[g])
        cf = conv_ref[g].astype(F32)
        log_decay = -8.0 * dg * rate
        decay = jnp.exp(log_decay) * keep
        scale = jnp.sqrt(keep * neg_expm1(2.0 * log_decay) + start)
        gscale = sg * ig * cf
        glog = sg * prev * decay - gscale * keep * jnp.exp(2.0 * log_decay) / scale
        gip = sg * scale * cf * ig * (1.0 - ig)
        gdp = -8.0 * rate * glog * dg * (1.0 - dg)
        gip_low, gdp_low = (gip.astype(BF16), gdp.astype(BF16))
        gip_ref[g] = gip_low
        gdp_ref[g] = gdp_low
        gconv = sg * scale * ig + lax.dot_general(
            jnp.concatenate([gip_low, gdp_low], axis=1), gw_ref[...],
            (((1,), (1,)), ((), ())), preferred_element_type=F32)
        lagged = shifted_inputs(xl_ref, halo_ref, g)
        spread = jnp.zeros((rows + pad, cols), F32)
        for k in range(4):
            masked = gconv * valid[k]
            sums[k] = sums[k] + jnp.sum(masked * lagged[k], axis=0, keepdims=True)
            full = jnp.concatenate(
                [jnp.zeros((pad, cols), F32), vec_ref[2 + k : 3 + k, :] * masked], axis=0)
            spread = spread + (full if k == 0 else pltpu.roll(full, rows + pad - k, 0))
        gx_ref[g] = spread[pad:].astype(BF16)
        tail_ref[g] = spread[pad + rows - tail :]
        edge_ref[g] = spread[:pad]
        sums[4] = sums[4] + jnp.sum(gconv, axis=0, keepdims=True)
        sums[5] = sums[5] + jnp.sum(gip, axis=0, keepdims=True)
        sums[6] = sums[6] + jnp.sum(gdp, axis=0, keepdims=True)
        sums[7] = sums[7] + jnp.sum(-8.0 * dg * glog, axis=0, keepdims=True) * rate_ref[1:2, :]
    rows_ref[...] = jnp.concatenate(sums, axis=0)


def by_head(body, flags, operands, outs):
    def spec(shape, rows_are_channels):
        if rows_are_channels:
            return pl.BlockSpec((BLK, shape[1]), lambda h: (h, 0))
        lead = shape[:-1]
        return pl.BlockSpec(lead + (BLK,), lambda h: (0,) * len(lead) + (h,))

    heads = outs[0].shape[-1] // BLK
    in_specs = [pl.BlockSpec(memory_space=pltpu.SMEM)]
    values = [flags]
    for value, is_gate in operands:
        in_specs.append(spec(value.shape, is_gate))
        values.append(value)
    size = sum(v.size * v.dtype.itemsize for v in values) + sum(
        o.size * o.dtype.itemsize for o in outs)
    return pl.pallas_call(
        body,
        grid=(heads,),
        in_specs=in_specs,
        out_specs=[spec(o.shape, False) for o in outs],
        out_shape=outs,
        compiler_params=pltpu.CompilerParams(vmem_limit_bytes=48 * 1024 * 1024),
        cost_estimate=work(7),
    )(*values)


def grad_hidden_of(parts, w_down):
    count = len(parts)
    rows, width = parts[0].shape
    total = count * rows
    ff = w_down.shape[1]

    def body(*refs):
        c_refs, (w_ref, out_ref, held, sem) = (refs[:count], refs[count:])

        @pl.when(pl.program_id(0) == 0)
        def _():
            copies = [
                pltpu.make_async_copy(c_refs[i], held.at[pl.ds(i * rows, rows)], sem.at[i])
                for i in range(count)
            ]
            for copy in copies:
                copy.start()
            for copy in copies:
                copy.wait()

        out_ref[...] = dot(held[...], w_ref[...])

    return pl.pallas_call(
        body,
        grid=(pl.cdiv(ff, BLK),),
        in_specs=[ANY] * count + [pl.BlockSpec((width, BLK), lambda j: (0, j))],
        out_specs=pl.BlockSpec((total, BLK), lambda j: (0, j)),
        out_shape=jax.ShapeDtypeStruct((total, ff), F32),
        scratch_shapes=[pltpu.VMEM((total, width), BF16), pltpu.SemaphoreType.DMA((count,))],
        compiler_params=pltpu.CompilerParams(vmem_limit_bytes=VMEM_MAX),
        cost_estimate=work(5 + total // 64),
    )(*parts, w_down)


def sections_of(total):
    found, at = ([], 0)
    while at < total:
        size = min(768, total - at)
        found.append((at, size))
        at += size
    return found


def mlp_forward(n2_parts, grad_hidden, w_gate, w_up):
    count = len(n2_parts)
    rows, width = n2_parts[0].shape
    total = count * rows
    ff = w_gate.shape[1]
    parts = sections_of(ff)
    widest = parts[0][1]
    far = total // 2

    def body(*refs):
        n_refs = refs[:count]
        gh_ref, wg_ref, wu_ref = refs[count : count + 3]
        hid_ref, gg_ref, gu_ref, far_ref, far_c_ref = refs[count + 3 : count + 8]
        n2_s, gh_s, wg_s, wu_s, acc, sem_n, sem_w = refs[count + 8 :]

        def load(k):
            at, size = parts[k]
            slot = k % 2
            return [
                pltpu.make_async_copy(
                    wg_ref.at[:, pl.ds(at, size)], wg_s.at[slot, :, pl.ds(0, size)], sem_w.at[slot, 0]),
                pltpu.make_async_copy(
                    wu_ref.at[:, pl.ds(at, size)], wu_s.at[slot, :, pl.ds(0, size)], sem_w.at[slot, 1]),
                pltpu.make_async_copy(
                    gh_ref.at[:, pl.ds(at, size)], gh_s.at[slot, :, pl.ds(0, size)], sem_w.at[slot, 2]),
            ]

        first = [
            pltpu.make_async_copy(n_refs[i], n2_s.at[pl.ds(i * rows, rows)], sem_n.at[i])
            for i in range(count)
        ]
        for copy in first + load(0):
            copy.start()
        for copy in first:
            copy.wait()
        for k, (at, size) in enumerate(parts):
            if k + 1 < len(parts):
                for copy in load(k + 1):
                    copy.start()
            for copy in load(k):
                copy.wait()
            slot = k % 2
            wg, wu = (wg_s[slot, :, :size], wu_s[slot, :, :size])
            gelu, slope = gelu_pair(dot(n2_s[...], wg))
            up = dot(n2_s[...], wu)
            gh = gh_s[slot, :, :size]
            hid_ref[:, at : at + size] = (gelu * up).astype(BF16)
            gg = (gh * up * slope).astype(BF16)
            gu = (gh * gelu).astype(BF16)
            gg_ref[:, at : at + size] = gg
            gu_ref[:, at : at + size] = gu

            def far_rows(v):
                return jnp.concatenate([v[rows : 2 * rows], v[3 * rows :]], axis=0)

            part = dot_cols(far_rows(gg), wg) + dot_cols(far_rows(gu), wu)
            if k == 0:
                acc[...] = part
            else:
                acc[...] += part
        far_ref[...] = acc[:rows]
        far_c_ref[...] = acc[rows:].astype(BF16)

    act = jax.ShapeDtypeStruct((total, ff), BF16)
    return pl.pallas_call(
        body,
        in_specs=[ANY] * (count + 3),
        out_shape=[act, act, act, jax.ShapeDtypeStruct((rows, width), F32),
                   jax.ShapeDtypeStruct((rows, width), BF16)],
        scratch_shapes=[
            pltpu.VMEM((total, width), BF16),
            pltpu.VMEM((2, total, widest), F32),
            pltpu.VMEM((2, width, widest), BF16),
            pltpu.VMEM((2, width, widest), BF16),
            pltpu.VMEM((far, width), F32),
            pltpu.SemaphoreType.DMA((count,)),
            pltpu.SemaphoreType.DMA((2, 3)),
        ],
        compiler_params=pltpu.CompilerParams(vmem_limit_bytes=VMEM_MAX),
        cost_estimate=work(23),
    )(*n2_parts, grad_hidden, w_gate, w_up)


def mlp_rest(hidden, grad_gate, grad_up, w_gate, w_up, w_down, rows):
    total, ff = hidden.shape
    width = w_gate.shape[0]
    block = 512

    def body(hid_ref, gg_ref, gu_ref, wg_ref, wu_ref, wd_ref, gn_ref, gn_c_ref, out_ref, out_c_ref):
        def near(ref):
            return jnp.concatenate([ref[:rows], ref[2 * rows : 3 * rows]], axis=0)

        gn = dot_cols(near(gg_ref), wg_ref[...]) + dot_cols(near(gu_ref), wu_ref[...])
        gn_ref[...] = gn[:rows]
        gn_c_ref[...] = gn[rows:].astype(BF16)
        out = dot_cols(hid_ref[...], wd_ref[...])
        out_ref[...] = out[: total // 2]
        out_c_ref[...] = out[total // 2 :].astype(BF16)

    whole = pl.BlockSpec((total, ff), lambda j: (0, 0))
    weight = pl.BlockSpec((block, ff), lambda j: (j, 0))
    tall = lambda n: pl.BlockSpec((n, block), lambda j: (0, j))
    shape = lambda n, dt: jax.ShapeDtypeStruct((n, width), dt)
    return pl.pallas_call(
        body,
        grid=(width // block,),
        in_specs=[whole] * 3 + [weight] * 3,
        out_specs=[tall(rows), tall(rows), tall(total // 2), tall(total // 2)],
        out_shape=[shape(rows, F32), shape(rows, BF16), shape(total // 2, F32), shape(total // 2, BF16)],
        compiler_params=pltpu.CompilerParams(vmem_limit_bytes=VMEM_MAX),
        cost_estimate=work(19),
    )(hidden, grad_gate, grad_up, w_gate, w_up, w_down)


def rows_of_tokens(place, parts, rows_out, each):
    tokens, width = parts[0].shape
    half = width // 2
    count = len(parts)

    def body(place_ref, *refs):
        out_ref, turned = (refs[count], refs[count + 1])
        for k in range(count):
            turned[...] = refs[k][...].T
            for i in range(rows_out // each):
                at = pl.multiple_of((2 * i + place_ref[2]) * each, 16)
                out_ref[i * each : (i + 1) * each, k * tokens : (k + 1) * tokens] = turned[pl.ds(at, each), :]

    return pl.pallas_call(
        body,
        grid_spec=pltpu.PrefetchScalarGridSpec(
            num_scalar_prefetch=1,
            grid=(1,),
            in_specs=[pl.BlockSpec((tokens, half), lambda i, place: (0, place[1]))] * count,
            out_specs=pl.BlockSpec((rows_out, count * tokens), lambda i, place: (0, 0)),
            scratch_shapes=[pltpu.VMEM((half, tokens), BF16)],
        ),
        out_shape=jax.ShapeDtypeStruct((rows_out, count * tokens), BF16),
        compiler_params=pltpu.CompilerParams(vmem_limit_bytes=VMEM_MAX),
        cost_estimate=work(5),
    )(place, *parts)


def mlp_weight_grads(place, n2_parts, first_hidden, cot_parts, acts, n2_rows, cot_rows, weights, at, size, each):
    groups = len(n2_parts)
    per = len(n2_parts[0])
    tokens, width = n2_parts[0][0].shape
    group = per * tokens
    both = group // 2
    rows = n2_rows[0].shape[0]
    flat_n = [p for g in n2_parts for p in g]
    flat_c = [p for g in cot_parts for p in g]
    total, total_c = (len(flat_n), len(flat_c))

    def body(place_ref, *refs):
        n_refs, c_refs, refs = (refs[:total], refs[total : total + total_c], refs[total + total_c :])
        gh_ref, wg_ref, wu_ref, wd_ref, hid_ref, gg_ref, gu_ref = refs[:7]
        n_rows, c_rows = (refs[7:11], refs[11:15])
        own_ref, rest_ref, n2_s, cot_s, acc, sem = refs[15:]

        def load(g, slot):
            found = []
            for i in range(per):
                to = pl.ds(i * tokens, tokens)
                found.append(pltpu.make_async_copy(n_refs[g * per + i], n2_s.at[slot, to], sem.at[slot, i]))
                if g > 0:
                    found.append(pltpu.make_async_copy(
                        c_refs[(g - 1) * per + i], cot_s.at[slot, to], sem.at[slot, per + i]))
            return found

        for copy in load(0, 0) + load(1, 1):
            copy.start()

        def add(g, act, fresh):
            fixed = isinstance(g, int)
            start = g * both if fixed else pl.multiple_of((g - 2) * both, both)
            for i, four in enumerate((c_rows, n_rows, n_rows)):
                mine, other = four[:2] if fixed else four[2:]
                part = dot(mine[:, pl.ds(start, both)], act[i][:both]) + dot(
                    other[:, pl.ds(start, both)], act[i][both:])
                if fresh:
                    acc[i] = part
                else:
                    acc[i] += part

        def recompute(g, slot, gh):
            gelu, slope = gelu_pair(dot(n2_s[slot], wg_ref[...]))
            up = dot(n2_s[slot], wu_ref[...])
            add(g + 1, ((gelu * up).astype(BF16), (gh * up * slope).astype(BF16), (gh * gelu).astype(BF16)), False)

        add(0, (hid_ref, gg_ref, gu_ref), True)
        for copy in load(0, 0):
            copy.wait()
        recompute(0, 0, gh_ref[...])

        def step(g, carry):
            slot = lax.rem(g, 2)
            for k in range(2, groups):
                @pl.when(g + 1 == k)
                def _():
                    for copy in load(k, k % 2):
                        copy.start()

            for copy in load(1, slot):
                copy.wait()
            recompute(g, slot, dot(cot_s[slot], wd_ref[...]))
            return carry

        lax.fori_loop(1, groups, step, 0)
        for j in range(rows // each):
            start = pl.multiple_of((place_ref[0] ^ j) * each, 8)
            for i in range(3):
                block = acc[i, pl.ds(start, each), :]
                if j == 0:
                    own_ref[:, i * size : (i + 1) * size] = block
                else:
                    rest_ref[(j - 1) * each : j * each, i * size : (i + 1) * size] = block.astype(BF16)

    index = at // size
    column = lambda n: pl.BlockSpec((n, size), lambda j, place: (0, index))
    whole = pl.BlockSpec(n2_rows[0].shape, lambda j, place: (0, 0))
    return pl.pallas_call(
        body,
        grid_spec=pltpu.PrefetchScalarGridSpec(
            num_scalar_prefetch=1,
            grid=(1,),
            in_specs=[ANY] * (total + total_c) + [column(group)] + [column(width)] * 3 + [column(group)] * 3
            + [whole] * 8,
            out_specs=[pl.BlockSpec((each, 3 * size), lambda j, place: (0, 0)),
                       pl.BlockSpec((rows - each, 3 * size), lambda j, place: (0, 0))],
            scratch_shapes=[
                pltpu.VMEM((2, group, width), BF16),
                pltpu.VMEM((2, group, width), BF16),
                pltpu.VMEM((3, rows, size), F32),
                pltpu.SemaphoreType.DMA((2, 2 * per)),
            ],
        ),
        out_shape=[jax.ShapeDtypeStruct((each, 3 * size), F32),
                   jax.ShapeDtypeStruct((rows - each, 3 * size), BF16)],
        compiler_params=pltpu.CompilerParams(vmem_limit_bytes=VMEM_MAX),
        cost_estimate=work(35 * size // 768),
    )(place, *flat_n, *flat_c, first_hidden, *weights, *acts, *n2_rows, *cot_rows)


def rows_by_device(place, parts, starts, block):
    columns, count = (len(parts), len(parts[0]))
    tokens, n = parts[0][0].shape
    rows = len(starts(0, 0)) * block
    flat = [block_of for column in parts for block_of in column]
    if block % 16:
        turned = [jnp.concatenate(column, axis=0).T for column in parts]
        turned = turned[0] if columns == 1 else jnp.where(
            place[2] == 0, jnp.concatenate(turned), jnp.concatenate(turned[::-1]))

        def taken(dc):
            return jnp.stack([
                jnp.concatenate([
                    lax.dynamic_slice_in_dim(turned, start, block, 0)
                    for start in starts(place[0] ^ dy, place[1] ^ dc)])
                for dy in range(2)])

        kept, sent = (taken(0), taken(1))
        return kept[0], sent[0], jnp.concatenate([kept[1], sent[1]], axis=0)

    def body(place_ref, *refs):
        keep_ref, send_ref, y_ref, turned = refs[len(flat):]
        for h in range(columns):
            base = 0 if columns == 1 else pl.multiple_of((place_ref[2] ^ h) * n, 16)
            for k in range(count):
                turned[pl.ds(base, n), k * tokens : (k + 1) * tokens] = refs[h * count + k][...].T
        for dy, dc, ref, at in ((0, 0, keep_ref, 0), (0, 1, send_ref, 0), (1, 0, y_ref, 0), (1, 1, y_ref, rows)):
            for i, start in enumerate(starts(place_ref[0] ^ dy, place_ref[1] ^ dc)):
                ref[at + i * block : at + (i + 1) * block, :] = turned[pl.ds(pl.multiple_of(start, 16), block), :]

    shape = (rows, count * tokens)
    return pl.pallas_call(
        body,
        grid_spec=pltpu.PrefetchScalarGridSpec(
            num_scalar_prefetch=1,
            grid=(1,),
            in_specs=[pl.BlockSpec((tokens, n), lambda i, place: (0, 0))] * len(flat),
            out_specs=[pl.BlockSpec((n_rows, shape[1]), lambda i, place: (0, 0)) for n_rows in (rows, rows, 2 * rows)],
            scratch_shapes=[pltpu.VMEM((columns * n, count * tokens), BF16)],
        ),
        out_shape=[jax.ShapeDtypeStruct((n_rows, shape[1]), BF16) for n_rows in (rows, rows, 2 * rows)],
        compiler_params=pltpu.CompilerParams(vmem_limit_bytes=VMEM_MAX),
        cost_estimate=work(3),
    )(place, *flat)


def joined_columns(pairs, total, before=None):
    rows = pairs[0][0].shape[0]
    widths = [a.shape[1] // 3 for a, _ in pairs]
    span = sum(widths)
    step = rows // 4 if rows % 64 == 0 else rows
    flat = [term for pair in pairs for term in pair]
    kept = [] if before is None else list(before)
    index = 0 if before is None else total // span - 1

    def body(*refs):
        refs = refs[len(kept) :]
        for i in range(3):
            at = 0
            for k, n in enumerate(widths):
                cols = slice(i * n, (i + 1) * n)
                refs[len(flat) + i][:, at : at + n] = refs[2 * k][:, cols].astype(F32) + refs[
                    2 * k + 1][:, cols].astype(F32)
                at += n

    return pl.pallas_call(
        body,
        grid=(rows // step,),
        in_specs=[ANY] * len(kept) + [pl.BlockSpec((step, term.shape[1]), lambda j: (j, 0)) for term in flat],
        out_specs=[pl.BlockSpec((step, span), lambda j: (j, index))] * 3,
        out_shape=[jax.ShapeDtypeStruct((rows, total), F32)] * 3,
        input_output_aliases={i: i for i in range(len(kept))},
        compiler_params=pltpu.CompilerParams(vmem_limit_bytes=VMEM_MAX),
        cost_estimate=work(5 if kept else 10),
    )(*kept, *flat)


def gate_weight_grad(place, conv, grad_in, grad_decay, block):
    tokens, n = conv.shape
    count = n // block // 2
    if block % 16:
        by_head = lambda v: v.reshape(tokens, n // BLK, BLK)
        blocks = jnp.einsum(
            "thi,thj->hij", by_head(conv), jnp.concatenate([by_head(grad_in), by_head(grad_decay)], 2),
            preferred_element_type=F32).reshape(count, 2, block, 2 * BLK)
        mine, theirs = [
            lax.dynamic_index_in_dim(blocks, core, 1, keepdims=False).reshape(n // 2, 2 * BLK)
            for core in (place[1], 1 - place[1])]
        return mine, theirs.astype(BF16)

    def body(place_ref, conv_ref, in_ref, decay_ref, keep_ref, away_ref, whole):
        for h in range(n // BLK):
            cols = slice(h * BLK, (h + 1) * BLK)
            turned = conv_ref[:, cols].T
            whole[cols, :BLK] = dot(turned, in_ref[:, cols])
            whole[cols, BLK:] = dot(turned, decay_ref[:, cols])
        for i in range(count):
            at = pl.multiple_of((2 * i + place_ref[1]) * block, 16)
            keep_ref[i * block : (i + 1) * block, :] = whole[pl.ds(at, block), :]
            at = pl.multiple_of((2 * i + 1 - place_ref[1]) * block, 16)
            away_ref[i * block : (i + 1) * block, :] = whole[pl.ds(at, block), :].astype(BF16)

    spec = pl.BlockSpec((tokens, n), lambda h, place: (0, 0))
    out = pl.BlockSpec((n // 2, 2 * BLK), lambda h, place: (0, 0))
    return pl.pallas_call(
        body,
        grid_spec=pltpu.PrefetchScalarGridSpec(
            num_scalar_prefetch=1,
            grid=(1,),
            in_specs=[spec] * 3,
            out_specs=[out, out],
            scratch_shapes=[pltpu.VMEM((n, 2 * BLK), F32)],
        ),
        out_shape=[jax.ShapeDtypeStruct((n // 2, 2 * BLK), F32), jax.ShapeDtypeStruct((n // 2, 2 * BLK), BF16)],
        compiler_params=pltpu.CompilerParams(vmem_limit_bytes=VMEM_MAX),
        cost_estimate=work(3),
    )(place, conv, grad_in, grad_decay)


def sum_of_dots(rows, values):
    count = len(rows)

    def body(*refs):
        total = dot(refs[0][...], refs[count][...])
        for k in range(1, count):
            total = total + dot(refs[k][...], refs[count + k][...])
        refs[2 * count][...] = total.astype(BF16)

    return pl.pallas_call(
        body,
        out_shape=jax.ShapeDtypeStruct((rows[0].shape[0], values[0].shape[1]), BF16),
        compiler_params=pltpu.CompilerParams(vmem_limit_bytes=VMEM_MAX),
        cost_estimate=work(5),
    )(*rows, *values)


def after(value, *others):
    return lax.optimization_barrier((value, others))[0]


class Live:
    def cut(self):
        names = sorted(vars(self))
        for name, value in zip(names, lax.optimization_barrier([getattr(self, n) for n in names])):
            setattr(self, name, value)

    def hold(self, **values):
        for name, value in values.items():
            setattr(self, name, value)
        self.cut()


def seq_bits(lay):
    found, bit = ([], 1)
    while bit < lay.seq:
        found.append(bit)
        bit *= 2
    return found


def scan_start(summary, groups):
    prod, state = (summary[:groups], summary[groups : 2 * groups])
    return (prod, state, jnp.ones_like(prod), jnp.zeros_like(state))


def scan_join(lay, held, other, bit, backward):
    prod, state, before_p, before_s = held
    groups = prod.shape[0]
    other_p, other_s = (other[:groups], other[groups:])
    is_later = (lay.seq_at & bit) != 0
    take = jnp.logical_not(is_later) if backward else is_later
    before_s = jnp.where(take, before_p * other_s + before_s, before_s)
    before_p = jnp.where(take, before_p * other_p, before_p)
    state = jnp.where(take, prod * other_s + state, other_p * state + other_s)
    return (prod * other_p, state, before_p, before_s)


def local(inputs, block_flags, decay_seed, vectors, in_y, in_x, gate_weight, out_proj,
          mlp_gate, mlp_up, mlp_down, cotangent):
    lay = Lay()
    nz, x, y, z, c = (lay.nz, lay.x, lay.y, lay.z, lay.c)
    tokens, width = inputs.shape[1:]
    half, quarter, two = (width // 2, width // 4, 2 * tokens)
    each = width // lay.seq
    own80 = each // 4
    bits = seq_bits(lay)
    place = jnp.stack([z % (nz // 2), lay.seq_at // nz, y]).astype(jnp.int32)
    at_yc = jnp.stack([y, c, x]).astype(jnp.int32)
    live = Live()

    def order_c(own, other, axis):
        return jnp.where(c == 0, jnp.concatenate([own, other], axis),
                         jnp.concatenate([other, own], axis))

    def order_f(rel):
        b = rel.shape[-1] // 4
        p = [rel[..., i * b : (i + 1) * b] for i in range(4)]
        by_c = jnp.where(c == 0, rel, jnp.concatenate([p[1], p[0], p[3], p[2]], -1))
        return jnp.where(x == 0, by_c, jnp.concatenate([by_c[..., 2 * b :], by_c[..., : 2 * b]], -1))

    def owner_parts(blocks):
        pick = lambda t: lax.dynamic_index_in_dim(blocks, t, 0, keepdims=False)
        come = [
            lay.send(pick((z + step) % nz), lambda z, y, x, c: ((z + step) % nz, y, x, c))
            for step in range(1, nz)
        ]
        return pick(z), come

    def total_of(own, come):
        total = own.astype(F32)
        for part in come:
            total = total + part.astype(F32)
        return total.astype(BF16)

    def half_of(value, which, n, axis):
        return lax.dynamic_slice_in_dim(value, which * n, n, axis)

    cot = cotangent[0]
    cut = tokens // 2
    gate_away, inputs, gate_weight, out_proj, vectors, decay_seed, block_flags = lax.optimization_barrier(
        (half_of(gate_weight, 1 - x, half, 0), inputs, gate_weight, out_proj, vectors, decay_seed, block_flags))
    halo_raw = lay.over_seq(inputs[0, tokens - 16 :], 1)
    gate_x = lay.over_x(gate_away)
    wx_c = lay.over_c(in_x)
    scaled_one, inverse_one = norm_scale(inputs[0].astype(F32))
    live.hold(n1=(scaled_one * vectors[0]).astype(BF16), inv1=inverse_one, halo_raw=halo_raw, cot_top=cot[:cut],
              cot_low=cot[cut:], wx_c=wx_c,
              params=(gate_weight, out_proj, vectors, decay_seed, block_flags))

    gate_weight, out_proj, vectors, decay_seed, block_flags = live.params
    n1_x = lay.over_x(live.n1)
    halo_own = (norm_scale(live.halo_raw.astype(F32))[0] * vectors[0]).astype(BF16)
    n_flags = block_flags.shape[1]
    flag_row = jnp.pad(block_flags.astype(BF16), ((0, 0), (0, width - n_flags)))
    halo_x = lay.over_x(jnp.concatenate([flag_row, halo_own[1:]], axis=0))
    gate_own = half_of(gate_weight, x, half, 0)
    gate_c = lay.over_c(gate_own)
    cot_z_top = lay.over_z(live.cot_top)
    base = -5.0 - decay_seed.astype(F32) + vectors[9]
    del live.params, live.halo_raw, live.cot_top
    live.hold(
        n1_x=n1_x, halo_x=halo_x, halo_own=halo_own, gate_x=gate_x, gate_c=gate_c, cot_z_top=cot_z_top,
        flags=jnp.concatenate([block_flags.astype(F32), halo_x[:1, :n_flags].astype(F32)], axis=0),
        gate_own=gate_own, out_away=half_of(out_proj, 2 * (1 - x) + y, quarter, 0),
        out_mine=half_of(out_proj, x, half, 0), vec=half_of(vectors, x, half, 1), gain_two=vectors[1],
        gain_one=vectors[0],
        rates=half_of(jnp.stack([jax.nn.softplus(base), jax.nn.sigmoid(base)]), x, half, 1))

    out_a = lay.over_x(live.out_away)
    cot_z_low, cot_y = (lay.over_z(live.cot_low), lay.over_y(after(cot, live.n1_x)))
    wy_c = lay.over_c(after(in_y, live.n1_x))
    gates = order_f(jnp.concatenate(
        [live.gate_own, live.gate_c, live.gate_x, lay.over_c(live.gate_x)], axis=1))
    normed = jnp.concatenate([live.n1, live.n1_x, live.halo_own, live.halo_x], axis=0)
    x_all = order_c(dot(normed, in_x).astype(BF16), dot(normed, live.wx_c).astype(BF16), 1)
    x_low = x_all[:two].reshape(2, tokens, half)
    halo = x_all[two:].reshape(2, 16, half)
    shape3 = lambda dt: jax.ShapeDtypeStruct((2, tokens, half), dt)
    summary_shape = jax.ShapeDtypeStruct((4, half), F32)
    conv_low, ig, dg, prods, local_state, summary = by_head(
        mixer_forward, live.flags,
        [(x_low, False), (halo, False), (gates, True), (live.vec, False), (live.rates, False)],
        [shape3(BF16), shape3(F32), shape3(F32), shape3(F32), shape3(F32), summary_shape])
    del live.gate_x, live.gate_own, live.gate_c, live.halo_own, live.halo_x
    live.hold(x_low=x_low, halo=halo, gates=gates, conv_low=conv_low, ig=ig, dg=dg, prods=prods,
              local_state=local_state, scan=scan_start(summary, 2), cot_y=cot_y, normed=normed[:two], wy_c=wy_c, out_a=out_a,
              cot_z_low=cot_z_low)
    del live.cot_low
    del live.out_away

    def n1_starts(at_y, at_c):
        return [((2 * i + at_y) * 4 + 2 * j + at_c) * own80 for i in range(nz) for j in range(2)]

    for bit in bits:
        come = lay.over_seq_bit(jnp.concatenate(live.scan[:2], axis=0), bit)
        live.scan = scan_join(lay, live.scan, come, bit, False)
        if bit == 1:
            live.cut()
            out_b = lay.over_y(live.out_a)
            out_c = lay.over_c(live.out_mine)
            cot_x = lay.over_x(after(cot, live.scan))
    out_x = jnp.where(y == 0, jnp.concatenate([live.out_a, out_b], 0), jnp.concatenate([out_b, live.out_a], 0))
    y_pre = order_c(dot(live.normed, in_y), dot(live.normed, live.wy_c), 1).reshape(2, tokens, half)
    n1_own, sent, n1_away = rows_by_device(
        at_yc, [after([live.n1, live.n1_x], live.scan[3])], n1_starts, own80)
    state_in = live.scan[3]
    del live.scan, live.out_a
    live.hold(state_in=state_in, y_pre=y_pre, out_left=jnp.concatenate([live.out_mine, out_c], axis=1),
              cot_z=jnp.concatenate([live.cot_z_top, live.cot_z_low], axis=0),
              out_x=out_x, cot_x=cot_x, n1_own=n1_own, n1_away=n1_away, n1_c=lay.over_c(sent))
    del live.out_mine, live.cot_z_top, live.cot_z_low

    n1_y = lay.over_y(live.n1_away[: live.n1_own.shape[0]])
    state = live.local_state + live.prods * live.state_in[:, None, :]
    mixed = (state * jax.nn.gelu(live.y_pre, approximate=True)).astype(BF16)
    mixed_two = mixed.reshape(two, half)
    out_right = jnp.concatenate([live.out_x, lay.over_c(live.out_x)], axis=1)
    part = jnp.concatenate([dot(mixed_two, live.out_left), dot(mixed_two, out_right)], axis=1)
    del live.out_x
    live.hold(mixed=mixed, part_own=part[:tokens], part_x=part[tokens:].astype(BF16), out_right=out_right, n1_y=n1_y)

    part_x = lay.over_x(live.part_x)
    cot_xy = lay.over_y(live.cot_x)
    gh_main = grad_hidden_of([cot, live.cot_x, lay.over_c(cot), lay.over_c(live.cot_x)], mlp_down)
    live.hold(part_x=part_x, gh_main=gh_main, cot_xy=cot_xy)

    swapped = jnp.concatenate([live.part_x[:, half:], live.part_x[:, :half]], axis=1)
    mid = inputs[0].astype(F32) + order_f(live.part_own + swapped.astype(F32))
    scaled_two, inverse_two = norm_scale(mid)
    del live.part_x, live.part_own
    live.hold(mid=mid, inv2=inverse_two, n2=(scaled_two * live.gain_two).astype(BF16))

    n2_x = lay.over_x(live.n2)
    n2_y = lay.over_y(live.n2)
    n2_z_top = lay.over_z(live.n2[:cut])
    n2_c = lay.over_c(live.n2)
    pair = [live.cot_y, live.cot_xy]
    gh_y = grad_hidden_of(pair + [lay.over_c(p) for p in pair], mlp_down)
    live.hold(n2_x=n2_x, n2_c=n2_c, n2_y=n2_y, n2_z_top=n2_z_top, gh_y=gh_y)

    live.hold(n2_xc=lay.over_c(live.n2_x), n2_low=live.n2[cut:], n2_x_top=live.n2_x[:cut], n2_x_low=live.n2_x[cut:])
    cot_xz = lay.over_x(live.cot_z)
    n2_xy = lay.over_y(live.n2_x)
    n2_z_low = lay.over_z(live.n2_low)
    hidden, grad_gate, grad_up, far, far_c = mlp_forward(
        [live.n2, live.n2_x, live.n2_c, live.n2_xc], live.gh_main, mlp_gate, mlp_up)
    del live.gh_main, live.n2_c
    live.hold(acts=(hidden, grad_gate, grad_up), far=far, far_c=far_c, cot_xz=cot_xz, n2_xy=n2_xy,
              n2_z_low=n2_z_low)
    live.hold(far=(live.far + lay.over_c(live.far_c).astype(F32)).astype(BF16),
              n2_z=jnp.concatenate([live.n2_z_top, live.n2_z_low], axis=0))

    arriving = lay.over_x(live.far)
    n2_yz, n2_y_c, n2_xy_c = (lay.over_y(live.n2_z), lay.over_c(live.n2_y), lay.over_c(live.n2_xy))
    n2_xz_top = lay.over_z(live.n2_x_top)
    near, near_c, out, out_c = mlp_rest(*live.acts, mlp_gate, mlp_up, mlp_down, tokens)
    del live.far, live.far_c, live.n2_z_top, live.n2_z_low
    live.hold(arriving=arriving, near=near, near_c=near_c, out=out, out_c=out_c, n2_yz=n2_yz, n2_y_c=n2_y_c, n2_xy_c=n2_xy_c, n2_xz_top=n2_xz_top)

    out_c = lay.over_c(live.out_c)
    grad_n2 = live.near + lay.over_c(live.near_c).astype(F32) + live.arriving.astype(F32)
    grad_mid_norm, grad_gain_two = norm_back(grad_n2, live.mid * live.inv2, live.inv2, live.gain_two)
    grad_mid = cot.astype(F32) + grad_mid_norm
    branch = grad_mid.astype(BF16)
    live.out_c = out_c
    del live.near, live.near_c, live.arriving
    live.hold(grad_gain_two=grad_gain_two, grad_mid=grad_mid, branch=branch, branch_rel=order_f(branch))

    arriving = lay.over_x(live.branch_rel)
    n2_xz_low = lay.over_z(live.n2_x_low)
    cot_yz = lay.over_y(live.cot_z)
    live.hold(arriving=arriving, n2_xz_low=n2_xz_low, cot_yz=cot_yz, out_sum=live.out + live.out_c.astype(F32),
              n2_z_c=lay.over_c(live.n2_z), cot_z_c=lay.over_c(live.cot_z),
              n2_rows_ahead=rows_of_tokens(place, [live.n2, live.n2_x, live.n2_y, live.n2_xy], half // 2, each),
              cot_rows_ahead=rows_of_tokens(place, [cot, live.cot_x, live.cot_y, live.cot_xy], half // 2, each))

    rows_each = live.n1_own.shape[0]
    n1_yc = lay.over_y(live.n1_away[rows_each:])
    cot_xz_c, n2_yz_c = (lay.over_c(live.cot_xz), lay.over_c(live.n2_yz))
    mixed_xa = lay.over_x(live.mixed[1])
    branch_x_rel = jnp.concatenate([live.arriving[:, half:], live.arriving[:, :half]], axis=1)
    both_rel = jnp.concatenate([live.branch_rel, branch_x_rel], 0)
    grad_mixed = dot_cols(both_rel[:, :half], live.out_left) + dot_cols(both_rel[:, half:], live.out_right)
    gy, bprod, blocal, back_summary = by_head(
        mixer_back_scan, live.flags,
        [(grad_mixed.reshape(2, tokens, half), False), (live.y_pre, False), (live.dg, False),
         (live.prods, False), (live.local_state, False), (live.state_in, False), (live.rates, False)],
        [shape3(BF16), shape3(F32), shape3(F32), summary_shape])
    del live.arriving, live.branch_rel, live.y_pre
    live.hold(gy=gy.reshape(two, half), bprod=bprod, blocal=blocal, scan=scan_start(back_summary, 2),
              branch_x_rel=branch_x_rel, n1_yc=n1_yc, cot_xz_c=cot_xz_c, n2_yz_c=n2_yz_c,
              mixed_xa=mixed_xa, mixed_b=live.mixed[0])

    n2_xyz = lay.over_x(live.n2_yz)
    own_cols = lambda value, which: half_of(value, which, quarter, 1)
    part_y = dot_cols(own_cols(live.gy, c), in_y) + dot_cols(own_cols(live.gy, 1 - c), live.wy_c)
    for bit in bits:
        come = lay.over_seq_bit(jnp.concatenate(live.scan[:2], axis=0), bit)
        live.scan = scan_join(lay, live.scan, come, bit, True)
        if bit == 1:
            live.cut()
            cot_xyz = lay.over_y(live.cot_xz)
            cot_yz_c = lay.over_c(live.cot_yz)
    back_in = live.scan[3]
    del live.scan
    live.hold(back_in=back_in, cot_xyz=cot_xyz, n2_xyz=n2_xyz, part_y=part_y, cot_yz_c=cot_yz_c)

    live.ahead_c = (lay.over_c(live.n2_rows_ahead), lay.over_c(live.cot_rows_ahead))
    live.n1_yc = lay.over_c(live.n1_yc)
    gip, gdp, gx_main, gx_tail, edge, vec_rows = by_head(
        mixer_backward, live.flags,
        [(live.bprod, False), (live.blocal, False), (live.back_in, False), (live.prods, False),
         (live.local_state, False), (live.state_in, False), (live.ig, False), (live.dg, False),
         (live.conv_low, False), (live.x_low, False), (live.halo, False), (live.gates, True),
         (live.vec, False), (live.rates, False)],
        [shape3(BF16), shape3(BF16), shape3(BF16), jax.ShapeDtypeStruct((2, 16, half), F32),
         jax.ShapeDtypeStruct((2, 8, half), F32), jax.ShapeDtypeStruct((8, half), F32)])
    for name in ("bprod", "blocal", "back_in", "prods", "local_state", "state_in", "ig", "dg", "x_low", "halo",
                 "gates", "vec", "rates", "flags"):
        delattr(live, name)
    live.hold(gip=gip, gdp=gdp, gx_main=gx_main, gx_tail=gx_tail, edge=edge, vec_rows=vec_rows)

    edge_next = lay.over_seq(live.edge, -1)
    mixed_xb = lay.over_x(live.mixed_b)
    n2_xz = jnp.concatenate([live.n2_xz_top, live.n2_xz_low], axis=0)
    n2_xz_c, n2_xyz_c, cot_xyz_c = (lay.over_c(n2_xz), lay.over_c(live.n2_xyz), lay.over_c(live.cot_xyz))
    live.n2s = [[live.n2, live.n2_x], [live.n2_y, live.n2_xy], [live.n2_z, n2_xz], [live.n2_yz, live.n2_xyz]]
    live.cots = [cot, live.cot_x, live.cot_y, live.cot_xy, live.cot_z, live.cot_xz, live.cot_yz, live.cot_xyz]
    n2_rows = rows_of_tokens(place, [p for group in live.n2s[2:] for p in group], half // 2, each)
    cot_rows = rows_of_tokens(place, live.cots[4:], half // 2, each)
    del live.edge
    live.hold(edge_next=edge_next, n2_rows=n2_rows, cot_rows=cot_rows,
              n2s_c=[[live.n2_y_c, live.n2_xy_c], [live.n2_z_c, n2_xz_c], [live.n2_yz_c, n2_xyz_c]],
              cots_c=[live.cot_z_c, live.cot_xz_c, live.cot_yz_c, cot_xyz_c], mixed_xb=mixed_xb)

    gx_last = (live.gx_tail + jnp.pad(live.edge_next, ((0, 0), (8, 0), (0, 0)))).astype(BF16)
    gx = jnp.concatenate([live.gx_main[:, : tokens - 16], gx_last], axis=1).reshape(two, half)
    gx_o, gx_c = (own_cols(gx, c), own_cols(gx, 1 - c))
    part_n1 = live.part_y + dot_cols(gx_o, in_x) + dot_cols(gx_c, live.wx_c)
    del live.gx_main, live.gx_tail, live.edge_next, live.part_y
    live.hold(gx=gx, n1_near=part_n1[:tokens], n1_far=part_n1[tokens:].astype(BF16),
              n2_rows_c=lay.over_c(live.n2_rows), cot_rows_c=lay.over_c(live.cot_rows))

    cuts = sections_of(mlp_gate.shape[1])

    def weight_piece(at, size):
        return mlp_weight_grads(
            place, [a + b for a, b in zip(live.n2s[1:], live.n2s_c)], live.gh_y,
            [live.cots[4:6] + live.cots_c[:2], live.cots[6:] + live.cots_c[2:]], live.acts,
            (live.n2_rows_ahead, live.ahead_c[0], live.n2_rows, live.n2_rows_c),
            (live.cot_rows_ahead, live.ahead_c[1], live.cot_rows, live.cot_rows_c),
            (mlp_gate, mlp_up, mlp_down), at, size, each)

    def piece_sum(own, rest):
        blocks = [own] + [rest[j * each : (j + 1) * each] for j in range(nz // 2 - 1)]
        bit = nz // 4
        while bit >= 1:
            gone = blocks[bit] if bit == 1 else jnp.concatenate(
                [b.astype(BF16) for b in blocks[bit : 2 * bit]], axis=0)
            come = lay.over_seq_bit(gone.astype(BF16), 2 * bit)
            blocks = [(blocks[j], come[j * each : (j + 1) * each]) for j in range(bit)]
            if bit > 1:
                blocks = [a.astype(F32) + b.astype(F32) for a, b in blocks]
            bit //= 2
        return blocks[0]

    arriving = lay.over_x(live.n1_far)
    gy_y = lay.over_y(live.gy)
    live.gy_c = lay.over_c(live.gy)
    live.hold(piece_a=weight_piece(*cuts[0]), arriving=arriving, gy_y=gy_y)

    grad_n1 = live.n1_near + live.arriving.astype(F32)
    scaled_one = inputs[0].astype(F32) * live.inv1
    grad_in_norm, grad_gain_one = norm_back(grad_n1, scaled_one, live.inv1, live.gain_one)
    input_grad = (live.grad_mid + grad_in_norm).astype(BF16)[None]
    rows_full = lax.dynamic_update_slice_in_dim(
        jnp.zeros((8, width), F32), live.vec_rows, x * half, 1)
    sums = jnp.concatenate([grad_gain_one[None], live.grad_gain_two[None], rows_full], axis=0)
    sums = sums + lay.over_c(sums)
    del live.n1_near, live.n1_far, live.arriving, live.vec_rows, live.grad_gain_two, live.grad_mid
    branch_far = half_of(order_f(live.branch_x_rel), x, half, 1)
    branch_near = half_of(live.branch, x, half, 1)
    del live.branch_x_rel
    live.hold(sums=sums, gy_yc=lay.over_c(live.gy_y), branch_two=jnp.concatenate([branch_near, branch_far], axis=0))

    def over_columns(value):
        split = value.reshape(2, own80, half)
        mine = lax.dynamic_index_in_dim(split, x, 0, keepdims=False)
        theirs = lay.over_x(lax.dynamic_index_in_dim(split, 1 - x, 0, keepdims=False))
        return jnp.where(x == 0, jnp.concatenate([mine, theirs], -1),
                         jnp.concatenate([theirs, mine], -1)).astype(F32)

    sums = live.sums + lay.over_x(live.sums)
    branch_two_y = lay.over_y(live.branch_two)
    sum_a = piece_sum(*live.piece_a)
    n1_all = [live.n1_own, live.n1_c, live.n1_y, live.n1_yc]
    in_y_part = sum_of_dots(n1_all, [live.gy, live.gy_c, live.gy_y, live.gy_yc])
    gate_part, gate_away = gate_weight_grad(
        at_yc, live.conv_low.reshape(two, half), live.gip.reshape(two, half), live.gdp.reshape(two, half), own80)
    gate_part = (gate_part + lay.over_c(gate_away).astype(F32)).reshape(2, nz, own80, 2 * BLK)
    pick = lambda value, at, axis: lax.dynamic_index_in_dim(value, at, axis, keepdims=False)
    gate_y = lay.over_y(pick(gate_part, 1 - y, 0).astype(BF16))
    mixed_own, sent, mixed_away = rows_by_device(
        at_yc, [[live.mixed[0], live.mixed[1]], [live.mixed_xa, live.mixed_xb]], n1_starts, own80)
    del live.gy, live.gy_c, live.gy_y, live.gy_yc, live.mixed, live.mixed_xa, live.mixed_xb, live.conv_low, live.gip, live.gdp
    live.hold(in_y_part=in_y_part, sums=sums, sum_a=sum_a, branch_two_y=branch_two_y, gate_keep=pick(gate_part, y, 0), gate_y=gate_y,
              mixed_own=mixed_own, mixed_away=mixed_away, mixed_c=lay.over_c(sent),
              gx_c=lay.over_c(live.gx), branch_c=lay.over_c(live.branch_two))

    in_y_own, in_y_come = owner_parts(live.in_y_part.reshape(nz, 2 * own80, half))
    gx_y = lay.over_y(live.gx)
    mixed_y = lay.over_y(live.mixed_away)
    piece_b = weight_piece(*cuts[1])
    del live.piece_a, live.mixed_away
    del live.in_y_part
    live.hold(piece_b=piece_b, gx_y=gx_y, mixed_y=mixed_y, in_y_own=in_y_own, in_y_come=in_y_come)

    sum_b = piece_sum(*live.piece_b)
    sums = live.sums
    for bit in bits[:1]:
        sums = sums + lay.over_seq_bit(sums, bit)
    in_x_part = sum_of_dots(n1_all, [live.gx, live.gx_c, live.gx_y, lay.over_c(live.gx_y)])
    out_part = sum_of_dots(
        [live.mixed_own, live.mixed_c, live.mixed_y[:rows_each], lay.over_c(live.mixed_y[rows_each:])],
        [live.branch_two, live.branch_c, live.branch_two_y, lay.over_c(live.branch_two_y)])
    gate_part = (live.gate_keep + live.gate_y.astype(F32)).astype(BF16)
    del live.piece_b, live.gate_keep, live.gate_y, live.mixed_own, live.mixed_c, live.mixed_y
    live.hold(in_x_part=jnp.concatenate(
        [in_x_part.reshape(nz, 2 * own80, half), gate_part.reshape(nz, own80 * 2 * BLK // half, half)], axis=1),
        out_part=out_part, sum_b=sum_b, sums=sums, in_y_total=total_of(live.in_y_own, live.in_y_come),
        out_far=live.out_sum[tokens:].astype(BF16))
    del live.in_y_own, live.in_y_come

    in_x_own, in_x_come = owner_parts(live.in_x_part)
    out_arriving = lay.over_x(live.out_far)
    sums_z = lay.over_seq_bit(live.sums, 2)
    piece_c = weight_piece(*cuts[2])
    del live.in_x_part
    live.hold(piece_c=piece_c, in_x_own=in_x_own, in_x_come=in_x_come, out_arriving=out_arriving,
              sums=live.sums + sums_z)

    sum_c = piece_sum(*live.piece_c)
    out_own, out_come = owner_parts(live.out_part.reshape(nz, 2 * own80, half))
    in_x_own, in_x_come, in_y_total = after((live.in_x_own, live.in_x_come, live.in_y_total), out_come[1])
    in_x_total = total_of(in_x_own, in_x_come)
    mlp_grads = joined_columns([live.sum_a, live.sum_b], mlp_gate.shape[1])
    live.hold(sum_c=sum_c, mlp_grads=mlp_grads, out_total=total_of(out_own, out_come),
              in_y_grad=over_columns(in_y_total), in_x_grad=over_columns(in_x_total[: 2 * own80]),
              gate_total=in_x_total[2 * own80 :].reshape(own80, 2 * BLK),
              output=(live.mid + after(live.out_sum, out_come[1])[:tokens] + live.out_arriving.astype(F32)
                      ).astype(BF16)[None])

    sums = live.sums
    for bit in bits[2:]:
        sums = sums + lay.over_seq_bit(sums, bit)
    mlp_down_grad, mlp_gate_grad, mlp_up_grad = joined_columns(
        [live.sum_c], mlp_gate.shape[1], live.mlp_grads)

    def final(z, y, x, c):
        at = ((x * 2 + y) * nz + z) * 2 + c
        s, f = (at // 4, at % 4)
        return (s // 2, s % 2, f // 2, f % 2)

    out_grad = over_columns(live.out_total)
    gate_grad = lay.send(live.gate_total, final).astype(F32)
    return (live.output, input_grad, sums, live.in_y_grad, live.in_x_grad, gate_grad, out_grad,
            mlp_gate_grad, mlp_up_grad, mlp_down_grad)


def solution(mesh):
    return jax.shard_map(
        local,
        mesh=mesh,
        in_specs=(
            P("fsdp", "seq", None),
            P("fsdp", "seq"),
            P(),
            P(),
            P(None, "fsdp"),
            P(None, "fsdp"),
            P(None, "fsdp"),
            P(None, "fsdp"),
            P(None, "fsdp"),
            P(None, "fsdp"),
            P(None, "fsdp"),
            P("fsdp", "seq", None),
        ),
        out_specs=(
            P("fsdp", "seq", None),
            P("fsdp", "seq", None),
            P(),
            P(("seq", "fsdp"), None),
            P(("seq", "fsdp"), None),
            P(("seq", "fsdp"), None),
            P(("seq", "fsdp"), None),
            P("seq", "fsdp"),
            P("seq", "fsdp"),
            P("seq", "fsdp"),
        ),
        check_vma=False,
    )
```
